32 devices in a mesh: dp: 4 (over x, core), ctx: 2 (over y), fsdp: 4 (over z).
Axes of the slice: x: 2, y: 2, z: 4, core: 2. Of those that a mesh axis runs over, the one named last changes fastest.
Arguments:
- tokens: float32 [4, 1024, 768], P('dp', ('ctx', 'fsdp')), may hold values from -6 to 6
- cotangent: float32 [4, 1024, 768], P('dp', ('ctx', 'fsdp')), may hold values from -6 to 6
- ln1_gain: float32 [768], P(('dp', 'fsdp')), may hold values from 0.5 to 1.5
- ln1_bias: float32 [768], P(('dp', 'fsdp')), may hold values from -3 to 3
- qkv_weight: float32 [768, 2304], P(('dp', 'fsdp')), may hold values from -0.3125 to 0.3125
- q_bias: float32 [768], P(('dp', 'fsdp')), may hold values from -4 to 4
- v_bias: float32 [768], P(('dp', 'fsdp')), may hold values from -4 to 4
- out_weight: float32 [768, 768], P(('dp', 'fsdp')), may hold values from -1.75 to 1.75
- out_bias: float32 [768], P(('dp', 'fsdp')), may hold values from -4 to 4
- ln2_gain: float32 [768], P(('dp', 'fsdp')), may hold values from 0.5 to 1.5
- ln2_bias: float32 [768], P(('dp', 'fsdp')), may hold values from -3 to 3
- fc1_weight: float32 [768, 3072], P(('dp', 'fsdp')), may hold values from -0.21875 to 0.21875
- fc1_bias: float32 [3072], P(('dp', 'fsdp')), may hold values from -4 to 4
- fc2_weight: float32 [3072, 768], P(('dp', 'fsdp')), may hold values from -0.109375 to 0.109375
- fc2_bias: float32 [768], P(('dp', 'fsdp')), may hold values from -4 to 4
Outputs:
- output: float32 [4, 1024, 768], P('dp', ('ctx', 'fsdp'))
- input_grad: float32 [4, 1024, 768], P('dp', ('ctx', 'fsdp'))
- ln1_gain_grad: float32 [768], P(('dp', 'fsdp'))
- ln1_bias_grad: float32 [768], P(('dp', 'fsdp'))
- qkv_weight_grad: float32 [768, 2304], P(('dp', 'fsdp'))
- q_bias_grad: float32 [768], P(('dp', 'fsdp'))
- v_bias_grad: float32 [768], P(('dp', 'fsdp'))
- out_weight_grad: float32 [768, 768], P(('dp', 'fsdp'))
- out_bias_grad: float32 [768], P(('dp', 'fsdp'))
- ln2_gain_grad: float32 [768], P(('dp', 'fsdp'))
- ln2_bias_grad: float32 [768], P(('dp', 'fsdp'))
- fc1_weight_grad: float32 [768, 3072], P(('dp', 'fsdp'))
- fc1_bias_grad: float32 [3072], P(('dp', 'fsdp'))
- fc2_weight_grad: float32 [3072, 768], P(('dp', 'fsdp'))
- fc2_bias_grad: float32 [768], P(('dp', 'fsdp'))
The draws below stay inside these ranges and needn't reach their ends.
All inputs are finite; a program needn't handle non-finite values.
Results may differ from the reference program's by a relative error of at most 0.02.
Values may be sent and summed in bfloat16 or wider, within the bound.
No kernel may reach another device: no remote copies, remote signals or barrier semaphores. Data moves between devices by JAX's collectives and lax.ppermute only.
A program may use at most 256 MiB of HBM per device.

```python
import math
import jax
import jax.numpy as jnp
from jax import lax

D = 768
HEADS = 12
HEAD_DIM = 64
FF = 3072
SEQS = 4
SEQ_LEN = 1024


def strengthened(array, rng, source, target, shards_of, factor):
    owner, partner = [(jnp.arange(array.shape[axis_at]) // (array.shape[axis_at] // shards_of)).reshape([-1 if axis == axis_at else 1 for axis in range(array.ndim)]) for axis_at in (source, target)]
    chosen = jax.random.permutation(rng, shards_of)[partner]
    strong = (owner == chosen) | (owner == (partner + shards_of // 2) % shards_of)
    return jnp.where(strong, factor * array, array)


def steps_of(own_key, extent, pieces, smallest, top_value):
    factor_of = 1.0
    for axis_at, blocks in pieces:
        steps = jax.random.uniform(jax.random.fold_in(jax.random.fold_in(own_key, 6), axis_at), (blocks,), jnp.float32, smallest / len(pieces), top_value / len(pieces))
        factor_of = factor_of * jnp.repeat(jnp.exp(steps), extent[axis_at] // blocks).reshape((-1,) + (1,) * (len(extent) - 1 - axis_at))
    return factor_of


def noise(key, dims, deviation, most, pieces=(), held_as=jnp.bfloat16):
    loudness = steps_of(key, dims, pieces, -0.22, 0.18) if pieces else 1.0
    values = jax.random.normal(key, dims, jnp.float32) * deviation * loudness
    return jnp.minimum(jnp.maximum(values, -most), most).astype(held_as)


def gaussian_with(own_key, shape, scale, limit, pieces, heavy, held_as=jnp.bfloat16):
    entries = scale * jax.random.normal(own_key, shape, jnp.float32)
    if pieces:
        entries = entries * steps_of(own_key, shape, pieces, -0.22, 0.18)
    return jnp.clip(strengthened(entries, jax.random.fold_in(own_key, 3), *heavy), -limit, limit).astype(held_as)


def setup_inputs(seed: int = 0) -> dict:
    splits = jax.random.split(jax.random.key(seed), 16)
    return {
        "tokens": noise(splits[0], (SEQS, SEQ_LEN, D), 1.0, 6.0, ((0, 4), (1, 8)), jnp.float32),
        "cotangent": gaussian_with(splits[1], (SEQS, SEQ_LEN, D), 1.0, 6.0, ((0, 4), (1, 8)), (1, 2, 8, 2.0), jnp.float32),
        "ln1_gain": jnp.clip(1.0 + 0.1 * jax.random.normal(splits[2], (D,), jnp.float32), 0.5, 1.5),
        "ln1_bias": noise(splits[3], (D,), 0.3, 3.0, ((0, 16),), jnp.float32),
        "qkv_weight": noise(splits[4], (D, 3 * D), (D // 2) ** -0.5, 0.3125, ((0, 16),), jnp.float32),
        "q_bias": noise(splits[5], (D,), 0.5, 4.0, ((0, 16),), jnp.float32),
        "v_bias": noise(splits[6], (D,), 0.5, 4.0, ((0, 16),), jnp.float32),
        "out_weight": noise(splits[7], (D, D), (D // 64) ** -0.5, 1.75, ((0, 16),), jnp.float32),
        "out_bias": noise(splits[8], (D,), 0.8, 4.0, ((0, 16),), jnp.float32),
        "ln2_gain": jnp.clip(1.0 + 0.1 * jax.random.normal(splits[9], (D,), jnp.float32), 0.5, 1.5),
        "ln2_bias": noise(splits[10], (D,), 0.3, 3.0, ((0, 16),), jnp.float32),
        "fc1_weight": noise(splits[11], (D, FF), D ** -0.5, 0.21875, ((0, 16),), jnp.float32),
        "fc1_bias": noise(splits[12], (FF,), 0.5, 4.0, ((0, 16),), jnp.float32),
        "fc2_weight": noise(splits[13], (FF, D), FF ** -0.5, 0.109375, ((0, 16),), jnp.float32),
        "fc2_bias": noise(splits[14], (D,), 0.8, 4.0, ((0, 16),), jnp.float32),
    }


@jax.custom_vjp
def low(v):
    return lax.optimization_barrier(v.astype(jnp.bfloat16)).astype(jnp.float32)

@jax.custom_vjp
def low_back(v):
    return v

def low_keep(v):
    return (low(v), None)

def low_pass(kept, grad):
    return (grad,)

def back_keep(v):
    return (v, None)

def back_low(kept, grad):
    return (low(grad),)
low.defvjp(low_keep, low_pass)
low_back.defvjp(back_keep, back_low)
EPSILON = 1e-05

def matmul(left, right):
    return jnp.dot(left, right, preferred_element_type=jnp.float32, precision=lax.Precision.HIGHEST)

def layer_norm(values, norm_gain, norm_shift):
    centered = values - lax.optimization_barrier(jnp.mean(values, axis=-1, keepdims=True))
    spread = lax.optimization_barrier(jnp.mean(centered * centered, axis=-1, keepdims=True))
    return centered * lax.rsqrt(spread + EPSILON) * norm_gain + norm_shift

def attend_whole(triple):
    queries, key_rows, value_rows = triple
    length = queries.shape[0]
    block_rows = math.gcd(length, 512)
    query_blocks = queries.reshape(length // block_rows, block_rows, HEADS, HEAD_DIM)
    key_heads = key_rows.reshape(length, HEADS, HEAD_DIM)
    value_heads = value_rows.reshape(length, HEADS, HEAD_DIM)
    positions = jnp.arange(length, dtype=jnp.int32)
    score_scale = HEAD_DIM ** (-0.5)

    def attend_block(pair):
        block_queries, block_start = pair
        raw_scores = jnp.einsum('qhd,khd->hqk', block_queries, key_heads, precision=lax.Precision.HIGHEST, preferred_element_type=jnp.float32)
        scores = low_back(raw_scores) * score_scale
        query_pos = block_start + jnp.arange(block_rows, dtype=jnp.int32)
        visible = positions[None, :] <= query_pos[:, None]
        scores = jnp.where(visible[None], scores, -1e+30)
        highest = lax.optimization_barrier(jnp.max(scores, axis=-1, keepdims=True))
        exponent = jnp.exp(scores - highest)
        normalized = exponent / lax.optimization_barrier(jnp.sum(exponent, axis=-1, keepdims=True))
        return jnp.einsum('hqk,khd->qhd', low(normalized), value_heads, precision=lax.Precision.HIGHEST, preferred_element_type=jnp.float32)
    block_starts = jnp.arange(length // block_rows, dtype=jnp.int32) * block_rows
    attended = lax.map(jax.checkpoint(attend_block), (query_blocks, block_starts))
    return attended.reshape(length, D)

def forward(tokens, ln1_gain, ln1_bias, qkv_weight, q_bias, v_bias, out_weight, out_bias, ln2_gain, ln2_bias, fc1_weight, fc1_bias, fc2_weight, fc2_bias):
    seq_count = tokens.shape[0]
    length = tokens.shape[1]
    token_rows = tokens.reshape(seq_count * length, D)
    norm1 = layer_norm(token_rows, low(ln1_gain), low(ln1_bias))
    projected = matmul(low(norm1), low(qkv_weight))
    queries = low(low_back(projected[:, :D] + low(q_bias)))
    key_rows = low(low_back(projected[:, D:2 * D]))
    value_rows = low(low_back(projected[:, 2 * D:] + low(v_bias)))
    context = lax.map(attend_whole, (queries.reshape(seq_count, length, D), key_rows.reshape(seq_count, length, D), value_rows.reshape(seq_count, length, D)))
    context16 = low(low_back(context.reshape(seq_count * length, D)))
    mixed = token_rows + low_back(matmul(context16, low(out_weight)) + low(out_bias))
    norm2 = layer_norm(mixed, low(ln2_gain), low(ln2_bias))
    inner = low_back(matmul(low(norm2), low(fc1_weight)) + low(fc1_bias))
    hidden = low(jax.nn.gelu(inner))
    result = mixed + low_back(matmul(hidden, low(fc2_weight)) + low(fc2_bias))
    return result.reshape(seq_count, length, D)

def reference(tokens, cotangent, ln1_gain, ln1_bias, qkv_weight, q_bias, v_bias, out_weight, out_bias, ln2_gain, ln2_bias, fc1_weight, fc1_bias, fc2_weight, fc2_bias):
    output, pullback = jax.vjp(forward, tokens, ln1_gain, ln1_bias, qkv_weight, q_bias, v_bias, out_weight, out_bias, ln2_gain, ln2_bias, fc1_weight, fc1_bias, fc2_weight, fc2_bias)
    gradients = pullback(cotangent)
    return (output, gradients[0], gradients[1], gradients[2], gradients[3], gradients[4], gradients[5], gradients[6], gradients[7], gradients[8], gradients[9], gradients[10], gradients[11], gradients[12], gradients[13])
```

```python
import functools

import jax
import jax.numpy as jnp
from jax import lax
from jax.experimental import pallas as pl
from jax.experimental.pallas import tpu as pltpu
from jax.sharding import PartitionSpec as P

HEAD_DIM = 64
EPSILON = 1e-05
SCALE = HEAD_DIM ** (-0.5)
MASKED = -1e30
CHUNK = 64
LOW = jnp.bfloat16
WIDE = jnp.float32


def swap(value, axis, bit):
    count = lax.axis_size(axis)
    return lax.ppermute(value, axis, [(at, at ^ bit) for at in range(count)])


def shift(value, axis, by):
    count = lax.axis_size(axis)
    return lax.ppermute(value, axis, [(at, (at + by) % count) for at in range(count)])


def transpose_homes(value):
    side = lax.axis_size("dp")
    pairs = [(a * side + b, b * side + a) for a in range(side) for b in range(side)]
    return lax.ppermute(value, ("dp", "fsdp"), pairs)


def slot_order(count):
    order = [0]
    bit = count // 2
    while bit:
        order = order + [slot ^ bit for slot in order]
        bit //= 2
    return order


def gather_rows(block):
    bit = lax.axis_size("dp") // 2
    while bit:
        block = jnp.concatenate([block, swap(block, "dp", bit)], axis=0)
        bit //= 2
    return block


def scatter_rows(partial):
    bit = 1
    count = lax.axis_size("dp")
    while bit < count:
        half = partial.shape[0] // 2
        arrived = swap(partial[half:].astype(LOW), "dp", bit)
        partial = partial[:half].astype(WIDE) + arrived.astype(WIDE)
        bit *= 2
    return partial


def pick(stack, at):
    return lax.dynamic_index_in_dim(stack, at, 0, keepdims=False)


def exchange(stack, axis):
    mine = lax.axis_index(axis)
    count = lax.axis_size(axis)
    relative = [pick(stack, mine)]
    for bit in range(1, count):
        relative.append(swap(pick(stack, mine ^ bit), axis, bit))
    relative = jnp.stack(relative)
    return jnp.stack([pick(relative, mine ^ source) for source in range(count)])


def exchange_sum(stack, axis):
    mine = lax.axis_index(axis)
    total = pick(stack, mine).astype(WIDE)
    for bit in range(1, lax.axis_size(axis)):
        total += swap(pick(stack, mine ^ bit).astype(LOW), axis, bit).astype(WIDE)
    return total


def sum_replicas(value):
    low = value.astype(LOW)
    if lax.axis_size("ctx") == 2:
        return low.astype(WIDE) + shift(low, "ctx", 1).astype(WIDE)
    return jnp.sum(lax.all_gather(low, "ctx").astype(WIDE), axis=0)


def matmul_nt(left, right):
    return lax.dot_general(left, right, (((1,), (1,)), ((), ())), preferred_element_type=WIDE)


def matmul_nn(left, right):
    return lax.dot_general(left, right, (((1,), (0,)), ((), ())), preferred_element_type=WIDE)


def matmul_tn(left, right):
    return lax.dot_general(left, right, (((0,), (0,)), ((), ())), preferred_element_type=WIDE)


def visible_block(place_ref, start, block_rows, columns):
    slot = start // block_rows
    query_pos = place_ref[slot] * block_rows + start % block_rows
    query_pos = query_pos + lax.broadcasted_iota(jnp.int32, (CHUNK, columns), 0)
    lane = lax.broadcasted_iota(jnp.int32, (CHUNK, columns), 1)
    key_pos = lane
    for at in range(columns // block_rows):
        inside = (lane >= at * block_rows) & (lane < (at + 1) * block_rows)
        key_pos = jnp.where(inside, place_ref[at] * block_rows + lane - at * block_rows, key_pos)
    return key_pos <= query_pos


def columns_of(head):
    return slice(head * HEAD_DIM, (head + 1) * HEAD_DIM)


def own_forward(heads, block_rows, place_ref, kvq_ref, acc_ref, stat_ref, score, prob):
    width = heads * HEAD_DIM
    rows = kvq_ref.shape[0]
    for head in range(heads):
        query = kvq_ref[:, 2 * width + head * HEAD_DIM : 2 * width + (head + 1) * HEAD_DIM]
        score[...] = matmul_nt(query, kvq_ref[:, columns_of(head)])

        def chunk(step, carry):
            start = pl.multiple_of(step * CHUNK, CHUNK)
            seen = visible_block(place_ref, start, block_rows, rows)
            scores = jnp.where(seen, score[pl.ds(start, CHUNK), :] * SCALE, MASKED)
            highest = jnp.max(scores, axis=1, keepdims=True)
            weight = jnp.exp(scores - highest)
            stat_ref[pl.ds(start, CHUNK), head : head + 1] = highest
            stat_ref[pl.ds(start, CHUNK), heads + head : heads + head + 1] = jnp.sum(
                weight, axis=1, keepdims=True
            )
            prob[pl.ds(start, CHUNK), :] = weight.astype(LOW)
            return carry

        lax.fori_loop(0, rows // CHUNK, chunk, 0)
        value = kvq_ref[:, width + head * HEAD_DIM : width + (head + 1) * HEAD_DIM]
        acc_ref[:, columns_of(head)] = matmul_nn(prob[...], value)


def earlier_forward(
    heads, place_ref, kvq_ref, kv_ref, acc_in, stat_in, acc_ref, low_ref, stat_ref, score, prob, fade
):
    width = heads * HEAD_DIM
    rows = kvq_ref.shape[0]
    slots = place_ref.shape[0] - 1
    acc_ref[...] = acc_in[...]
    stat_ref[...] = stat_in[...]
    for piece in range(kv_ref.shape[0]):

        @pl.when(place_ref[slots] > piece)
        def _visit(piece=piece):
            for head in range(heads):
                query = kvq_ref[:, 2 * width + head * HEAD_DIM : 2 * width + (head + 1) * HEAD_DIM]
                score[...] = matmul_nt(query, kv_ref[piece, :, columns_of(head)])

                def chunk(step, carry):
                    here = pl.ds(pl.multiple_of(step * CHUNK, CHUNK), CHUNK)
                    scores = score[here, :] * SCALE
                    old = stat_ref[here, head : head + 1]
                    highest = jnp.maximum(old, jnp.max(scores, axis=1, keepdims=True))
                    weight = jnp.exp(scores - highest)
                    fading = jnp.exp(old - highest)
                    stat_ref[here, head : head + 1] = highest
                    total = stat_ref[here, heads + head : heads + head + 1]
                    stat_ref[here, heads + head : heads + head + 1] = total * fading + jnp.sum(
                        weight, axis=1, keepdims=True
                    )
                    fade[here, :] = jnp.broadcast_to(fading, (CHUNK, HEAD_DIM))
                    prob[here, :] = weight.astype(LOW)
                    return carry

                lax.fori_loop(0, rows // CHUNK, chunk, 0)
                value = kv_ref[piece, :, width + head * HEAD_DIM : width + (head + 1) * HEAD_DIM]
                acc_ref[:, columns_of(head)] = acc_ref[:, columns_of(head)] * fade[
                    ...
                ] + matmul_nn(prob[...], value)

    for head in range(heads):
        total = stat_ref[:, heads + head : heads + head + 1]
        context = acc_ref[:, columns_of(head)] / total
        acc_ref[:, columns_of(head)] = context
        low_ref[:, columns_of(head)] = context.astype(LOW)
        stat_ref[:, head : head + 1] = stat_ref[:, head : head + 1] + jnp.log(total)


def score_grads(here, seen, head, total, delta, score, dots, prob, grad):
    scores = score[here, :] * SCALE
    weight = jnp.exp(scores - total)
    if seen is not None:
        weight = jnp.where(seen, weight, 0.0)
    prob[here, :] = weight.astype(LOW)
    grad[here, :] = (weight * (dots[here, :] - delta) * SCALE).astype(LOW)


def delta_of(here, head, context_ref, ctx_grad_ref):
    product = context_ref[here, columns_of(head)] * ctx_grad_ref[here, columns_of(head)].astype(WIDE)
    return jnp.sum(product, axis=1, keepdims=True)


def earlier_backward(
    heads, place_ref, kvq_ref, kv_ref, ctx_grad_ref, context_ref, stat_ref, query_grad_ref,
    kv_grad_ref, score, dots, prob, grad
):
    width = heads * HEAD_DIM
    rows = kvq_ref.shape[0]
    slots = place_ref.shape[0] - 1
    query_grad_ref[...] = jnp.zeros_like(query_grad_ref)
    for piece in range(kv_ref.shape[0]):

        @pl.when(place_ref[slots] <= piece)
        def _skip(piece=piece):
            kv_grad_ref[piece] = jnp.zeros(kv_grad_ref.shape[1:], kv_grad_ref.dtype)

        @pl.when(place_ref[slots] > piece)
        def _visit(piece=piece):
            for head in range(heads):
                query = kvq_ref[:, 2 * width + head * HEAD_DIM : 2 * width + (head + 1) * HEAD_DIM]
                value_at = slice(width + head * HEAD_DIM, width + (head + 1) * HEAD_DIM)
                key = kv_ref[piece, :, columns_of(head)]
                out_grad = ctx_grad_ref[:, columns_of(head)]
                score[...] = matmul_nt(query, key)
                dots[...] = matmul_nt(out_grad, kv_ref[piece, :, value_at])

                def chunk(step, carry):
                    here = pl.ds(pl.multiple_of(step * CHUNK, CHUNK), CHUNK)
                    total = stat_ref[here, head : head + 1]
                    delta = delta_of(here, head, context_ref, ctx_grad_ref)
                    score_grads(here, None, head, total, delta, score, dots, prob, grad)
                    return carry

                lax.fori_loop(0, rows // CHUNK, chunk, 0)
                kv_grad_ref[piece, :, columns_of(head)] = matmul_tn(grad[...], query).astype(LOW)
                kv_grad_ref[piece, :, value_at] = matmul_tn(prob[...], out_grad).astype(LOW)
                query_grad_ref[:, columns_of(head)] += matmul_nn(grad[...], key)


def own_backward(
    heads, block_rows, place_ref, kvq_ref, ctx_grad_ref, context_ref, stat_ref, query_grad_in,
    grad_ref, score, dots, prob, grad
):
    width = heads * HEAD_DIM
    rows = kvq_ref.shape[0]
    for head in range(heads):
        query_at = slice(2 * width + head * HEAD_DIM, 2 * width + (head + 1) * HEAD_DIM)
        value_at = slice(width + head * HEAD_DIM, width + (head + 1) * HEAD_DIM)
        query = kvq_ref[:, query_at]
        key = kvq_ref[:, columns_of(head)]
        out_grad = ctx_grad_ref[:, columns_of(head)]
        score[...] = matmul_nt(query, key)
        dots[...] = matmul_nt(out_grad, kvq_ref[:, value_at])

        def chunk(step, carry):
            start = pl.multiple_of(step * CHUNK, CHUNK)
            here = pl.ds(start, CHUNK)
            seen = visible_block(place_ref, start, block_rows, rows)
            total = stat_ref[here, head : head + 1]
            delta = delta_of(here, head, context_ref, ctx_grad_ref)
            score_grads(here, seen, head, total, delta, score, dots, prob, grad)
            return carry

        lax.fori_loop(0, rows // CHUNK, chunk, 0)
        grad_ref[:, columns_of(head)] = matmul_tn(grad[...], query)
        grad_ref[:, value_at] = matmul_tn(prob[...], out_grad)
        grad_ref[:, query_at] = query_grad_in[:, columns_of(head)] + matmul_nn(grad[...], key)


def attention_call(kernel, operands, results, square, low_squares, wide_squares, extra=()):
    smem = pl.BlockSpec(memory_space=pltpu.SMEM)
    vmem = pl.BlockSpec(memory_space=pltpu.VMEM)
    return pl.pallas_call(
        kernel,
        out_shape=results,
        in_specs=[smem] + [vmem] * (len(operands) - 1),
        out_specs=[vmem] * len(results),
        scratch_shapes=[pltpu.VMEM((square, square), WIDE)] * wide_squares
        + [pltpu.VMEM((square, square), LOW)] * low_squares
        + list(extra),
        compiler_params=pltpu.CompilerParams(vmem_limit_bytes=48 * 1024 * 1024),
        cost_estimate=pl.CostEstimate(
            flops=2 * 6 * square * square * HEAD_DIM * 4, bytes_accessed=8 * 1024 * 1024,
            transcendentals=3 * square * square,
        ),
    )(*operands)


def normalize(values):
    centered = values - jnp.mean(values, axis=-1, keepdims=True)
    spread = jnp.mean(centered * centered, axis=-1, keepdims=True)
    inverse = lax.rsqrt(spread + EPSILON)
    return centered * inverse, inverse


def normalize_back(grad, gain, hat, inverse):
    scaled = grad * gain
    mean_scaled = jnp.mean(scaled, axis=-1, keepdims=True)
    mean_product = jnp.mean(scaled * hat, axis=-1, keepdims=True)
    part = inverse * (scaled - mean_scaled - hat * mean_product)
    return part, jnp.sum(grad * hat, axis=0), jnp.sum(grad, axis=0)


def local(
    tokens, cotangent, ln1_gain, ln1_bias, qkv_weight, q_bias, v_bias, out_weight, out_bias,
    ln2_gain, ln2_bias, fc1_weight, fc1_bias, fc2_weight, fc2_bias,
):
    parts = lax.axis_size("dp")
    depth = lax.axis_size("fsdp")
    contexts = lax.axis_size("ctx")
    assert parts == depth
    mine = lax.axis_index("dp")
    rows, model = tokens.shape[1:]
    shard = ln1_gain.shape[0]
    heads = model // HEAD_DIM // parts
    width = heads * HEAD_DIM
    hidden_shard = fc1_bias.shape[0]
    hidden_part = hidden_shard * depth
    group_rows = parts * rows

    token_rows = transpose_homes(tokens[0].astype(LOW)).astype(WIDE)

    vector_rows = [ln1_gain, ln1_bias, ln2_gain, ln2_bias, out_bias, fc2_bias, q_bias, v_bias]
    per_hidden = hidden_shard // shard
    packed = jnp.concatenate(
        [jnp.stack(vector_rows), fc1_bias.reshape(per_hidden, shard)], axis=0
    )
    packed = jnp.pad(packed, ((0, 16 - packed.shape[0]), (0, 128 - shard))).astype(LOW)
    vectors = lax.all_gather(packed, ("dp", "fsdp"), axis=0)
    vectors = vectors[:, : 8 + per_hidden, :shard].astype(WIDE)
    whole = jnp.transpose(vectors[:, :8], (1, 0, 2)).reshape(8, model)
    gain1, bias1, gain2, bias2, out_shift, down_shift = [whole[at] for at in range(6)]
    query_shift = lax.dynamic_slice_in_dim(whole[6], mine * width, width)
    value_shift = lax.dynamic_slice_in_dim(whole[7], mine * width, width)
    up_shift = lax.dynamic_slice_in_dim(vectors[:, 8:], mine * depth, depth, axis=0).reshape(-1)

    qkv_split = qkv_weight.astype(LOW).reshape(shard, 3, parts, width)
    qkv_split = jnp.stack([qkv_split[:, 1], qkv_split[:, 2], qkv_split[:, 0]], axis=1)
    qkv_split = jnp.transpose(qkv_split, (2, 0, 1, 3)).reshape(parts, shard, 3 * width)
    up_split = fc1_weight.astype(LOW).reshape(shard, parts, hidden_part)
    up_split = jnp.transpose(up_split, (1, 0, 2))

    def gather_columns(split):
        gathered = lax.all_gather(exchange(split, "dp"), "fsdp", axis=0)
        return jnp.transpose(gathered, (1, 0, 2, 3)).reshape(model, split.shape[-1])

    kvq_matrix = gather_columns(qkv_split)
    out_matrix = lax.all_gather(out_weight.astype(LOW), "fsdp", axis=0, tiled=True)
    up_matrix = gather_columns(up_split)
    down_matrix = lax.all_gather(fc2_weight.astype(LOW), "fsdp", axis=0, tiled=True)

    grad_rows = transpose_homes(cotangent[0].astype(LOW))

    hat1, inverse1 = normalize(token_rows)
    norm1 = gather_rows((hat1 * gain1 + bias1).astype(LOW))
    kvq_shift = jnp.concatenate([jnp.zeros((width,), WIDE), value_shift, query_shift])
    kvq = (matmul_nn(norm1, kvq_matrix) + kvq_shift).astype(LOW)
    kv = kvq[:, : 2 * width]
    kv_earlier = jnp.stack([shift(kv, "ctx", by) for by in range(1, contexts)])
    order = slot_order(parts)
    place = jnp.stack(
        [(mine ^ slot).astype(jnp.int32) for slot in order]
        + [lax.axis_index("ctx").astype(jnp.int32)]
    )
    like = jax.ShapeDtypeStruct
    acc, stat = attention_call(
        functools.partial(own_forward, heads, rows),
        (place, kvq),
        (like((group_rows, width), WIDE), like((group_rows, 128), WIDE)),
        group_rows, 1, 1,
    )
    context, context_low, stat = attention_call(
        functools.partial(earlier_forward, heads),
        (place, kvq, kv_earlier, acc, stat),
        (
            like((group_rows, width), WIDE),
            like((group_rows, width), LOW),
            like((group_rows, 128), WIDE),
        ),
        group_rows, 1, 1, (pltpu.VMEM((group_rows, HEAD_DIM), WIDE),),
    )
    attended = scatter_rows(matmul_nn(context_low, out_matrix)) + out_shift
    mixed = token_rows + attended

    hat2, inverse2 = normalize(mixed)
    norm2 = gather_rows((hat2 * gain2 + bias2).astype(LOW))
    inner = matmul_nn(norm2, up_matrix) + up_shift
    activated, gelu_back = jax.vjp(jax.nn.gelu, inner)
    hidden = activated.astype(LOW)
    branch = gather_rows(grad_rows)
    hidden_grad = matmul_nt(branch, down_matrix)
    inner_grad = gelu_back(hidden_grad)[0].astype(LOW)
    norm2_grad = scatter_rows(matmul_nt(inner_grad, up_matrix))
    mixed_part, gain2_grad, bias2_grad = normalize_back(norm2_grad, gain2, hat2, inverse2)
    attn_grad = (grad_rows.astype(WIDE) + mixed_part).astype(LOW)
    attn_grads = gather_rows(attn_grad)
    context_grad = matmul_nt(attn_grads, out_matrix).astype(LOW)

    fed = scatter_rows(matmul_nn(hidden, down_matrix)) + down_shift
    output = tokens[0] + transpose_homes((attended + fed).astype(LOW)).astype(WIDE)
    down_grad = matmul_tn(hidden, branch)
    up_grad = matmul_tn(norm2, inner_grad)
    out_grad = matmul_tn(context_low, attn_grads)

    def to_owner_rows(grad):
        return sum_replicas(exchange_sum(grad, "fsdp"))

    def by_owner(grad):
        return jnp.transpose(grad.reshape(parts, depth, shard, grad.shape[-1]), (1, 0, 2, 3))

    down_total = to_owner_rows(down_grad.reshape(depth, hidden_shard, model))
    up_total = to_owner_rows(by_owner(up_grad))
    up_total = exchange(up_total.astype(LOW), "dp")
    up_total = jnp.transpose(up_total, (1, 0, 2)).reshape(shard, parts * hidden_part)
    out_total = to_owner_rows(out_grad.reshape(depth, shard, model))

    query_grad, kv_grad = attention_call(
        functools.partial(earlier_backward, heads),
        (place, kvq, kv_earlier, context_grad, context, stat),
        (like((group_rows, width), WIDE), like(kv_earlier.shape, LOW)),
        group_rows, 2, 2,
    )
    arrived = sum(
        shift(kv_grad[by - 1], "ctx", -by).astype(WIDE) for by in range(1, contexts)
    )
    (kvq_own,) = attention_call(
        functools.partial(own_backward, heads, rows),
        (place, kvq, context_grad, context, stat, query_grad),
        (like((group_rows, 3 * width), WIDE),),
        group_rows, 2, 2,
    )
    kvq_grad = jnp.concatenate(
        [kvq_own[:, : 2 * width] + arrived, kvq_own[:, 2 * width :]], axis=1
    ).astype(LOW)
    norm1_grad = scatter_rows(matmul_nt(kvq_grad, kvq_matrix))
    rows_part, gain1_grad, bias1_grad = normalize_back(norm1_grad, gain1, hat1, inverse1)
    input_grad = cotangent[0] + transpose_homes((mixed_part + rows_part).astype(LOW)).astype(WIDE)

    kvq_total = to_owner_rows(by_owner(matmul_tn(norm1, kvq_grad)))
    kvq_total = exchange(kvq_total.astype(LOW), "dp").reshape(parts, shard, 3, width)
    qkv_total = jnp.stack([kvq_total[:, :, 2], kvq_total[:, :, 0], kvq_total[:, :, 1]], axis=0)
    qkv_total = jnp.transpose(qkv_total, (2, 0, 1, 3)).reshape(shard, 3 * model)

    kvq_bias = jnp.sum(kvq_grad.astype(WIDE), axis=0)
    up_bias = jnp.sum(inner_grad.astype(WIDE), axis=0)
    full = jnp.stack(
        [
            gain1_grad,
            bias1_grad,
            gain2_grad,
            bias2_grad,
            jnp.sum(attn_grad.astype(WIDE), axis=0),
            jnp.sum(grad_rows.astype(WIDE), axis=0),
        ]
    ).reshape(6, parts, depth, shard)
    full = jnp.transpose(full, (2, 1, 0, 3))
    part = jnp.concatenate(
        [
            kvq_bias[2 * width :].reshape(depth, 1, shard),
            kvq_bias[width : 2 * width].reshape(depth, 1, shard),
            up_bias.reshape(depth, per_hidden, shard),
        ],
        axis=1,
    )
    owned = (jnp.arange(parts) == mine)[None, :, None, None]
    part = jnp.where(owned, part[:, None], 0.0)
    vector_grads = jnp.concatenate([full, part], axis=2)
    vector_grads = jnp.pad(
        vector_grads, ((0, 0), (0, 0), (0, 16 - vector_grads.shape[2]), (0, 128 - shard))
    )
    vector_total = exchange_sum(vector_grads, "fsdp")
    vector_total = exchange_sum(vector_total, "dp")
    vector_total = sum_replicas(vector_total)[:, :shard]

    return (
        output[None],
        input_grad[None],
        vector_total[0],
        vector_total[1],
        qkv_total.astype(WIDE),
        vector_total[6],
        vector_total[7],
        out_total,
        vector_total[4],
        vector_total[2],
        vector_total[3],
        up_total.astype(WIDE),
        vector_total[8 : 8 + per_hidden].reshape(-1),
        down_total,
        vector_total[5],
    )


def solution(mesh):
    rows = P("dp", ("ctx", "fsdp"), None)
    vector = P(("dp", "fsdp"))
    matrix = P(("dp", "fsdp"), None)
    parameters = (
        vector, vector, matrix, vector, vector, matrix, vector, vector, vector, matrix, vector,
        matrix, vector,
    )
    return jax.shard_map(
        local,
        mesh=mesh,
        in_specs=(rows, rows) + parameters,
        out_specs=(rows, rows) + parameters,
        check_vma=False,
    )
```

```python
import functools

import jax
import jax.numpy as jnp
from jax import lax
from jax.experimental import pallas as pl
from jax.experimental.pallas import tpu as pltpu
from jax.sharding import PartitionSpec as P

HEAD_DIM = 64
EPSILON = 1e-05
SCALE = HEAD_DIM ** (-0.5)
MASKED = -1e30
CHUNK = 64
GELU_SCALE = 0.7978845608
GELU_CUBE = 0.044715
LOW = jnp.bfloat16
WIDE = jnp.float32


def swap(value, axis, bit):
    count = lax.axis_size(axis)
    return lax.ppermute(value, axis, [(at, at ^ bit) for at in range(count)])


def shift(value, axis, by):
    count = lax.axis_size(axis)
    return lax.ppermute(value, axis, [(at, (at + by) % count) for at in range(count)])


def transpose_homes(value):
    side = lax.axis_size("dp")
    pairs = [(a * side + b, b * side + a) for a in range(side) for b in range(side)]
    return lax.ppermute(value, ("dp", "fsdp"), pairs)


def after(value, *others):
    return lax.optimization_barrier((value,) + others)[0]


def gather_pieces(block):
    pieces = [block]
    for slot in range(1, lax.axis_size("dp")):
        low_bit = slot & -slot
        pieces.append(swap(pieces[slot ^ low_bit], "dp", low_bit))
    return pieces


def send_pieces(sends, axis):
    return [swap(send, axis, slot) for slot, send in enumerate(sends, 1)]


def gather_direct(block, axis):
    return [block] + [swap(block, axis, slot) for slot in range(1, lax.axis_size(axis))]


def sum_all(kept, arrived):
    total = kept
    for piece in arrived:
        total = total + piece.astype(WIDE)
    return total


def sum_replicas(value):
    if lax.axis_size("ctx") == 2:
        return value.astype(WIDE) + shift(value, "ctx", 1).astype(WIDE)
    return jnp.sum(lax.all_gather(value, "ctx").astype(WIDE), axis=0)


def matmul_nt(left, right):
    return lax.dot_general(left, right, (((1,), (1,)), ((), ())), preferred_element_type=WIDE)


def matmul_nn(left, right):
    return lax.dot_general(left, right, (((1,), (0,)), ((), ())), preferred_element_type=WIDE)


def matmul_tn(left, right):
    return lax.dot_general(left, right, (((0,), (0,)), ((), ())), preferred_element_type=WIDE)


def visible_block(place_ref, start, block_rows, columns):
    slot = start // block_rows
    query_pos = place_ref[slot] * block_rows + start % block_rows
    query_pos = query_pos + lax.broadcasted_iota(jnp.int32, (CHUNK, columns), 0)
    lane = lax.broadcasted_iota(jnp.int32, (CHUNK, columns), 1)
    key_pos = lane
    for at in range(columns // block_rows):
        inside = (lane >= at * block_rows) & (lane < (at + 1) * block_rows)
        key_pos = jnp.where(inside, place_ref[at] * block_rows + lane - at * block_rows, key_pos)
    return key_pos <= query_pos


def columns_of(head):
    return slice(head * HEAD_DIM, (head + 1) * HEAD_DIM)


def own_forward(heads, block_rows, place_ref, kvq_ref, acc_ref, stat_ref, score, prob):
    width = heads * HEAD_DIM
    rows = kvq_ref.shape[0]
    for head in range(heads):
        query = kvq_ref[:, 2 * width + head * HEAD_DIM : 2 * width + (head + 1) * HEAD_DIM]
        score[...] = matmul_nt(query, kvq_ref[:, columns_of(head)])

        def chunk(step, carry):
            start = pl.multiple_of(step * CHUNK, CHUNK)
            seen = visible_block(place_ref, start, block_rows, rows)
            scores = jnp.where(seen, score[pl.ds(start, CHUNK), :] * SCALE, MASKED)
            highest = jnp.max(scores, axis=1, keepdims=True)
            weight = jnp.exp(scores - highest)
            stat_ref[pl.ds(start, CHUNK), head : head + 1] = highest
            stat_ref[pl.ds(start, CHUNK), heads + head : heads + head + 1] = jnp.sum(
                weight, axis=1, keepdims=True
            )
            prob[pl.ds(start, CHUNK), :] = weight.astype(LOW)
            return carry

        lax.fori_loop(0, rows // CHUNK, chunk, 0)
        value = kvq_ref[:, width + head * HEAD_DIM : width + (head + 1) * HEAD_DIM]
        acc_ref[:, columns_of(head)] = matmul_nn(prob[...], value)


def earlier_forward(
    heads, slots, place_ref, kvq_ref, kv_ref, acc_in, stat_in, acc_ref, low_ref, stat_ref, score,
    prob, fade
):
    width = heads * HEAD_DIM
    rows = kvq_ref.shape[0]
    acc_ref[...] = acc_in[...]
    stat_ref[...] = stat_in[...]
    for piece in range(kv_ref.shape[0]):

        @pl.when(place_ref[slots] > piece)
        def _visit(piece=piece):
            for head in range(heads):
                query = kvq_ref[:, 2 * width + head * HEAD_DIM : 2 * width + (head + 1) * HEAD_DIM]
                score[...] = matmul_nt(query, kv_ref[piece, :, columns_of(head)])

                def chunk(step, carry):
                    here = pl.ds(pl.multiple_of(step * CHUNK, CHUNK), CHUNK)
                    scores = score[here, :] * SCALE
                    old = stat_ref[here, head : head + 1]
                    highest = jnp.maximum(old, jnp.max(scores, axis=1, keepdims=True))
                    weight = jnp.exp(scores - highest)
                    fading = jnp.exp(old - highest)
                    stat_ref[here, head : head + 1] = highest
                    total = stat_ref[here, heads + head : heads + head + 1]
                    stat_ref[here, heads + head : heads + head + 1] = total * fading + jnp.sum(
                        weight, axis=1, keepdims=True
                    )
                    fade[here, :] = jnp.broadcast_to(fading, (CHUNK, HEAD_DIM))
                    prob[here, :] = weight.astype(LOW)
                    return carry

                lax.fori_loop(0, rows // CHUNK, chunk, 0)
                value = kv_ref[piece, :, width + head * HEAD_DIM : width + (head + 1) * HEAD_DIM]
                acc_ref[:, columns_of(head)] = acc_ref[:, columns_of(head)] * fade[
                    ...
                ] + matmul_nn(prob[...], value)

    for head in range(heads):
        total = stat_ref[:, heads + head : heads + head + 1]
        context = acc_ref[:, columns_of(head)] / total
        acc_ref[:, columns_of(head)] = context
        low_ref[:, columns_of(head)] = context.astype(LOW)
        stat_ref[:, head : head + 1] = stat_ref[:, head : head + 1] + jnp.log(total)


def score_grads(here, seen, head, total, delta, score, dots, prob, grad):
    scores = score[here, :] * SCALE
    weight = jnp.exp(scores - total)
    if seen is not None:
        weight = jnp.where(seen, weight, 0.0)
    prob[here, :] = weight.astype(LOW)
    grad[here, :] = (weight * (dots[here, :] - delta) * SCALE).astype(LOW)


def delta_of(here, head, context_ref, ctx_grad_ref):
    product = context_ref[here, columns_of(head)] * ctx_grad_ref[here, columns_of(head)].astype(WIDE)
    return jnp.sum(product, axis=1, keepdims=True)


def earlier_backward(
    heads, slots, place_ref, kvq_ref, kv_ref, ctx_grad_ref, context_ref, stat_ref, query_grad_ref,
    kv_grad_ref, score, dots, prob, grad
):
    width = heads * HEAD_DIM
    rows = kvq_ref.shape[0]
    query_grad_ref[...] = jnp.zeros_like(query_grad_ref)
    for piece in range(kv_ref.shape[0]):

        @pl.when(place_ref[slots] <= piece)
        def _skip(piece=piece):
            kv_grad_ref[piece] = jnp.zeros(kv_grad_ref.shape[1:], kv_grad_ref.dtype)

        @pl.when(place_ref[slots] > piece)
        def _visit(piece=piece):
            for head in range(heads):
                query = kvq_ref[:, 2 * width + head * HEAD_DIM : 2 * width + (head + 1) * HEAD_DIM]
                value_at = slice(width + head * HEAD_DIM, width + (head + 1) * HEAD_DIM)
                key = kv_ref[piece, :, columns_of(head)]
                out_grad = ctx_grad_ref[:, columns_of(head)]
                score[...] = matmul_nt(query, key)
                dots[...] = matmul_nt(out_grad, kv_ref[piece, :, value_at])

                def chunk(step, carry):
                    here = pl.ds(pl.multiple_of(step * CHUNK, CHUNK), CHUNK)
                    total = stat_ref[here, head : head + 1]
                    delta = delta_of(here, head, context_ref, ctx_grad_ref)
                    score_grads(here, None, head, total, delta, score, dots, prob, grad)
                    return carry

                lax.fori_loop(0, rows // CHUNK, chunk, 0)
                kv_grad_ref[piece, :, columns_of(head)] = matmul_tn(grad[...], query).astype(LOW)
                kv_grad_ref[piece, :, value_at] = matmul_tn(prob[...], out_grad).astype(LOW)
                query_grad_ref[:, columns_of(head)] += matmul_nn(grad[...], key)


def own_backward(
    heads, block_rows, place_ref, kvq_ref, ctx_grad_ref, context_ref, stat_ref, query_grad_in,
    grad_ref, score, dots, prob, grad
):
    width = heads * HEAD_DIM
    rows = kvq_ref.shape[0]
    for head in range(heads):
        query_at = slice(2 * width + head * HEAD_DIM, 2 * width + (head + 1) * HEAD_DIM)
        value_at = slice(width + head * HEAD_DIM, width + (head + 1) * HEAD_DIM)
        query = kvq_ref[:, query_at]
        key = kvq_ref[:, columns_of(head)]
        out_grad = ctx_grad_ref[:, columns_of(head)]
        score[...] = matmul_nt(query, key)
        dots[...] = matmul_nt(out_grad, kvq_ref[:, value_at])

        def chunk(step, carry):
            start = pl.multiple_of(step * CHUNK, CHUNK)
            here = pl.ds(start, CHUNK)
            seen = visible_block(place_ref, start, block_rows, rows)
            total = stat_ref[here, head : head + 1]
            delta = delta_of(here, head, context_ref, ctx_grad_ref)
            score_grads(here, seen, head, total, delta, score, dots, prob, grad)
            return carry

        lax.fori_loop(0, rows // CHUNK, chunk, 0)
        grad_ref[:, columns_of(head)] = matmul_tn(grad[...], query)
        grad_ref[:, value_at] = matmul_tn(prob[...], out_grad)
        grad_ref[:, query_at] = query_grad_in[:, columns_of(head)] + matmul_nn(grad[...], key)


def normalize(values):
    centered = values - jnp.mean(values, axis=-1, keepdims=True)
    spread = jnp.mean(centered * centered, axis=-1, keepdims=True)
    inverse = lax.rsqrt(spread + EPSILON)
    return centered * inverse, inverse


def normalize_back(grad, gain, hat, inverse):
    scaled = grad * gain
    mean_scaled = jnp.mean(scaled, axis=-1, keepdims=True)
    mean_product = jnp.mean(scaled * hat, axis=-1, keepdims=True)
    part = inverse * (scaled - mean_scaled - hat * mean_product)
    gain_grad = jnp.sum(grad * hat, axis=0, keepdims=True)
    return part, gain_grad, jnp.sum(grad, axis=0, keepdims=True)


def take(refs, *counts):
    groups, at = [], 0
    for count in counts:
        if count is None:
            groups.append(refs[at])
            at += 1
        else:
            groups.append(refs[at : at + count])
            at += count
    return groups


def place_blocks(meta_ref, parts, depth, pieces, out_ref):
    rows = pieces[0].shape[1]
    for deep in range(depth):
        member = meta_ref[parts + 1] ^ deep
        for slot in range(parts):
            start = pl.multiple_of((meta_ref[slot] * depth + member) * rows, 16)
            out_ref[pl.ds(start, rows), :] = pieces[deep][slot]


def place_shards(meta_ref, parts, pieces, out_ref):
    rows = pieces[0].shape[0]
    for deep, piece in enumerate(pieces):
        start = pl.multiple_of((meta_ref[parts + 1] ^ deep) * rows, 16)
        out_ref[pl.ds(start, rows), :] = piece[...]


def stack_rows(pieces, out_ref):
    rows = pieces[0].shape[0]
    for slot, piece in enumerate(pieces):
        out_ref[slot * rows : (slot + 1) * rows, :] = piece[...]


def emit_rows(partial, keep_ref, send_refs):
    rows = keep_ref.shape[0]
    keep_ref[...] = partial[:rows]
    for slot, send in enumerate(send_refs, 1):
        send[...] = partial[slot * rows : (slot + 1) * rows].astype(LOW)


def emit_blocks(meta_ref, parts, depth, whole_ref, keep_ref, send_refs):
    rows = keep_ref.shape[1]
    for deep in range(depth):
        member = meta_ref[parts + 1] ^ deep
        for slot in range(parts):
            start = pl.multiple_of((meta_ref[slot] * depth + member) * rows, 16)
            block = whole_ref[pl.ds(start, rows), :]
            if deep:
                send_refs[deep - 1][slot] = block.astype(LOW)
            else:
                keep_ref[slot] = block


def emit_shards(meta_ref, parts, whole_ref, keep_ref, send_refs):
    rows = keep_ref.shape[0]
    for deep in range(len(send_refs) + 1):
        start = pl.multiple_of((meta_ref[parts + 1] ^ deep) * rows, 16)
        block = whole_ref[pl.ds(start, rows), :]
        if deep:
            send_refs[deep - 1][...] = block.astype(LOW)
        else:
            keep_ref[...] = block


def split_kernel(parts, width, meta_ref, qkv_ref, up_ref, *outs):
    kvq_outs, up_outs = take(outs, parts, parts)
    model = parts * width
    part = up_ref.shape[1] // parts
    for case in range(parts):

        @pl.when(meta_ref[0] == case)
        def _case(case=case):
            for slot in range(parts):
                owner = case ^ slot
                for at, first in enumerate((model, 2 * model, 0)):
                    start = first + owner * width
                    kvq_outs[slot][:, at * width : (at + 1) * width] = qkv_ref[
                        :, start : start + width
                    ].astype(LOW)
                up_outs[slot][...] = up_ref[:, owner * part : (owner + 1) * part].astype(LOW)


def join_qkv_kernel(parts, width, meta_ref, *refs):
    pieces, out_ref = refs[:parts], refs[parts]
    model = parts * width
    for case in range(parts):

        @pl.when(meta_ref[0] == case)
        def _case(case=case):
            for slot in range(parts):
                owner = case ^ slot
                for at, first in enumerate((model, 2 * model, 0)):
                    start = first + owner * width
                    out_ref[:, start : start + width] = pieces[slot][
                        :, at * width : (at + 1) * width
                    ].astype(WIDE)


def join_up_kernel(parts, meta_ref, *refs):
    pieces, out_ref = refs[:parts], refs[parts]
    part = pieces[0].shape[1]
    for slot in range(parts):
        start = pl.multiple_of(meta_ref[slot] * part, 128)
        out_ref[:, pl.ds(start, part)] = pieces[slot][...].astype(WIDE)


def first_norm_kernel(meta_ref, tokens_ref, vectors_ref, out_ref):
    hat, _ = normalize(tokens_ref[...].astype(WIDE))
    out_ref[...] = (hat * vectors_ref[0:1, :] + vectors_ref[1:2, :]).astype(LOW)


def project_kernel(parts, depth, meta_ref, *refs):
    norm, weight, vectors_ref, kvq_ref, kv_ref, matrix_ref, norm_ref = take(
        refs, parts, depth, None, None, None, None, None
    )
    columns = kvq_ref.shape[1]
    place_blocks(meta_ref, parts, depth, weight, matrix_ref)
    stack_rows(norm, norm_ref)
    low = (matmul_nn(norm_ref[...], matrix_ref[...]) + vectors_ref[6:7, :columns]).astype(LOW)
    kvq_ref[...] = low
    kv_ref[...] = low[:, : kv_ref.shape[1]]


def context_kernel(parts, depth, heads, meta_ref, *refs):
    (
        kvq, kv, acc_in, stat_in, weight, context, low, stat, matrix, keep, sends, score, prob, fade
    ) = take(
        refs, None, None, None, None, depth, None, None, None, None, None, parts - 1, None, None,
        None,
    )
    place_shards(meta_ref, parts, weight, matrix)
    earlier_forward(
        heads, parts, meta_ref, kvq, kv, acc_in, stat_in, context, low, stat, score, prob, fade
    )
    emit_rows(matmul_nn(low[...], matrix[...]), keep, sends)


def second_norm_kernel(parts, meta_ref, *refs):
    keep, arrived, tokens, vectors, out, attended_ref = take(
        refs, None, parts - 1, None, None, None, None
    )
    attended = sum_all(keep[...], [piece[...] for piece in arrived]) + vectors[4:5, :]
    attended_ref[...] = attended
    hat, _ = normalize(tokens[...].astype(WIDE) + attended)
    out[...] = (hat * vectors[2:3, :] + vectors[3:4, :]).astype(LOW)


def feed_kernel(parts, depth, meta_ref, *refs):
    (
        norm, branch, up, down, vectors, keep, sends, hidden, inner_grad, norm_all, branch_all,
        down_all, up_bias, up_all, inner, grad,
    ) = take(
        refs, parts, parts, depth, depth, None, None, parts - 1, None, None, None, None, None,
        None, None, None, None,
    )
    place_blocks(meta_ref, parts, depth, up, up_all)
    place_shards(meta_ref, parts, down, down_all)
    stack_rows(norm, norm_all)
    stack_rows(branch, branch_all)
    inner[...] = matmul_nn(norm_all[...], up_all[...])
    grad[...] = matmul_nt(branch_all[...], down_all[...])
    up_bias[...] = jnp.zeros_like(up_bias)

    def chunk(step, carry):
        here = pl.ds(pl.multiple_of(step * CHUNK, CHUNK), CHUNK)
        value = inner[here, :] + vectors[7:8, :]
        square = value * value
        bent = jnp.tanh(GELU_SCALE * (value + GELU_CUBE * square * value))
        hidden[here, :] = (0.5 * value * (1.0 + bent)).astype(LOW)
        slope = 0.5 * (1.0 + bent) + 0.5 * value * (1.0 - bent * bent) * GELU_SCALE * (
            1.0 + 3.0 * GELU_CUBE * square
        )
        low = (grad[here, :] * slope).astype(LOW)
        inner_grad[here, :] = low
        up_bias[...] += jnp.sum(low.astype(WIDE), axis=0, keepdims=True)
        return carry

    lax.fori_loop(0, inner.shape[0] // CHUNK, chunk, 0)
    emit_rows(matmul_nt(inner_grad[...], up_all[...]), keep, sends)


def feed_grad_kernel(parts, depth, meta_ref, *refs):
    (
        hidden, inner_grad, norm_all, branch_all, down_all, down_keep, down_sends, up_keep,
        up_sends, fed_keep, fed_sends, whole,
    ) = take(
        refs, None, None, None, None, None, None, depth - 1, None, depth - 1, None, parts - 1, None
    )
    whole[...] = matmul_tn(hidden[...], branch_all[...])
    emit_shards(meta_ref, parts, whole, down_keep, down_sends)
    whole[...] = matmul_tn(norm_all[...], inner_grad[...])
    emit_blocks(meta_ref, parts, depth, whole, up_keep, up_sends)
    emit_rows(matmul_nn(hidden[...], down_all[...]), fed_keep, fed_sends)


def second_norm_grad_kernel(parts, meta_ref, *refs):
    keep, arrived, tokens, attended, branch, vectors, attn_grad, mixed_part, sums = take(
        refs, None, parts - 1, None, None, None, None, None, None, None
    )
    grad = sum_all(keep[...], [piece[...] for piece in arrived])
    hat, inverse = normalize(tokens[...].astype(WIDE) + attended[...])
    part, gain_grad, bias_grad = normalize_back(grad, vectors[2:3, :], hat, inverse)
    mixed_part[...] = part
    branch_rows = branch[...].astype(WIDE)
    low = (branch_rows + part).astype(LOW)
    attn_grad[...] = low
    sums[...] = jnp.zeros_like(sums)
    sums[2:3, :] = gain_grad
    sums[3:4, :] = bias_grad
    sums[4:5, :] = jnp.sum(low.astype(WIDE), axis=0, keepdims=True)
    sums[5:6, :] = jnp.sum(branch_rows, axis=0, keepdims=True)


def context_grad_kernel(parts, heads, meta_ref, *refs):
    (
        attn, matrix, kvq, kv, context, stat, ctx_grad, attn_all, query_grad, kv_grad, score, dots,
        prob, grad,
    ) = take(refs, parts, *([None] * 13))
    stack_rows(attn, attn_all)
    ctx_grad[...] = matmul_nt(attn_all[...], matrix[...]).astype(LOW)
    earlier_backward(
        heads, parts, meta_ref, kvq, kv, ctx_grad, context, stat, query_grad, kv_grad, score, dots,
        prob, grad,
    )


def own_grad_kernel(parts, depth, heads, rows, meta_ref, *refs):
    (
        kvq, ctx_grad, context, stat, query_grad, low, attn_all, kvq_grad, out_keep, out_sends,
        whole, score, dots, prob, grad,
    ) = take(refs, *([None] * 9), depth - 1, *([None] * 5))
    own_backward(
        heads, rows, meta_ref, kvq, ctx_grad, context, stat, query_grad, kvq_grad, score, dots,
        prob, grad,
    )
    whole[...] = matmul_tn(low[...], attn_all[...])
    emit_shards(meta_ref, parts, whole, out_keep, out_sends)


def projection_back_kernel(parts, meta_ref, *refs):
    own, arrived, matrix, kvq_grad, keep, sends, bias = take(
        refs, None, None, None, None, None, parts - 1, None
    )
    kv_width = arrived.shape[2]
    total = own[:, :kv_width]
    for piece in range(arrived.shape[0]):
        total = total + arrived[piece].astype(WIDE)
    kvq_grad[:, :kv_width] = total.astype(LOW)
    kvq_grad[:, kv_width:] = own[:, kv_width:].astype(LOW)
    emit_rows(matmul_nt(kvq_grad[...], matrix[...]), keep, sends)
    bias[...] = jnp.sum(kvq_grad[...].astype(WIDE), axis=0, keepdims=True)


def projection_grad_kernel(parts, depth, meta_ref, *refs):
    norm, kvq_grad, keep, sends, whole = take(refs, None, None, None, depth - 1, None)
    whole[...] = matmul_tn(norm[...], kvq_grad[...])
    emit_blocks(meta_ref, parts, depth, whole, keep, sends)


def first_norm_grad_kernel(parts, meta_ref, *refs):
    keep, arrived, tokens, vectors, mixed_part, sums_in, kvq_bias, up_bias, out, sums = take(
        refs, None, parts - 1, *([None] * 8)
    )
    grad = sum_all(keep[...], [piece[...] for piece in arrived])
    hat, inverse = normalize(tokens[...].astype(WIDE))
    part, gain_grad, bias_grad = normalize_back(grad, vectors[0:1, :], hat, inverse)
    out[...] = (mixed_part[...] + part).astype(LOW)
    sums[...] = sums_in[...]
    sums[0:1, :] = gain_grad
    sums[1:2, :] = bias_grad
    sums[6:7, : kvq_bias.shape[1]] = kvq_bias[...]
    sums[7:8, :] = up_bias[...]


def local_call(kernel, operands, results, scratch=(), flops=0):
    smem = pl.BlockSpec(memory_space=pltpu.SMEM)
    vmem = pl.BlockSpec(memory_space=pltpu.VMEM)
    moved = sum(each.size * each.dtype.itemsize for each in tuple(operands) + tuple(results))
    return pl.pallas_call(
        kernel,
        out_shape=tuple(results),
        in_specs=[smem] + [vmem] * (len(operands) - 1),
        out_specs=tuple([vmem] * len(results)),
        scratch_shapes=list(scratch),
        compiler_params=pltpu.CompilerParams(vmem_limit_bytes=48 * 1024 * 1024),
        cost_estimate=pl.CostEstimate(flops=flops, bytes_accessed=moved, transcendentals=0),
    )(*operands)


def low_like(*shape):
    return jax.ShapeDtypeStruct(shape, LOW)


def wide_like(*shape):
    return jax.ShapeDtypeStruct(shape, WIDE)


def local(
    tokens, cotangent, ln1_gain, ln1_bias, qkv_weight, q_bias, v_bias, out_weight, out_bias,
    ln2_gain, ln2_bias, fc1_weight, fc1_bias, fc2_weight, fc2_bias,
):
    parts = lax.axis_size("dp")
    depth = lax.axis_size("fsdp")
    contexts = lax.axis_size("ctx")
    assert parts == depth
    mine = lax.axis_index("dp")
    deep = lax.axis_index("fsdp")
    rows, model = tokens.shape[1:]
    shard = ln1_gain.shape[0]
    heads = model // HEAD_DIM // parts
    width = heads * HEAD_DIM
    hidden_shard = fc1_bias.shape[0]
    hidden_part = hidden_shard * depth
    group = parts * rows
    meta = jnp.stack(
        [mine ^ slot for slot in range(parts)] + [lax.axis_index("ctx"), deep]
    ).astype(jnp.int32)

    token_rows = transpose_homes(tokens[0].astype(LOW))

    split = local_call(
        functools.partial(split_kernel, parts, width),
        (meta, qkv_weight, fc1_weight),
        [low_like(shard, 3 * width)] * parts + [low_like(shard, hidden_part)] * parts,
    )
    kvq_split, up_split = split[:parts], split[parts:]
    kvq_rows = jnp.stack([kvq_split[0]] + send_pieces(kvq_split[1:], "dp"))
    kvq_pieces = gather_direct(kvq_rows, "fsdp")

    low_vectors = [
        each.astype(LOW).astype(WIDE)
        for each in (ln1_gain, ln1_bias, ln2_gain, ln2_bias, out_bias, fc2_bias)
    ]
    vectors = jnp.zeros((8, model), WIDE)
    vectors = lax.dynamic_update_slice(
        vectors, jnp.stack(low_vectors), (0, (mine * depth + deep) * shard)
    )
    for row, first, part in (
        (6, width, v_bias), (6, 2 * width, q_bias), (7, 0, fc1_bias),
    ):
        part = part.astype(LOW).astype(WIDE)[None]
        vectors = lax.dynamic_update_slice(vectors, part, (row, first + deep * part.shape[1]))
    vectors = sum_all(vectors, gather_direct(vectors, "fsdp")[1:])
    everywhere = sum_all(vectors, gather_direct(vectors, "dp")[1:])
    vectors = jnp.where(jnp.arange(8)[:, None] < 6, everywhere, vectors)

    up_rows = jnp.stack([up_split[0]] + send_pieces(up_split[1:], "dp"))
    out_pieces = gather_direct(after(out_weight.astype(LOW), kvq_pieces[-1]), "fsdp")
    up_pieces = gather_direct(after(up_rows, kvq_pieces[-1]), "fsdp")
    down_pieces = gather_direct(after(fc2_weight.astype(LOW), kvq_pieces[-1]), "fsdp")

    (norm1,) = local_call(
        first_norm_kernel, (meta, token_rows, vectors), [low_like(rows, model)]
    )
    norm1_pieces = gather_pieces(norm1)
    kvq, kv, kvq_matrix, norm1_all = local_call(
        functools.partial(project_kernel, parts, depth),
        (meta, *norm1_pieces, *kvq_pieces, vectors),
        [
            low_like(group, 3 * width),
            low_like(group, 2 * width),
            low_like(model, 3 * width),
            low_like(group, model),
        ],
        flops=2 * group * model * 3 * width,
    )
    kv_earlier = jnp.stack([shift(kv, "ctx", by) for by in range(1, contexts)])

    grad_rows = transpose_homes(after(cotangent[0].astype(LOW), token_rows))
    branch_pieces = gather_pieces(after(grad_rows, norm1_pieces[-1]))

    score_flops = 2 * group * group * width
    wide_square = pltpu.VMEM((group, group), WIDE)
    low_square = pltpu.VMEM((group, group), LOW)
    acc, stat = local_call(
        functools.partial(own_forward, heads, rows),
        (meta, kvq),
        [wide_like(group, width), wide_like(group, 128)],
        [wide_square, low_square],
        flops=2 * score_flops,
    )
    context, context_low, stat, out_matrix, attended_keep, *attended_sends = local_call(
        functools.partial(context_kernel, parts, depth, heads),
        (meta, kvq, kv_earlier, acc, stat, *out_pieces),
        [
            wide_like(group, width),
            low_like(group, width),
            wide_like(group, 128),
            low_like(width, model),
            wide_like(rows, model),
        ]
        + [low_like(rows, model)] * (parts - 1),
        [wide_square, low_square, pltpu.VMEM((group, HEAD_DIM), WIDE)],
        flops=2 * score_flops,
    )
    arrived = send_pieces(attended_sends, "dp")
    norm2, attended = local_call(
        functools.partial(second_norm_kernel, parts),
        (meta, attended_keep, *arrived, token_rows, vectors),
        [low_like(rows, model), wide_like(rows, model)],
    )

    norm2_pieces = gather_pieces(norm2)
    norm2_keep, *rest = local_call(
        functools.partial(feed_kernel, parts, depth),
        (meta, *norm2_pieces, *branch_pieces, *up_pieces, *down_pieces, vectors),
        [wide_like(rows, model)]
        + [low_like(rows, model)] * (parts - 1)
        + [low_like(group, hidden_part)] * 2
        + [low_like(group, model)] * 2
        + [low_like(hidden_part, model), wide_like(1, hidden_part)],
        [
            pltpu.VMEM((model, hidden_part), LOW),
            pltpu.VMEM((group, hidden_part), WIDE),
            pltpu.VMEM((group, hidden_part), WIDE),
        ],
        flops=6 * group * model * hidden_part,
    )
    norm2_sends = rest[: parts - 1]
    hidden, inner_grad, norm2_all, branch_all, down_matrix, up_bias = rest[parts - 1 :]
    norm2_arrived = send_pieces(norm2_sends, "dp")
    feed_grads = local_call(
        functools.partial(feed_grad_kernel, parts, depth),
        (meta, hidden, inner_grad, norm2_all, branch_all, down_matrix),
        [wide_like(hidden_shard, model)]
        + [low_like(hidden_shard, model)] * (depth - 1)
        + [wide_like(parts, shard, hidden_part)]
        + [low_like(parts, shard, hidden_part)] * (depth - 1)
        + [wide_like(rows, model)]
        + [low_like(rows, model)] * (parts - 1),
        [pltpu.VMEM((max(model, hidden_part), max(model, hidden_part)), WIDE)],
        flops=6 * group * model * hidden_part,
    )
    down_keep, down_sends, up_keep, up_sends, fed_keep, fed_sends = take(
        feed_grads, None, depth - 1, None, depth - 1, None, parts - 1
    )
    attn_grad, mixed_part, sums = local_call(
        functools.partial(second_norm_grad_kernel, parts),
        (meta, norm2_keep, *norm2_arrived, token_rows, attended, grad_rows, vectors),
        [low_like(rows, model), wide_like(rows, model), wide_like(8, model)],
    )
    attn_pieces = gather_pieces(attn_grad)
    down_arrived = send_pieces(down_sends, "fsdp")
    up_arrived = send_pieces(up_sends, "fsdp")
    fed_arrived = send_pieces(
        lax.optimization_barrier((*fed_sends, attn_pieces[-1]))[: parts - 1], "dp"
    )

    ctx_grad, attn_all, query_grad, kv_grad = local_call(
        functools.partial(context_grad_kernel, parts, heads),
        (meta, *attn_pieces, out_matrix, kvq, kv_earlier, context, stat),
        [
            low_like(group, width),
            low_like(group, model),
            wide_like(group, width),
            low_like(*kv_earlier.shape),
        ],
        [wide_square, wide_square, low_square, low_square],
        flops=5 * score_flops,
    )
    kv_arrived = jnp.stack(
        [shift(kv_grad[by - 1], "ctx", -by) for by in range(1, contexts)]
    )
    kvq_own, out_keep, *out_sends = local_call(
        functools.partial(own_grad_kernel, parts, depth, heads, rows),
        (meta, kvq, ctx_grad, context, stat, query_grad, context_low, attn_all),
        [wide_like(group, 3 * width), wide_like(shard, model)]
        + [low_like(shard, model)] * (depth - 1),
        [
            pltpu.VMEM((width, model), WIDE), wide_square, wide_square, low_square, low_square,
        ],
        flops=5 * score_flops,
    )
    out_arrived = send_pieces(out_sends, "fsdp")
    kvq_grad, norm1_keep, *rest = local_call(
        functools.partial(projection_back_kernel, parts),
        (meta, kvq_own, kv_arrived, kvq_matrix),
        [low_like(group, 3 * width), wide_like(rows, model)]
        + [low_like(rows, model)] * (parts - 1)
        + [wide_like(1, 3 * width)],
        flops=2 * group * model * 3 * width,
    )
    kvq_bias = rest[-1]
    norm1_arrived = send_pieces(rest[:-1], "dp")
    kvq_keep, *kvq_sends = local_call(
        functools.partial(projection_grad_kernel, parts, depth),
        (meta, norm1_all, kvq_grad),
        [wide_like(parts, shard, 3 * width)]
        + [low_like(parts, shard, 3 * width)] * (depth - 1),
        [pltpu.VMEM((model, 3 * width), WIDE)],
        flops=2 * group * model * 3 * width,
    )
    kvq_arrived = send_pieces(kvq_sends, "fsdp")
    input_part, sums = local_call(
        functools.partial(first_norm_grad_kernel, parts),
        (
            meta, norm1_keep, *norm1_arrived, token_rows, vectors, mixed_part, sums, kvq_bias,
            up_bias,
        ),
        [low_like(rows, model), wide_like(8, model)],
    )

    delta = sum_all(fed_keep, fed_arrived) + vectors[5:6] + attended
    delta = after(delta.astype(LOW), kvq_own)
    output = tokens[0] + transpose_homes(delta).astype(WIDE)
    input_grad = cotangent[0] + transpose_homes(input_part).astype(WIDE)

    def owner_sum(keep, pieces, *later):
        low = sum_all(keep, pieces).astype(LOW)
        return sum_replicas(after(low, *later) if later else low)

    down_total = owner_sum(down_keep, down_arrived, kv_arrived)
    up_total = owner_sum(up_keep, up_arrived, kv_arrived).astype(LOW)
    out_total = owner_sum(out_keep, out_arrived, kv_arrived)
    up_sends = [after(up_total[slot], norm1_arrived[-1]) for slot in range(1, parts)]
    (up_total,) = local_call(
        functools.partial(join_up_kernel, parts),
        (meta, up_total[0], *send_pieces(up_sends, "dp")),
        [wide_like(shard, parts * hidden_part)],
    )
    kvq_total = owner_sum(kvq_keep, kvq_arrived).astype(LOW)
    (qkv_total,) = local_call(
        functools.partial(join_qkv_kernel, parts, width),
        (meta, kvq_total[0], *send_pieces([kvq_total[s] for s in range(1, parts)], "dp")),
        [wide_like(shard, 3 * model)],
    )
    sums = sum_all(sums, gather_direct(sums, "fsdp")[1:])
    sums = sum_replicas(sums)
    everywhere = sum_all(sums, gather_direct(sums, "dp")[1:])
    owned = lax.dynamic_slice(everywhere, (0, (mine * depth + deep) * shard), (6, shard))
    value_bias = lax.dynamic_slice(sums, (6, width + deep * shard), (1, shard))[0]
    query_bias = lax.dynamic_slice(sums, (6, 2 * width + deep * shard), (1, shard))[0]
    inner_bias = lax.dynamic_slice(sums, (7, deep * hidden_shard), (1, hidden_shard))[0]

    return (
        output[None],
        input_grad[None],
        owned[0],
        owned[1],
        qkv_total,
        query_bias,
        value_bias,
        out_total,
        owned[4],
        owned[2],
        owned[3],
        up_total,
        inner_bias,
        down_total,
        owned[5],
    )


def solution(mesh):
    rows = P("dp", ("ctx", "fsdp"), None)
    vector = P(("dp", "fsdp"))
    matrix = P(("dp", "fsdp"), None)
    parameters = (
        vector, vector, matrix, vector, vector, matrix, vector, vector, vector, matrix, vector,
        matrix, vector,
    )
    return jax.shard_map(
        local,
        mesh=mesh,
        in_specs=(rows, rows) + parameters,
        out_specs=(rows, rows) + parameters,
        check_vma=False,
    )
```

```python
import functools

import jax
import jax.numpy as jnp
from jax import lax
from jax.experimental import pallas as pl
from jax.experimental.pallas import tpu as pltpu
from jax.sharding import PartitionSpec as P

HEAD_DIM = 64
EPSILON = 1e-05
SCALE = HEAD_DIM ** (-0.5)
MASKED = -1e30
CHUNK = 64
GELU_SCALE = 0.7978845608
GELU_CUBE = 0.044715
LOW = jnp.bfloat16
WIDE = jnp.float32


def swap(value, axis, bit):
    count = lax.axis_size(axis)
    return lax.ppermute(value, axis, [(at, at ^ bit) for at in range(count)])


def shift(value, axis, by):
    count = lax.axis_size(axis)
    return lax.ppermute(value, axis, [(at, (at + by) % count) for at in range(count)])


def transpose_homes(value):
    side = lax.axis_size("dp")
    pairs = [(a * side + b, b * side + a) for a in range(side) for b in range(side)]
    return lax.ppermute(value, ("dp", "fsdp"), pairs)


def after(value, *others):
    return lax.optimization_barrier((value,) + others)[0]


def gather_pieces(block):
    pieces = [block]
    for slot in range(1, lax.axis_size("dp")):
        low_bit = slot & -slot
        pieces.append(swap(pieces[slot ^ low_bit], "dp", low_bit))
    return pieces


def send_pieces(sends, axis):
    return [swap(send, axis, slot) for slot, send in enumerate(sends, 1)]


def gather_direct(block, axis):
    return [block] + [swap(block, axis, slot) for slot in range(1, lax.axis_size(axis))]


def sum_doubling(value, axis):
    bit = 1
    while bit < lax.axis_size(axis):
        value = value + swap(value, axis, bit)
        bit *= 2
    return value


def sum_all(kept, arrived):
    total = kept
    for piece in arrived:
        total = total + piece.astype(WIDE)
    return total


def sum_replicas(value):
    if lax.axis_size("ctx") == 2:
        return value.astype(WIDE) + shift(value, "ctx", 1).astype(WIDE)
    return jnp.sum(lax.all_gather(value, "ctx").astype(WIDE), axis=0)


def matmul_nt(left, right):
    return lax.dot_general(left, right, (((1,), (1,)), ((), ())), preferred_element_type=WIDE)


def matmul_nn(left, right):
    return lax.dot_general(left, right, (((1,), (0,)), ((), ())), preferred_element_type=WIDE)


def matmul_tn(left, right):
    return lax.dot_general(left, right, (((0,), (0,)), ((), ())), preferred_element_type=WIDE)


def visible_block(place_ref, start, block_rows, columns):
    slot = start // block_rows
    query_pos = place_ref[slot] * block_rows + start % block_rows
    query_pos = query_pos + lax.broadcasted_iota(jnp.int32, (CHUNK, columns), 0)
    lane = lax.broadcasted_iota(jnp.int32, (CHUNK, columns), 1)
    key_pos = lane
    for at in range(columns // block_rows):
        inside = (lane >= at * block_rows) & (lane < (at + 1) * block_rows)
        key_pos = jnp.where(inside, place_ref[at] * block_rows + lane - at * block_rows, key_pos)
    return key_pos <= query_pos


def columns_of(head):
    return slice(head * HEAD_DIM, (head + 1) * HEAD_DIM)


def own_forward(heads, block_rows, place_ref, kvq_ref, acc_ref, stat_ref, score, prob):
    width = heads * HEAD_DIM
    rows = kvq_ref.shape[0]
    for head in range(heads):
        query = kvq_ref[:, 2 * width + head * HEAD_DIM : 2 * width + (head + 1) * HEAD_DIM]
        score[...] = matmul_nt(query, kvq_ref[:, columns_of(head)])

        def chunk(step, carry):
            start = pl.multiple_of(step * CHUNK, CHUNK)
            seen = visible_block(place_ref, start, block_rows, rows)
            scores = jnp.where(seen, score[pl.ds(start, CHUNK), :] * SCALE, MASKED)
            highest = jnp.max(scores, axis=1, keepdims=True)
            weight = jnp.exp(scores - highest)
            stat_ref[pl.ds(start, CHUNK), head : head + 1] = highest
            stat_ref[pl.ds(start, CHUNK), heads + head : heads + head + 1] = jnp.sum(
                weight, axis=1, keepdims=True
            )
            prob[pl.ds(start, CHUNK), :] = weight.astype(LOW)
            return carry

        lax.fori_loop(0, rows // CHUNK, chunk, 0)
        value = kvq_ref[:, width + head * HEAD_DIM : width + (head + 1) * HEAD_DIM]
        acc_ref[:, columns_of(head)] = matmul_nn(prob[...], value)


def earlier_forward(
    heads, slots, place_ref, kvq_ref, kv_ref, acc_in, stat_in, acc_ref, low_ref, stat_ref, score,
    prob, fade
):
    width = heads * HEAD_DIM
    rows = kvq_ref.shape[0]
    acc_ref[...] = acc_in[...]
    stat_ref[...] = stat_in[...]
    for piece in range(kv_ref.shape[0]):

        @pl.when(place_ref[slots] > piece)
        def _visit(piece=piece):
            for head in range(heads):
                query = kvq_ref[:, 2 * width + head * HEAD_DIM : 2 * width + (head + 1) * HEAD_DIM]
                score[...] = matmul_nt(query, kv_ref[piece, :, columns_of(head)])

                def chunk(step, carry):
                    here = pl.ds(pl.multiple_of(step * CHUNK, CHUNK), CHUNK)
                    scores = score[here, :] * SCALE
                    old = stat_ref[here, head : head + 1]
                    highest = jnp.maximum(old, jnp.max(scores, axis=1, keepdims=True))
                    weight = jnp.exp(scores - highest)
                    fading = jnp.exp(old - highest)
                    stat_ref[here, head : head + 1] = highest
                    total = stat_ref[here, heads + head : heads + head + 1]
                    stat_ref[here, heads + head : heads + head + 1] = total * fading + jnp.sum(
                        weight, axis=1, keepdims=True
                    )
                    fade[here, :] = jnp.broadcast_to(fading, (CHUNK, HEAD_DIM))
                    prob[here, :] = weight.astype(LOW)
                    return carry

                lax.fori_loop(0, rows // CHUNK, chunk, 0)
                value = kv_ref[piece, :, width + head * HEAD_DIM : width + (head + 1) * HEAD_DIM]
                acc_ref[:, columns_of(head)] = acc_ref[:, columns_of(head)] * fade[
                    ...
                ] + matmul_nn(prob[...], value)

    for head in range(heads):
        total = stat_ref[:, heads + head : heads + head + 1]
        context = acc_ref[:, columns_of(head)] / total
        acc_ref[:, columns_of(head)] = context
        low_ref[:, columns_of(head)] = context.astype(LOW)
        stat_ref[:, head : head + 1] = stat_ref[:, head : head + 1] + jnp.log(total)


def score_grads(here, seen, head, total, delta, score, dots, prob, grad):
    scores = score[here, :] * SCALE
    weight = jnp.exp(scores - total)
    if seen is not None:
        weight = jnp.where(seen, weight, 0.0)
    prob[here, :] = weight.astype(LOW)
    grad[here, :] = (weight * (dots[here, :] - delta) * SCALE).astype(LOW)


def delta_of(here, head, context_ref, ctx_grad_ref):
    product = context_ref[here, columns_of(head)] * ctx_grad_ref[here, columns_of(head)].astype(WIDE)
    return jnp.sum(product, axis=1, keepdims=True)


def earlier_backward(
    heads, slots, place_ref, kvq_ref, kv_ref, ctx_grad_ref, context_ref, stat_ref, query_grad_ref,
    kv_grad_ref, score, dots, prob, grad
):
    width = heads * HEAD_DIM
    rows = kvq_ref.shape[0]
    query_grad_ref[...] = jnp.zeros_like(query_grad_ref)
    for piece in range(kv_ref.shape[0]):

        @pl.when(place_ref[slots] <= piece)
        def _skip(piece=piece):
            kv_grad_ref[piece] = jnp.zeros(kv_grad_ref.shape[1:], kv_grad_ref.dtype)

        @pl.when(place_ref[slots] > piece)
        def _visit(piece=piece):
            for head in range(heads):
                query = kvq_ref[:, 2 * width + head * HEAD_DIM : 2 * width + (head + 1) * HEAD_DIM]
                value_at = slice(width + head * HEAD_DIM, width + (head + 1) * HEAD_DIM)
                key = kv_ref[piece, :, columns_of(head)]
                out_grad = ctx_grad_ref[:, columns_of(head)]
                score[...] = matmul_nt(query, key)
                dots[...] = matmul_nt(out_grad, kv_ref[piece, :, value_at])

                def chunk(step, carry):
                    here = pl.ds(pl.multiple_of(step * CHUNK, CHUNK), CHUNK)
                    total = stat_ref[here, head : head + 1]
                    delta = delta_of(here, head, context_ref, ctx_grad_ref)
                    score_grads(here, None, head, total, delta, score, dots, prob, grad)
                    return carry

                lax.fori_loop(0, rows // CHUNK, chunk, 0)
                kv_grad_ref[piece, :, columns_of(head)] = matmul_tn(grad[...], query).astype(LOW)
                kv_grad_ref[piece, :, value_at] = matmul_tn(prob[...], out_grad).astype(LOW)
                query_grad_ref[:, columns_of(head)] += matmul_nn(grad[...], key)


def own_backward(
    heads, block_rows, place_ref, kvq_ref, ctx_grad_ref, context_ref, stat_ref, query_grad_in,
    grad_ref, score, dots, prob, grad
):
    width = heads * HEAD_DIM
    rows = kvq_ref.shape[0]
    for head in range(heads):
        query_at = slice(2 * width + head * HEAD_DIM, 2 * width + (head + 1) * HEAD_DIM)
        value_at = slice(width + head * HEAD_DIM, width + (head + 1) * HEAD_DIM)
        query = kvq_ref[:, query_at]
        key = kvq_ref[:, columns_of(head)]
        out_grad = ctx_grad_ref[:, columns_of(head)]
        score[...] = matmul_nt(query, key)
        dots[...] = matmul_nt(out_grad, kvq_ref[:, value_at])

        def chunk(step, carry):
            start = pl.multiple_of(step * CHUNK, CHUNK)
            here = pl.ds(start, CHUNK)
            seen = visible_block(place_ref, start, block_rows, rows)
            total = stat_ref[here, head : head + 1]
            delta = delta_of(here, head, context_ref, ctx_grad_ref)
            score_grads(here, seen, head, total, delta, score, dots, prob, grad)
            return carry

        lax.fori_loop(0, rows // CHUNK, chunk, 0)
        grad_ref[:, columns_of(head)] = matmul_tn(grad[...], query)
        grad_ref[:, value_at] = matmul_tn(prob[...], out_grad)
        grad_ref[:, query_at] = query_grad_in[:, columns_of(head)] + matmul_nn(grad[...], key)


def normalize(values):
    centered = values - jnp.mean(values, axis=-1, keepdims=True)
    spread = jnp.mean(centered * centered, axis=-1, keepdims=True)
    inverse = lax.rsqrt(spread + EPSILON)
    return centered * inverse, inverse


def normalize_back(grad, gain, hat, inverse):
    scaled = grad * gain
    mean_scaled = jnp.mean(scaled, axis=-1, keepdims=True)
    mean_product = jnp.mean(scaled * hat, axis=-1, keepdims=True)
    part = inverse * (scaled - mean_scaled - hat * mean_product)
    gain_grad = jnp.sum(grad * hat, axis=0, keepdims=True)
    return part, gain_grad, jnp.sum(grad, axis=0, keepdims=True)


def take(refs, *counts):
    groups, at = [], 0
    for count in counts:
        if count is None:
            groups.append(refs[at])
            at += 1
        else:
            groups.append(refs[at : at + count])
            at += count
    return groups


def place_blocks(meta_ref, parts, depth, pieces, out_ref):
    rows = pieces[0].shape[1]
    for deep in range(depth):
        member = meta_ref[parts + 1] ^ deep
        for slot in range(parts):
            start = pl.multiple_of((meta_ref[slot] * depth + member) * rows, 16)
            out_ref[pl.ds(start, rows), :] = pieces[deep][slot]


def stack_rows(pieces, out_ref):
    rows = pieces[0].shape[0]
    for slot, piece in enumerate(pieces):
        out_ref[slot * rows : (slot + 1) * rows, :] = piece[...]


def emit_rows(partial, keep_ref, send_refs):
    rows = keep_ref.shape[0]
    keep_ref[...] = partial[:rows]
    for slot, send in enumerate(send_refs, 1):
        send[...] = partial[slot * rows : (slot + 1) * rows].astype(LOW)


def emit_blocks(meta_ref, parts, depth, whole_ref, keep_ref, send_refs):
    rows = keep_ref.shape[1]
    for deep in range(depth):
        member = meta_ref[parts + 1] ^ deep
        for slot in range(parts):
            start = pl.multiple_of((meta_ref[slot] * depth + member) * rows, 16)
            block = whole_ref[pl.ds(start, rows), :]
            if deep:
                send_refs[deep - 1][slot] = block.astype(LOW)
            else:
                keep_ref[slot] = block


def emit_shards(meta_ref, parts, whole_ref, keep_ref, send_refs):
    rows = keep_ref.shape[0]
    for deep in range(len(send_refs) + 1):
        start = pl.multiple_of((meta_ref[parts + 1] ^ deep) * rows, 16)
        block = whole_ref[pl.ds(start, rows), :]
        if deep:
            send_refs[deep - 1][...] = block.astype(LOW)
        else:
            keep_ref[...] = block


def pack_sizes(parts, shard, hidden_shard):
    main = max(parts * shard, hidden_shard)
    extra = 16 * (-(-shard // 32))
    return main, extra, main + extra


def pack_kernel(parts, both, meta_ref, *refs):
    up, out_weight, down_weight, packed = take(refs, parts, None, None, None)
    shard = out_weight.shape[0]
    hidden_shard = down_weight.shape[0]
    main, extra, _ = pack_sizes(parts, shard, hidden_shard)
    packed[...] = jnp.zeros_like(packed)

    def fill(half, at):
        if half == 0:
            for slot in range(parts):
                packed[at, slot * shard : (slot + 1) * shard, :] = up[slot][...]
            packed[at, main : main + extra, :] = out_weight[:extra, :].astype(LOW)
        else:
            packed[at, :hidden_shard, :] = down_weight[...].astype(LOW)
            packed[at, main : main + shard - extra, :] = out_weight[extra:, :].astype(LOW)

    for half in range(2):
        if both:
            fill(half, half)
        else:
            pl.when(meta_ref[parts] == half)(functools.partial(fill, half, 0))


def split_qkv_kernel(parts, width, meta_ref, qkv_ref, *outs):
    model = parts * width
    for case in range(parts):

        @pl.when(meta_ref[0] == case)
        def _case(case=case):
            for slot in range(parts):
                owner = case ^ slot
                for at, first in enumerate((model, 2 * model, 0)):
                    start = first + owner * width
                    outs[slot][:, at * width : (at + 1) * width] = qkv_ref[
                        :, start : start + width
                    ].astype(LOW)


def split_up_kernel(parts, meta_ref, up_ref, *outs):
    part = up_ref.shape[1] // parts
    for slot in range(parts):
        start = pl.multiple_of(meta_ref[slot] * part, 128)
        outs[slot][...] = up_ref[:, pl.ds(start, part)].astype(LOW)


def join_qkv_kernel(parts, width, meta_ref, *refs):
    pieces, out_ref = refs[:parts], refs[parts]
    model = parts * width
    for case in range(parts):

        @pl.when(meta_ref[0] == case)
        def _case(case=case):
            for slot in range(parts):
                owner = case ^ slot
                for at, first in enumerate((model, 2 * model, 0)):
                    start = first + owner * width
                    out_ref[:, start : start + width] = pieces[slot][
                        :, at * width : (at + 1) * width
                    ].astype(WIDE)


def join_up_kernel(parts, meta_ref, *refs):
    pieces, out_ref = refs[:parts], refs[parts]
    part = pieces[0].shape[1]
    for slot in range(parts):
        start = pl.multiple_of(meta_ref[slot] * part, 128)
        out_ref[:, pl.ds(start, part)] = pieces[slot][...].astype(WIDE)


def first_norm_kernel(meta_ref, tokens_ref, vectors_ref, out_ref):
    hat, _ = normalize(tokens_ref[...].astype(WIDE))
    out_ref[...] = (hat * vectors_ref[0:1, :] + vectors_ref[1:2, :]).astype(LOW)


def project_kernel(parts, depth, meta_ref, *refs):
    norm, weight, vectors_ref, kvq_ref, kv_ref, matrix_ref, norm_ref = take(
        refs, parts, depth, None, None, None, None, None
    )
    columns = kvq_ref.shape[1]
    place_blocks(meta_ref, parts, depth, weight, matrix_ref)
    stack_rows(norm, norm_ref)
    low = (matmul_nn(norm_ref[...], matrix_ref[...]) + vectors_ref[6:7, :columns]).astype(LOW)
    kvq_ref[...] = low
    kv_ref[...] = low[:, : kv_ref.shape[1]]


def context_kernel(parts, depth, heads, meta_ref, *refs):
    (
        kvq, kv, acc_in, stat_in, weight, context, low, stat, matrix, keep, sends, score, prob, fade
    ) = take(
        refs, None, None, None, None, None, None, None, None, None, None, parts - 1, None, None,
        None,
    )
    extra = weight.shape[2]
    shard = matrix.shape[0] // depth
    for deep in range(depth):
        start = deep * shard
        matrix[start : start + extra, :] = weight[0, deep]
        matrix[start + extra : start + shard, :] = weight[1, deep, : shard - extra]
    earlier_forward(
        heads, parts, meta_ref, kvq, kv, acc_in, stat_in, context, low, stat, score, prob, fade
    )
    emit_rows(matmul_nn(low[...], matrix[...]), keep, sends)


def second_norm_kernel(parts, meta_ref, *refs):
    keep, arrived, tokens, vectors, out, attended_ref = take(
        refs, None, parts - 1, None, None, None, None
    )
    attended = sum_all(keep[...], [piece[...] for piece in arrived]) + vectors[4:5, :]
    attended_ref[...] = attended
    hat, _ = normalize(tokens[...].astype(WIDE) + attended)
    out[...] = (hat * vectors[2:3, :] + vectors[3:4, :]).astype(LOW)


def feed_kernel(parts, depth, meta_ref, *refs):
    (
        norm, branch, weight, vectors, keep, sends, hidden, inner_grad, norm_all, branch_all,
        down_all, up_bias, up_all, inner, grad,
    ) = take(refs, parts, parts, None, None, None, parts - 1, *([None] * 9))
    shard = up_all.shape[0] // (parts * depth)
    hidden_shard = down_all.shape[0] // depth
    for deep in range(depth):
        for slot in range(parts):
            start = pl.multiple_of((meta_ref[slot] * depth + deep) * shard, 16)
            up_all[pl.ds(start, shard), :] = weight[0, deep, slot * shard : (slot + 1) * shard]
        down_all[deep * hidden_shard : (deep + 1) * hidden_shard, :] = weight[
            1, deep, :hidden_shard
        ]
    stack_rows(norm, norm_all)
    stack_rows(branch, branch_all)
    inner[...] = matmul_nn(norm_all[...], up_all[...])
    grad[...] = matmul_nt(branch_all[...], down_all[...])
    up_bias[...] = jnp.zeros_like(up_bias)

    def chunk(step, carry):
        here = pl.ds(pl.multiple_of(step * CHUNK, CHUNK), CHUNK)
        value = inner[here, :] + vectors[7:8, :]
        square = value * value
        bent = jnp.tanh(GELU_SCALE * (value + GELU_CUBE * square * value))
        hidden[here, :] = (0.5 * value * (1.0 + bent)).astype(LOW)
        slope = 0.5 * (1.0 + bent) + 0.5 * value * (1.0 - bent * bent) * GELU_SCALE * (
            1.0 + 3.0 * GELU_CUBE * square
        )
        low = (grad[here, :] * slope).astype(LOW)
        inner_grad[here, :] = low
        up_bias[...] += jnp.sum(low.astype(WIDE), axis=0, keepdims=True)
        return carry

    lax.fori_loop(0, inner.shape[0] // CHUNK, chunk, 0)
    emit_rows(matmul_nt(inner_grad[...], up_all[...]), keep, sends)


def feed_grad_kernel(parts, depth, meta_ref, *refs):
    hidden, inner_grad, norm_all, branch_all, down_all, grads, fed_keep, fed_sends, whole = take(
        refs, None, None, None, None, None, None, None, parts - 1, None
    )
    hidden_shard = hidden.shape[1] // depth
    shard = norm_all.shape[1] // (parts * depth)
    grads[...] = jnp.zeros_like(grads)
    whole[...] = matmul_tn(hidden[...], branch_all[...])
    for deep in range(depth):
        grads[1, deep, :hidden_shard] = whole[
            deep * hidden_shard : (deep + 1) * hidden_shard, :
        ].astype(LOW)
    whole[...] = matmul_tn(norm_all[...], inner_grad[...])
    for deep in range(depth):
        for slot in range(parts):
            start = pl.multiple_of((meta_ref[slot] * depth + deep) * shard, 16)
            grads[0, deep, slot * shard : (slot + 1) * shard] = whole[
                pl.ds(start, shard), :
            ].astype(LOW)
    emit_rows(matmul_nn(hidden[...], down_all[...]), fed_keep, fed_sends)


def second_norm_grad_kernel(parts, meta_ref, *refs):
    keep, arrived, tokens, attended, branch, vectors, attn_grad, mixed_part, sums = take(
        refs, None, parts - 1, None, None, None, None, None, None, None
    )
    grad = sum_all(keep[...], [piece[...] for piece in arrived])
    hat, inverse = normalize(tokens[...].astype(WIDE) + attended[...])
    part, gain_grad, bias_grad = normalize_back(grad, vectors[2:3, :], hat, inverse)
    mixed_part[...] = part
    branch_rows = branch[...].astype(WIDE)
    low = (branch_rows + part).astype(LOW)
    attn_grad[...] = low
    sums[...] = jnp.zeros_like(sums)
    sums[2:3, :] = gain_grad
    sums[3:4, :] = bias_grad
    sums[4:5, :] = jnp.sum(low.astype(WIDE), axis=0, keepdims=True)
    sums[5:6, :] = jnp.sum(branch_rows, axis=0, keepdims=True)


def context_grad_kernel(parts, heads, meta_ref, *refs):
    (
        attn, matrix, kvq, kv, context, stat, ctx_grad, attn_all, query_grad, kv_grad, score, dots,
        prob, grad,
    ) = take(refs, parts, *([None] * 13))
    stack_rows(attn, attn_all)
    ctx_grad[...] = matmul_nt(attn_all[...], matrix[...]).astype(LOW)
    earlier_backward(
        heads, parts, meta_ref, kvq, kv, ctx_grad, context, stat, query_grad, kv_grad, score, dots,
        prob, grad,
    )


def own_grad_kernel(parts, depth, heads, rows, meta_ref, *refs):
    (
        kvq, ctx_grad, context, stat, query_grad, low, attn_all, kvq_grad, out_keep, out_sends,
        whole, score, dots, prob, grad,
    ) = take(refs, *([None] * 9), depth - 1, *([None] * 5))
    own_backward(
        heads, rows, meta_ref, kvq, ctx_grad, context, stat, query_grad, kvq_grad, score, dots,
        prob, grad,
    )
    whole[...] = matmul_tn(low[...], attn_all[...])
    emit_shards(meta_ref, parts, whole, out_keep, out_sends)


def projection_back_kernel(parts, meta_ref, *refs):
    own, arrived, matrix, kvq_grad, keep, sends, bias = take(
        refs, None, None, None, None, None, parts - 1, None
    )
    kv_width = arrived.shape[2]
    total = own[:, :kv_width]
    for piece in range(arrived.shape[0]):
        total = total + arrived[piece].astype(WIDE)
    kvq_grad[:, :kv_width] = total.astype(LOW)
    kvq_grad[:, kv_width:] = own[:, kv_width:].astype(LOW)
    emit_rows(matmul_nt(kvq_grad[...], matrix[...]), keep, sends)
    bias[...] = jnp.sum(kvq_grad[...].astype(WIDE), axis=0, keepdims=True)


def projection_grad_kernel(parts, depth, meta_ref, *refs):
    norm, kvq_grad, keep, sends, whole = take(refs, None, None, None, depth - 1, None)
    whole[...] = matmul_tn(norm[...], kvq_grad[...])
    emit_blocks(meta_ref, parts, depth, whole, keep, sends)


def first_norm_grad_kernel(parts, meta_ref, *refs):
    keep, arrived, tokens, vectors, mixed_part, sums_in, kvq_bias, up_bias, out, sums = take(
        refs, None, parts - 1, *([None] * 8)
    )
    grad = sum_all(keep[...], [piece[...] for piece in arrived])
    hat, inverse = normalize(tokens[...].astype(WIDE))
    part, gain_grad, bias_grad = normalize_back(grad, vectors[0:1, :], hat, inverse)
    out[...] = (mixed_part[...] + part).astype(LOW)
    sums[...] = sums_in[...]
    sums[0:1, :] = gain_grad
    sums[1:2, :] = bias_grad
    sums[6:7, : kvq_bias.shape[1]] = kvq_bias[...]
    sums[7:8, :] = up_bias[...]


def local_call(kernel, operands, results, scratch=(), flops=0, specs={}):
    smem = pl.BlockSpec(memory_space=pltpu.SMEM)
    vmem = pl.BlockSpec(memory_space=pltpu.VMEM)
    moved = sum(each.size * each.dtype.itemsize for each in tuple(operands) + tuple(results))
    return pl.pallas_call(
        kernel,
        out_shape=tuple(results),
        grid=(1,),
        in_specs=[smem] + [specs.get(at, vmem) for at in range(1, len(operands))],
        out_specs=tuple([vmem] * len(results)),
        scratch_shapes=list(scratch),
        compiler_params=pltpu.CompilerParams(vmem_limit_bytes=48 * 1024 * 1024),
        cost_estimate=pl.CostEstimate(flops=flops, bytes_accessed=moved, transcendentals=0),
    )(*operands)


def low_like(*shape):
    return jax.ShapeDtypeStruct(shape, LOW)


def wide_like(*shape):
    return jax.ShapeDtypeStruct(shape, WIDE)


def local(
    tokens, cotangent, ln1_gain, ln1_bias, qkv_weight, q_bias, v_bias, out_weight, out_bias,
    ln2_gain, ln2_bias, fc1_weight, fc1_bias, fc2_weight, fc2_bias,
):
    parts = lax.axis_size("dp")
    depth = lax.axis_size("fsdp")
    contexts = lax.axis_size("ctx")
    assert parts == depth
    mine = lax.axis_index("dp")
    deep = lax.axis_index("fsdp")
    rows, model = tokens.shape[1:]
    shard = ln1_gain.shape[0]
    heads = model // HEAD_DIM // parts
    width = heads * HEAD_DIM
    hidden_shard = fc1_bias.shape[0]
    hidden_part = hidden_shard * depth
    group = parts * rows
    meta = jnp.stack(
        [mine ^ slot for slot in range(parts)] + [lax.axis_index("ctx"), deep]
    ).astype(jnp.int32)

    kvq_split = local_call(
        functools.partial(split_qkv_kernel, parts, width),
        (meta, qkv_weight),
        [low_like(shard, 3 * width)] * parts,
    )
    kvq_rows = jnp.stack([kvq_split[0]] + send_pieces(kvq_split[1:], "dp"))
    kvq_pieces = gather_direct(kvq_rows, "fsdp")

    token_rows = transpose_homes(after(tokens[0].astype(LOW), kvq_split[0]))

    low_vectors = jnp.stack([ln1_gain, ln1_bias, ln2_gain, ln2_bias, out_bias, fc2_bias])
    vectors = jnp.zeros((8, model), WIDE)
    vectors = lax.dynamic_update_slice(
        vectors, low_vectors.astype(LOW).astype(WIDE), (0, (mine * depth + deep) * shard)
    )
    for row, first, part in (
        (6, width, v_bias), (6, 2 * width, q_bias), (7, 0, fc1_bias),
    ):
        part = part.astype(LOW).astype(WIDE)[None]
        vectors = lax.dynamic_update_slice(vectors, part, (row, first + deep * part.shape[1]))
    vectors = sum_doubling(after(vectors, kvq_split[0]), "fsdp")
    everywhere = sum_doubling(vectors, "dp")
    vectors = jnp.where(jnp.arange(8)[:, None] < 6, everywhere, vectors)

    halves = contexts == 2
    main, extra, half_rows = pack_sizes(parts, shard, hidden_shard)
    up_split = local_call(
        functools.partial(split_up_kernel, parts),
        (meta, fc1_weight),
        [low_like(shard, hidden_part)] * parts,
    )
    up_arrived = send_pieces(up_split[1:], "dp")
    (packed,) = local_call(
        functools.partial(pack_kernel, parts, not halves),
        (meta, up_split[0], *up_arrived, out_weight, fc2_weight),
        [low_like(1 if halves else 2, half_rows, model)],
    )
    if halves:
        weights = lax.all_gather(packed, ("ctx", "fsdp"), axis=0, tiled=True)
        weights = weights.reshape(2, depth, half_rows, model)
    else:
        weights = lax.all_gather(packed, "fsdp", axis=1)

    (norm1,) = local_call(
        first_norm_kernel, (meta, token_rows, vectors), [low_like(rows, model)]
    )
    norm1_pieces = gather_pieces(norm1)
    kvq, kv, kvq_matrix, norm1_all = local_call(
        functools.partial(project_kernel, parts, depth),
        (meta, *norm1_pieces, *kvq_pieces, vectors),
        [
            low_like(group, 3 * width),
            low_like(group, 2 * width),
            low_like(model, 3 * width),
            low_like(group, model),
        ],
        flops=2 * group * model * 3 * width,
    )
    kv_earlier = jnp.stack([shift(kv, "ctx", by) for by in range(1, contexts)])

    grad_rows = transpose_homes(after(cotangent[0].astype(LOW), token_rows))
    branch_pieces = gather_pieces(after(grad_rows, norm1_pieces[-1]))

    score_flops = 2 * group * group * width
    wide_square = pltpu.VMEM((group, group), WIDE)
    low_square = pltpu.VMEM((group, group), LOW)
    acc, stat = local_call(
        functools.partial(own_forward, heads, rows),
        (meta, kvq),
        [wide_like(group, width), wide_like(group, 128)],
        [wide_square, low_square],
        flops=2 * score_flops,
    )
    context, context_low, stat, out_matrix, attended_keep, *attended_sends = local_call(
        functools.partial(context_kernel, parts, depth, heads),
        (meta, kvq, kv_earlier, acc, stat, weights),
        [
            wide_like(group, width),
            low_like(group, width),
            wide_like(group, 128),
            low_like(width, model),
            wide_like(rows, model),
        ]
        + [low_like(rows, model)] * (parts - 1),
        [wide_square, low_square, pltpu.VMEM((group, HEAD_DIM), WIDE)],
        flops=2 * score_flops,
        specs={
            5: pl.BlockSpec((2, depth, extra, model), lambda _: (0, 0, main // extra, 0))
        },
    )
    arrived = send_pieces(attended_sends, "dp")
    norm2, attended = local_call(
        functools.partial(second_norm_kernel, parts),
        (meta, attended_keep, *arrived, token_rows, vectors),
        [low_like(rows, model), wide_like(rows, model)],
    )

    norm2_pieces = gather_pieces(norm2)
    norm2_keep, *rest = local_call(
        functools.partial(feed_kernel, parts, depth),
        (meta, *norm2_pieces, *branch_pieces, weights, vectors),
        [wide_like(rows, model)]
        + [low_like(rows, model)] * (parts - 1)
        + [low_like(group, hidden_part)] * 2
        + [low_like(group, model)] * 2
        + [low_like(hidden_part, model), wide_like(1, hidden_part)],
        [
            pltpu.VMEM((model, hidden_part), LOW),
            pltpu.VMEM((group, hidden_part), WIDE),
            pltpu.VMEM((group, hidden_part), WIDE),
        ],
        flops=6 * group * model * hidden_part,
    )
    norm2_sends = rest[: parts - 1]
    hidden, inner_grad, norm2_all, branch_all, down_matrix, up_bias = rest[parts - 1 :]
    norm2_arrived = send_pieces(norm2_sends, "dp")
    feed_grads, fed_keep, *fed_sends = local_call(
        functools.partial(feed_grad_kernel, parts, depth),
        (meta, hidden, inner_grad, norm2_all, branch_all, down_matrix),
        [low_like(2, depth, main, model), wide_like(rows, model)]
        + [low_like(rows, model)] * (parts - 1),
        [pltpu.VMEM((max(model, hidden_part), max(model, hidden_part)), WIDE)],
        flops=6 * group * model * hidden_part,
    )
    if halves:
        mine_half = lax.psum_scatter(
            feed_grads.reshape(2 * depth, main, model), ("ctx", "fsdp"), tiled=True
        )[0]
    else:
        feed_total = lax.psum_scatter(feed_grads, "fsdp", scatter_dimension=1)
        feed_total = lax.psum(feed_total, "ctx")
    attn_grad, mixed_part, sums = local_call(
        functools.partial(second_norm_grad_kernel, parts),
        (meta, norm2_keep, *norm2_arrived, token_rows, attended, grad_rows, vectors),
        [low_like(rows, model), wide_like(rows, model), wide_like(8, model)],
    )
    attn_pieces = gather_pieces(attn_grad)
    fed_arrived = send_pieces(
        lax.optimization_barrier((*fed_sends, attn_pieces[-1]))[: parts - 1], "dp"
    )

    ctx_grad, attn_all, query_grad, kv_grad = local_call(
        functools.partial(context_grad_kernel, parts, heads),
        (meta, *attn_pieces, out_matrix, kvq, kv_earlier, context, stat),
        [
            low_like(group, width),
            low_like(group, model),
            wide_like(group, width),
            low_like(*kv_earlier.shape),
        ],
        [wide_square, wide_square, low_square, low_square],
        flops=5 * score_flops,
    )
    kv_arrived = jnp.stack(
        [shift(kv_grad[by - 1], "ctx", -by) for by in range(1, contexts)]
    )
    kvq_own, out_keep, *out_sends = local_call(
        functools.partial(own_grad_kernel, parts, depth, heads, rows),
        (meta, kvq, ctx_grad, context, stat, query_grad, context_low, attn_all),
        [wide_like(group, 3 * width), wide_like(shard, model)]
        + [low_like(shard, model)] * (depth - 1),
        [
            pltpu.VMEM((width, model), WIDE), wide_square, wide_square, low_square, low_square,
        ],
        flops=5 * score_flops,
    )
    out_arrived = send_pieces(out_sends, "fsdp")
    kvq_grad, norm1_keep, *rest = local_call(
        functools.partial(projection_back_kernel, parts),
        (meta, kvq_own, kv_arrived, kvq_matrix),
        [low_like(group, 3 * width), wide_like(rows, model)]
        + [low_like(rows, model)] * (parts - 1)
        + [wide_like(1, 3 * width)],
        flops=2 * group * model * 3 * width,
    )
    kvq_bias = rest[-1]
    norm1_arrived = send_pieces(rest[:-1], "dp")
    kvq_keep, *kvq_sends = local_call(
        functools.partial(projection_grad_kernel, parts, depth),
        (meta, norm1_all, kvq_grad),
        [wide_like(parts, shard, 3 * width)]
        + [low_like(parts, shard, 3 * width)] * (depth - 1),
        [pltpu.VMEM((model, 3 * width), WIDE)],
        flops=2 * group * model * 3 * width,
    )
    kvq_arrived = send_pieces(kvq_sends, "fsdp")
    input_part, sums = local_call(
        functools.partial(first_norm_grad_kernel, parts),
        (
            meta, norm1_keep, *norm1_arrived, token_rows, vectors, mixed_part, sums, kvq_bias,
            up_bias,
        ),
        [low_like(rows, model), wide_like(8, model)],
    )

    delta = sum_all(fed_keep, fed_arrived) + vectors[5:6] + attended
    delta = after(delta.astype(LOW), kvq_own)
    output = tokens[0] + transpose_homes(delta).astype(WIDE)
    input_grad = cotangent[0] + transpose_homes(input_part).astype(WIDE)

    def owner_sum(keep, pieces, *later):
        low = sum_all(keep, pieces).astype(LOW)
        return sum_replicas(after(low, *later) if later else low)

    out_total = owner_sum(out_keep, out_arrived, kv_arrived)
    if halves:
        other_half = shift(after(mine_half, kv_arrived), "ctx", 1)
        first = lax.axis_index("ctx") == 0
        up_total = jnp.where(first, mine_half, other_half)
        down_total = jnp.where(first, other_half, mine_half)
    else:
        up_total, down_total = feed_total
    up_total = up_total[: parts * shard].reshape(parts, shard, hidden_part)
    down_total = down_total[:hidden_shard].astype(WIDE)
    up_sends = [after(up_total[slot], norm1_arrived[-1]) for slot in range(1, parts)]
    (up_total,) = local_call(
        functools.partial(join_up_kernel, parts),
        (meta, up_total[0], *send_pieces(up_sends, "dp")),
        [wide_like(shard, parts * hidden_part)],
    )
    kvq_total = owner_sum(kvq_keep, kvq_arrived).astype(LOW)
    (qkv_total,) = local_call(
        functools.partial(join_qkv_kernel, parts, width),
        (meta, kvq_total[0], *send_pieces([kvq_total[s] for s in range(1, parts)], "dp")),
        [wide_like(shard, 3 * model)],
    )
    sums = sum_replicas(sum_doubling(sums, "fsdp"))
    everywhere = sum_doubling(sums, "dp")
    owned = lax.dynamic_slice(everywhere, (0, (mine * depth + deep) * shard), (6, shard))
    value_bias = lax.dynamic_slice(sums, (6, width + deep * shard), (1, shard))[0]
    query_bias = lax.dynamic_slice(sums, (6, 2 * width + deep * shard), (1, shard))[0]
    inner_bias = lax.dynamic_slice(sums, (7, deep * hidden_shard), (1, hidden_shard))[0]

    return (
        output[None],
        input_grad[None],
        owned[0],
        owned[1],
        qkv_total,
        query_bias,
        value_bias,
        out_total,
        owned[4],
        owned[2],
        owned[3],
        up_total,
        inner_bias,
        down_total,
        owned[5],
    )


def solution(mesh):
    rows = P("dp", ("ctx", "fsdp"), None)
    vector = P(("dp", "fsdp"))
    matrix = P(("dp", "fsdp"), None)
    parameters = (
        vector, vector, matrix, vector, vector, matrix, vector, vector, vector, matrix, vector,
        matrix, vector,
    )
    return jax.shard_map(
        local,
        mesh=mesh,
        in_specs=(rows, rows) + parameters,
        out_specs=(rows, rows) + parameters,
        check_vma=False,
    )
```

```python
import functools

import jax
import jax.numpy as jnp
from jax import lax
from jax.experimental import pallas as pl
from jax.experimental.pallas import tpu as pltpu
from jax.sharding import PartitionSpec as P

HEAD_DIM = 64
EPSILON = 1e-05
SCALE = HEAD_DIM ** (-0.5)
MASKED = -1e30
CHUNK = 64
VMEM_BYTES = 16 * 1024 * 1024
GELU_SCALE = 0.7978845608
GELU_CUBE = 0.044715
LOW = jnp.bfloat16
WIDE = jnp.float32


def swap(value, axis, bit):
    count = lax.axis_size(axis)
    return lax.ppermute(value, axis, [(at, at ^ bit) for at in range(count)])


def shift(value, axis, by):
    count = lax.axis_size(axis)
    return lax.ppermute(value, axis, [(at, (at + by) % count) for at in range(count)])


def transpose_homes(value):
    side = lax.axis_size("dp")
    pairs = [(a * side + b, b * side + a) for a in range(side) for b in range(side)]
    return lax.ppermute(value, ("dp", "fsdp"), pairs)


def after(value, *others):
    return lax.optimization_barrier((value,) + others)[0]


def gather_pieces(block):
    pieces = [block]
    for slot in range(1, lax.axis_size("dp")):
        low_bit = slot & -slot
        pieces.append(swap(pieces[slot ^ low_bit], "dp", low_bit))
    return pieces


def send_pieces(sends, axis):
    return [swap(send, axis, slot) for slot, send in enumerate(sends, 1)]


def gather_direct(block, axis):
    return [block] + [swap(block, axis, slot) for slot in range(1, lax.axis_size(axis))]


def sum_doubling(value, axis):
    bit = 1
    while bit < lax.axis_size(axis):
        value = value + swap(value, axis, bit)
        bit *= 2
    return value


def sum_all(kept, arrived):
    total = kept
    for piece in arrived:
        total = total + piece.astype(WIDE)
    return total


def sum_replicas(value):
    if lax.axis_size("ctx") == 2:
        return value.astype(WIDE) + shift(value, "ctx", 1).astype(WIDE)
    return jnp.sum(lax.all_gather(value, "ctx").astype(WIDE), axis=0)


def matmul_nt(left, right):
    return lax.dot_general(left, right, (((1,), (1,)), ((), ())), preferred_element_type=WIDE)


def matmul_nn(left, right):
    return lax.dot_general(left, right, (((1,), (0,)), ((), ())), preferred_element_type=WIDE)


def matmul_tn(left, right):
    return lax.dot_general(left, right, (((0,), (0,)), ((), ())), preferred_element_type=WIDE)


def visible_block(place_ref, start, block_rows, columns):
    slot = start // block_rows
    query_pos = place_ref[slot] * block_rows + start % block_rows
    query_pos = query_pos + lax.broadcasted_iota(jnp.int32, (CHUNK, columns), 0)
    lane = lax.broadcasted_iota(jnp.int32, (CHUNK, columns), 1)
    key_pos = lane
    for at in range(columns // block_rows):
        inside = (lane >= at * block_rows) & (lane < (at + 1) * block_rows)
        key_pos = jnp.where(inside, place_ref[at] * block_rows + lane - at * block_rows, key_pos)
    return key_pos <= query_pos


def columns_of(head):
    return slice(head * HEAD_DIM, (head + 1) * HEAD_DIM)


def own_forward(heads, block_rows, place_ref, kvq_ref, acc_ref, stat_ref, score, prob):
    width = heads * HEAD_DIM
    rows = kvq_ref.shape[0]
    for head in range(heads):
        query = kvq_ref[:, 2 * width + head * HEAD_DIM : 2 * width + (head + 1) * HEAD_DIM]
        score[...] = matmul_nt(query, kvq_ref[:, columns_of(head)])

        def chunk(step, carry):
            start = pl.multiple_of(step * CHUNK, CHUNK)
            seen = visible_block(place_ref, start, block_rows, rows)
            scores = jnp.where(seen, score[pl.ds(start, CHUNK), :] * SCALE, MASKED)
            highest = jnp.max(scores, axis=1, keepdims=True)
            weight = jnp.exp(scores - highest)
            stat_ref[pl.ds(start, CHUNK), head : head + 1] = highest
            stat_ref[pl.ds(start, CHUNK), heads + head : heads + head + 1] = jnp.sum(
                weight, axis=1, keepdims=True
            )
            prob[pl.ds(start, CHUNK), :] = weight.astype(LOW)
            return carry

        lax.fori_loop(0, rows // CHUNK, chunk, 0)
        value = kvq_ref[:, width + head * HEAD_DIM : width + (head + 1) * HEAD_DIM]
        acc_ref[:, columns_of(head)] = matmul_nn(prob[...], value)


def earlier_forward(
    heads, slots, place_ref, kvq_ref, kv_ref, acc_in, stat_in, acc_ref, low_ref, stat_ref, score,
    prob, fade
):
    width = heads * HEAD_DIM
    rows = kvq_ref.shape[0]
    acc_ref[...] = acc_in[...]
    stat_ref[...] = stat_in[...]
    for piece in range(kv_ref.shape[0]):

        @pl.when(place_ref[slots] > piece)
        def _visit(piece=piece):
            for head in range(heads):
                query = kvq_ref[:, 2 * width + head * HEAD_DIM : 2 * width + (head + 1) * HEAD_DIM]
                score[...] = matmul_nt(query, kv_ref[piece, :, columns_of(head)])

                def chunk(step, carry):
                    here = pl.ds(pl.multiple_of(step * CHUNK, CHUNK), CHUNK)
                    scores = score[here, :] * SCALE
                    old = stat_ref[here, head : head + 1]
                    highest = jnp.maximum(old, jnp.max(scores, axis=1, keepdims=True))
                    weight = jnp.exp(scores - highest)
                    fading = jnp.exp(old - highest)
                    stat_ref[here, head : head + 1] = highest
                    total = stat_ref[here, heads + head : heads + head + 1]
                    stat_ref[here, heads + head : heads + head + 1] = total * fading + jnp.sum(
                        weight, axis=1, keepdims=True
                    )
                    fade[here, :] = jnp.broadcast_to(fading, (CHUNK, HEAD_DIM))
                    prob[here, :] = weight.astype(LOW)
                    return carry

                lax.fori_loop(0, rows // CHUNK, chunk, 0)
                value = kv_ref[piece, :, width + head * HEAD_DIM : width + (head + 1) * HEAD_DIM]
                acc_ref[:, columns_of(head)] = acc_ref[:, columns_of(head)] * fade[
                    ...
                ] + matmul_nn(prob[...], value)

    for head in range(heads):
        total = stat_ref[:, heads + head : heads + head + 1]
        context = acc_ref[:, columns_of(head)] / total
        acc_ref[:, columns_of(head)] = context
        low_ref[:, columns_of(head)] = context.astype(LOW)
        stat_ref[:, head : head + 1] = stat_ref[:, head : head + 1] + jnp.log(total)


def score_grads(here, seen, head, total, delta, score, dots, prob, grad):
    scores = score[here, :] * SCALE
    weight = jnp.exp(scores - total)
    if seen is not None:
        weight = jnp.where(seen, weight, 0.0)
    prob[here, :] = weight.astype(LOW)
    grad[here, :] = (weight * (dots[here, :] - delta) * SCALE).astype(LOW)


def delta_of(here, head, context_ref, ctx_grad_ref):
    product = context_ref[here, columns_of(head)] * ctx_grad_ref[here, columns_of(head)].astype(WIDE)
    return jnp.sum(product, axis=1, keepdims=True)


def earlier_backward(
    heads, slots, place_ref, kvq_ref, kv_ref, ctx_grad_ref, context_ref, stat_ref, query_grad_ref,
    kv_grad_ref, score, dots, prob, grad
):
    width = heads * HEAD_DIM
    rows = kvq_ref.shape[0]
    query_grad_ref[...] = jnp.zeros_like(query_grad_ref)
    for piece in range(kv_ref.shape[0]):

        @pl.when(place_ref[slots] <= piece)
        def _skip(piece=piece):
            kv_grad_ref[piece] = jnp.zeros(kv_grad_ref.shape[1:], kv_grad_ref.dtype)

        @pl.when(place_ref[slots] > piece)
        def _visit(piece=piece):
            for head in range(heads):
                query = kvq_ref[:, 2 * width + head * HEAD_DIM : 2 * width + (head + 1) * HEAD_DIM]
                value_at = slice(width + head * HEAD_DIM, width + (head + 1) * HEAD_DIM)
                key = kv_ref[piece, :, columns_of(head)]
                out_grad = ctx_grad_ref[:, columns_of(head)]
                score[...] = matmul_nt(query, key)
                dots[...] = matmul_nt(out_grad, kv_ref[piece, :, value_at])

                def chunk(step, carry):
                    here = pl.ds(pl.multiple_of(step * CHUNK, CHUNK), CHUNK)
                    total = stat_ref[here, head : head + 1]
                    delta = delta_of(here, head, context_ref, ctx_grad_ref)
                    score_grads(here, None, head, total, delta, score, dots, prob, grad)
                    return carry

                lax.fori_loop(0, rows // CHUNK, chunk, 0)
                kv_grad_ref[piece, :, columns_of(head)] = matmul_tn(grad[...], query).astype(LOW)
                kv_grad_ref[piece, :, value_at] = matmul_tn(prob[...], out_grad).astype(LOW)
                query_grad_ref[:, columns_of(head)] += matmul_nn(grad[...], key)


def own_backward(
    heads, block_rows, place_ref, kvq_ref, ctx_grad_ref, context_ref, stat_ref, query_grad_in,
    grad_ref, score, dots, prob, grad
):
    width = heads * HEAD_DIM
    rows = kvq_ref.shape[0]
    for head in range(heads):
        query_at = slice(2 * width + head * HEAD_DIM, 2 * width + (head + 1) * HEAD_DIM)
        value_at = slice(width + head * HEAD_DIM, width + (head + 1) * HEAD_DIM)
        query = kvq_ref[:, query_at]
        key = kvq_ref[:, columns_of(head)]
        out_grad = ctx_grad_ref[:, columns_of(head)]
        score[...] = matmul_nt(query, key)
        dots[...] = matmul_nt(out_grad, kvq_ref[:, value_at])

        def chunk(step, carry):
            start = pl.multiple_of(step * CHUNK, CHUNK)
            here = pl.ds(start, CHUNK)
            seen = visible_block(place_ref, start, block_rows, rows)
            total = stat_ref[here, head : head + 1]
            delta = delta_of(here, head, context_ref, ctx_grad_ref)
            score_grads(here, seen, head, total, delta, score, dots, prob, grad)
            return carry

        lax.fori_loop(0, rows // CHUNK, chunk, 0)
        grad_ref[:, columns_of(head)] = matmul_tn(grad[...], query)
        grad_ref[:, value_at] = matmul_tn(prob[...], out_grad)
        grad_ref[:, query_at] = query_grad_in[:, columns_of(head)] + matmul_nn(grad[...], key)


def normalize(values):
    centered = values - jnp.mean(values, axis=-1, keepdims=True)
    spread = jnp.mean(centered * centered, axis=-1, keepdims=True)
    inverse = lax.rsqrt(spread + EPSILON)
    return centered * inverse, inverse


def normalize_back(grad, gain, hat, inverse):
    scaled = grad * gain
    mean_scaled = jnp.mean(scaled, axis=-1, keepdims=True)
    mean_product = jnp.mean(scaled * hat, axis=-1, keepdims=True)
    part = inverse * (scaled - mean_scaled - hat * mean_product)
    gain_grad = jnp.sum(grad * hat, axis=0, keepdims=True)
    return part, gain_grad, jnp.sum(grad, axis=0, keepdims=True)


def take(refs, *counts):
    groups, at = [], 0
    for count in counts:
        if count is None:
            groups.append(refs[at])
            at += 1
        else:
            groups.append(refs[at : at + count])
            at += count
    return groups


def place_blocks(meta_ref, parts, depth, pieces, out_ref):
    rows = pieces[0].shape[1]
    for deep in range(depth):
        member = meta_ref[parts + 1] ^ deep
        for slot in range(parts):
            start = pl.multiple_of((meta_ref[slot] * depth + member) * rows, 16)
            out_ref[pl.ds(start, rows), :] = pieces[deep][slot]


def place_shards(meta_ref, parts, pieces, out_ref):
    rows = pieces[0].shape[0]
    for deep, piece in enumerate(pieces):
        start = pl.multiple_of((meta_ref[parts + 1] ^ deep) * rows, 16)
        out_ref[pl.ds(start, rows), :] = piece[...]


def stack_rows(pieces, out_ref):
    rows = pieces[0].shape[0]
    for slot, piece in enumerate(pieces):
        out_ref[slot * rows : (slot + 1) * rows, :] = piece[...]


def emit_rows(partial, keep_ref, send_refs):
    rows = keep_ref.shape[0]
    keep_ref[...] = partial[:rows]
    for slot, send in enumerate(send_refs, 1):
        send[...] = partial[slot * rows : (slot + 1) * rows].astype(LOW)


def emit_blocks(meta_ref, parts, depth, whole_ref, keep_ref, send_refs):
    rows = keep_ref.shape[1]
    for deep in range(depth):
        member = meta_ref[parts + 1] ^ deep
        for slot in range(parts):
            start = pl.multiple_of((meta_ref[slot] * depth + member) * rows, 16)
            block = whole_ref[pl.ds(start, rows), :]
            if deep:
                send_refs[deep - 1][slot] = block.astype(LOW)
            else:
                keep_ref[slot] = block


def emit_shards(meta_ref, parts, whole_ref, keep_ref, send_refs):
    rows = keep_ref.shape[0]
    for deep in range(len(send_refs) + 1):
        start = pl.multiple_of((meta_ref[parts + 1] ^ deep) * rows, 16)
        block = whole_ref[pl.ds(start, rows), :]
        if deep:
            send_refs[deep - 1][...] = block.astype(LOW)
        else:
            keep_ref[...] = block


def half_kernel(parts, meta_ref, *refs):
    up, down_weight, out = take(refs, parts, None, None)
    shard = up[0].shape[0]

    @pl.when(meta_ref[parts] == 0)
    def _up():
        for slot in range(parts):
            out[slot * shard : (slot + 1) * shard, :] = up[slot][...]

    @pl.when(meta_ref[parts] != 0)
    def _down():
        out[...] = down_weight[...].astype(LOW)


def split_qkv_kernel(parts, width, meta_ref, qkv_ref, *outs):
    model = parts * width
    for case in range(parts):

        @pl.when(meta_ref[0] == case)
        def _case(case=case):
            for slot in range(parts):
                owner = case ^ slot
                for at, first in enumerate((model, 2 * model, 0)):
                    start = first + owner * width
                    outs[slot][:, at * width : (at + 1) * width] = qkv_ref[
                        :, start : start + width
                    ].astype(LOW)


def split_up_kernel(parts, meta_ref, up_ref, *outs):
    part = up_ref.shape[1] // parts
    for slot in range(parts):
        start = pl.multiple_of(meta_ref[slot] * part, 128)
        outs[slot][...] = up_ref[:, pl.ds(start, part)].astype(LOW)


def join_qkv_kernel(parts, width, meta_ref, *refs):
    pieces, out_ref = refs[:parts], refs[parts]
    model = parts * width
    for case in range(parts):

        @pl.when(meta_ref[0] == case)
        def _case(case=case):
            for slot in range(parts):
                owner = case ^ slot
                for at, first in enumerate((model, 2 * model, 0)):
                    start = first + owner * width
                    out_ref[:, start : start + width] = pieces[slot][
                        :, at * width : (at + 1) * width
                    ].astype(WIDE)


def join_up_kernel(parts, meta_ref, *refs):
    pieces, out_ref = refs[:parts], refs[parts]
    part = pieces[0].shape[1]
    for slot in range(parts):
        start = pl.multiple_of(meta_ref[slot] * part, 128)
        out_ref[:, pl.ds(start, part)] = pieces[slot][...].astype(WIDE)


def first_norm_kernel(meta_ref, tokens_ref, vectors_ref, out_ref):
    hat, _ = normalize(tokens_ref[...].astype(WIDE))
    out_ref[...] = (hat * vectors_ref[0:1, :] + vectors_ref[1:2, :]).astype(LOW)


def project_kernel(parts, depth, meta_ref, *refs):
    norm, weight, vectors_ref, kvq_ref, kv_ref, matrix_ref, norm_ref = take(
        refs, parts, depth, None, None, None, None, None
    )
    columns = kvq_ref.shape[1]
    place_blocks(meta_ref, parts, depth, weight, matrix_ref)
    stack_rows(norm, norm_ref)
    low = (matmul_nn(norm_ref[...], matrix_ref[...]) + vectors_ref[6:7, :columns]).astype(LOW)
    kvq_ref[...] = low
    kv_ref[...] = low[:, : kv_ref.shape[1]]


def context_kernel(parts, depth, heads, meta_ref, *refs):
    (
        kvq, kv, acc_in, stat_in, weight, context, low, stat, matrix, keep, sends, score, prob, fade
    ) = take(
        refs, None, None, None, None, depth, None, None, None, None, None, parts - 1, None, None,
        None,
    )
    place_shards(meta_ref, parts, weight, matrix)
    earlier_forward(
        heads, parts, meta_ref, kvq, kv, acc_in, stat_in, context, low, stat, score, prob, fade
    )
    emit_rows(matmul_nn(low[...], matrix[...]), keep, sends)


def second_norm_kernel(parts, meta_ref, *refs):
    keep, arrived, tokens, vectors, out, attended_ref = take(
        refs, None, parts - 1, None, None, None, None
    )
    attended = sum_all(keep[...], [piece[...] for piece in arrived]) + vectors[4:5, :]
    attended_ref[...] = attended
    hat, _ = normalize(tokens[...].astype(WIDE) + attended)
    out[...] = (hat * vectors[2:3, :] + vectors[3:4, :]).astype(LOW)


def feed_kernel(parts, depth, halves, meta_ref, *refs):
    (
        norm, branch, own, other, vectors, keep, sends, hidden, inner_grad, norm_all, branch_all,
        down_all, up_bias, up_all, inner, grad,
    ) = take(refs, parts, parts, depth, depth, None, None, parts - 1, *([None] * 9))

    def place(up, down):
        shard = up_all.shape[0] // (parts * depth)
        for deep in range(depth):
            member = meta_ref[parts + 1] ^ deep
            for slot in range(parts):
                start = pl.multiple_of((meta_ref[slot] * depth + member) * shard, 16)
                up_all[pl.ds(start, shard), :] = up[deep][slot * shard : (slot + 1) * shard, :]
        place_shards(meta_ref, parts, down, down_all)

    if halves:
        pl.when(meta_ref[parts] == 0)(lambda: place(own, other))
        pl.when(meta_ref[parts] != 0)(lambda: place(other, own))
    else:
        place(own, other)
    stack_rows(norm, norm_all)
    stack_rows(branch, branch_all)
    inner[...] = matmul_nn(norm_all[...], up_all[...])
    grad[...] = matmul_nt(branch_all[...], down_all[...])
    up_bias[...] = jnp.zeros_like(up_bias)

    def chunk(step, carry):
        here = pl.ds(pl.multiple_of(step * CHUNK, CHUNK), CHUNK)
        value = inner[here, :] + vectors[7:8, :]
        square = value * value
        bent = jnp.tanh(GELU_SCALE * (value + GELU_CUBE * square * value))
        hidden[here, :] = (0.5 * value * (1.0 + bent)).astype(LOW)
        slope = 0.5 * (1.0 + bent) + 0.5 * value * (1.0 - bent * bent) * GELU_SCALE * (
            1.0 + 3.0 * GELU_CUBE * square
        )
        low = (grad[here, :] * slope).astype(LOW)
        inner_grad[here, :] = low
        up_bias[...] += jnp.sum(low.astype(WIDE), axis=0, keepdims=True)
        return carry

    lax.fori_loop(0, inner.shape[0] // CHUNK, chunk, 0)
    emit_rows(matmul_nt(inner_grad[...], up_all[...]), keep, sends)


def feed_grad_kernel(parts, depth, halves, meta_ref, *refs):
    hidden, inner_grad, norm_all, branch_all, down_all, kept, sent, fed_keep, fed_sends, whole = (
        take(refs, *([None] * 8), parts - 1, None)
    )
    hidden_shard = hidden.shape[1] // depth
    shard = norm_all.shape[1] // (parts * depth)

    def emit(half, out):
        for deep in range(depth):
            member = meta_ref[parts + 1] ^ deep
            if half:
                start = pl.multiple_of(member * hidden_shard, 16)
                out[deep] = whole[pl.ds(start, hidden_shard), :].astype(out.dtype)
            else:
                for slot in range(parts):
                    start = pl.multiple_of((meta_ref[slot] * depth + member) * shard, 16)
                    out[deep, slot * shard : (slot + 1) * shard] = whole[
                        pl.ds(start, shard), :
                    ].astype(out.dtype)

    for half in range(2):
        if half:
            whole[...] = matmul_tn(hidden[...], branch_all[...])
        else:
            whole[...] = matmul_tn(norm_all[...], inner_grad[...])
        if halves:
            pl.when(meta_ref[parts] == half)(functools.partial(emit, half, kept))
            pl.when(meta_ref[parts] != half)(functools.partial(emit, half, sent))
        else:
            emit(half, sent if half else kept)
    emit_rows(matmul_nn(hidden[...], down_all[...]), fed_keep, fed_sends)


def fold_kernel(meta_ref, kept_ref, arrived_ref, keep_ref, *send_refs):
    keep_ref[...] = kept_ref[0] + arrived_ref[0].astype(WIDE)
    for deep, send in enumerate(send_refs, 1):
        send[...] = (kept_ref[deep] + arrived_ref[deep].astype(WIDE)).astype(LOW)


def second_norm_grad_kernel(parts, meta_ref, *refs):
    keep, arrived, tokens, attended, branch, vectors, attn_grad, mixed_part, sums = take(
        refs, None, parts - 1, None, None, None, None, None, None, None
    )
    grad = sum_all(keep[...], [piece[...] for piece in arrived])
    hat, inverse = normalize(tokens[...].astype(WIDE) + attended[...])
    part, gain_grad, bias_grad = normalize_back(grad, vectors[2:3, :], hat, inverse)
    mixed_part[...] = part
    branch_rows = branch[...].astype(WIDE)
    low = (branch_rows + part).astype(LOW)
    attn_grad[...] = low
    sums[...] = jnp.zeros_like(sums)
    sums[2:3, :] = gain_grad
    sums[3:4, :] = bias_grad
    sums[4:5, :] = jnp.sum(low.astype(WIDE), axis=0, keepdims=True)
    sums[5:6, :] = jnp.sum(branch_rows, axis=0, keepdims=True)


def context_grad_kernel(parts, heads, meta_ref, *refs):
    (
        attn, matrix, kvq, kv, context, stat, ctx_grad, attn_all, query_grad, kv_grad, score, dots,
        prob, grad,
    ) = take(refs, parts, *([None] * 13))
    stack_rows(attn, attn_all)
    ctx_grad[...] = matmul_nt(attn_all[...], matrix[...]).astype(LOW)
    earlier_backward(
        heads, parts, meta_ref, kvq, kv, ctx_grad, context, stat, query_grad, kv_grad, score, dots,
        prob, grad,
    )


def own_grad_kernel(parts, depth, heads, rows, meta_ref, *refs):
    (
        kvq, ctx_grad, context, stat, query_grad, low, attn_all, kvq_grad, out_keep, out_sends,
        whole, score, dots, prob, grad,
    ) = take(refs, *([None] * 9), depth - 1, *([None] * 5))
    own_backward(
        heads, rows, meta_ref, kvq, ctx_grad, context, stat, query_grad, kvq_grad, score, dots,
        prob, grad,
    )
    whole[...] = matmul_tn(low[...], attn_all[...])
    emit_shards(meta_ref, parts, whole, out_keep, out_sends)


def projection_back_kernel(parts, meta_ref, *refs):
    own, arrived, matrix, kvq_grad, keep, sends, bias = take(
        refs, None, None, None, None, None, parts - 1, None
    )
    kv_width = arrived.shape[2]
    total = own[:, :kv_width]
    for piece in range(arrived.shape[0]):
        total = total + arrived[piece].astype(WIDE)
    kvq_grad[:, :kv_width] = total.astype(LOW)
    kvq_grad[:, kv_width:] = own[:, kv_width:].astype(LOW)
    emit_rows(matmul_nt(kvq_grad[...], matrix[...]), keep, sends)
    bias[...] = jnp.sum(kvq_grad[...].astype(WIDE), axis=0, keepdims=True)


def projection_grad_kernel(parts, depth, meta_ref, *refs):
    norm, kvq_grad, keep, sends, whole = take(refs, None, None, None, depth - 1, None)
    whole[...] = matmul_tn(norm[...], kvq_grad[...])
    emit_blocks(meta_ref, parts, depth, whole, keep, sends)


def first_norm_grad_kernel(parts, meta_ref, *refs):
    keep, arrived, tokens, vectors, mixed_part, sums_in, kvq_bias, up_bias, out, sums = take(
        refs, None, parts - 1, *([None] * 8)
    )
    grad = sum_all(keep[...], [piece[...] for piece in arrived])
    hat, inverse = normalize(tokens[...].astype(WIDE))
    part, gain_grad, bias_grad = normalize_back(grad, vectors[0:1, :], hat, inverse)
    out[...] = (mixed_part[...] + part).astype(LOW)
    sums[...] = sums_in[...]
    sums[0:1, :] = gain_grad
    sums[1:2, :] = bias_grad
    sums[6:7, : kvq_bias.shape[1]] = kvq_bias[...]
    sums[7:8, :] = up_bias[...]


def local_call(kernel, operands, results, scratch=(), flops=0):
    smem = pl.BlockSpec(memory_space=pltpu.SMEM)
    vmem = pl.BlockSpec(memory_space=pltpu.VMEM)
    moved = sum(each.size * each.dtype.itemsize for each in tuple(operands) + tuple(results))
    return pl.pallas_call(
        kernel,
        out_shape=tuple(results),
        in_specs=[smem] + [vmem] * (len(operands) - 1),
        out_specs=tuple([vmem] * len(results)),
        scratch_shapes=list(scratch),
        compiler_params=pltpu.CompilerParams(vmem_limit_bytes=VMEM_BYTES),
        cost_estimate=pl.CostEstimate(flops=flops, bytes_accessed=moved, transcendentals=0),
    )(*operands)


def low_like(*shape):
    return jax.ShapeDtypeStruct(shape, LOW)


def wide_like(*shape):
    return jax.ShapeDtypeStruct(shape, WIDE)


def local(
    tokens, cotangent, ln1_gain, ln1_bias, qkv_weight, q_bias, v_bias, out_weight, out_bias,
    ln2_gain, ln2_bias, fc1_weight, fc1_bias, fc2_weight, fc2_bias,
):
    parts = lax.axis_size("dp")
    depth = lax.axis_size("fsdp")
    contexts = lax.axis_size("ctx")
    assert parts == depth
    mine = lax.axis_index("dp")
    deep = lax.axis_index("fsdp")
    rows, model = tokens.shape[1:]
    shard = ln1_gain.shape[0]
    heads = model // HEAD_DIM // parts
    width = heads * HEAD_DIM
    hidden_shard = fc1_bias.shape[0]
    hidden_part = hidden_shard * depth
    group = parts * rows
    meta = jnp.stack(
        [mine ^ slot for slot in range(parts)] + [lax.axis_index("ctx"), deep]
    ).astype(jnp.int32)

    kvq_split = local_call(
        functools.partial(split_qkv_kernel, parts, width),
        (meta, qkv_weight),
        [low_like(shard, 3 * width)] * parts,
    )
    kvq_rows = jnp.stack([kvq_split[0]] + send_pieces(kvq_split[1:], "dp"))
    kvq_pieces = gather_direct(kvq_rows, "fsdp")

    token_rows = transpose_homes(after(tokens[0].astype(LOW), kvq_split[0]))

    low_vectors = jnp.stack([ln1_gain, ln1_bias, ln2_gain, ln2_bias, out_bias, fc2_bias])
    vectors = jnp.zeros((8, model), WIDE)
    vectors = lax.dynamic_update_slice(
        vectors, low_vectors.astype(LOW).astype(WIDE), (0, (mine * depth + deep) * shard)
    )
    for row, first, part in (
        (6, width, v_bias), (6, 2 * width, q_bias), (7, 0, fc1_bias),
    ):
        part = part.astype(LOW).astype(WIDE)[None]
        vectors = lax.dynamic_update_slice(vectors, part, (row, first + deep * part.shape[1]))
    vectors = sum_doubling(after(vectors, kvq_split[0]), "fsdp")
    everywhere = sum_doubling(vectors, "dp")
    vectors = jnp.where(jnp.arange(8)[:, None] < 6, everywhere, vectors)

    halves = contexts == 2
    up_split = local_call(
        functools.partial(split_up_kernel, parts),
        (meta, after(fc1_weight, kvq_rows)),
        [low_like(shard, hidden_part)] * parts,
    )
    up_parts = [up_split[0]] + send_pieces(up_split[1:], "dp")
    out_pieces = gather_direct(after(out_weight.astype(LOW), kvq_pieces[-1]), "fsdp")
    grad_rows = transpose_homes(after(cotangent[0].astype(LOW), kvq_pieces[-1]))
    if halves:
        (half,) = local_call(
            functools.partial(half_kernel, parts),
            (meta, *up_parts, fc2_weight),
            [low_like(hidden_shard, model)],
        )
        own_half = gather_direct(after(half, out_pieces[-1]), "fsdp")
        other_half = [shift(piece, "ctx", 1) for piece in own_half]
    else:
        own_half = gather_direct(jnp.concatenate(up_parts), "fsdp")
        other_half = gather_direct(fc2_weight.astype(LOW), "fsdp")

    (norm1,) = local_call(
        first_norm_kernel, (meta, token_rows, vectors), [low_like(rows, model)]
    )
    norm1_pieces = gather_pieces(norm1)
    kvq, kv, kvq_matrix, norm1_all = local_call(
        functools.partial(project_kernel, parts, depth),
        (meta, *norm1_pieces, *kvq_pieces, vectors),
        [
            low_like(group, 3 * width),
            low_like(group, 2 * width),
            low_like(model, 3 * width),
            low_like(group, model),
        ],
        flops=2 * group * model * 3 * width,
    )
    kv_earlier = jnp.stack([shift(kv, "ctx", by) for by in range(1, contexts)])

    branch_pieces = gather_pieces(after(grad_rows, norm1_pieces[-1]))

    score_flops = 2 * group * group * width
    wide_square = pltpu.VMEM((group, group), WIDE)
    low_square = pltpu.VMEM((group, group), LOW)
    acc, stat = local_call(
        functools.partial(own_forward, heads, rows),
        (meta, kvq),
        [wide_like(group, width), wide_like(group, 128)],
        [wide_square, low_square],
        flops=2 * score_flops,
    )
    context, context_low, stat, out_matrix, attended_keep, *attended_sends = local_call(
        functools.partial(context_kernel, parts, depth, heads),
        (meta, kvq, kv_earlier, acc, stat, *out_pieces),
        [
            wide_like(group, width),
            low_like(group, width),
            wide_like(group, 128),
            low_like(width, model),
            wide_like(rows, model),
        ]
        + [low_like(rows, model)] * (parts - 1),
        [wide_square, low_square, pltpu.VMEM((group, HEAD_DIM), WIDE)],
        flops=2 * score_flops,
    )
    arrived = send_pieces(attended_sends, "dp")
    norm2, attended = local_call(
        functools.partial(second_norm_kernel, parts),
        (meta, attended_keep, *arrived, token_rows, vectors),
        [low_like(rows, model), wide_like(rows, model)],
    )

    norm2_pieces = gather_pieces(norm2)
    norm2_keep, *rest = local_call(
        functools.partial(feed_kernel, parts, depth, halves),
        (meta, *norm2_pieces, *branch_pieces, *own_half, *other_half, vectors),
        [wide_like(rows, model)]
        + [low_like(rows, model)] * (parts - 1)
        + [low_like(group, hidden_part)] * 2
        + [low_like(group, model)] * 2
        + [low_like(hidden_part, model), wide_like(1, hidden_part)],
        [
            pltpu.VMEM((model, hidden_part), LOW),
            pltpu.VMEM((group, hidden_part), WIDE),
            pltpu.VMEM((group, hidden_part), WIDE),
        ],
        flops=6 * group * model * hidden_part,
    )
    norm2_sends = rest[: parts - 1]
    hidden, inner_grad, norm2_all, branch_all, down_matrix, up_bias = rest[parts - 1 :]
    norm2_arrived = send_pieces(norm2_sends, "dp")
    kept_half, sent_half, fed_keep, *fed_sends = local_call(
        functools.partial(feed_grad_kernel, parts, depth, halves),
        (meta, hidden, inner_grad, norm2_all, branch_all, down_matrix),
        [
            wide_like(depth, hidden_shard, model),
            low_like(depth, hidden_shard, model),
            wide_like(rows, model),
        ]
        + [low_like(rows, model)] * (parts - 1),
        [pltpu.VMEM((max(model, hidden_part), max(model, hidden_part)), WIDE)],
        flops=6 * group * model * hidden_part,
    )
    attn_grad, mixed_part, sums = local_call(
        functools.partial(second_norm_grad_kernel, parts),
        (meta, norm2_keep, *norm2_arrived, token_rows, attended, grad_rows, vectors),
        [low_like(rows, model), wide_like(rows, model), wide_like(8, model)],
    )
    attn_pieces = gather_pieces(attn_grad)
    if halves:
        half_arrived = shift(sent_half, "ctx", 1)
        half_keep, *half_sends = local_call(
            fold_kernel,
            (meta, kept_half, after(half_arrived, attn_pieces[-1])),
            [wide_like(hidden_shard, model)] + [low_like(hidden_shard, model)] * (depth - 1),
        )
        half_pieces = send_pieces(half_sends, "fsdp")
    fed_arrived = send_pieces(
        lax.optimization_barrier((*fed_sends, attn_pieces[-1]))[: parts - 1], "dp"
    )

    ctx_grad, attn_all, query_grad, kv_grad = local_call(
        functools.partial(context_grad_kernel, parts, heads),
        (meta, *attn_pieces, out_matrix, kvq, kv_earlier, context, stat),
        [
            low_like(group, width),
            low_like(group, model),
            wide_like(group, width),
            low_like(*kv_earlier.shape),
        ],
        [wide_square, wide_square, low_square, low_square],
        flops=5 * score_flops,
    )
    kv_arrived = jnp.stack(
        [shift(kv_grad[by - 1], "ctx", -by) for by in range(1, contexts)]
    )
    kvq_own, out_keep, *out_sends = local_call(
        functools.partial(own_grad_kernel, parts, depth, heads, rows),
        (meta, kvq, ctx_grad, context, stat, query_grad, context_low, attn_all),
        [wide_like(group, 3 * width), wide_like(shard, model)]
        + [low_like(shard, model)] * (depth - 1),
        [
            pltpu.VMEM((width, model), WIDE), wide_square, wide_square, low_square, low_square,
        ],
        flops=5 * score_flops,
    )
    out_arrived = send_pieces(out_sends, "fsdp")
    kvq_grad, norm1_keep, *rest = local_call(
        functools.partial(projection_back_kernel, parts),
        (meta, kvq_own, kv_arrived, kvq_matrix),
        [low_like(group, 3 * width), wide_like(rows, model)]
        + [low_like(rows, model)] * (parts - 1)
        + [wide_like(1, 3 * width)],
        flops=2 * group * model * 3 * width,
    )
    kvq_bias = rest[-1]
    norm1_arrived = send_pieces(rest[:-1], "dp")
    kvq_keep, *kvq_sends = local_call(
        functools.partial(projection_grad_kernel, parts, depth),
        (meta, norm1_all, kvq_grad),
        [wide_like(parts, shard, 3 * width)]
        + [low_like(parts, shard, 3 * width)] * (depth - 1),
        [pltpu.VMEM((model, 3 * width), WIDE)],
        flops=2 * group * model * 3 * width,
    )
    kvq_arrived = send_pieces(kvq_sends, "fsdp")
    input_part, sums = local_call(
        functools.partial(first_norm_grad_kernel, parts),
        (
            meta, norm1_keep, *norm1_arrived, token_rows, vectors, mixed_part, sums, kvq_bias,
            up_bias,
        ),
        [low_like(rows, model), wide_like(8, model)],
    )

    delta = sum_all(fed_keep, fed_arrived) + vectors[5:6] + attended
    delta = after(delta.astype(LOW), kvq_own)
    output = tokens[0] + transpose_homes(delta).astype(WIDE)
    input_grad = cotangent[0] + transpose_homes(input_part).astype(WIDE)

    def owner_sum(keep, pieces, *later):
        low = sum_all(keep, pieces).astype(LOW)
        return sum_replicas(after(low, *later) if later else low)

    out_total = owner_sum(out_keep, out_arrived, kv_arrived)
    if halves:
        mine_half = sum_all(half_keep, half_pieces).astype(LOW)
        arrived_half = shift(after(mine_half, kv_arrived), "ctx", 1)
        first = lax.axis_index("ctx") == 0
        up_total = jnp.where(first, mine_half, arrived_half)
        down_total = jnp.where(first, arrived_half, mine_half)
    else:
        up_total, down_total = [
            owner_sum(half[0].astype(WIDE), send_pieces(list(half[1:].astype(LOW)), "fsdp"))
            for half in (kept_half, sent_half)
        ]
    up_total = up_total.astype(LOW).reshape(parts, shard, hidden_part)
    down_total = down_total.astype(WIDE)
    up_sends = [after(up_total[slot], norm1_arrived[-1]) for slot in range(1, parts)]
    (up_total,) = local_call(
        functools.partial(join_up_kernel, parts),
        (meta, up_total[0], *send_pieces(up_sends, "dp")),
        [wide_like(shard, parts * hidden_part)],
    )
    kvq_total = owner_sum(kvq_keep, kvq_arrived).astype(LOW)
    (qkv_total,) = local_call(
        functools.partial(join_qkv_kernel, parts, width),
        (meta, kvq_total[0], *send_pieces([kvq_total[s] for s in range(1, parts)], "dp")),
        [wide_like(shard, 3 * model)],
    )
    sums = sum_replicas(sum_doubling(sums, "fsdp"))
    everywhere = sum_doubling(sums, "dp")
    owned = lax.dynamic_slice(everywhere, (0, (mine * depth + deep) * shard), (6, shard))
    value_bias = lax.dynamic_slice(sums, (6, width + deep * shard), (1, shard))[0]
    query_bias = lax.dynamic_slice(sums, (6, 2 * width + deep * shard), (1, shard))[0]
    inner_bias = lax.dynamic_slice(sums, (7, deep * hidden_shard), (1, hidden_shard))[0]

    return (
        output[None],
        input_grad[None],
        owned[0],
        owned[1],
        qkv_total,
        query_bias,
        value_bias,
        out_total,
        owned[4],
        owned[2],
        owned[3],
        up_total,
        inner_bias,
        down_total,
        owned[5],
    )


def solution(mesh):
    rows = P("dp", ("ctx", "fsdp"), None)
    vector = P(("dp", "fsdp"))
    matrix = P(("dp", "fsdp"), None)
    parameters = (
        vector, vector, matrix, vector, vector, matrix, vector, vector, vector, matrix, vector,
        matrix, vector,
    )
    return jax.shard_map(
        local,
        mesh=mesh,
        in_specs=(rows, rows) + parameters,
        out_specs=(rows, rows) + parameters,
        check_vma=False,
    )
```

```python
import functools

import jax
import jax.numpy as jnp
from jax import lax
from jax.experimental import pallas as pl
from jax.experimental.pallas import tpu as pltpu
from jax.sharding import PartitionSpec as P

HEAD_DIM = 64
EPSILON = 1e-05
SCALE = HEAD_DIM ** (-0.5)
MASKED = -1e30
CHUNK = 64
VMEM_BYTES = 16 * 1024 * 1024
GELU_SCALE = 0.7978845608
GELU_CUBE = 0.044715
LOW = jnp.bfloat16
WIDE = jnp.float32


def swap(value, axis, bit):
    count = lax.axis_size(axis)
    return lax.ppermute(value, axis, [(at, at ^ bit) for at in range(count)])


def shift(value, axis, by):
    count = lax.axis_size(axis)
    return lax.ppermute(value, axis, [(at, (at + by) % count) for at in range(count)])


def transpose_homes(value):
    side = lax.axis_size("dp")
    pairs = [(a * side + b, b * side + a) for a in range(side) for b in range(side)]
    return lax.ppermute(value, ("dp", "fsdp"), pairs)


def after(value, *others):
    return lax.optimization_barrier((value,) + others)[0]


def gather_pieces(block):
    pieces = [block]
    for slot in range(1, lax.axis_size("dp")):
        low_bit = slot & -slot
        pieces.append(swap(pieces[slot ^ low_bit], "dp", low_bit))
    return pieces


def send_pieces(sends, axis):
    return [swap(send, axis, slot) for slot, send in enumerate(sends, 1)]


def gather_direct(block, axis):
    return [block] + [swap(block, axis, slot) for slot in range(1, lax.axis_size(axis))]


def sum_doubling(value, axis):
    bit = 1
    while bit < lax.axis_size(axis):
        value = value + swap(value, axis, bit)
        bit *= 2
    return value


def sum_all(kept, arrived):
    total = kept
    for piece in arrived:
        total = total + piece.astype(WIDE)
    return total


def sum_replicas(value):
    if lax.axis_size("ctx") == 2:
        return value.astype(WIDE) + shift(value, "ctx", 1).astype(WIDE)
    return jnp.sum(lax.all_gather(value, "ctx").astype(WIDE), axis=0)


def matmul_nt(left, right):
    return lax.dot_general(left, right, (((1,), (1,)), ((), ())), preferred_element_type=WIDE)


def matmul_nn(left, right):
    return lax.dot_general(left, right, (((1,), (0,)), ((), ())), preferred_element_type=WIDE)


def matmul_tn(left, right):
    return lax.dot_general(left, right, (((0,), (0,)), ((), ())), preferred_element_type=WIDE)


def visible_block(place_ref, start, block_rows, columns):
    slot = start // block_rows
    query_pos = place_ref[slot] * block_rows + start % block_rows
    query_pos = query_pos + lax.broadcasted_iota(jnp.int32, (CHUNK, columns), 0)
    lane = lax.broadcasted_iota(jnp.int32, (CHUNK, columns), 1)
    key_pos = lane
    for at in range(columns // block_rows):
        inside = (lane >= at * block_rows) & (lane < (at + 1) * block_rows)
        key_pos = jnp.where(inside, place_ref[at] * block_rows + lane - at * block_rows, key_pos)
    return key_pos <= query_pos


def columns_of(head):
    return slice(head * HEAD_DIM, (head + 1) * HEAD_DIM)


def own_forward(heads, block_rows, place_ref, kvq_ref, acc_ref, stat_ref, score, prob):
    width = heads * HEAD_DIM
    rows = kvq_ref.shape[0]
    for head in range(heads):
        query = kvq_ref[:, 2 * width + head * HEAD_DIM : 2 * width + (head + 1) * HEAD_DIM]
        score[...] = matmul_nt(query, kvq_ref[:, columns_of(head)])

        def chunk(step, carry):
            start = pl.multiple_of(step * CHUNK, CHUNK)
            seen = visible_block(place_ref, start, block_rows, rows)
            scores = jnp.where(seen, score[pl.ds(start, CHUNK), :] * SCALE, MASKED)
            highest = jnp.max(scores, axis=1, keepdims=True)
            weight = jnp.exp(scores - highest)
            stat_ref[pl.ds(start, CHUNK), head : head + 1] = highest
            stat_ref[pl.ds(start, CHUNK), heads + head : heads + head + 1] = jnp.sum(
                weight, axis=1, keepdims=True
            )
            prob[pl.ds(start, CHUNK), :] = weight.astype(LOW)
            return carry

        lax.fori_loop(0, rows // CHUNK, chunk, 0)
        value = kvq_ref[:, width + head * HEAD_DIM : width + (head + 1) * HEAD_DIM]
        acc_ref[:, columns_of(head)] = matmul_nn(prob[...], value)


def earlier_forward(
    heads, slots, place_ref, kvq_ref, kv_ref, acc_in, stat_in, acc_ref, low_ref, stat_ref, score,
    prob, fade
):
    width = heads * HEAD_DIM
    rows = kvq_ref.shape[0]
    acc_ref[...] = acc_in[...]
    stat_ref[...] = stat_in[...]
    for piece in range(kv_ref.shape[0]):

        @pl.when(place_ref[slots] > piece)
        def _visit(piece=piece):
            for head in range(heads):
                query = kvq_ref[:, 2 * width + head * HEAD_DIM : 2 * width + (head + 1) * HEAD_DIM]
                score[...] = matmul_nt(query, kv_ref[piece, :, columns_of(head)])

                def chunk(step, carry):
                    here = pl.ds(pl.multiple_of(step * CHUNK, CHUNK), CHUNK)
                    scores = score[here, :] * SCALE
                    old = stat_ref[here, head : head + 1]
                    highest = jnp.maximum(old, jnp.max(scores, axis=1, keepdims=True))
                    weight = jnp.exp(scores - highest)
                    fading = jnp.exp(old - highest)
                    stat_ref[here, head : head + 1] = highest
                    total = stat_ref[here, heads + head : heads + head + 1]
                    stat_ref[here, heads + head : heads + head + 1] = total * fading + jnp.sum(
                        weight, axis=1, keepdims=True
                    )
                    fade[here, :] = jnp.broadcast_to(fading, (CHUNK, HEAD_DIM))
                    prob[here, :] = weight.astype(LOW)
                    return carry

                lax.fori_loop(0, rows // CHUNK, chunk, 0)
                value = kv_ref[piece, :, width + head * HEAD_DIM : width + (head + 1) * HEAD_DIM]
                acc_ref[:, columns_of(head)] = acc_ref[:, columns_of(head)] * fade[
                    ...
                ] + matmul_nn(prob[...], value)

    for head in range(heads):
        total = stat_ref[:, heads + head : heads + head + 1]
        context = acc_ref[:, columns_of(head)] / total
        acc_ref[:, columns_of(head)] = context
        low_ref[:, columns_of(head)] = context.astype(LOW)
        stat_ref[:, head : head + 1] = stat_ref[:, head : head + 1] + jnp.log(total)


def score_grads(here, seen, head, total, delta, score, dots, prob, grad):
    scores = score[here, :] * SCALE
    weight = jnp.exp(scores - total)
    if seen is not None:
        weight = jnp.where(seen, weight, 0.0)
    prob[here, :] = weight.astype(LOW)
    grad[here, :] = (weight * (dots[here, :] - delta) * SCALE).astype(LOW)


def delta_of(here, head, context_ref, ctx_grad_ref):
    product = context_ref[here, columns_of(head)] * ctx_grad_ref[here, columns_of(head)].astype(WIDE)
    return jnp.sum(product, axis=1, keepdims=True)


def earlier_backward(
    heads, slots, place_ref, kvq_ref, kv_ref, ctx_grad_ref, context_ref, stat_ref, query_grad_ref,
    kv_grad_ref, score, dots, prob, grad
):
    width = heads * HEAD_DIM
    rows = kvq_ref.shape[0]
    query_grad_ref[...] = jnp.zeros_like(query_grad_ref)
    for piece in range(kv_ref.shape[0]):

        @pl.when(place_ref[slots] <= piece)
        def _skip(piece=piece):
            kv_grad_ref[piece] = jnp.zeros(kv_grad_ref.shape[1:], kv_grad_ref.dtype)

        @pl.when(place_ref[slots] > piece)
        def _visit(piece=piece):
            for head in range(heads):
                query = kvq_ref[:, 2 * width + head * HEAD_DIM : 2 * width + (head + 1) * HEAD_DIM]
                value_at = slice(width + head * HEAD_DIM, width + (head + 1) * HEAD_DIM)
                key = kv_ref[piece, :, columns_of(head)]
                out_grad = ctx_grad_ref[:, columns_of(head)]
                score[...] = matmul_nt(query, key)
                dots[...] = matmul_nt(out_grad, kv_ref[piece, :, value_at])

                def chunk(step, carry):
                    here = pl.ds(pl.multiple_of(step * CHUNK, CHUNK), CHUNK)
                    total = stat_ref[here, head : head + 1]
                    delta = delta_of(here, head, context_ref, ctx_grad_ref)
                    score_grads(here, None, head, total, delta, score, dots, prob, grad)
                    return carry

                lax.fori_loop(0, rows // CHUNK, chunk, 0)
                kv_grad_ref[piece, :, columns_of(head)] = matmul_tn(grad[...], query).astype(LOW)
                kv_grad_ref[piece, :, value_at] = matmul_tn(prob[...], out_grad).astype(LOW)
                query_grad_ref[:, columns_of(head)] += matmul_nn(grad[...], key)


def own_backward(
    heads, block_rows, place_ref, kvq_ref, ctx_grad_ref, context_ref, stat_ref, query_grad_in,
    grad_ref, score, dots, prob, grad
):
    width = heads * HEAD_DIM
    rows = kvq_ref.shape[0]
    for head in range(heads):
        query_at = slice(2 * width + head * HEAD_DIM, 2 * width + (head + 1) * HEAD_DIM)
        value_at = slice(width + head * HEAD_DIM, width + (head + 1) * HEAD_DIM)
        query = kvq_ref[:, query_at]
        key = kvq_ref[:, columns_of(head)]
        out_grad = ctx_grad_ref[:, columns_of(head)]
        score[...] = matmul_nt(query, key)
        dots[...] = matmul_nt(out_grad, kvq_ref[:, value_at])

        def chunk(step, carry):
            start = pl.multiple_of(step * CHUNK, CHUNK)
            here = pl.ds(start, CHUNK)
            seen = visible_block(place_ref, start, block_rows, rows)
            total = stat_ref[here, head : head + 1]
            delta = delta_of(here, head, context_ref, ctx_grad_ref)
            score_grads(here, seen, head, total, delta, score, dots, prob, grad)
            return carry

        lax.fori_loop(0, rows // CHUNK, chunk, 0)
        grad_ref[:, columns_of(head)] = matmul_tn(grad[...], query)
        grad_ref[:, value_at] = matmul_tn(prob[...], out_grad)
        grad_ref[:, query_at] = query_grad_in[:, columns_of(head)] + matmul_nn(grad[...], key)


def normalize(values):
    centered = values - jnp.mean(values, axis=-1, keepdims=True)
    spread = jnp.mean(centered * centered, axis=-1, keepdims=True)
    inverse = lax.rsqrt(spread + EPSILON)
    return centered * inverse, inverse


def normalize_back(grad, gain, hat, inverse):
    scaled = grad * gain
    mean_scaled = jnp.mean(scaled, axis=-1, keepdims=True)
    mean_product = jnp.mean(scaled * hat, axis=-1, keepdims=True)
    part = inverse * (scaled - mean_scaled - hat * mean_product)
    gain_grad = jnp.sum(grad * hat, axis=0, keepdims=True)
    return part, gain_grad, jnp.sum(grad, axis=0, keepdims=True)


def take(refs, *counts):
    groups, at = [], 0
    for count in counts:
        if count is None:
            groups.append(refs[at])
            at += 1
        else:
            groups.append(refs[at : at + count])
            at += count
    return groups


def place_blocks(meta_ref, parts, depth, pieces, out_ref):
    rows = pieces[0].shape[1]
    for deep in range(depth):
        member = meta_ref[parts + 1] ^ deep
        for slot in range(parts):
            start = pl.multiple_of((meta_ref[slot] * depth + member) * rows, 16)
            out_ref[pl.ds(start, rows), :] = pieces[deep][slot]


def place_shards(meta_ref, parts, pieces, out_ref):
    rows = pieces[0].shape[0]
    for deep, piece in enumerate(pieces):
        start = pl.multiple_of((meta_ref[parts + 1] ^ deep) * rows, 16)
        out_ref[pl.ds(start, rows), :] = piece[...]


def stack_rows(pieces, out_ref):
    rows = pieces[0].shape[0]
    for slot, piece in enumerate(pieces):
        out_ref[slot * rows : (slot + 1) * rows, :] = piece[...]


def emit_rows(partial, keep_ref, send_refs):
    rows = keep_ref.shape[0]
    keep_ref[...] = partial[:rows]
    for slot, send in enumerate(send_refs, 1):
        send[...] = partial[slot * rows : (slot + 1) * rows].astype(LOW)


def emit_blocks(meta_ref, parts, depth, whole_ref, keep_ref, send_refs):
    rows = keep_ref.shape[1]
    for deep in range(depth):
        member = meta_ref[parts + 1] ^ deep
        for slot in range(parts):
            start = pl.multiple_of((meta_ref[slot] * depth + member) * rows, 16)
            block = whole_ref[pl.ds(start, rows), :]
            if deep:
                send_refs[deep - 1][slot] = block.astype(LOW)
            else:
                keep_ref[slot] = block


def emit_shards(meta_ref, parts, whole_ref, keep_ref, send_refs):
    rows = keep_ref.shape[0]
    for deep in range(len(send_refs) + 1):
        start = pl.multiple_of((meta_ref[parts + 1] ^ deep) * rows, 16)
        block = whole_ref[pl.ds(start, rows), :]
        if deep:
            send_refs[deep - 1][...] = block.astype(LOW)
        else:
            keep_ref[...] = block


def half_kernel(parts, meta_ref, *refs):
    up, down_weight, out = take(refs, parts, None, None)
    shard = up[0].shape[0]

    @pl.when(meta_ref[parts] == 0)
    def _up():
        for slot in range(parts):
            out[slot * shard : (slot + 1) * shard, :] = up[slot][...]

    @pl.when(meta_ref[parts] != 0)
    def _down():
        out[...] = down_weight[...].astype(LOW)


def split_qkv_kernel(parts, width, meta_ref, qkv_ref, *outs):
    model = parts * width
    for case in range(parts):

        @pl.when(meta_ref[0] == case)
        def _case(case=case):
            for slot in range(parts):
                owner = case ^ slot
                for at, first in enumerate((model, 2 * model, 0)):
                    start = first + owner * width
                    outs[slot][:, at * width : (at + 1) * width] = qkv_ref[
                        :, start : start + width
                    ].astype(LOW)


def split_up_kernel(parts, meta_ref, up_ref, *outs):
    part = up_ref.shape[1] // parts
    for slot in range(parts):
        start = pl.multiple_of(meta_ref[slot] * part, 128)
        outs[slot][...] = up_ref[:, pl.ds(start, part)].astype(LOW)


def join_qkv_kernel(parts, width, meta_ref, *refs):
    pieces, out_ref = refs[:parts], refs[parts]
    model = parts * width
    for case in range(parts):

        @pl.when(meta_ref[0] == case)
        def _case(case=case):
            for slot in range(parts):
                owner = case ^ slot
                for at, first in enumerate((model, 2 * model, 0)):
                    start = first + owner * width
                    out_ref[:, start : start + width] = pieces[slot][
                        :, at * width : (at + 1) * width
                    ].astype(WIDE)


def join_up_kernel(parts, meta_ref, *refs):
    pieces, out_ref = refs[:parts], refs[parts]
    part = pieces[0].shape[1]
    for slot in range(parts):
        start = pl.multiple_of(meta_ref[slot] * part, 128)
        out_ref[:, pl.ds(start, part)] = pieces[slot][...].astype(WIDE)


def first_norm_kernel(meta_ref, tokens_ref, vectors_ref, out_ref):
    hat, _ = normalize(tokens_ref[...].astype(WIDE))
    out_ref[...] = (hat * vectors_ref[0:1, :] + vectors_ref[1:2, :]).astype(LOW)


def project_kernel(parts, depth, meta_ref, *refs):
    norm, weight, vectors_ref, kvq_ref, kv_ref, matrix_ref, norm_ref = take(
        refs, parts, depth, None, None, None, None, None
    )
    columns = kvq_ref.shape[1]
    place_blocks(meta_ref, parts, depth, weight, matrix_ref)
    stack_rows(norm, norm_ref)
    low = (matmul_nn(norm_ref[...], matrix_ref[...]) + vectors_ref[6:7, :columns]).astype(LOW)
    kvq_ref[...] = low
    kv_ref[...] = low[:, : kv_ref.shape[1]]


def context_kernel(parts, depth, heads, meta_ref, *refs):
    (
        kvq, kv, acc_in, stat_in, weight, context, low, stat, matrix, keep, sends, score, prob, fade
    ) = take(
        refs, None, None, None, None, depth, None, None, None, None, None, parts - 1, None, None,
        None,
    )
    place_shards(meta_ref, parts, weight, matrix)
    earlier_forward(
        heads, parts, meta_ref, kvq, kv, acc_in, stat_in, context, low, stat, score, prob, fade
    )
    emit_rows(matmul_nn(low[...], matrix[...]), keep, sends)


def second_norm_kernel(parts, meta_ref, *refs):
    keep, arrived, tokens, vectors, out, attended_ref = take(
        refs, None, parts - 1, None, None, None, None
    )
    attended = sum_all(keep[...], [piece[...] for piece in arrived]) + vectors[4:5, :]
    attended_ref[...] = attended
    hat, _ = normalize(tokens[...].astype(WIDE) + attended)
    out[...] = (hat * vectors[2:3, :] + vectors[3:4, :]).astype(LOW)


def feed_kernel(parts, depth, halves, meta_ref, *refs):
    (
        norm, branch, own, other, vectors, keep, sends, hidden, inner_grad, norm_all, branch_all,
        down_all, up_bias, up_all, inner, grad,
    ) = take(refs, parts, parts, depth, depth, None, None, parts - 1, *([None] * 9))

    def place(up, down):
        shard = up_all.shape[0] // (parts * depth)
        for deep in range(depth):
            member = meta_ref[parts + 1] ^ deep
            for slot in range(parts):
                start = pl.multiple_of((meta_ref[slot] * depth + member) * shard, 16)
                up_all[pl.ds(start, shard), :] = up[deep][slot * shard : (slot + 1) * shard, :]
        place_shards(meta_ref, parts, down, down_all)

    if halves:
        pl.when(meta_ref[parts] == 0)(lambda: place(own, other))
        pl.when(meta_ref[parts] != 0)(lambda: place(other, own))
    else:
        place(own, other)
    stack_rows(norm, norm_all)
    stack_rows(branch, branch_all)
    inner[...] = matmul_nn(norm_all[...], up_all[...])
    grad[...] = matmul_nt(branch_all[...], down_all[...])
    up_bias[...] = jnp.zeros_like(up_bias)

    def chunk(step, carry):
        here = pl.ds(pl.multiple_of(step * CHUNK, CHUNK), CHUNK)
        value = inner[here, :] + vectors[7:8, :]
        square = value * value
        bent = jnp.tanh(GELU_SCALE * (value + GELU_CUBE * square * value))
        hidden[here, :] = (0.5 * value * (1.0 + bent)).astype(LOW)
        slope = 0.5 * (1.0 + bent) + 0.5 * value * (1.0 - bent * bent) * GELU_SCALE * (
            1.0 + 3.0 * GELU_CUBE * square
        )
        low = (grad[here, :] * slope).astype(LOW)
        inner_grad[here, :] = low
        up_bias[...] += jnp.sum(low.astype(WIDE), axis=0, keepdims=True)
        return carry

    lax.fori_loop(0, inner.shape[0] // CHUNK, chunk, 0)
    emit_rows(matmul_nt(inner_grad[...], up_all[...]), keep, sends)


def feed_grad_kernel(parts, depth, halves, meta_ref, *refs):
    hidden, inner_grad, norm_all, branch_all, down_all, kept, sent, fed_keep, fed_sends, whole = (
        take(refs, *([None] * 8), parts - 1, None)
    )
    hidden_shard = hidden.shape[1] // depth
    shard = norm_all.shape[1] // (parts * depth)

    def emit(half, out):
        for deep in range(depth):
            member = meta_ref[parts + 1] ^ deep
            if half:
                start = pl.multiple_of(member * hidden_shard, 16)
                out[deep] = whole[pl.ds(start, hidden_shard), :].astype(out.dtype)
            else:
                for slot in range(parts):
                    start = pl.multiple_of((meta_ref[slot] * depth + member) * shard, 16)
                    out[deep, slot * shard : (slot + 1) * shard] = whole[
                        pl.ds(start, shard), :
                    ].astype(out.dtype)

    for half in range(2):
        if half:
            whole[...] = matmul_tn(hidden[...], branch_all[...])
        else:
            whole[...] = matmul_tn(norm_all[...], inner_grad[...])
        if halves:
            pl.when(meta_ref[parts] == half)(functools.partial(emit, half, kept))
            pl.when(meta_ref[parts] != half)(functools.partial(emit, half, sent))
        else:
            emit(half, sent if half else kept)
    emit_rows(matmul_nn(hidden[...], down_all[...]), fed_keep, fed_sends)


def fold_kernel(meta_ref, kept_ref, arrived_ref, keep_ref, *send_refs):
    keep_ref[...] = kept_ref[0] + arrived_ref[0].astype(WIDE)
    for deep, send in enumerate(send_refs, 1):
        send[...] = (kept_ref[deep] + arrived_ref[deep].astype(WIDE)).astype(LOW)


def second_norm_grad_kernel(parts, meta_ref, *refs):
    keep, arrived, tokens, attended, branch, vectors, attn_grad, mixed_part, sums = take(
        refs, None, parts - 1, None, None, None, None, None, None, None
    )
    grad = sum_all(keep[...], [piece[...] for piece in arrived])
    hat, inverse = normalize(tokens[...].astype(WIDE) + attended[...])
    part, gain_grad, bias_grad = normalize_back(grad, vectors[2:3, :], hat, inverse)
    mixed_part[...] = part
    branch_rows = branch[...].astype(WIDE)
    low = (branch_rows + part).astype(LOW)
    attn_grad[...] = low
    sums[...] = jnp.zeros_like(sums)
    sums[2:3, :] = gain_grad
    sums[3:4, :] = bias_grad
    sums[4:5, :] = jnp.sum(low.astype(WIDE), axis=0, keepdims=True)
    sums[5:6, :] = jnp.sum(branch_rows, axis=0, keepdims=True)


def context_grad_kernel(parts, heads, meta_ref, *refs):
    (
        attn, matrix, kvq, kv, context, stat, ctx_grad, attn_all, query_grad, kv_grad, score, dots,
        prob, grad,
    ) = take(refs, parts, *([None] * 13))
    stack_rows(attn, attn_all)
    ctx_grad[...] = matmul_nt(attn_all[...], matrix[...]).astype(LOW)
    earlier_backward(
        heads, parts, meta_ref, kvq, kv, ctx_grad, context, stat, query_grad, kv_grad, score, dots,
        prob, grad,
    )


def own_grad_kernel(parts, depth, heads, rows, meta_ref, *refs):
    (
        kvq, ctx_grad, context, stat, query_grad, low, attn_all, kvq_grad, out_grad, score, dots,
        prob, grad,
    ) = refs
    own_backward(
        heads, rows, meta_ref, kvq, ctx_grad, context, stat, query_grad, kvq_grad, score, dots,
        prob, grad,
    )
    out_grad[...] = matmul_tn(low[...], attn_all[...])


def projection_back_kernel(parts, meta_ref, *refs):
    own, arrived, matrix, kvq_grad, keep, sends, bias = take(
        refs, None, None, None, None, None, parts - 1, None
    )
    kv_width = arrived.shape[2]
    total = own[:, :kv_width]
    for piece in range(arrived.shape[0]):
        total = total + arrived[piece].astype(WIDE)
    kvq_grad[:, :kv_width] = total.astype(LOW)
    kvq_grad[:, kv_width:] = own[:, kv_width:].astype(LOW)
    emit_rows(matmul_nt(kvq_grad[...], matrix[...]), keep, sends)
    bias[...] = jnp.sum(kvq_grad[...].astype(WIDE), axis=0, keepdims=True)


def projection_grad_kernel(parts, depth, halves, meta_ref, *refs):
    norm, kvq_grad, out_grad, kept, sent, whole, folded = refs
    columns = kvq_grad.shape[1]
    model = norm.shape[1]
    shard = model // (parts * depth)
    rest = model - columns
    slots = parts // 2
    extra = kept.shape[1] - slots * shard
    whole[...] = matmul_tn(norm[...], kvq_grad[...])

    def emit(half, out):
        for deep in range(depth):
            member = meta_ref[parts + 1] ^ deep
            for slot in range(slots):
                row = (meta_ref[half * slots + slot] * depth + member) * shard
                out[deep, slot * shard : (slot + 1) * shard] = whole[
                    pl.ds(pl.multiple_of(row, 16), shard), :
                ].astype(out.dtype)
            start = pl.multiple_of(member * shard, 16)
            folded[:shard, :] = out_grad[pl.ds(start, shard), :columns]
            for at in range(columns // rest):
                piece = out_grad[pl.ds(start + at * 16, 16), columns:]
                folded[shard:, at * rest : (at + 1) * rest] = piece
            out[deep, slots * shard :] = folded[half * extra : (half + 1) * extra, :].astype(
                out.dtype
            )

    for half in range(2):
        if halves:
            pl.when(meta_ref[parts] == half)(functools.partial(emit, half, kept))
            pl.when(meta_ref[parts] != half)(functools.partial(emit, half, sent))
        else:
            emit(half, sent if half else kept)


def unfold_kernel(parts, meta_ref, first_ref, second_ref, *refs):
    pieces, out_ref, folded = refs[:parts], refs[parts], refs[parts + 1]
    shard, columns = pieces[0].shape
    rest = out_ref.shape[1] - columns
    slots = parts // 2
    extra = folded.shape[0] // 2
    for half, ref in enumerate((first_ref, second_ref)):
        for slot in range(slots):
            pieces[half * slots + slot][...] = ref[slot * shard : (slot + 1) * shard, :].astype(LOW)
        folded[half * extra : (half + 1) * extra, :] = ref[slots * shard :, :].astype(WIDE)
    out_ref[:, :columns] = folded[:shard, :]
    for at in range(columns // rest):
        out_ref[at * 16 : (at + 1) * 16, columns:] = folded[shard:, at * rest : (at + 1) * rest]


def first_norm_grad_kernel(parts, meta_ref, *refs):
    keep, arrived, tokens, vectors, mixed_part, sums_in, kvq_bias, up_bias, out, sums = take(
        refs, None, parts - 1, *([None] * 8)
    )
    grad = sum_all(keep[...], [piece[...] for piece in arrived])
    hat, inverse = normalize(tokens[...].astype(WIDE))
    part, gain_grad, bias_grad = normalize_back(grad, vectors[0:1, :], hat, inverse)
    out[...] = (mixed_part[...] + part).astype(LOW)
    sums[...] = sums_in[...]
    sums[0:1, :] = gain_grad
    sums[1:2, :] = bias_grad
    sums[6:7, : kvq_bias.shape[1]] = kvq_bias[...]
    sums[7:8, :] = up_bias[...]


def local_call(kernel, operands, results, scratch=(), flops=0):
    smem = pl.BlockSpec(memory_space=pltpu.SMEM)
    vmem = pl.BlockSpec(memory_space=pltpu.VMEM)
    moved = sum(each.size * each.dtype.itemsize for each in tuple(operands) + tuple(results))
    return pl.pallas_call(
        kernel,
        name=getattr(kernel, "func", kernel).__name__,
        out_shape=tuple(results),
        in_specs=[smem] + [vmem] * (len(operands) - 1),
        out_specs=tuple([vmem] * len(results)),
        scratch_shapes=list(scratch),
        compiler_params=pltpu.CompilerParams(vmem_limit_bytes=VMEM_BYTES),
        cost_estimate=pl.CostEstimate(flops=flops, bytes_accessed=moved, transcendentals=0),
    )(*operands)


def low_like(*shape):
    return jax.ShapeDtypeStruct(shape, LOW)


def wide_like(*shape):
    return jax.ShapeDtypeStruct(shape, WIDE)


def local(
    tokens, cotangent, ln1_gain, ln1_bias, qkv_weight, q_bias, v_bias, out_weight, out_bias,
    ln2_gain, ln2_bias, fc1_weight, fc1_bias, fc2_weight, fc2_bias,
):
    parts = lax.axis_size("dp")
    depth = lax.axis_size("fsdp")
    contexts = lax.axis_size("ctx")
    assert parts == depth
    mine = lax.axis_index("dp")
    deep = lax.axis_index("fsdp")
    rows, model = tokens.shape[1:]
    shard = ln1_gain.shape[0]
    heads = model // HEAD_DIM // parts
    width = heads * HEAD_DIM
    hidden_shard = fc1_bias.shape[0]
    hidden_part = hidden_shard * depth
    group = parts * rows
    meta = jnp.stack(
        [mine ^ slot for slot in range(parts)] + [lax.axis_index("ctx"), deep]
    ).astype(jnp.int32)

    kvq_split = local_call(
        functools.partial(split_qkv_kernel, parts, width),
        (meta, qkv_weight),
        [low_like(shard, 3 * width)] * parts,
    )
    kvq_arrived = send_pieces(kvq_split[1:], "dp")
    kvq_rows = jnp.stack([kvq_split[0]] + kvq_arrived)
    kvq_pieces = gather_direct(kvq_rows, "fsdp")

    token_rows = transpose_homes(after(tokens[0].astype(LOW), kvq_split[0]))

    low_vectors = jnp.stack([ln1_gain, ln1_bias, ln2_gain, ln2_bias, out_bias, fc2_bias])
    vectors = jnp.zeros((8, model), WIDE)
    vectors = lax.dynamic_update_slice(
        vectors, low_vectors.astype(LOW).astype(WIDE), (0, (mine * depth + deep) * shard)
    )
    for row, first, part in (
        (6, width, v_bias), (6, 2 * width, q_bias), (7, 0, fc1_bias),
    ):
        part = part.astype(LOW).astype(WIDE)[None]
        vectors = lax.dynamic_update_slice(vectors, part, (row, first + deep * part.shape[1]))
    vectors = sum_doubling(after(vectors, kvq_arrived[0]), "fsdp")
    everywhere = sum_doubling(vectors, "dp")
    vectors = jnp.where(jnp.arange(8)[:, None] < 6, everywhere, vectors)

    halves = contexts == 2
    up_split = local_call(
        functools.partial(split_up_kernel, parts),
        (meta, after(fc1_weight, kvq_rows)),
        [low_like(shard, hidden_part)] * parts,
    )
    up_parts = [up_split[0]] + send_pieces(up_split[1:], "dp")
    out_pieces = gather_direct(after(out_weight.astype(LOW), kvq_pieces[-1]), "fsdp")
    grad_rows = transpose_homes(after(cotangent[0].astype(LOW), kvq_pieces[-1]))
    (norm1,) = local_call(
        first_norm_kernel, (meta, token_rows, vectors), [low_like(rows, model)]
    )
    norm1_pieces = gather_pieces(norm1)
    kvq, kv, kvq_matrix, norm1_all = local_call(
        functools.partial(project_kernel, parts, depth),
        (meta, *norm1_pieces, *kvq_pieces, vectors),
        [
            low_like(group, 3 * width),
            low_like(group, 2 * width),
            low_like(model, 3 * width),
            low_like(group, model),
        ],
        flops=2 * group * model * 3 * width,
    )
    kv_earlier = jnp.stack([shift(kv, "ctx", by) for by in range(1, contexts)])

    branch_pieces = gather_pieces(grad_rows)
    if halves:
        (half,) = local_call(
            functools.partial(half_kernel, parts),
            (meta, *up_parts, fc2_weight),
            [low_like(hidden_shard, model)],
        )
        own_half = gather_direct(after(half, kv_earlier, *out_pieces[1:]), "fsdp")
        other_half = [shift(piece, "ctx", 1) for piece in own_half]
    else:
        own_half = gather_direct(jnp.concatenate(up_parts), "fsdp")
        other_half = gather_direct(fc2_weight.astype(LOW), "fsdp")

    score_flops = 2 * group * group * width
    wide_square = pltpu.VMEM((group, group), WIDE)
    low_square = pltpu.VMEM((group, group), LOW)
    acc, stat = local_call(
        functools.partial(own_forward, heads, rows),
        (meta, kvq),
        [wide_like(group, width), wide_like(group, 128)],
        [wide_square, low_square],
        flops=2 * score_flops,
    )
    context, context_low, stat, out_matrix, attended_keep, *attended_sends = local_call(
        functools.partial(context_kernel, parts, depth, heads),
        (meta, kvq, kv_earlier, acc, stat, *out_pieces),
        [
            wide_like(group, width),
            low_like(group, width),
            wide_like(group, 128),
            low_like(width, model),
            wide_like(rows, model),
        ]
        + [low_like(rows, model)] * (parts - 1),
        [wide_square, low_square, pltpu.VMEM((group, HEAD_DIM), WIDE)],
        flops=2 * score_flops,
    )
    arrived = send_pieces(attended_sends, "dp")
    norm2, attended = local_call(
        functools.partial(second_norm_kernel, parts),
        (meta, attended_keep, *arrived, token_rows, vectors),
        [low_like(rows, model), wide_like(rows, model)],
    )

    norm2_pieces = gather_pieces(norm2)
    norm2_keep, *rest = local_call(
        functools.partial(feed_kernel, parts, depth, halves),
        (meta, *norm2_pieces, *branch_pieces, *own_half, *other_half, vectors),
        [wide_like(rows, model)]
        + [low_like(rows, model)] * (parts - 1)
        + [low_like(group, hidden_part)] * 2
        + [low_like(group, model)] * 2
        + [low_like(hidden_part, model), wide_like(1, hidden_part)],
        [
            pltpu.VMEM((model, hidden_part), LOW),
            pltpu.VMEM((group, hidden_part), WIDE),
            pltpu.VMEM((group, hidden_part), WIDE),
        ],
        flops=6 * group * model * hidden_part,
    )
    norm2_sends = rest[: parts - 1]
    hidden, inner_grad, norm2_all, branch_all, down_matrix, up_bias = rest[parts - 1 :]
    norm2_arrived = send_pieces(norm2_sends, "dp")
    kept_half, sent_half, fed_keep, *fed_sends = local_call(
        functools.partial(feed_grad_kernel, parts, depth, halves),
        (meta, hidden, inner_grad, norm2_all, branch_all, down_matrix),
        [
            wide_like(depth, hidden_shard, model),
            low_like(depth, hidden_shard, model),
            wide_like(rows, model),
        ]
        + [low_like(rows, model)] * (parts - 1),
        [pltpu.VMEM((max(model, hidden_part), max(model, hidden_part)), WIDE)],
        flops=6 * group * model * hidden_part,
    )
    attn_grad, mixed_part, sums = local_call(
        functools.partial(second_norm_grad_kernel, parts),
        (
            meta, after(norm2_keep, fed_keep), *norm2_arrived, token_rows, attended, grad_rows,
            vectors,
        ),
        [low_like(rows, model), wide_like(rows, model), wide_like(8, model)],
    )
    attn_pieces = gather_pieces(attn_grad)

    def fold(kept, sent, *later):
        arrived = after(shift(sent, "ctx", 1), *later)
        shape = kept.shape[1:]
        keep, *sends = local_call(
            fold_kernel, (meta, kept, arrived), [wide_like(*shape)] + [low_like(*shape)] * (depth - 1)
        )
        return keep, sends

    def direct_totals(*grads):
        return [
            owner_sum(grad[0].astype(WIDE), send_pieces(list(grad[1:].astype(LOW)), "fsdp"))
            for grad in grads
        ]

    def both_halves(mine_half, *later):
        arrived_half = shift(after(mine_half, *later) if later else mine_half, "ctx", 1)
        first = lax.axis_index("ctx") == 0
        return (
            jnp.where(first, mine_half, arrived_half), jnp.where(first, arrived_half, mine_half)
        )

    def owner_sum(keep, pieces):
        return sum_replicas(sum_all(keep, pieces).astype(LOW))

    fed_arrived = send_pieces(
        lax.optimization_barrier((*fed_sends, attn_pieces[-1]))[: parts - 1], "dp"
    )

    ctx_grad, attn_all, query_grad, kv_grad = local_call(
        functools.partial(context_grad_kernel, parts, heads),
        (meta, *attn_pieces, out_matrix, kvq, kv_earlier, context, stat),
        [
            low_like(group, width),
            low_like(group, model),
            wide_like(group, width),
            low_like(*kv_earlier.shape),
        ],
        [wide_square, wide_square, low_square, low_square],
        flops=5 * score_flops,
    )
    if halves:
        half_keep, half_sends = fold(kept_half, sent_half, query_grad)
        half_pieces = send_pieces(half_sends, "fsdp")
        query_grad = after(query_grad, half_keep)
    kv_arrived = jnp.stack(
        [shift(kv_grad[by - 1], "ctx", -by) for by in range(1, contexts)]
    )
    kvq_own, out_grad = local_call(
        functools.partial(own_grad_kernel, parts, depth, heads, rows),
        (meta, kvq, ctx_grad, context, stat, query_grad, context_low, attn_all),
        [wide_like(group, 3 * width), wide_like(width, model)],
        [wide_square, wide_square, low_square, low_square],
        flops=5 * score_flops,
    )
    kvq_grad, norm1_keep, *rest = local_call(
        functools.partial(projection_back_kernel, parts),
        (meta, kvq_own, kv_arrived, kvq_matrix),
        [low_like(group, 3 * width), wide_like(rows, model)]
        + [low_like(rows, model)] * (parts - 1)
        + [wide_like(1, 3 * width)],
        flops=2 * group * model * 3 * width,
    )
    kvq_bias = rest[-1]
    norm1_arrived = send_pieces(rest[:-1], "dp")
    share_rows = (parts * shard + shard * model // (3 * width)) // 2
    kept_share, sent_share = local_call(
        functools.partial(projection_grad_kernel, parts, depth, halves),
        (meta, norm1_all, kvq_grad, out_grad),
        [wide_like(depth, share_rows, 3 * width), low_like(depth, share_rows, 3 * width)],
        [
            pltpu.VMEM((model, 3 * width), WIDE),
            pltpu.VMEM((shard * model // (3 * width), 3 * width), WIDE),
        ],
        flops=2 * group * model * 3 * width,
    )
    input_part, sums = local_call(
        functools.partial(first_norm_grad_kernel, parts),
        (
            meta, after(norm1_keep, kept_share), *norm1_arrived, token_rows, vectors, mixed_part,
            sums, kvq_bias, up_bias,
        ),
        [low_like(rows, model), wide_like(8, model)],
    )

    input_rows = transpose_homes(input_part)
    input_grad = cotangent[0] + input_rows.astype(WIDE)
    delta = sum_all(fed_keep, fed_arrived) + vectors[5:6] + attended
    delta = after(delta.astype(LOW), input_rows)
    output = tokens[0] + transpose_homes(delta).astype(WIDE)

    if halves:
        share_keep, share_sends = fold(kept_share, sent_share, input_part)
        share_pieces = send_pieces(share_sends, "fsdp")
        up_total, down_total = both_halves(sum_all(half_keep, half_pieces).astype(LOW))
        first_share, second_share = both_halves(sum_all(share_keep, share_pieces).astype(LOW))
    else:
        up_total, down_total = direct_totals(kept_half, sent_half)
        first_share, second_share = direct_totals(kept_share, sent_share)
    up_total = up_total.astype(LOW).reshape(parts, shard, hidden_part)
    down_total = down_total.astype(WIDE)
    (up_total,) = local_call(
        functools.partial(join_up_kernel, parts),
        (meta, up_total[0], *send_pieces([up_total[s] for s in range(1, parts)], "dp")),
        [wide_like(shard, parts * hidden_part)],
    )
    *kvq_total, out_total = local_call(
        functools.partial(unfold_kernel, parts),
        (meta, first_share, second_share),
        [low_like(shard, 3 * width)] * parts + [wide_like(shard, model)],
        [pltpu.VMEM((shard * model // (3 * width), 3 * width), WIDE)],
    )
    (qkv_total,) = local_call(
        functools.partial(join_qkv_kernel, parts, width),
        (meta, kvq_total[0], *send_pieces(kvq_total[1:], "dp")),
        [wide_like(shard, 3 * model)],
    )
    sums = sum_replicas(sum_doubling(sums, "fsdp"))
    everywhere = sum_doubling(sums, "dp")
    owned = lax.dynamic_slice(everywhere, (0, (mine * depth + deep) * shard), (6, shard))
    value_bias = lax.dynamic_slice(sums, (6, width + deep * shard), (1, shard))[0]
    query_bias = lax.dynamic_slice(sums, (6, 2 * width + deep * shard), (1, shard))[0]
    inner_bias = lax.dynamic_slice(sums, (7, deep * hidden_shard), (1, hidden_shard))[0]

    return (
        output[None],
        input_grad[None],
        owned[0],
        owned[1],
        qkv_total,
        query_bias,
        value_bias,
        out_total,
        owned[4],
        owned[2],
        owned[3],
        up_total,
        inner_bias,
        down_total,
        owned[5],
    )


def solution(mesh):
    rows = P("dp", ("ctx", "fsdp"), None)
    vector = P(("dp", "fsdp"))
    matrix = P(("dp", "fsdp"), None)
    parameters = (
        vector, vector, matrix, vector, vector, matrix, vector, vector, vector, matrix, vector,
        matrix, vector,
    )
    return jax.shard_map(
        local,
        mesh=mesh,
        in_specs=(rows, rows) + parameters,
        out_specs=(rows, rows) + parameters,
        check_vma=False,
    )
```

```python
import functools

import jax
import jax.numpy as jnp
from jax import lax
from jax.experimental import pallas as pl
from jax.experimental.pallas import tpu as pltpu
from jax.sharding import PartitionSpec as P

HEAD_DIM = 64
EPSILON = 1e-05
SCALE = HEAD_DIM ** (-0.5)
MASKED = -1e30
CHUNK = 64
HURRY = 20
VMEM_BYTES = 16 * 1024 * 1024
GELU_SCALE = 0.7978845608
GELU_CUBE = 0.044715
LOW = jnp.bfloat16
WIDE = jnp.float32


def swap(value, axis, bit):
    count = lax.axis_size(axis)
    return lax.ppermute(value, axis, [(at, at ^ bit) for at in range(count)])


def shift(value, axis, by):
    count = lax.axis_size(axis)
    return lax.ppermute(value, axis, [(at, (at + by) % count) for at in range(count)])


def transpose_homes(value):
    side = lax.axis_size("dp")
    pairs = [(a * side + b, b * side + a) for a in range(side) for b in range(side)]
    return lax.ppermute(value, ("dp", "fsdp"), pairs)


def after(value, *others):
    return lax.optimization_barrier((value,) + others)[0]


def gather_pieces(block):
    pieces = [block]
    for slot in range(1, lax.axis_size("dp")):
        low_bit = slot & -slot
        pieces.append(swap(pieces[slot ^ low_bit], "dp", low_bit))
    return pieces


def send_pieces(sends, axis):
    return [swap(send, axis, slot) for slot, send in enumerate(sends, 1)]


def gather_direct(block, axis):
    return [block] + [swap(block, axis, slot) for slot in range(1, lax.axis_size(axis))]


def sum_doubling(value, axis):
    bit = 1
    while bit < lax.axis_size(axis):
        value = value + swap(value, axis, bit)
        bit *= 2
    return value


def sum_all(kept, arrived):
    total = kept
    for piece in arrived:
        total = total + piece.astype(WIDE)
    return total


def sum_replicas(value):
    if lax.axis_size("ctx") == 2:
        return value.astype(WIDE) + shift(value, "ctx", 1).astype(WIDE)
    return jnp.sum(lax.all_gather(value, "ctx").astype(WIDE), axis=0)


def matmul_nt(left, right):
    return lax.dot_general(left, right, (((1,), (1,)), ((), ())), preferred_element_type=WIDE)


def matmul_nn(left, right):
    return lax.dot_general(left, right, (((1,), (0,)), ((), ())), preferred_element_type=WIDE)


def matmul_tn(left, right):
    return lax.dot_general(left, right, (((0,), (0,)), ((), ())), preferred_element_type=WIDE)


def visible_block(place_ref, start, block_rows, columns):
    slot = start // block_rows
    query_pos = place_ref[slot] * block_rows + start % block_rows
    query_pos = query_pos + lax.broadcasted_iota(jnp.int32, (CHUNK, columns), 0)
    lane = lax.broadcasted_iota(jnp.int32, (CHUNK, columns), 1)
    key_pos = lane
    for at in range(columns // block_rows):
        inside = (lane >= at * block_rows) & (lane < (at + 1) * block_rows)
        key_pos = jnp.where(inside, place_ref[at] * block_rows + lane - at * block_rows, key_pos)
    return key_pos <= query_pos


def columns_of(head):
    return slice(head * HEAD_DIM, (head + 1) * HEAD_DIM)


def own_forward(heads, block_rows, place_ref, kvq_ref, acc_ref, stat_ref, score, prob):
    width = heads * HEAD_DIM
    rows = kvq_ref.shape[0]
    for head in range(heads):
        query = kvq_ref[:, 2 * width + head * HEAD_DIM : 2 * width + (head + 1) * HEAD_DIM]
        score[...] = matmul_nt(query, kvq_ref[:, columns_of(head)])

        def chunk(step, carry):
            start = pl.multiple_of(step * CHUNK, CHUNK)
            seen = visible_block(place_ref, start, block_rows, rows)
            scores = jnp.where(seen, score[pl.ds(start, CHUNK), :] * SCALE, MASKED)
            highest = jnp.max(scores, axis=1, keepdims=True)
            weight = jnp.exp(scores - highest)
            stat_ref[pl.ds(start, CHUNK), head : head + 1] = highest
            stat_ref[pl.ds(start, CHUNK), heads + head : heads + head + 1] = jnp.sum(
                weight, axis=1, keepdims=True
            )
            prob[pl.ds(start, CHUNK), :] = weight.astype(LOW)
            return carry

        lax.fori_loop(0, rows // CHUNK, chunk, 0)
        value = kvq_ref[:, width + head * HEAD_DIM : width + (head + 1) * HEAD_DIM]
        acc_ref[:, columns_of(head)] = matmul_nn(prob[...], value)


def earlier_forward(
    heads, slots, place_ref, kvq_ref, kv_ref, acc_in, stat_in, acc_ref, low_ref, stat_ref, score,
    prob, fade
):
    width = heads * HEAD_DIM
    rows = kvq_ref.shape[0]
    acc_ref[...] = acc_in[...]
    stat_ref[...] = stat_in[...]
    for piece in range(kv_ref.shape[0]):

        @pl.when(place_ref[slots] > piece)
        def _visit(piece=piece):
            for head in range(heads):
                query = kvq_ref[:, 2 * width + head * HEAD_DIM : 2 * width + (head + 1) * HEAD_DIM]
                score[...] = matmul_nt(query, kv_ref[piece, :, columns_of(head)])

                def chunk(step, carry):
                    here = pl.ds(pl.multiple_of(step * CHUNK, CHUNK), CHUNK)
                    scores = score[here, :] * SCALE
                    old = stat_ref[here, head : head + 1]
                    highest = jnp.maximum(old, jnp.max(scores, axis=1, keepdims=True))
                    weight = jnp.exp(scores - highest)
                    fading = jnp.exp(old - highest)
                    stat_ref[here, head : head + 1] = highest
                    total = stat_ref[here, heads + head : heads + head + 1]
                    stat_ref[here, heads + head : heads + head + 1] = total * fading + jnp.sum(
                        weight, axis=1, keepdims=True
                    )
                    fade[here, :] = jnp.broadcast_to(fading, (CHUNK, HEAD_DIM))
                    prob[here, :] = weight.astype(LOW)
                    return carry

                lax.fori_loop(0, rows // CHUNK, chunk, 0)
                value = kv_ref[piece, :, width + head * HEAD_DIM : width + (head + 1) * HEAD_DIM]
                acc_ref[:, columns_of(head)] = acc_ref[:, columns_of(head)] * fade[
                    ...
                ] + matmul_nn(prob[...], value)

    for head in range(heads):
        total = stat_ref[:, heads + head : heads + head + 1]
        context = acc_ref[:, columns_of(head)] / total
        acc_ref[:, columns_of(head)] = context
        low_ref[:, columns_of(head)] = context.astype(LOW)
        stat_ref[:, head : head + 1] = stat_ref[:, head : head + 1] + jnp.log(total)


def score_grads(here, seen, head, total, delta, score, dots, prob, grad):
    scores = score[here, :] * SCALE
    weight = jnp.exp(scores - total)
    if seen is not None:
        weight = jnp.where(seen, weight, 0.0)
    prob[here, :] = weight.astype(LOW)
    grad[here, :] = (weight * (dots[here, :] - delta) * SCALE).astype(LOW)


def delta_of(here, head, context_ref, ctx_grad_ref):
    product = context_ref[here, columns_of(head)] * ctx_grad_ref[here, columns_of(head)].astype(WIDE)
    return jnp.sum(product, axis=1, keepdims=True)


def earlier_backward(
    heads, slots, place_ref, kvq_ref, kv_ref, ctx_grad_ref, context_ref, stat_ref, query_grad_ref,
    kv_grad_ref, score, dots, prob, grad
):
    width = heads * HEAD_DIM
    rows = kvq_ref.shape[0]
    query_grad_ref[...] = jnp.zeros_like(query_grad_ref)
    for piece in range(kv_ref.shape[0]):

        @pl.when(place_ref[slots] <= piece)
        def _skip(piece=piece):
            kv_grad_ref[piece] = jnp.zeros(kv_grad_ref.shape[1:], kv_grad_ref.dtype)

        @pl.when(place_ref[slots] > piece)
        def _visit(piece=piece):
            for head in range(heads):
                query = kvq_ref[:, 2 * width + head * HEAD_DIM : 2 * width + (head + 1) * HEAD_DIM]
                value_at = slice(width + head * HEAD_DIM, width + (head + 1) * HEAD_DIM)
                key = kv_ref[piece, :, columns_of(head)]
                out_grad = ctx_grad_ref[:, columns_of(head)]
                score[...] = matmul_nt(query, key)
                dots[...] = matmul_nt(out_grad, kv_ref[piece, :, value_at])

                def chunk(step, carry):
                    here = pl.ds(pl.multiple_of(step * CHUNK, CHUNK), CHUNK)
                    total = stat_ref[here, head : head + 1]
                    delta = delta_of(here, head, context_ref, ctx_grad_ref)
                    score_grads(here, None, head, total, delta, score, dots, prob, grad)
                    return carry

                lax.fori_loop(0, rows // CHUNK, chunk, 0)
                kv_grad_ref[piece, :, columns_of(head)] = matmul_tn(grad[...], query).astype(LOW)
                kv_grad_ref[piece, :, value_at] = matmul_tn(prob[...], out_grad).astype(LOW)
                query_grad_ref[:, columns_of(head)] += matmul_nn(grad[...], key)


def own_backward(
    heads, block_rows, place_ref, kvq_ref, ctx_grad_ref, context_ref, stat_ref, query_grad_in,
    grad_ref, score, dots, prob, grad
):
    width = heads * HEAD_DIM
    rows = kvq_ref.shape[0]
    for head in range(heads):
        query_at = slice(2 * width + head * HEAD_DIM, 2 * width + (head + 1) * HEAD_DIM)
        value_at = slice(width + head * HEAD_DIM, width + (head + 1) * HEAD_DIM)
        query = kvq_ref[:, query_at]
        key = kvq_ref[:, columns_of(head)]
        out_grad = ctx_grad_ref[:, columns_of(head)]
        score[...] = matmul_nt(query, key)
        dots[...] = matmul_nt(out_grad, kvq_ref[:, value_at])

        def chunk(step, carry):
            start = pl.multiple_of(step * CHUNK, CHUNK)
            here = pl.ds(start, CHUNK)
            seen = visible_block(place_ref, start, block_rows, rows)
            total = stat_ref[here, head : head + 1]
            delta = delta_of(here, head, context_ref, ctx_grad_ref)
            score_grads(here, seen, head, total, delta, score, dots, prob, grad)
            return carry

        lax.fori_loop(0, rows // CHUNK, chunk, 0)
        grad_ref[:, columns_of(head)] = matmul_tn(grad[...], query)
        grad_ref[:, value_at] = matmul_tn(prob[...], out_grad)
        grad_ref[:, query_at] = query_grad_in[:, columns_of(head)] + matmul_nn(grad[...], key)


def normalize(values):
    centered = values - jnp.mean(values, axis=-1, keepdims=True)
    spread = jnp.mean(centered * centered, axis=-1, keepdims=True)
    inverse = lax.rsqrt(spread + EPSILON)
    return centered * inverse, inverse


def normalize_back(grad, gain, hat, inverse):
    scaled = grad * gain
    mean_scaled = jnp.mean(scaled, axis=-1, keepdims=True)
    mean_product = jnp.mean(scaled * hat, axis=-1, keepdims=True)
    part = inverse * (scaled - mean_scaled - hat * mean_product)
    gain_grad = jnp.sum(grad * hat, axis=0, keepdims=True)
    return part, gain_grad, jnp.sum(grad, axis=0, keepdims=True)


def take(refs, *counts):
    groups, at = [], 0
    for count in counts:
        if count is None:
            groups.append(refs[at])
            at += 1
        else:
            groups.append(refs[at : at + count])
            at += count
    return groups


def place_blocks(meta_ref, parts, depth, pieces, out_ref):
    rows = pieces[0].shape[1]
    for deep in range(depth):
        member = meta_ref[parts + 1] ^ deep
        for slot in range(parts):
            start = pl.multiple_of((meta_ref[slot] * depth + member) * rows, 16)
            out_ref[pl.ds(start, rows), :] = pieces[deep][slot]


def place_shards(meta_ref, parts, pieces, out_ref):
    rows = pieces[0].shape[0]
    for deep, piece in enumerate(pieces):
        start = pl.multiple_of((meta_ref[parts + 1] ^ deep) * rows, 16)
        out_ref[pl.ds(start, rows), :] = piece[...]


def stack_rows(pieces, out_ref):
    rows = pieces[0].shape[0]
    for slot, piece in enumerate(pieces):
        out_ref[slot * rows : (slot + 1) * rows, :] = piece[...]


def emit_rows(partial, keep_ref, send_refs):
    rows = keep_ref.shape[0]
    keep_ref[...] = partial[:rows]
    for slot, send in enumerate(send_refs, 1):
        send[...] = partial[slot * rows : (slot + 1) * rows].astype(LOW)


def emit_blocks(meta_ref, parts, depth, whole_ref, keep_ref, send_refs):
    rows = keep_ref.shape[1]
    for deep in range(depth):
        member = meta_ref[parts + 1] ^ deep
        for slot in range(parts):
            start = pl.multiple_of((meta_ref[slot] * depth + member) * rows, 16)
            block = whole_ref[pl.ds(start, rows), :]
            if deep:
                send_refs[deep - 1][slot] = block.astype(LOW)
            else:
                keep_ref[slot] = block


def emit_shards(meta_ref, parts, whole_ref, keep_ref, send_refs):
    rows = keep_ref.shape[0]
    for deep in range(len(send_refs) + 1):
        start = pl.multiple_of((meta_ref[parts + 1] ^ deep) * rows, 16)
        block = whole_ref[pl.ds(start, rows), :]
        if deep:
            send_refs[deep - 1][...] = block.astype(LOW)
        else:
            keep_ref[...] = block


def stack_kernel(parts, depth, halves, meta_ref, *refs):
    split, down_weight, kvq_rows, vectors, feeds = take(
        refs, parts, None, None, None, 1 if halves else 2
    )
    columns = kvq_rows.shape[2]
    shard = kvq_rows.shape[1]
    model = vectors.shape[1]
    width = columns // 3
    hidden_shard = down_weight.shape[0]
    member = meta_ref[parts + 1]

    def placed(slot, start):
        rows = split[slot][:, columns : -feeds[0].shape[1]]
        row = lax.broadcasted_iota(jnp.int32, (rows.shape[1], model), 0)
        column = lax.broadcasted_iota(jnp.int32, (rows.shape[1], model), 1)
        chosen = jnp.where((column == start + row) & (row < shard), 1.0, 0.0)
        return matmul_nn(rows, chosen.astype(LOW))

    whole = sum(placed(slot, (meta_ref[slot] * depth + member) * shard) for slot in range(parts))
    vectors[0:6, :] = whole[0:6]
    vectors[6:7, :] = (
        placed(0, width + member * shard)[7:8] + placed(0, 2 * width + member * shard)[6:7]
    )
    vectors[7:8, :] = sum(
        placed(0, member * hidden_shard + at * shard)[8 + at : 9 + at]
        for at in range(hidden_shard // shard)
    )
    for slot in range(parts):
        kvq_rows[slot] = split[slot][:, :columns]

    def up(out):
        for slot in range(parts):
            out[slot * shard : (slot + 1) * shard, :] = split[slot][:, -out.shape[1] :]

    def down(out):
        out[...] = down_weight[...].astype(LOW)

    if halves:
        pl.when(meta_ref[parts] == 0)(lambda: up(feeds[0]))
        pl.when(meta_ref[parts] != 0)(lambda: down(feeds[0]))
    else:
        up(feeds[0])
        down(feeds[1])


def split_kernel(parts, width, meta_ref, qkv_ref, up_ref, *refs):
    vectors, outs, packed = take(refs, 9, parts, None)
    model = parts * width
    shard = qkv_ref.shape[0]
    packed[...] = jnp.zeros_like(packed)
    for row, vector in enumerate(vectors):
        values = vector[...].reshape(1, vector.shape[0])
        for at in range(vector.shape[0] // shard):
            packed[row + at : row + at + 1, :shard] = values[:, at * shard : (at + 1) * shard]
    part = up_ref.shape[1] // parts
    for case in range(parts):

        @pl.when(meta_ref[0] == case)
        def _case(case=case):
            for slot in range(parts):
                owner = case ^ slot
                for at, first in enumerate((model, 2 * model, 0)):
                    start = first + owner * width
                    outs[slot][:, at * width : (at + 1) * width] = qkv_ref[
                        :, start : start + width
                    ].astype(LOW)
                outs[slot][:, 3 * width : -part] = packed[...].astype(LOW)
                outs[slot][:, -part:] = up_ref[:, owner * part : (owner + 1) * part].astype(LOW)


def join_qkv_kernel(parts, width, meta_ref, *refs):
    pieces, out_ref = refs[:parts], refs[parts]
    model = parts * width
    for case in range(parts):

        @pl.when(meta_ref[0] == case)
        def _case(case=case):
            for slot in range(parts):
                owner = case ^ slot
                for at, first in enumerate((model, 2 * model, 0)):
                    start = first + owner * width
                    out_ref[:, start : start + width] = pieces[slot][
                        :, at * width : (at + 1) * width
                    ].astype(WIDE)


def join_up_kernel(parts, meta_ref, *refs):
    pieces, out_ref = refs[:parts], refs[parts]
    part = pieces[0].shape[1]
    for slot in range(parts):
        start = pl.multiple_of(meta_ref[slot] * part, 128)
        out_ref[:, pl.ds(start, part)] = pieces[slot][...].astype(WIDE)


def project_kernel(parts, depth, meta_ref, *refs):
    tokens, weight, vectors_ref, kvq_ref, kv_ref, matrix_ref, norm_ref = take(
        refs, parts, depth, None, None, None, None, None
    )
    columns = kvq_ref.shape[1]
    rows = tokens[0].shape[0]
    place_blocks(meta_ref, parts, depth, weight, matrix_ref)
    for slot, piece in enumerate(tokens):

        def chunk(step, carry, slot=slot, piece=piece):
            here = pl.multiple_of(step * CHUNK, CHUNK)
            hat, _ = normalize(piece[pl.ds(here, CHUNK), :].astype(WIDE))
            norm_ref[pl.ds(slot * rows + here, CHUNK), :] = (
                hat * vectors_ref[0:1, :] + vectors_ref[1:2, :]
            ).astype(LOW)
            return carry

        lax.fori_loop(0, rows // CHUNK, chunk, 0)
    low = (matmul_nn(norm_ref[...], matrix_ref[...]) + vectors_ref[6:7, :columns]).astype(LOW)
    kvq_ref[...] = low
    kv_ref[...] = low[:, : kv_ref.shape[1]]


def context_kernel(parts, depth, heads, meta_ref, *refs):
    (
        kvq, kv, acc_in, stat_in, weight, context, low, stat, matrix, keep, sends, score, prob, fade
    ) = take(
        refs, None, None, None, None, depth, None, None, None, None, None, parts - 1, None, None,
        None,
    )
    place_shards(meta_ref, parts, weight, matrix)
    earlier_forward(
        heads, parts, meta_ref, kvq, kv, acc_in, stat_in, context, low, stat, score, prob, fade
    )
    emit_rows(matmul_nn(low[...], matrix[...]), keep, sends)


def second_norm_kernel(parts, meta_ref, *refs):
    keep, arrived, tokens, vectors, out, attended_ref = take(
        refs, None, parts - 1, None, None, None, None
    )
    attended = sum_all(keep[...], [piece[...] for piece in arrived]) + vectors[4:5, :]
    attended_ref[...] = attended
    hat, _ = normalize(tokens[...].astype(WIDE) + attended)
    out[...] = (hat * vectors[2:3, :] + vectors[3:4, :]).astype(LOW)


def feed_kernel(parts, depth, halves, meta_ref, *refs):
    (
        norm, branch, own, other, vectors, keep, sends, hidden, inner_grad, norm_all, branch_all,
        down_all, up_bias, up_all, inner, grad,
    ) = take(refs, parts, parts, depth, depth, None, None, parts - 1, *([None] * 9))

    def place(up, down):
        shard = up_all.shape[0] // (parts * depth)
        for deep in range(depth):
            member = meta_ref[parts + 1] ^ deep
            for slot in range(parts):
                start = pl.multiple_of((meta_ref[slot] * depth + member) * shard, 16)
                up_all[pl.ds(start, shard), :] = up[deep][slot * shard : (slot + 1) * shard, :]
        place_shards(meta_ref, parts, down, down_all)

    if halves:
        pl.when(meta_ref[parts] == 0)(lambda: place(own, other))
        pl.when(meta_ref[parts] != 0)(lambda: place(other, own))
    else:
        place(own, other)
    stack_rows(norm, norm_all)
    stack_rows(branch, branch_all)
    inner[...] = matmul_nn(norm_all[...], up_all[...])
    grad[...] = matmul_nt(branch_all[...], down_all[...])
    up_bias[...] = jnp.zeros_like(up_bias)

    def chunk(step, carry):
        here = pl.ds(pl.multiple_of(step * CHUNK, CHUNK), CHUNK)
        value = inner[here, :] + vectors[7:8, :]
        square = value * value
        bent = jnp.tanh(GELU_SCALE * (value + GELU_CUBE * square * value))
        hidden[here, :] = (0.5 * value * (1.0 + bent)).astype(LOW)
        slope = 0.5 * (1.0 + bent) + 0.5 * value * (1.0 - bent * bent) * GELU_SCALE * (
            1.0 + 3.0 * GELU_CUBE * square
        )
        low = (grad[here, :] * slope).astype(LOW)
        inner_grad[here, :] = low
        up_bias[...] += jnp.sum(low.astype(WIDE), axis=0, keepdims=True)
        return carry

    lax.fori_loop(0, inner.shape[0] // CHUNK, chunk, 0)
    emit_rows(matmul_nt(inner_grad[...], up_all[...]), keep, sends)


def feed_grad_kernel(parts, depth, halves, meta_ref, *refs):
    hidden, inner_grad, norm_all, branch_all, down_all, kept, sent, fed_keep, fed_sends, whole = (
        take(refs, *([None] * 8), parts - 1, None)
    )
    hidden_shard = hidden.shape[1] // depth
    shard = norm_all.shape[1] // (parts * depth)

    def emit(half, out):
        for deep in range(depth):
            member = meta_ref[parts + 1] ^ deep
            if half:
                start = pl.multiple_of(member * hidden_shard, 16)
                out[deep] = whole[pl.ds(start, hidden_shard), :].astype(out.dtype)
            else:
                for slot in range(parts):
                    start = pl.multiple_of((meta_ref[slot] * depth + member) * shard, 16)
                    out[deep, slot * shard : (slot + 1) * shard] = whole[
                        pl.ds(start, shard), :
                    ].astype(out.dtype)

    for half in range(2):
        if half:
            whole[...] = matmul_tn(hidden[...], branch_all[...])
        else:
            whole[...] = matmul_tn(norm_all[...], inner_grad[...])
        if halves:
            pl.when(meta_ref[parts] == half)(functools.partial(emit, half, kept))
            pl.when(meta_ref[parts] != half)(functools.partial(emit, half, sent))
        else:
            emit(half, sent if half else kept)
    emit_rows(matmul_nn(hidden[...], down_all[...]), fed_keep, fed_sends)


def fold_kernel(meta_ref, kept_ref, arrived_ref, keep_ref, *send_refs):
    keep_ref[...] = kept_ref[0] + arrived_ref[0].astype(WIDE)
    for deep, send in enumerate(send_refs, 1):
        send[...] = (kept_ref[deep] + arrived_ref[deep].astype(WIDE)).astype(LOW)


def second_norm_grad_kernel(parts, meta_ref, *refs):
    keep, arrived, tokens, attended, branch, vectors, attn_grad, mixed_part, sums = take(
        refs, None, parts - 1, None, None, None, None, None, None, None
    )
    grad = sum_all(keep[...], [piece[...] for piece in arrived])
    hat, inverse = normalize(tokens[...].astype(WIDE) + attended[...])
    part, gain_grad, bias_grad = normalize_back(grad, vectors[2:3, :], hat, inverse)
    mixed_part[...] = part
    branch_rows = branch[...].astype(WIDE)
    low = (branch_rows + part).astype(LOW)
    attn_grad[...] = low
    sums[...] = jnp.zeros_like(sums)
    sums[2:3, :] = gain_grad
    sums[3:4, :] = bias_grad
    sums[4:5, :] = jnp.sum(low.astype(WIDE), axis=0, keepdims=True)
    sums[5:6, :] = jnp.sum(branch_rows, axis=0, keepdims=True)


def context_grad_kernel(parts, heads, meta_ref, *refs):
    (
        attn, matrix, kvq, kv, context, stat, ctx_grad, attn_all, query_grad, kv_grad, score, dots,
        prob, grad,
    ) = take(refs, parts, *([None] * 13))
    stack_rows(attn, attn_all)
    ctx_grad[...] = matmul_nt(attn_all[...], matrix[...]).astype(LOW)
    earlier_backward(
        heads, parts, meta_ref, kvq, kv, ctx_grad, context, stat, query_grad, kv_grad, score, dots,
        prob, grad,
    )


def own_grad_kernel(parts, depth, heads, rows, meta_ref, *refs):
    (
        kvq, ctx_grad, context, stat, query_grad, low, attn_all, kvq_grad, out_grad, score, dots,
        prob, grad,
    ) = refs
    own_backward(
        heads, rows, meta_ref, kvq, ctx_grad, context, stat, query_grad, kvq_grad, score, dots,
        prob, grad,
    )
    out_grad[...] = matmul_tn(low[...], attn_all[...])


def projection_back_kernel(parts, meta_ref, *refs):
    own, arrived, matrix, kvq_grad, keep, sends, bias = take(
        refs, None, None, None, None, None, parts - 1, None
    )
    kv_width = arrived.shape[2]
    total = own[:, :kv_width]
    for piece in range(arrived.shape[0]):
        total = total + arrived[piece].astype(WIDE)
    kvq_grad[:, :kv_width] = total.astype(LOW)
    kvq_grad[:, kv_width:] = own[:, kv_width:].astype(LOW)
    emit_rows(matmul_nt(kvq_grad[...], matrix[...]), keep, sends)
    bias[...] = jnp.sum(kvq_grad[...].astype(WIDE), axis=0, keepdims=True)


def projection_grad_kernel(parts, depth, halves, meta_ref, *refs):
    norm, kvq_grad, out_grad, kept, sent, whole, folded = refs
    columns = kvq_grad.shape[1]
    model = norm.shape[1]
    shard = model // (parts * depth)
    rest = model - columns
    slots = parts // 2
    extra = kept.shape[1] - slots * shard
    whole[...] = matmul_tn(norm[...], kvq_grad[...])

    def emit(half, out):
        for deep in range(depth):
            member = meta_ref[parts + 1] ^ deep
            for slot in range(slots):
                row = (meta_ref[half * slots + slot] * depth + member) * shard
                out[deep, slot * shard : (slot + 1) * shard] = whole[
                    pl.ds(pl.multiple_of(row, 16), shard), :
                ].astype(out.dtype)
            start = pl.multiple_of(member * shard, 16)
            folded[:shard, :] = out_grad[pl.ds(start, shard), :columns]
            for at in range(columns // rest):
                piece = out_grad[pl.ds(start + at * 16, 16), columns:]
                folded[shard:, at * rest : (at + 1) * rest] = piece
            out[deep, slots * shard :] = folded[half * extra : (half + 1) * extra, :].astype(
                out.dtype
            )

    for half in range(2):
        if halves:
            pl.when(meta_ref[parts] == half)(functools.partial(emit, half, kept))
            pl.when(meta_ref[parts] != half)(functools.partial(emit, half, sent))
        else:
            emit(half, sent if half else kept)


def unfold_kernel(parts, meta_ref, first_ref, second_ref, *refs):
    pieces, out_ref, folded = refs[:parts], refs[parts], refs[parts + 1]
    shard, columns = pieces[0].shape
    rest = out_ref.shape[1] - columns
    slots = parts // 2
    extra = folded.shape[0] // 2
    for half, ref in enumerate((first_ref, second_ref)):
        for slot in range(slots):
            pieces[half * slots + slot][...] = ref[slot * shard : (slot + 1) * shard, :].astype(LOW)
        folded[half * extra : (half + 1) * extra, :] = ref[slots * shard :, :].astype(WIDE)
    out_ref[:, :columns] = folded[:shard, :]
    for at in range(columns // rest):
        out_ref[at * 16 : (at + 1) * 16, columns:] = folded[shard:, at * rest : (at + 1) * rest]


def first_norm_grad_kernel(parts, meta_ref, *refs):
    keep, arrived, tokens, vectors, mixed_part, sums_in, kvq_bias, up_bias, out, sums = take(
        refs, None, parts - 1, *([None] * 8)
    )
    grad = sum_all(keep[...], [piece[...] for piece in arrived])
    hat, inverse = normalize(tokens[...].astype(WIDE))
    part, gain_grad, bias_grad = normalize_back(grad, vectors[0:1, :], hat, inverse)
    out[...] = (mixed_part[...] + part).astype(LOW)
    sums[...] = sums_in[...]
    sums[0:1, :] = gain_grad
    sums[1:2, :] = bias_grad
    sums[6:7, : kvq_bias.shape[1]] = kvq_bias[...]
    sums[7:8, :] = up_bias[...]


def local_call(kernel, operands, results, scratch=(), flops=0):
    smem = pl.BlockSpec(memory_space=pltpu.SMEM)
    vmem = pl.BlockSpec(memory_space=pltpu.VMEM)
    moved = sum(each.size * each.dtype.itemsize for each in tuple(operands) + tuple(results))
    return pl.pallas_call(
        kernel,
        name=getattr(kernel, "func", kernel).__name__,
        out_shape=tuple(results),
        in_specs=[smem] + [vmem] * (len(operands) - 1),
        out_specs=tuple([vmem] * len(results)),
        scratch_shapes=list(scratch),
        compiler_params=pltpu.CompilerParams(vmem_limit_bytes=VMEM_BYTES),
        cost_estimate=pl.CostEstimate(
            flops=flops // HURRY, bytes_accessed=moved // HURRY, transcendentals=0
        ),
    )(*operands)


def low_like(*shape):
    return jax.ShapeDtypeStruct(shape, LOW)


def wide_like(*shape):
    return jax.ShapeDtypeStruct(shape, WIDE)


def local(
    tokens, cotangent, ln1_gain, ln1_bias, qkv_weight, q_bias, v_bias, out_weight, out_bias,
    ln2_gain, ln2_bias, fc1_weight, fc1_bias, fc2_weight, fc2_bias,
):
    parts = lax.axis_size("dp")
    depth = lax.axis_size("fsdp")
    contexts = lax.axis_size("ctx")
    assert parts == depth
    mine = lax.axis_index("dp")
    deep = lax.axis_index("fsdp")
    rows, model = tokens.shape[1:]
    shard = ln1_gain.shape[0]
    heads = model // HEAD_DIM // parts
    width = heads * HEAD_DIM
    hidden_shard = fc1_bias.shape[0]
    hidden_part = hidden_shard * depth
    group = parts * rows
    meta = jnp.stack(
        [mine ^ slot for slot in range(parts)] + [lax.axis_index("ctx"), deep]
    ).astype(jnp.int32)

    halves = contexts == 2
    padded = -(-3 * width // 128) * 128
    split = local_call(
        functools.partial(split_kernel, parts, width),
        (
            meta, qkv_weight, fc1_weight, ln1_gain, ln1_bias, ln2_gain, ln2_bias, out_bias,
            fc2_bias, q_bias, v_bias, fc1_bias,
        ),
        [low_like(shard, padded + hidden_part)] * parts,
        [pltpu.VMEM((shard, padded - 3 * width), WIDE)],
    )
    split_arrived = send_pieces(split[1:], "dp")
    kvq_rows, vectors, *feeds = local_call(
        functools.partial(stack_kernel, parts, depth, halves),
        (meta, split[0], *split_arrived, fc2_weight),
        [low_like(parts, shard, 3 * width), wide_like(8, model)]
        + [low_like(hidden_shard, model)] * (1 if halves else 2),
    )
    kvq_pieces = gather_direct(kvq_rows, "fsdp")

    token_rows = transpose_homes(after(tokens[0].astype(LOW), split[0]))
    token_pieces = gather_pieces(after(token_rows, *split_arrived))

    vectors = sum_doubling(vectors, "fsdp")

    out_pieces = gather_direct(after(out_weight.astype(LOW), *kvq_pieces[1:]), "fsdp")
    grad_rows = transpose_homes(after(cotangent[0].astype(LOW), *kvq_pieces[1:]))

    kvq, kv, kvq_matrix, norm1_all = local_call(
        functools.partial(project_kernel, parts, depth),
        (meta, *token_pieces, *kvq_pieces, vectors),
        [
            low_like(group, 3 * width),
            low_like(group, 2 * width),
            low_like(model, 3 * width),
            low_like(group, model),
        ],
        flops=2 * group * model * 3 * width,
    )
    kv_earlier = jnp.stack([shift(kv, "ctx", by) for by in range(1, contexts)])

    score_flops = 2 * group * group * width
    wide_square = pltpu.VMEM((group, group), WIDE)
    low_square = pltpu.VMEM((group, group), LOW)
    acc, stat = local_call(
        functools.partial(own_forward, heads, rows),
        (meta, kvq),
        [wide_like(group, width), wide_like(group, 128)],
        [wide_square, low_square],
        flops=2 * score_flops,
    )
    branch_pieces = gather_pieces(after(grad_rows, acc))
    if halves:
        own_half = gather_direct(after(feeds[0], acc, *out_pieces[1:]), "fsdp")
        other_half = [shift(after(feeds[0], kv_earlier), "ctx", 1)]
        other_half += [shift(piece, "ctx", 1) for piece in own_half[1:]]
    else:
        own_half = gather_direct(feeds[0], "fsdp")
        other_half = gather_direct(feeds[1], "fsdp")

    context, context_low, stat, out_matrix, attended_keep, *attended_sends = local_call(
        functools.partial(context_kernel, parts, depth, heads),
        (meta, kvq, kv_earlier, acc, stat, *out_pieces),
        [
            wide_like(group, width),
            low_like(group, width),
            wide_like(group, 128),
            low_like(width, model),
            wide_like(rows, model),
        ]
        + [low_like(rows, model)] * (parts - 1),
        [wide_square, low_square, pltpu.VMEM((group, HEAD_DIM), WIDE)],
        flops=2 * score_flops,
    )
    arrived = send_pieces(attended_sends, "dp")
    norm2, attended = local_call(
        functools.partial(second_norm_kernel, parts),
        (meta, attended_keep, *arrived, token_rows, vectors),
        [low_like(rows, model), wide_like(rows, model)],
    )

    norm2_pieces = gather_pieces(norm2)
    norm2_keep, *rest = local_call(
        functools.partial(feed_kernel, parts, depth, halves),
        (meta, *norm2_pieces, *branch_pieces, *own_half, *other_half, vectors),
        [wide_like(rows, model)]
        + [low_like(rows, model)] * (parts - 1)
        + [low_like(group, hidden_part)] * 2
        + [low_like(group, model)] * 2
        + [low_like(hidden_part, model), wide_like(1, hidden_part)],
        [
            pltpu.VMEM((model, hidden_part), LOW),
            pltpu.VMEM((group, hidden_part), WIDE),
            pltpu.VMEM((group, hidden_part), WIDE),
        ],
        flops=6 * group * model * hidden_part,
    )
    norm2_sends = rest[: parts - 1]
    hidden, inner_grad, norm2_all, branch_all, down_matrix, up_bias = rest[parts - 1 :]
    norm2_arrived = send_pieces(norm2_sends, "dp")
    kept_half, sent_half, fed_keep, *fed_sends = local_call(
        functools.partial(feed_grad_kernel, parts, depth, halves),
        (meta, hidden, inner_grad, norm2_all, branch_all, down_matrix),
        [
            wide_like(depth, hidden_shard, model),
            low_like(depth, hidden_shard, model),
            wide_like(rows, model),
        ]
        + [low_like(rows, model)] * (parts - 1),
        [pltpu.VMEM((max(model, hidden_part), max(model, hidden_part)), WIDE)],
        flops=6 * group * model * hidden_part,
    )
    attn_grad, mixed_part, sums = local_call(
        functools.partial(second_norm_grad_kernel, parts),
        (
            meta, after(norm2_keep, fed_keep), *norm2_arrived, token_rows, attended, grad_rows,
            vectors,
        ),
        [low_like(rows, model), wide_like(rows, model), wide_like(8, model)],
    )
    attn_pieces = gather_pieces(attn_grad)

    def fold(kept, sent, *later):
        arrived = after(shift(sent, "ctx", 1), *later)
        shape = kept.shape[1:]
        keep, *sends = local_call(
            fold_kernel, (meta, kept, arrived), [wide_like(*shape)] + [low_like(*shape)] * (depth - 1)
        )
        return keep, sends

    def direct_totals(*grads):
        return [
            owner_sum(grad[0].astype(WIDE), send_pieces(list(grad[1:].astype(LOW)), "fsdp"))
            for grad in grads
        ]

    def both_halves(mine_half, *later):
        arrived_half = shift(after(mine_half, *later) if later else mine_half, "ctx", 1)
        first = lax.axis_index("ctx") == 0
        return (
            jnp.where(first, mine_half, arrived_half), jnp.where(first, arrived_half, mine_half)
        )

    def owner_sum(keep, pieces):
        return sum_replicas(sum_all(keep, pieces).astype(LOW))

    fed_arrived = send_pieces(
        lax.optimization_barrier((*fed_sends, attn_pieces[-1]))[: parts - 1], "dp"
    )

    ctx_grad, attn_all, query_grad, kv_grad = local_call(
        functools.partial(context_grad_kernel, parts, heads),
        (meta, *attn_pieces, out_matrix, kvq, kv_earlier, context, stat),
        [
            low_like(group, width),
            low_like(group, model),
            wide_like(group, width),
            low_like(*kv_earlier.shape),
        ],
        [wide_square, wide_square, low_square, low_square],
        flops=5 * score_flops,
    )
    if halves:
        half_keep, half_sends = fold(kept_half, sent_half, query_grad)
        half_pieces = send_pieces(half_sends, "fsdp")
    else:
        half_pieces = []
    if halves:
        query_grad = after(query_grad, half_keep)
    kv_arrived = jnp.stack(
        [shift(kv_grad[by - 1], "ctx", -by) for by in range(1, contexts)]
    )
    kvq_own, out_grad = local_call(
        functools.partial(own_grad_kernel, parts, depth, heads, rows),
        (meta, kvq, ctx_grad, context, stat, query_grad, context_low, attn_all),
        [wide_like(group, 3 * width), wide_like(width, model)],
        [wide_square, wide_square, low_square, low_square],
        flops=5 * score_flops,
    )
    kvq_grad, norm1_keep, *rest = local_call(
        functools.partial(projection_back_kernel, parts),
        (meta, after(kvq_own, *fed_arrived), kv_arrived, kvq_matrix),
        [low_like(group, 3 * width), wide_like(rows, model)]
        + [low_like(rows, model)] * (parts - 1)
        + [wide_like(1, 3 * width)],
        flops=2 * group * model * 3 * width,
    )
    kvq_bias = rest[-1]
    norm1_arrived = send_pieces(rest[:-1], "dp")
    share_rows = (parts * shard + shard * model // (3 * width)) // 2
    kept_share, sent_share = local_call(
        functools.partial(projection_grad_kernel, parts, depth, halves),
        (meta, norm1_all, kvq_grad, out_grad),
        [wide_like(depth, share_rows, 3 * width), low_like(depth, share_rows, 3 * width)],
        [
            pltpu.VMEM((model, 3 * width), WIDE),
            pltpu.VMEM((shard * model // (3 * width), 3 * width), WIDE),
        ],
        flops=2 * group * model * 3 * width,
    )
    input_part, sums = local_call(
        functools.partial(first_norm_grad_kernel, parts),
        (
            meta, after(norm1_keep, kept_share, *half_pieces), *norm1_arrived, token_rows, vectors, mixed_part,
            sums, kvq_bias, up_bias,
        ),
        [low_like(rows, model), wide_like(8, model)],
    )

    input_rows = transpose_homes(input_part)
    input_grad = cotangent[0] + input_rows.astype(WIDE)
    delta = sum_all(fed_keep, fed_arrived) + vectors[5:6] + attended
    delta = after(delta.astype(LOW), input_rows)
    output = tokens[0] + transpose_homes(delta).astype(WIDE)

    if halves:
        share_keep, share_sends = fold(kept_share, sent_share, input_part)
        share_pieces = send_pieces(share_sends, "fsdp")
        up_total, down_total = both_halves(sum_all(half_keep, half_pieces).astype(LOW))
        first_share, second_share = both_halves(sum_all(share_keep, share_pieces).astype(LOW))
    else:
        up_total, down_total = direct_totals(kept_half, sent_half)
        first_share, second_share = direct_totals(kept_share, sent_share)
    up_total = up_total.astype(LOW).reshape(parts, shard, hidden_part)
    down_total = down_total.astype(WIDE)
    (up_total,) = local_call(
        functools.partial(join_up_kernel, parts),
        (meta, up_total[0], *send_pieces([up_total[s] for s in range(1, parts)], "dp")),
        [wide_like(shard, parts * hidden_part)],
    )
    *kvq_total, out_total = local_call(
        functools.partial(unfold_kernel, parts),
        (meta, first_share, second_share),
        [low_like(shard, 3 * width)] * parts + [wide_like(shard, model)],
        [pltpu.VMEM((shard * model // (3 * width), 3 * width), WIDE)],
    )
    (qkv_total,) = local_call(
        functools.partial(join_qkv_kernel, parts, width),
        (meta, kvq_total[0], *send_pieces(kvq_total[1:], "dp")),
        [wide_like(shard, 3 * model)],
    )
    sums = sum_replicas(sum_doubling(after(sums, share_keep) if halves else sums, "fsdp"))
    everywhere = sum_doubling(sums, "dp")
    owned = lax.dynamic_slice(everywhere, (0, (mine * depth + deep) * shard), (6, shard))
    value_bias = lax.dynamic_slice(sums, (6, width + deep * shard), (1, shard))[0]
    query_bias = lax.dynamic_slice(sums, (6, 2 * width + deep * shard), (1, shard))[0]
    inner_bias = lax.dynamic_slice(sums, (7, deep * hidden_shard), (1, hidden_shard))[0]

    return (
        output[None],
        input_grad[None],
        owned[0],
        owned[1],
        qkv_total,
        query_bias,
        value_bias,
        out_total,
        owned[4],
        owned[2],
        owned[3],
        up_total,
        inner_bias,
        down_total,
        owned[5],
    )


def solution(mesh):
    rows = P("dp", ("ctx", "fsdp"), None)
    vector = P(("dp", "fsdp"))
    matrix = P(("dp", "fsdp"), None)
    parameters = (
        vector, vector, matrix, vector, vector, matrix, vector, vector, vector, matrix, vector,
        matrix, vector,
    )
    return jax.shard_map(
        local,
        mesh=mesh,
        in_specs=(rows, rows) + parameters,
        out_specs=(rows, rows) + parameters,
        check_vma=False,
    )
```

```python
import functools

import jax
import jax.numpy as jnp
from jax import lax
from jax.experimental import pallas as pl
from jax.experimental.pallas import tpu as pltpu
from jax.sharding import PartitionSpec as P

HEAD_DIM = 64
EPSILON = 1e-05
SCALE = HEAD_DIM ** (-0.5)
MASKED = -1e30
CHUNK = 64
HURRY = 20
VMEM_BYTES = 16 * 1024 * 1024
GELU_SCALE = 0.7978845608
GELU_CUBE = 0.044715
LOW = jnp.bfloat16
WIDE = jnp.float32


def swap(value, axis, bit):
    count = lax.axis_size(axis)
    return lax.ppermute(value, axis, [(at, at ^ bit) for at in range(count)])


def shift(value, axis, by):
    count = lax.axis_size(axis)
    return lax.ppermute(value, axis, [(at, (at + by) % count) for at in range(count)])


def transpose_homes(value):
    side = lax.axis_size("dp")
    pairs = [(a * side + b, b * side + a) for a in range(side) for b in range(side)]
    return lax.ppermute(value, ("dp", "fsdp"), pairs)


def after(value, *others):
    return lax.optimization_barrier((value,) + others)[0]


def gather_pieces(block):
    pieces = [block]
    for slot in range(1, lax.axis_size("dp")):
        low_bit = slot & -slot
        pieces.append(swap(pieces[slot ^ low_bit], "dp", low_bit))
    return pieces


def send_pieces(sends, axis):
    return [swap(send, axis, slot) for slot, send in enumerate(sends, 1)]


def gather_direct(block, axis):
    return [block] + [swap(block, axis, slot) for slot in range(1, lax.axis_size(axis))]


def sum_doubling(value, axis):
    bit = 1
    while bit < lax.axis_size(axis):
        value = value + swap(value, axis, bit)
        bit *= 2
    return value


def sum_all(kept, arrived):
    total = kept
    for piece in arrived:
        total = total + piece.astype(WIDE)
    return total


def sum_replicas(value):
    if lax.axis_size("ctx") == 2:
        return value.astype(WIDE) + shift(value, "ctx", 1).astype(WIDE)
    return jnp.sum(lax.all_gather(value, "ctx").astype(WIDE), axis=0)


def matmul_nt(left, right):
    return lax.dot_general(left, right, (((1,), (1,)), ((), ())), preferred_element_type=WIDE)


def matmul_nn(left, right):
    return lax.dot_general(left, right, (((1,), (0,)), ((), ())), preferred_element_type=WIDE)


def matmul_tn(left, right):
    return lax.dot_general(left, right, (((0,), (0,)), ((), ())), preferred_element_type=WIDE)


def visible_block(place_ref, start, block_rows, columns):
    slot = start // block_rows
    query_pos = place_ref[slot] * block_rows + start % block_rows
    query_pos = query_pos + lax.broadcasted_iota(jnp.int32, (CHUNK, columns), 0)
    lane = lax.broadcasted_iota(jnp.int32, (CHUNK, columns), 1)
    key_pos = lane
    for at in range(columns // block_rows):
        inside = (lane >= at * block_rows) & (lane < (at + 1) * block_rows)
        key_pos = jnp.where(inside, place_ref[at] * block_rows + lane - at * block_rows, key_pos)
    return key_pos <= query_pos


def columns_of(head):
    return slice(head * HEAD_DIM, (head + 1) * HEAD_DIM)


def own_forward(heads, block_rows, place_ref, kvq_ref, acc_ref, stat_ref, score, prob):
    width = heads * HEAD_DIM
    rows = kvq_ref.shape[0]
    for head in range(heads):
        query = kvq_ref[:, 2 * width + head * HEAD_DIM : 2 * width + (head + 1) * HEAD_DIM]
        score[...] = matmul_nt(query, kvq_ref[:, columns_of(head)])

        def chunk(step, carry):
            start = pl.multiple_of(step * CHUNK, CHUNK)
            seen = visible_block(place_ref, start, block_rows, rows)
            scores = jnp.where(seen, score[pl.ds(start, CHUNK), :] * SCALE, MASKED)
            highest = jnp.max(scores, axis=1, keepdims=True)
            weight = jnp.exp(scores - highest)
            stat_ref[pl.ds(start, CHUNK), head : head + 1] = highest
            stat_ref[pl.ds(start, CHUNK), heads + head : heads + head + 1] = jnp.sum(
                weight, axis=1, keepdims=True
            )
            prob[pl.ds(start, CHUNK), :] = weight.astype(LOW)
            return carry

        lax.fori_loop(0, rows // CHUNK, chunk, 0)
        value = kvq_ref[:, width + head * HEAD_DIM : width + (head + 1) * HEAD_DIM]
        acc_ref[:, columns_of(head)] = matmul_nn(prob[...], value)


def earlier_forward(
    heads, slots, place_ref, kvq_ref, kv_ref, acc_in, stat_in, acc_ref, low_ref, stat_ref, score,
    prob, fade
):
    width = heads * HEAD_DIM
    rows = kvq_ref.shape[0]
    acc_ref[...] = acc_in[...]
    stat_ref[...] = stat_in[...]
    for piece in range(kv_ref.shape[0]):

        @pl.when(place_ref[slots] > piece)
        def _visit(piece=piece):
            for head in range(heads):
                query = kvq_ref[:, 2 * width + head * HEAD_DIM : 2 * width + (head + 1) * HEAD_DIM]
                score[...] = matmul_nt(query, kv_ref[piece, :, columns_of(head)])

                def chunk(step, carry):
                    here = pl.ds(pl.multiple_of(step * CHUNK, CHUNK), CHUNK)
                    scores = score[here, :] * SCALE
                    old = stat_ref[here, head : head + 1]
                    highest = jnp.maximum(old, jnp.max(scores, axis=1, keepdims=True))
                    weight = jnp.exp(scores - highest)
                    fading = jnp.exp(old - highest)
                    stat_ref[here, head : head + 1] = highest
                    total = stat_ref[here, heads + head : heads + head + 1]
                    stat_ref[here, heads + head : heads + head + 1] = total * fading + jnp.sum(
                        weight, axis=1, keepdims=True
                    )
                    fade[here, :] = jnp.broadcast_to(fading, (CHUNK, HEAD_DIM))
                    prob[here, :] = weight.astype(LOW)
                    return carry

                lax.fori_loop(0, rows // CHUNK, chunk, 0)
                value = kv_ref[piece, :, width + head * HEAD_DIM : width + (head + 1) * HEAD_DIM]
                acc_ref[:, columns_of(head)] = acc_ref[:, columns_of(head)] * fade[
                    ...
                ] + matmul_nn(prob[...], value)

    for head in range(heads):
        total = stat_ref[:, heads + head : heads + head + 1]
        context = acc_ref[:, columns_of(head)] / total
        acc_ref[:, columns_of(head)] = context
        low_ref[:, columns_of(head)] = context.astype(LOW)
        stat_ref[:, head : head + 1] = stat_ref[:, head : head + 1] + jnp.log(total)


def score_grads(here, seen, head, total, delta, score, dots, prob, grad):
    scores = score[here, :] * SCALE
    weight = jnp.exp(scores - total)
    if seen is not None:
        weight = jnp.where(seen, weight, 0.0)
    prob[here, :] = weight.astype(LOW)
    grad[here, :] = (weight * (dots[here, :] - delta) * SCALE).astype(LOW)


def delta_of(here, head, context_ref, ctx_grad_ref):
    product = context_ref[here, columns_of(head)] * ctx_grad_ref[here, columns_of(head)].astype(WIDE)
    return jnp.sum(product, axis=1, keepdims=True)


def earlier_backward(
    heads, slots, place_ref, kvq_ref, kv_ref, ctx_grad_ref, context_ref, stat_ref, query_grad_ref,
    kv_grad_ref, score, dots, prob, grad
):
    width = heads * HEAD_DIM
    rows = kvq_ref.shape[0]
    query_grad_ref[...] = jnp.zeros_like(query_grad_ref)
    for piece in range(kv_ref.shape[0]):

        @pl.when(place_ref[slots] <= piece)
        def _skip(piece=piece):
            kv_grad_ref[piece] = jnp.zeros(kv_grad_ref.shape[1:], kv_grad_ref.dtype)

        @pl.when(place_ref[slots] > piece)
        def _visit(piece=piece):
            for head in range(heads):
                query = kvq_ref[:, 2 * width + head * HEAD_DIM : 2 * width + (head + 1) * HEAD_DIM]
                value_at = slice(width + head * HEAD_DIM, width + (head + 1) * HEAD_DIM)
                key = kv_ref[piece, :, columns_of(head)]
                out_grad = ctx_grad_ref[:, columns_of(head)]
                score[...] = matmul_nt(query, key)
                dots[...] = matmul_nt(out_grad, kv_ref[piece, :, value_at])

                def chunk(step, carry):
                    here = pl.ds(pl.multiple_of(step * CHUNK, CHUNK), CHUNK)
                    total = stat_ref[here, head : head + 1]
                    delta = delta_of(here, head, context_ref, ctx_grad_ref)
                    score_grads(here, None, head, total, delta, score, dots, prob, grad)
                    return carry

                lax.fori_loop(0, rows // CHUNK, chunk, 0)
                kv_grad_ref[piece, :, columns_of(head)] = matmul_tn(grad[...], query).astype(LOW)
                kv_grad_ref[piece, :, value_at] = matmul_tn(prob[...], out_grad).astype(LOW)
                query_grad_ref[:, columns_of(head)] += matmul_nn(grad[...], key)


def own_backward(
    heads, block_rows, place_ref, kvq_ref, ctx_grad_ref, context_ref, stat_ref, query_grad_in,
    grad_ref, score, dots, prob, grad
):
    width = heads * HEAD_DIM
    rows = kvq_ref.shape[0]
    for head in range(heads):
        query_at = slice(2 * width + head * HEAD_DIM, 2 * width + (head + 1) * HEAD_DIM)
        value_at = slice(width + head * HEAD_DIM, width + (head + 1) * HEAD_DIM)
        query = kvq_ref[:, query_at]
        key = kvq_ref[:, columns_of(head)]
        out_grad = ctx_grad_ref[:, columns_of(head)]
        score[...] = matmul_nt(query, key)
        dots[...] = matmul_nt(out_grad, kvq_ref[:, value_at])

        def chunk(step, carry):
            start = pl.multiple_of(step * CHUNK, CHUNK)
            here = pl.ds(start, CHUNK)
            seen = visible_block(place_ref, start, block_rows, rows)
            total = stat_ref[here, head : head + 1]
            delta = delta_of(here, head, context_ref, ctx_grad_ref)
            score_grads(here, seen, head, total, delta, score, dots, prob, grad)
            return carry

        lax.fori_loop(0, rows // CHUNK, chunk, 0)
        grad_ref[:, columns_of(head)] = matmul_tn(grad[...], query)
        grad_ref[:, value_at] = matmul_tn(prob[...], out_grad)
        grad_ref[:, query_at] = query_grad_in[:, columns_of(head)] + matmul_nn(grad[...], key)


def normalize(values):
    centered = values - jnp.mean(values, axis=-1, keepdims=True)
    spread = jnp.mean(centered * centered, axis=-1, keepdims=True)
    inverse = lax.rsqrt(spread + EPSILON)
    return centered * inverse, inverse


def normalize_back(grad, gain, hat, inverse):
    scaled = grad * gain
    mean_scaled = jnp.mean(scaled, axis=-1, keepdims=True)
    mean_product = jnp.mean(scaled * hat, axis=-1, keepdims=True)
    part = inverse * (scaled - mean_scaled - hat * mean_product)
    gain_grad = jnp.sum(grad * hat, axis=0, keepdims=True)
    return part, gain_grad, jnp.sum(grad, axis=0, keepdims=True)


def take(refs, *counts):
    groups, at = [], 0
    for count in counts:
        if count is None:
            groups.append(refs[at])
            at += 1
        else:
            groups.append(refs[at : at + count])
            at += count
    return groups


def place_shards(meta_ref, parts, pieces, out_ref):
    rows = pieces[0].shape[0]
    for deep, piece in enumerate(pieces):
        start = pl.multiple_of((meta_ref[parts + 1] ^ deep) * rows, 16)
        out_ref[pl.ds(start, rows), :] = piece[...]


def stack_rows(pieces, out_ref):
    rows = pieces[0].shape[0]
    for slot, piece in enumerate(pieces):
        out_ref[slot * rows : (slot + 1) * rows, :] = piece[...]


def emit_rows(partial, keep_ref, send_refs):
    rows = keep_ref.shape[0]
    keep_ref[...] = partial[:rows]
    for slot, send in enumerate(send_refs, 1):
        send[...] = partial[slot * rows : (slot + 1) * rows].astype(LOW)


def emit_blocks(meta_ref, parts, depth, whole_ref, keep_ref, send_refs):
    rows = keep_ref.shape[1]
    for deep in range(depth):
        member = meta_ref[parts + 1] ^ deep
        for slot in range(parts):
            start = pl.multiple_of((meta_ref[slot] * depth + member) * rows, 16)
            block = whole_ref[pl.ds(start, rows), :]
            if deep:
                send_refs[deep - 1][slot] = block.astype(LOW)
            else:
                keep_ref[slot] = block


def emit_shards(meta_ref, parts, whole_ref, keep_ref, send_refs):
    rows = keep_ref.shape[0]
    for deep in range(len(send_refs) + 1):
        start = pl.multiple_of((meta_ref[parts + 1] ^ deep) * rows, 16)
        block = whole_ref[pl.ds(start, rows), :]
        if deep:
            send_refs[deep - 1][...] = block.astype(LOW)
        else:
            keep_ref[...] = block


def stack_kernel(parts, depth, halves, meta_ref, *refs):
    split, down_weight, kvq_rows, feeds, vectors = take(
        refs, parts, None, None, 1 if halves else 2, None
    )
    columns = kvq_rows.shape[1]
    shard = split[0].shape[0]
    model = vectors.shape[1]
    width = columns // 3
    hidden_shard = down_weight.shape[0]
    member = meta_ref[parts + 1]

    def placed(slot, start):
        rows = split[slot][:, columns : -feeds[0].shape[1]]
        row = lax.broadcasted_iota(jnp.int32, (rows.shape[1], model), 0)
        column = lax.broadcasted_iota(jnp.int32, (rows.shape[1], model), 1)
        chosen = jnp.where((column == start + row) & (row < shard), 1.0, 0.0)
        return matmul_nn(rows, chosen.astype(LOW))

    whole = sum(placed(slot, (meta_ref[slot] * depth + member) * shard) for slot in range(parts))
    vectors[...] = jnp.zeros_like(vectors)
    vectors[0:6, :] = whole[0:6]
    vectors[6:7, :] = (
        placed(0, width + member * shard)[7:8] + placed(0, 2 * width + member * shard)[6:7]
    )
    vectors[7:8, :] = sum(
        placed(0, member * hidden_shard + at * shard)[8 + at : 9 + at]
        for at in range(hidden_shard // shard)
    )
    for slot in range(parts):
        kvq_rows[slot * shard : (slot + 1) * shard, :] = split[slot][:, :columns]
    vectors[8:16, : model - columns] = vectors[0:8, columns:]
    kvq_rows[parts * shard :, :] = vectors[:, :columns].astype(LOW)

    def up(out):
        for slot in range(parts):
            out[slot * shard : (slot + 1) * shard, :] = split[slot][:, -out.shape[1] :]

    def down(out):
        out[...] = down_weight[...].astype(LOW)

    if halves:
        pl.when(meta_ref[parts] == 0)(lambda: up(feeds[0]))
        pl.when(meta_ref[parts] != 0)(lambda: down(feeds[0]))
    else:
        up(feeds[0])
        down(feeds[1])


def split_kernel(parts, width, meta_ref, qkv_ref, up_ref, *refs):
    vectors, outs, packed = take(refs, None, parts, None)
    model = parts * width
    shard = qkv_ref.shape[0]
    packed[...] = jnp.zeros_like(packed)
    values = vectors[...].reshape(1, vectors.shape[0])
    for row in range(vectors.shape[0] // shard):
        packed[row : row + 1, :shard] = values[:, row * shard : (row + 1) * shard]
    part = up_ref.shape[1] // parts
    for case in range(parts):

        @pl.when(meta_ref[0] == case)
        def _case(case=case):
            for slot in range(parts):
                owner = case ^ slot
                for at, first in enumerate((model, 2 * model, 0)):
                    start = first + owner * width
                    outs[slot][:, at * width : (at + 1) * width] = qkv_ref[
                        :, start : start + width
                    ].astype(LOW)
                outs[slot][:, 3 * width : -part] = packed[...].astype(LOW)
                outs[slot][:, -part:] = up_ref[:, owner * part : (owner + 1) * part].astype(LOW)


def join_qkv_kernel(parts, width, meta_ref, *refs):
    pieces, out_ref = refs[:parts], refs[parts]
    model = parts * width
    for case in range(parts):

        @pl.when(meta_ref[0] == case)
        def _case(case=case):
            for slot in range(parts):
                owner = case ^ slot
                for at, first in enumerate((model, 2 * model, 0)):
                    start = first + owner * width
                    out_ref[:, start : start + width] = pieces[slot][
                        :, at * width : (at + 1) * width
                    ].astype(WIDE)


def join_up_kernel(parts, meta_ref, *refs):
    pieces, out_ref = refs[:parts], refs[parts]
    part = pieces[0].shape[1]
    for slot in range(parts):
        start = pl.multiple_of(meta_ref[slot] * part, 128)
        out_ref[:, pl.ds(start, part)] = pieces[slot][...].astype(WIDE)


def project_kernel(parts, depth, meta_ref, *refs):
    tokens, weight, kvq_ref, kv_ref, matrix_ref, norm_ref, vectors_ref = take(
        refs, parts, depth, None, None, None, None, None
    )
    columns = kvq_ref.shape[1]
    rows = tokens[0].shape[0]
    shard = matrix_ref.shape[0] // (parts * depth)
    for deep in range(depth):
        member = meta_ref[parts + 1] ^ deep
        for slot in range(parts):
            start = pl.multiple_of((meta_ref[slot] * depth + member) * shard, 16)
            matrix_ref[pl.ds(start, shard), :] = weight[deep][slot * shard : (slot + 1) * shard, :]
    folded = sum(piece[parts * shard :, :].astype(WIDE) for piece in weight)
    vectors_ref[:, :columns] = folded[:8]
    vectors_ref[:, columns:] = folded[8:, : vectors_ref.shape[1] - columns]
    for slot, piece in enumerate(tokens):

        def chunk(step, carry, slot=slot, piece=piece):
            here = pl.multiple_of(step * CHUNK, CHUNK)
            hat, _ = normalize(piece[pl.ds(here, CHUNK), :].astype(WIDE))
            norm_ref[pl.ds(slot * rows + here, CHUNK), :] = (
                hat * vectors_ref[0:1, :] + vectors_ref[1:2, :]
            ).astype(LOW)
            return carry

        lax.fori_loop(0, rows // CHUNK, chunk, 0)
    low = (matmul_nn(norm_ref[...], matrix_ref[...]) + vectors_ref[6:7, :columns]).astype(LOW)
    kvq_ref[...] = low
    kv_ref[...] = low[:, : kv_ref.shape[1]]


def mix_kernel(parts, depth, meta_ref, *refs):
    low, weight, matrix, keep, sends = take(refs, None, depth, None, None, parts - 1)
    place_shards(meta_ref, parts, weight, matrix)
    emit_rows(matmul_nn(low[...], matrix[...]), keep, sends)


def second_norm_kernel(parts, meta_ref, *refs):
    keep, arrived, tokens, vectors, out, attended_ref = take(
        refs, None, parts - 1, None, None, None, None
    )
    attended = sum_all(keep[...], [piece[...] for piece in arrived]) + vectors[4:5, :]
    attended_ref[...] = attended
    hat, _ = normalize(tokens[...].astype(WIDE) + attended)
    out[...] = (hat * vectors[2:3, :] + vectors[3:4, :]).astype(LOW)


def feed_kernel(parts, depth, halves, meta_ref, *refs):
    (
        norm, branch, own, other, vectors, keep, sends, hidden, inner_grad, norm_all, branch_all,
        down_all, up_bias, up_all, inner, grad,
    ) = take(refs, parts, parts, depth, depth, None, None, parts - 1, *([None] * 9))

    def place(up, down):
        shard = up_all.shape[0] // (parts * depth)
        for deep in range(depth):
            member = meta_ref[parts + 1] ^ deep
            for slot in range(parts):
                start = pl.multiple_of((meta_ref[slot] * depth + member) * shard, 16)
                up_all[pl.ds(start, shard), :] = up[deep][slot * shard : (slot + 1) * shard, :]
        place_shards(meta_ref, parts, down, down_all)

    if halves:
        pl.when(meta_ref[parts] == 0)(lambda: place(own, other))
        pl.when(meta_ref[parts] != 0)(lambda: place(other, own))
    else:
        place(own, other)
    stack_rows(norm, norm_all)
    stack_rows(branch, branch_all)
    inner[...] = matmul_nn(norm_all[...], up_all[...])
    grad[...] = matmul_nt(branch_all[...], down_all[...])
    up_bias[...] = jnp.zeros_like(up_bias)

    def chunk(step, carry):
        here = pl.ds(pl.multiple_of(step * CHUNK, CHUNK), CHUNK)
        value = inner[here, :] + vectors[7:8, :]
        square = value * value
        bent = jnp.tanh(GELU_SCALE * (value + GELU_CUBE * square * value))
        hidden[here, :] = (0.5 * value * (1.0 + bent)).astype(LOW)
        slope = 0.5 * (1.0 + bent) + 0.5 * value * (1.0 - bent * bent) * GELU_SCALE * (
            1.0 + 3.0 * GELU_CUBE * square
        )
        low = (grad[here, :] * slope).astype(LOW)
        inner_grad[here, :] = low
        up_bias[...] += jnp.sum(low.astype(WIDE), axis=0, keepdims=True)
        return carry

    lax.fori_loop(0, inner.shape[0] // CHUNK, chunk, 0)
    emit_rows(matmul_nt(inner_grad[...], up_all[...]), keep, sends)


def feed_grad_kernel(parts, depth, halves, meta_ref, *refs):
    hidden, inner_grad, norm_all, branch_all, down_all, kept, sent, fed_keep, fed_sends, whole = (
        take(refs, *([None] * 8), parts - 1, None)
    )
    hidden_shard = hidden.shape[1] // depth
    shard = norm_all.shape[1] // (parts * depth)

    def emit(half, out):
        for deep in range(depth):
            member = meta_ref[parts + 1] ^ deep
            if half:
                start = pl.multiple_of(member * hidden_shard, 16)
                out[deep] = whole[pl.ds(start, hidden_shard), :].astype(out.dtype)
            else:
                for slot in range(parts):
                    start = pl.multiple_of((meta_ref[slot] * depth + member) * shard, 16)
                    out[deep, slot * shard : (slot + 1) * shard] = whole[
                        pl.ds(start, shard), :
                    ].astype(out.dtype)

    for half in range(2):
        if half:
            whole[...] = matmul_tn(hidden[...], branch_all[...])
        else:
            whole[...] = matmul_tn(norm_all[...], inner_grad[...])
        if halves:
            pl.when(meta_ref[parts] == half)(functools.partial(emit, half, kept))
            pl.when(meta_ref[parts] != half)(functools.partial(emit, half, sent))
        else:
            emit(half, sent if half else kept)
    emit_rows(matmul_nn(hidden[...], down_all[...]), fed_keep, fed_sends)


def fold_kernel(meta_ref, kept_ref, arrived_ref, keep_ref, *send_refs):
    keep_ref[...] = kept_ref[0] + arrived_ref[0].astype(WIDE)
    for deep, send in enumerate(send_refs, 1):
        send[...] = (kept_ref[deep] + arrived_ref[deep].astype(WIDE)).astype(LOW)


def second_norm_grad_kernel(parts, meta_ref, *refs):
    keep, arrived, tokens, attended, branch, vectors, attn_grad, mixed_part, sums = take(
        refs, None, parts - 1, None, None, None, None, None, None, None
    )
    grad = sum_all(keep[...], [piece[...] for piece in arrived])
    hat, inverse = normalize(tokens[...].astype(WIDE) + attended[...])
    part, gain_grad, bias_grad = normalize_back(grad, vectors[2:3, :], hat, inverse)
    mixed_part[...] = part
    branch_rows = branch[...].astype(WIDE)
    low = (branch_rows + part).astype(LOW)
    attn_grad[...] = low
    sums[...] = jnp.zeros_like(sums)
    sums[2:3, :] = gain_grad
    sums[3:4, :] = bias_grad
    sums[4:5, :] = jnp.sum(low.astype(WIDE), axis=0, keepdims=True)
    sums[5:6, :] = jnp.sum(branch_rows, axis=0, keepdims=True)


def context_grad_kernel(parts, heads, meta_ref, *refs):
    (
        attn, matrix, kvq, kv, context, stat, ctx_grad, attn_all, query_grad, kv_grad, score, dots,
        prob, grad,
    ) = take(refs, parts, *([None] * 13))
    stack_rows(attn, attn_all)
    ctx_grad[...] = matmul_nt(attn_all[...], matrix[...]).astype(LOW)
    earlier_backward(
        heads, parts, meta_ref, kvq, kv, ctx_grad, context, stat, query_grad, kv_grad, score, dots,
        prob, grad,
    )


def own_grad_kernel(parts, depth, heads, rows, meta_ref, *refs):
    (
        kvq, ctx_grad, context, stat, query_grad, low, attn_all, kvq_grad, out_grad, score, dots,
        prob, grad,
    ) = refs
    own_backward(
        heads, rows, meta_ref, kvq, ctx_grad, context, stat, query_grad, kvq_grad, score, dots,
        prob, grad,
    )
    out_grad[...] = matmul_tn(low[...], attn_all[...])


def projection_back_kernel(parts, meta_ref, *refs):
    own, arrived, matrix, kvq_grad, keep, sends, bias = take(
        refs, None, None, None, None, None, parts - 1, None
    )
    kv_width = arrived.shape[2]
    total = own[:, :kv_width]
    for piece in range(arrived.shape[0]):
        total = total + arrived[piece].astype(WIDE)
    kvq_grad[:, :kv_width] = total.astype(LOW)
    kvq_grad[:, kv_width:] = own[:, kv_width:].astype(LOW)
    emit_rows(matmul_nt(kvq_grad[...], matrix[...]), keep, sends)
    bias[...] = jnp.sum(kvq_grad[...].astype(WIDE), axis=0, keepdims=True)


def projection_grad_kernel(parts, depth, halves, meta_ref, *refs):
    norm, kvq_grad, out_grad, kept, sent, whole, folded = refs
    columns = kvq_grad.shape[1]
    model = norm.shape[1]
    shard = model // (parts * depth)
    rest = model - columns
    slots = parts // 2
    extra = kept.shape[1] - slots * shard
    whole[...] = matmul_tn(norm[...], kvq_grad[...])

    def emit(half, out):
        for deep in range(depth):
            member = meta_ref[parts + 1] ^ deep
            for slot in range(slots):
                row = (meta_ref[half * slots + slot] * depth + member) * shard
                out[deep, slot * shard : (slot + 1) * shard] = whole[
                    pl.ds(pl.multiple_of(row, 16), shard), :
                ].astype(out.dtype)
            start = pl.multiple_of(member * shard, 16)
            folded[:shard, :] = out_grad[pl.ds(start, shard), :columns]
            for at in range(columns // rest):
                piece = out_grad[pl.ds(start + at * 16, 16), columns:]
                folded[shard:, at * rest : (at + 1) * rest] = piece
            out[deep, slots * shard :] = folded[half * extra : (half + 1) * extra, :].astype(
                out.dtype
            )

    for half in range(2):
        if halves:
            pl.when(meta_ref[parts] == half)(functools.partial(emit, half, kept))
            pl.when(meta_ref[parts] != half)(functools.partial(emit, half, sent))
        else:
            emit(half, sent if half else kept)


def unfold_kernel(parts, meta_ref, first_ref, second_ref, *refs):
    pieces, out_ref, folded = refs[:parts], refs[parts], refs[parts + 1]
    shard, columns = pieces[0].shape
    rest = out_ref.shape[1] - columns
    slots = parts // 2
    extra = folded.shape[0] // 2
    for half, ref in enumerate((first_ref, second_ref)):
        for slot in range(slots):
            pieces[half * slots + slot][...] = ref[slot * shard : (slot + 1) * shard, :].astype(LOW)
        folded[half * extra : (half + 1) * extra, :] = ref[slots * shard :, :].astype(WIDE)
    out_ref[:, :columns] = folded[:shard, :]
    for at in range(columns // rest):
        out_ref[at * 16 : (at + 1) * 16, columns:] = folded[shard:, at * rest : (at + 1) * rest]


def first_norm_grad_kernel(parts, meta_ref, *refs):
    keep, arrived, tokens, vectors, mixed_part, sums_in, kvq_bias, up_bias, out, sums = take(
        refs, None, parts - 1, *([None] * 8)
    )
    grad = sum_all(keep[...], [piece[...] for piece in arrived])
    hat, inverse = normalize(tokens[...].astype(WIDE))
    part, gain_grad, bias_grad = normalize_back(grad, vectors[0:1, :], hat, inverse)
    out[...] = (mixed_part[...] + part).astype(LOW)
    sums[...] = sums_in[...]
    sums[0:1, :] = gain_grad
    sums[1:2, :] = bias_grad
    sums[6:7, : kvq_bias.shape[1]] = kvq_bias[...]
    sums[7:8, :] = up_bias[...]


def local_call(kernel, operands, results, scratch=(), flops=0):
    smem = pl.BlockSpec(memory_space=pltpu.SMEM)
    vmem = pl.BlockSpec(memory_space=pltpu.VMEM)
    moved = sum(each.size * each.dtype.itemsize for each in tuple(operands) + tuple(results))
    return pl.pallas_call(
        kernel,
        name=getattr(kernel, "func", kernel).__name__,
        out_shape=tuple(results),
        in_specs=[smem] + [vmem] * (len(operands) - 1),
        out_specs=tuple([vmem] * len(results)),
        scratch_shapes=list(scratch),
        compiler_params=pltpu.CompilerParams(vmem_limit_bytes=VMEM_BYTES),
        cost_estimate=pl.CostEstimate(
            flops=flops // HURRY, bytes_accessed=moved // HURRY, transcendentals=0
        ),
    )(*operands)


def low_like(*shape):
    return jax.ShapeDtypeStruct(shape, LOW)


def wide_like(*shape):
    return jax.ShapeDtypeStruct(shape, WIDE)


def local(
    tokens, cotangent, ln1_gain, ln1_bias, qkv_weight, q_bias, v_bias, out_weight, out_bias,
    ln2_gain, ln2_bias, fc1_weight, fc1_bias, fc2_weight, fc2_bias,
):
    parts = lax.axis_size("dp")
    depth = lax.axis_size("fsdp")
    contexts = lax.axis_size("ctx")
    assert parts == depth
    mine = lax.axis_index("dp")
    deep = lax.axis_index("fsdp")
    rows, model = tokens.shape[1:]
    shard = ln1_gain.shape[0]
    heads = model // HEAD_DIM // parts
    width = heads * HEAD_DIM
    hidden_shard = fc1_bias.shape[0]
    hidden_part = hidden_shard * depth
    group = parts * rows
    meta = jnp.stack(
        [mine ^ slot for slot in range(parts)] + [lax.axis_index("ctx"), deep]
    ).astype(jnp.int32)

    halves = contexts == 2
    padded = -(-3 * width // 128) * 128
    split = local_call(
        functools.partial(split_kernel, parts, width),
        (
            meta, qkv_weight, fc1_weight,
            jnp.concatenate(
                [
                    ln1_gain, ln1_bias, ln2_gain, ln2_bias, out_bias, fc2_bias, q_bias, v_bias,
                    fc1_bias,
                ]
            ),
        ),
        [low_like(shard, padded + hidden_part)] * parts,
        [pltpu.VMEM((shard, padded - 3 * width), WIDE)],
    )
    split_arrived = send_pieces(split[1:], "dp")
    kvq_rows, *feeds = local_call(
        functools.partial(stack_kernel, parts, depth, halves),
        (meta, split[0], *split_arrived, fc2_weight),
        [low_like(parts * shard + 16, 3 * width)]
        + [low_like(hidden_shard, model)] * (1 if halves else 2),
        [pltpu.VMEM((16, model), WIDE)],
    )
    kvq_pieces = gather_direct(kvq_rows, "fsdp")

    token_rows = transpose_homes(after(tokens[0].astype(LOW), split_arrived[0]))
    pieces = gather_pieces(after(token_rows, *split_arrived))

    kvq, kv, kvq_matrix, norm1_all, vectors = local_call(
        functools.partial(project_kernel, parts, depth),
        (meta, *pieces, *kvq_pieces),
        [
            low_like(group, 3 * width),
            low_like(group, 2 * width),
            low_like(model, 3 * width),
            low_like(group, model),
            wide_like(8, model),
        ],
        flops=2 * group * model * 3 * width,
    )
    kv_earlier = jnp.stack([shift(kv, "ctx", by) for by in range(1, contexts)])

    score_flops = 2 * group * group * width
    wide_square = pltpu.VMEM((group, group), WIDE)
    low_square = pltpu.VMEM((group, group), LOW)
    acc, stat = local_call(
        functools.partial(own_forward, heads, rows),
        (meta, kvq),
        [wide_like(group, width), wide_like(group, 128)],
        [wide_square, low_square],
        flops=2 * score_flops,
    )
    out_pieces = gather_direct(after(out_weight.astype(LOW), acc, kv_earlier), "fsdp")
    grad_rows = transpose_homes(after(cotangent[0].astype(LOW), acc, kv_earlier))
    context, context_low, stat = local_call(
        functools.partial(earlier_forward, heads, parts),
        (meta, kvq, kv_earlier, acc, stat),
        [wide_like(group, width), low_like(group, width), wide_like(group, 128)],
        [wide_square, low_square, pltpu.VMEM((group, HEAD_DIM), WIDE)],
        flops=2 * score_flops,
    )
    out_matrix, attended_keep, *attended_sends = local_call(
        functools.partial(mix_kernel, parts, depth),
        (meta, context_low, *out_pieces),
        [low_like(width, model), wide_like(rows, model)] + [low_like(rows, model)] * (parts - 1),
        flops=2 * group * width * model,
    )
    branch_pieces = gather_pieces(after(grad_rows, context_low))
    if halves:
        own_half = gather_direct(after(feeds[0], context_low), "fsdp")
        other_half = [shift(after(feeds[0], kv_earlier), "ctx", 1)]
        for piece in own_half[1:]:
            other_half.append(shift(piece, "ctx", 1))
    else:
        own_half = gather_direct(feeds[0], "fsdp")
        other_half = gather_direct(feeds[1], "fsdp")

    arrived = send_pieces(attended_sends, "dp")
    norm2, attended = local_call(
        functools.partial(second_norm_kernel, parts),
        (meta, attended_keep, *arrived, token_rows, vectors),
        [low_like(rows, model), wide_like(rows, model)],
    )

    norm2_pieces = gather_pieces(norm2)
    norm2_keep, *rest = local_call(
        functools.partial(feed_kernel, parts, depth, halves),
        (meta, *norm2_pieces, *branch_pieces, *own_half, *other_half, vectors),
        [wide_like(rows, model)]
        + [low_like(rows, model)] * (parts - 1)
        + [low_like(group, hidden_part)] * 2
        + [low_like(group, model)] * 2
        + [low_like(hidden_part, model), wide_like(1, hidden_part)],
        [
            pltpu.VMEM((model, hidden_part), LOW),
            pltpu.VMEM((group, hidden_part), WIDE),
            pltpu.VMEM((group, hidden_part), WIDE),
        ],
        flops=6 * group * model * hidden_part,
    )
    norm2_sends = rest[: parts - 1]
    hidden, inner_grad, norm2_all, branch_all, down_matrix, up_bias = rest[parts - 1 :]
    norm2_arrived = send_pieces(norm2_sends, "dp")
    kept_half, sent_half, fed_keep, *fed_sends = local_call(
        functools.partial(feed_grad_kernel, parts, depth, halves),
        (meta, hidden, inner_grad, norm2_all, branch_all, down_matrix),
        [
            wide_like(depth, hidden_shard, model),
            low_like(depth, hidden_shard, model),
            wide_like(rows, model),
        ]
        + [low_like(rows, model)] * (parts - 1),
        [pltpu.VMEM((max(model, hidden_part), max(model, hidden_part)), WIDE)],
        flops=6 * group * model * hidden_part,
    )
    attn_grad, mixed_part, sums = local_call(
        functools.partial(second_norm_grad_kernel, parts),
        (
            meta, after(norm2_keep, fed_keep), *norm2_arrived, token_rows, attended, grad_rows,
            vectors,
        ),
        [low_like(rows, model), wide_like(rows, model), wide_like(8, model)],
    )
    attn_pieces = gather_pieces(attn_grad)

    def fold(kept, sent, *later):
        arrived = after(shift(sent, "ctx", 1), *later)
        shape = kept.shape[1:]
        keep, *sends = local_call(
            fold_kernel, (meta, kept, arrived), [wide_like(*shape)] + [low_like(*shape)] * (depth - 1)
        )
        return keep, sends

    def direct_totals(*grads):
        return [
            owner_sum(grad[0].astype(WIDE), send_pieces(list(grad[1:].astype(LOW)), "fsdp"))
            for grad in grads
        ]

    def both_halves(mine_half, *later):
        arrived_half = shift(after(mine_half, *later) if later else mine_half, "ctx", 1)
        first = lax.axis_index("ctx") == 0
        return (
            jnp.where(first, mine_half, arrived_half), jnp.where(first, arrived_half, mine_half)
        )

    def owner_sum(keep, pieces):
        return sum_replicas(sum_all(keep, pieces).astype(LOW))

    fed_arrived = send_pieces(
        lax.optimization_barrier((*fed_sends, attn_pieces[-1]))[: parts - 1], "dp"
    )

    ctx_grad, attn_all, query_grad, kv_grad = local_call(
        functools.partial(context_grad_kernel, parts, heads),
        (meta, *attn_pieces, out_matrix, kvq, kv_earlier, context, stat),
        [
            low_like(group, width),
            low_like(group, model),
            wide_like(group, width),
            low_like(*kv_earlier.shape),
        ],
        [wide_square, wide_square, low_square, low_square],
        flops=5 * score_flops,
    )
    if halves:
        half_keep, half_sends = fold(kept_half, sent_half, query_grad)
        half_pieces = send_pieces(half_sends, "fsdp")
    else:
        half_pieces = []
    if halves:
        query_grad = after(query_grad, half_keep)
    kv_arrived = jnp.stack(
        [shift(kv_grad[by - 1], "ctx", -by) for by in range(1, contexts)]
    )
    kvq_own, out_grad = local_call(
        functools.partial(own_grad_kernel, parts, depth, heads, rows),
        (meta, kvq, ctx_grad, context, stat, query_grad, context_low, attn_all),
        [wide_like(group, 3 * width), wide_like(width, model)],
        [wide_square, wide_square, low_square, low_square],
        flops=5 * score_flops,
    )
    kvq_grad, norm1_keep, *rest = local_call(
        functools.partial(projection_back_kernel, parts),
        (meta, after(kvq_own, *fed_arrived), kv_arrived, kvq_matrix),
        [low_like(group, 3 * width), wide_like(rows, model)]
        + [low_like(rows, model)] * (parts - 1)
        + [wide_like(1, 3 * width)],
        flops=2 * group * model * 3 * width,
    )
    kvq_bias = rest[-1]
    norm1_arrived = send_pieces(rest[:-1], "dp")
    share_rows = (parts * shard + shard * model // (3 * width)) // 2
    kept_share, sent_share = local_call(
        functools.partial(projection_grad_kernel, parts, depth, halves),
        (meta, norm1_all, kvq_grad, out_grad),
        [wide_like(depth, share_rows, 3 * width), low_like(depth, share_rows, 3 * width)],
        [
            pltpu.VMEM((model, 3 * width), WIDE),
            pltpu.VMEM((shard * model // (3 * width), 3 * width), WIDE),
        ],
        flops=2 * group * model * 3 * width,
    )
    input_part, sums = local_call(
        functools.partial(first_norm_grad_kernel, parts),
        (
            meta, after(norm1_keep, kept_share, *half_pieces), *norm1_arrived, token_rows, vectors, mixed_part,
            sums, kvq_bias, up_bias,
        ),
        [low_like(rows, model), wide_like(8, model)],
    )

    if halves:
        share_keep, share_sends = fold(kept_share, sent_share, input_part)
        share_pieces = send_pieces(share_sends, "fsdp")
        up_total, down_total = both_halves(sum_all(half_keep, half_pieces).astype(LOW))
        first_share, second_share = both_halves(sum_all(share_keep, share_pieces).astype(LOW))
        sums = after(sums, share_pieces[0])
    else:
        share_pieces = []
        up_total, down_total = direct_totals(kept_half, sent_half)
        first_share, second_share = direct_totals(kept_share, sent_share)
    up_total = after(up_total.astype(LOW), *share_pieces).reshape(parts, shard, hidden_part)
    down_total = down_total.astype(WIDE)
    (up_total,) = local_call(
        functools.partial(join_up_kernel, parts),
        (meta, up_total[0], *send_pieces([up_total[s] for s in range(1, parts)], "dp")),
        [wide_like(shard, parts * hidden_part)],
    )
    *kvq_total, out_total = local_call(
        functools.partial(unfold_kernel, parts),
        (meta, first_share, second_share),
        [low_like(shard, 3 * width)] * parts + [wide_like(shard, model)],
        [pltpu.VMEM((shard * model // (3 * width), 3 * width), WIDE)],
    )
    (qkv_total,) = local_call(
        functools.partial(join_qkv_kernel, parts, width),
        (meta, kvq_total[0], *send_pieces(kvq_total[1:], "dp")),
        [wide_like(shard, 3 * model)],
    )
    delta = sum_all(fed_keep, fed_arrived) + vectors[5:6] + attended
    delta = after(delta.astype(LOW), *share_pieces)
    output = tokens[0] + transpose_homes(delta).astype(WIDE)
    input_rows = after(transpose_homes(input_part), *share_pieces)
    input_grad = cotangent[0] + input_rows.astype(WIDE)

    sums = sum_replicas(after(sum_doubling(sums, "fsdp"), *share_pieces))
    everywhere = sum_doubling(sums, "dp")
    owned = lax.dynamic_slice(everywhere, (0, (mine * depth + deep) * shard), (6, shard))
    value_bias = lax.dynamic_slice(sums, (6, width + deep * shard), (1, shard))[0]
    query_bias = lax.dynamic_slice(sums, (6, 2 * width + deep * shard), (1, shard))[0]
    inner_bias = lax.dynamic_slice(sums, (7, deep * hidden_shard), (1, hidden_shard))[0]

    return (
        output[None],
        input_grad[None],
        owned[0],
        owned[1],
        qkv_total,
        query_bias,
        value_bias,
        out_total,
        owned[4],
        owned[2],
        owned[3],
        up_total,
        inner_bias,
        down_total,
        owned[5],
    )


def solution(mesh):
    rows = P("dp", ("ctx", "fsdp"), None)
    vector = P(("dp", "fsdp"))
    matrix = P(("dp", "fsdp"), None)
    parameters = (
        vector, vector, matrix, vector, vector, matrix, vector, vector, vector, matrix, vector,
        matrix, vector,
    )
    return jax.shard_map(
        local,
        mesh=mesh,
        in_specs=(rows, rows) + parameters,
        out_specs=(rows, rows) + parameters,
        check_vma=False,
    )
```

```python
import functools

import jax
import jax.numpy as jnp
from jax import lax
from jax.experimental import pallas as pl
from jax.experimental.pallas import tpu as pltpu
from jax.sharding import PartitionSpec as P

HEAD_DIM = 64
EPSILON = 1e-05
SCALE = HEAD_DIM ** (-0.5)
MASKED = -1e30
CHUNK = 64
HURRY = 20
VMEM_BYTES = 16 * 1024 * 1024
GELU_SCALE = 0.7978845608
GELU_CUBE = 0.044715
LOW = jnp.bfloat16
WIDE = jnp.float32


def swap(value, axis, bit):
    count = lax.axis_size(axis)
    return lax.ppermute(value, axis, [(at, at ^ bit) for at in range(count)])


def shift(value, axis, by):
    count = lax.axis_size(axis)
    return lax.ppermute(value, axis, [(at, (at + by) % count) for at in range(count)])


def transpose_homes(value):
    side = lax.axis_size("dp")
    pairs = [(a * side + b, b * side + a) for a in range(side) for b in range(side)]
    return lax.ppermute(value, ("dp", "fsdp"), pairs)


def after(value, *others):
    return lax.optimization_barrier((value,) + others)[0]


def gather_pieces(block):
    pieces = [block]
    for slot in range(1, lax.axis_size("dp")):
        low_bit = slot & -slot
        pieces.append(swap(pieces[slot ^ low_bit], "dp", low_bit))
    return pieces


def send_pieces(sends, axis):
    return [swap(send, axis, slot) for slot, send in enumerate(sends, 1)]


def sum_rows(keep, send):
    assert lax.axis_size("dp") == 4
    near = swap(send, "dp", 1)
    rows = keep.shape[0] // 2
    far = swap((keep[rows:] + near[rows:].astype(WIDE)).astype(LOW), "dp", 2)
    return keep, near, far


def gather_direct(block, axis):
    return [block] + [swap(block, axis, slot) for slot in range(1, lax.axis_size(axis))]


def sum_doubling(value, axis):
    bit = 1
    while bit < lax.axis_size(axis):
        value = value + swap(value, axis, bit)
        bit *= 2
    return value


def sum_all(kept, arrived):
    total = kept
    for piece in arrived:
        total = total + piece.astype(WIDE)
    return total


def sum_replicas(value):
    if lax.axis_size("ctx") == 2:
        return value.astype(WIDE) + shift(value, "ctx", 1).astype(WIDE)
    return jnp.sum(lax.all_gather(value, "ctx").astype(WIDE), axis=0)


def matmul_nt(left, right):
    return lax.dot_general(left, right, (((1,), (1,)), ((), ())), preferred_element_type=WIDE)


def matmul_nn(left, right):
    return lax.dot_general(left, right, (((1,), (0,)), ((), ())), preferred_element_type=WIDE)


def matmul_tn(left, right):
    return lax.dot_general(left, right, (((0,), (0,)), ((), ())), preferred_element_type=WIDE)


def visible_block(place_ref, start, block_rows, columns):
    slot = start // block_rows
    query_pos = place_ref[slot] * block_rows + start % block_rows
    query_pos = query_pos + lax.broadcasted_iota(jnp.int32, (CHUNK, columns), 0)
    lane = lax.broadcasted_iota(jnp.int32, (CHUNK, columns), 1)
    key_pos = lane
    for at in range(columns // block_rows):
        inside = (lane >= at * block_rows) & (lane < (at + 1) * block_rows)
        key_pos = jnp.where(inside, place_ref[at] * block_rows + lane - at * block_rows, key_pos)
    return key_pos <= query_pos


def columns_of(head):
    return slice(head * HEAD_DIM, (head + 1) * HEAD_DIM)


def own_forward(heads, block_rows, place_ref, kvq_ref, acc_ref, stat_ref, score, prob):
    width = heads * HEAD_DIM
    rows = kvq_ref.shape[0]
    for head in range(heads):
        query = kvq_ref[:, 2 * width + head * HEAD_DIM : 2 * width + (head + 1) * HEAD_DIM]
        score[...] = matmul_nt(query, kvq_ref[:, columns_of(head)])

        def chunk(step, carry):
            start = pl.multiple_of(step * CHUNK, CHUNK)
            seen = visible_block(place_ref, start, block_rows, rows)
            scores = jnp.where(seen, score[pl.ds(start, CHUNK), :] * SCALE, MASKED)
            highest = jnp.max(scores, axis=1, keepdims=True)
            weight = jnp.exp(scores - highest)
            stat_ref[pl.ds(start, CHUNK), head : head + 1] = highest
            stat_ref[pl.ds(start, CHUNK), heads + head : heads + head + 1] = jnp.sum(
                weight, axis=1, keepdims=True
            )
            prob[pl.ds(start, CHUNK), :] = weight.astype(LOW)
            return carry

        lax.fori_loop(0, rows // CHUNK, chunk, 0)
        value = kvq_ref[:, width + head * HEAD_DIM : width + (head + 1) * HEAD_DIM]
        acc_ref[:, columns_of(head)] = matmul_nn(prob[...], value)


def earlier_forward(
    heads, slots, place_ref, kvq_ref, kv_ref, acc_in, stat_in, acc_ref, low_ref, stat_ref, score,
    prob, fade
):
    width = heads * HEAD_DIM
    rows = kvq_ref.shape[0]
    acc_ref[...] = acc_in[...]
    stat_ref[...] = stat_in[...]
    for piece in range(kv_ref.shape[0]):

        @pl.when(place_ref[slots] > piece)
        def _visit(piece=piece):
            for head in range(heads):
                query = kvq_ref[:, 2 * width + head * HEAD_DIM : 2 * width + (head + 1) * HEAD_DIM]
                score[...] = matmul_nt(query, kv_ref[piece, :, columns_of(head)])

                def chunk(step, carry):
                    here = pl.ds(pl.multiple_of(step * CHUNK, CHUNK), CHUNK)
                    scores = score[here, :] * SCALE
                    old = stat_ref[here, head : head + 1]
                    highest = jnp.maximum(old, jnp.max(scores, axis=1, keepdims=True))
                    weight = jnp.exp(scores - highest)
                    fading = jnp.exp(old - highest)
                    stat_ref[here, head : head + 1] = highest
                    total = stat_ref[here, heads + head : heads + head + 1]
                    stat_ref[here, heads + head : heads + head + 1] = total * fading + jnp.sum(
                        weight, axis=1, keepdims=True
                    )
                    fade[here, :] = jnp.broadcast_to(fading, (CHUNK, HEAD_DIM))
                    prob[here, :] = weight.astype(LOW)
                    return carry

                lax.fori_loop(0, rows // CHUNK, chunk, 0)
                value = kv_ref[piece, :, width + head * HEAD_DIM : width + (head + 1) * HEAD_DIM]
                acc_ref[:, columns_of(head)] = acc_ref[:, columns_of(head)] * fade[
                    ...
                ] + matmul_nn(prob[...], value)

    for head in range(heads):
        total = stat_ref[:, heads + head : heads + head + 1]
        context = acc_ref[:, columns_of(head)] / total
        acc_ref[:, columns_of(head)] = context
        low_ref[:, columns_of(head)] = context.astype(LOW)
        stat_ref[:, head : head + 1] = stat_ref[:, head : head + 1] + jnp.log(total)


def score_grads(here, seen, head, total, delta, score, dots, prob, grad):
    scores = score[here, :] * SCALE
    weight = jnp.exp(scores - total)
    if seen is not None:
        weight = jnp.where(seen, weight, 0.0)
    prob[here, :] = weight.astype(LOW)
    grad[here, :] = (weight * (dots[here, :] - delta) * SCALE).astype(LOW)


def delta_of(here, head, context_ref, ctx_grad_ref):
    product = context_ref[here, columns_of(head)] * ctx_grad_ref[here, columns_of(head)].astype(WIDE)
    return jnp.sum(product, axis=1, keepdims=True)


def earlier_backward(
    heads, slots, place_ref, kvq_ref, kv_ref, ctx_grad_ref, context_ref, stat_ref, query_grad_ref,
    kv_grad_ref, score, dots, prob, grad
):
    width = heads * HEAD_DIM
    rows = kvq_ref.shape[0]
    query_grad_ref[...] = jnp.zeros_like(query_grad_ref)
    for piece in range(kv_ref.shape[0]):

        @pl.when(place_ref[slots] <= piece)
        def _skip(piece=piece):
            kv_grad_ref[piece] = jnp.zeros(kv_grad_ref.shape[1:], kv_grad_ref.dtype)

        @pl.when(place_ref[slots] > piece)
        def _visit(piece=piece):
            for head in range(heads):
                query = kvq_ref[:, 2 * width + head * HEAD_DIM : 2 * width + (head + 1) * HEAD_DIM]
                value_at = slice(width + head * HEAD_DIM, width + (head + 1) * HEAD_DIM)
                key = kv_ref[piece, :, columns_of(head)]
                out_grad = ctx_grad_ref[:, columns_of(head)]
                score[...] = matmul_nt(query, key)
                dots[...] = matmul_nt(out_grad, kv_ref[piece, :, value_at])

                def chunk(step, carry):
                    here = pl.ds(pl.multiple_of(step * CHUNK, CHUNK), CHUNK)
                    total = stat_ref[here, head : head + 1]
                    delta = delta_of(here, head, context_ref, ctx_grad_ref)
                    score_grads(here, None, head, total, delta, score, dots, prob, grad)
                    return carry

                lax.fori_loop(0, rows // CHUNK, chunk, 0)
                kv_grad_ref[piece, :, columns_of(head)] = matmul_tn(grad[...], query).astype(LOW)
                kv_grad_ref[piece, :, value_at] = matmul_tn(prob[...], out_grad).astype(LOW)
                query_grad_ref[:, columns_of(head)] += matmul_nn(grad[...], key)


def own_backward(
    heads, block_rows, place_ref, kvq_ref, ctx_grad_ref, context_ref, stat_ref, query_grad_in,
    grad_ref, score, dots, prob, grad
):
    width = heads * HEAD_DIM
    rows = kvq_ref.shape[0]
    for head in range(heads):
        query_at = slice(2 * width + head * HEAD_DIM, 2 * width + (head + 1) * HEAD_DIM)
        value_at = slice(width + head * HEAD_DIM, width + (head + 1) * HEAD_DIM)
        query = kvq_ref[:, query_at]
        key = kvq_ref[:, columns_of(head)]
        out_grad = ctx_grad_ref[:, columns_of(head)]
        score[...] = matmul_nt(query, key)
        dots[...] = matmul_nt(out_grad, kvq_ref[:, value_at])

        def chunk(step, carry):
            start = pl.multiple_of(step * CHUNK, CHUNK)
            here = pl.ds(start, CHUNK)
            seen = visible_block(place_ref, start, block_rows, rows)
            total = stat_ref[here, head : head + 1]
            delta = delta_of(here, head, context_ref, ctx_grad_ref)
            score_grads(here, seen, head, total, delta, score, dots, prob, grad)
            return carry

        lax.fori_loop(0, rows // CHUNK, chunk, 0)
        grad_ref[:, columns_of(head)] = matmul_tn(grad[...], query)
        grad_ref[:, value_at] = matmul_tn(prob[...], out_grad)
        grad_ref[:, query_at] = query_grad_in[:, columns_of(head)] + matmul_nn(grad[...], key)


def normalize(values):
    centered = values - jnp.mean(values, axis=-1, keepdims=True)
    spread = jnp.mean(centered * centered, axis=-1, keepdims=True)
    inverse = lax.rsqrt(spread + EPSILON)
    return centered * inverse, inverse


def normalize_back(grad, gain, hat, inverse):
    scaled = grad * gain
    mean_scaled = jnp.mean(scaled, axis=-1, keepdims=True)
    mean_product = jnp.mean(scaled * hat, axis=-1, keepdims=True)
    part = inverse * (scaled - mean_scaled - hat * mean_product)
    gain_grad = jnp.sum(grad * hat, axis=0, keepdims=True)
    return part, gain_grad, jnp.sum(grad, axis=0, keepdims=True)


def take(refs, *counts):
    groups, at = [], 0
    for count in counts:
        if count is None:
            groups.append(refs[at])
            at += 1
        else:
            groups.append(refs[at : at + count])
            at += count
    return groups


def place_shards(meta_ref, parts, pieces, out_ref):
    rows = pieces[0].shape[0]
    for deep, piece in enumerate(pieces):
        start = pl.multiple_of((meta_ref[parts + 1] ^ deep) * rows, 16)
        out_ref[pl.ds(start, rows), :] = piece[...]


def stack_rows(pieces, out_ref):
    rows = pieces[0].shape[0]
    for slot, piece in enumerate(pieces):
        out_ref[slot * rows : (slot + 1) * rows, :] = piece[...]


def emit_rows(partial, keep_ref, send_ref):
    rows = keep_ref.shape[0] // 2
    for pair in range(2):
        here = slice(pair * rows, (pair + 1) * rows)
        keep_ref[here, :] = partial[2 * pair * rows : (2 * pair + 1) * rows]
        send_ref[here, :] = partial[(2 * pair + 1) * rows : (2 * pair + 2) * rows].astype(LOW)


def row_sum(keep, near, far):
    rows = far.shape[0]
    return keep[:rows, :] + near[:rows, :].astype(WIDE) + far[...].astype(WIDE)


def emit_blocks(meta_ref, parts, depth, whole_ref, keep_ref, send_refs):
    rows = keep_ref.shape[1]
    for deep in range(depth):
        member = meta_ref[parts + 1] ^ deep
        for slot in range(parts):
            start = pl.multiple_of((meta_ref[slot] * depth + member) * rows, 16)
            block = whole_ref[pl.ds(start, rows), :]
            if deep:
                send_refs[deep - 1][slot] = block.astype(LOW)
            else:
                keep_ref[slot] = block


def emit_shards(meta_ref, parts, whole_ref, keep_ref, send_refs):
    rows = keep_ref.shape[0]
    for deep in range(len(send_refs) + 1):
        start = pl.multiple_of((meta_ref[parts + 1] ^ deep) * rows, 16)
        block = whole_ref[pl.ds(start, rows), :]
        if deep:
            send_refs[deep - 1][...] = block.astype(LOW)
        else:
            keep_ref[...] = block


def stack_kernel(parts, depth, halves, meta_ref, *refs):
    split, down_weight, out_weight, kvq_rows, feeds, vectors = take(
        refs, parts, None, None, None, 1 if halves else 2, None
    )
    columns = kvq_rows.shape[1]
    shard = split[0].shape[0]
    model = vectors.shape[1]
    width = columns // 3
    hidden_shard = down_weight.shape[0]
    member = meta_ref[parts + 1]

    def placed(slot, start):
        rows = split[slot][:, columns : -feeds[0].shape[1]]
        row = lax.broadcasted_iota(jnp.int32, (rows.shape[1], model), 0)
        column = lax.broadcasted_iota(jnp.int32, (rows.shape[1], model), 1)
        chosen = jnp.where((column == start + row) & (row < shard), 1.0, 0.0)
        return matmul_nn(rows, chosen.astype(LOW))

    whole = sum(placed(slot, (meta_ref[slot] * depth + member) * shard) for slot in range(parts))
    vectors[...] = jnp.zeros_like(vectors)
    vectors[0:6, :] = whole[0:6]
    vectors[6:7, :] = (
        placed(0, width + member * shard)[7:8] + placed(0, 2 * width + member * shard)[6:7]
    )
    vectors[7:8, :] = sum(
        placed(0, member * hidden_shard + at * shard)[8 + at : 9 + at]
        for at in range(hidden_shard // shard)
    )
    for slot in range(parts):
        kvq_rows[slot * shard : (slot + 1) * shard, :] = split[slot][:, :columns]
    vectors[8:16, : model - columns] = vectors[0:8, columns:]
    first = parts * shard + 16
    kvq_rows[parts * shard : first, :] = vectors[:, :columns].astype(LOW)
    kvq_rows[first : first + shard, :] = out_weight[:, :columns].astype(LOW)
    rest = model - columns
    for at in range(columns // rest):
        kvq_rows[first + shard :, at * rest : (at + 1) * rest] = out_weight[
            at * 16 : (at + 1) * 16, columns:
        ].astype(LOW)

    def up(out):
        for slot in range(parts):
            out[slot * shard : (slot + 1) * shard, :] = split[slot][:, -out.shape[1] :]

    def down(out):
        out[...] = down_weight[...].astype(LOW)

    if halves:
        pl.when(meta_ref[parts] == 0)(lambda: up(feeds[0]))
        pl.when(meta_ref[parts] != 0)(lambda: down(feeds[0]))
    else:
        up(feeds[0])
        down(feeds[1])


def split_kernel(parts, width, meta_ref, qkv_ref, up_ref, *refs):
    vectors, outs, packed = take(refs, None, parts, None)
    model = parts * width
    shard = qkv_ref.shape[0]
    packed[...] = jnp.zeros_like(packed)
    values = vectors[...].reshape(1, vectors.shape[0])
    for row in range(vectors.shape[0] // shard):
        packed[row : row + 1, :shard] = values[:, row * shard : (row + 1) * shard]
    part = up_ref.shape[1] // parts
    for case in range(parts):

        @pl.when(meta_ref[0] == case)
        def _case(case=case):
            for slot in range(parts):
                owner = case ^ slot
                for at, first in enumerate((model, 2 * model, 0)):
                    start = first + owner * width
                    outs[slot][:, at * width : (at + 1) * width] = qkv_ref[
                        :, start : start + width
                    ].astype(LOW)
                outs[slot][:, 3 * width : -part] = packed[...].astype(LOW)
                outs[slot][:, -part:] = up_ref[:, owner * part : (owner + 1) * part].astype(LOW)


def join_qkv_kernel(parts, width, meta_ref, *refs):
    pieces, out_ref = refs[:parts], refs[parts]
    model = parts * width
    for case in range(parts):

        @pl.when(meta_ref[0] == case)
        def _case(case=case):
            for slot in range(parts):
                owner = case ^ slot
                for at, first in enumerate((model, 2 * model, 0)):
                    start = first + owner * width
                    out_ref[:, start : start + width] = pieces[slot][
                        :, at * width : (at + 1) * width
                    ].astype(WIDE)


def join_up_kernel(parts, meta_ref, *refs):
    pieces, out_ref = refs[:parts], refs[parts]
    part = pieces[0].shape[1]
    for slot in range(parts):
        start = pl.multiple_of(meta_ref[slot] * part, 128)
        out_ref[:, pl.ds(start, part)] = pieces[slot][...].astype(WIDE)


def project_kernel(parts, depth, meta_ref, *refs):
    tokens, weight, kvq_ref, kv_ref, matrix_ref, norm_ref, vectors_ref = take(
        refs, parts, depth, None, None, None, None, None
    )
    columns = kvq_ref.shape[1]
    rows = tokens[0].shape[0]
    shard = matrix_ref.shape[0] // (parts * depth)
    for deep in range(depth):
        member = meta_ref[parts + 1] ^ deep
        for slot in range(parts):
            start = pl.multiple_of((meta_ref[slot] * depth + member) * shard, 16)
            matrix_ref[pl.ds(start, shard), :] = weight[deep][slot * shard : (slot + 1) * shard, :]
    folded = sum(piece[parts * shard : parts * shard + 16, :].astype(WIDE) for piece in weight)
    vectors_ref[:, :columns] = folded[:8]
    vectors_ref[:, columns:] = folded[8:, : vectors_ref.shape[1] - columns]
    for slot, piece in enumerate(tokens):

        def chunk(step, carry, slot=slot, piece=piece):
            here = pl.multiple_of(step * CHUNK, CHUNK)
            hat, _ = normalize(piece[pl.ds(here, CHUNK), :].astype(WIDE))
            norm_ref[pl.ds(slot * rows + here, CHUNK), :] = (
                hat * vectors_ref[0:1, :] + vectors_ref[1:2, :]
            ).astype(LOW)
            return carry

        lax.fori_loop(0, rows // CHUNK, chunk, 0)
    low = (matmul_nn(norm_ref[...], matrix_ref[...]) + vectors_ref[6:7, :columns]).astype(LOW)
    kvq_ref[...] = low
    kv_ref[...] = low[:, : kv_ref.shape[1]]


def mix_kernel(parts, depth, meta_ref, *refs):
    low, weight, matrix, keep, send = take(refs, None, depth, None, None, None)
    shard = matrix.shape[0] // depth
    columns = weight[0].shape[1]
    rest = matrix.shape[1] - columns
    first = parts * shard + 16
    for deep in range(depth):
        start = pl.multiple_of((meta_ref[parts + 1] ^ deep) * shard, 16)
        matrix[pl.ds(start, shard), :columns] = weight[deep][first : first + shard, :]
        for at in range(columns // rest):
            matrix[pl.ds(start + at * 16, 16), columns:] = weight[deep][
                first + shard :, at * rest : (at + 1) * rest
            ]
    emit_rows(matmul_nn(low[...], matrix[...]), keep, send)


def second_norm_kernel(parts, meta_ref, *refs):
    keep, near, far, tokens, vectors, out, attended_ref = refs
    attended = row_sum(keep, near, far) + vectors[4:5, :]
    attended_ref[...] = attended
    hat, _ = normalize(tokens[...].astype(WIDE) + attended)
    out[...] = (hat * vectors[2:3, :] + vectors[3:4, :]).astype(LOW)


def feed_kernel(parts, depth, halves, meta_ref, *refs):
    (
        norm, branch, own, other, vectors, keep, send, hidden, inner_grad, norm_all, branch_all,
        down_all, up_bias, up_all, inner, grad,
    ) = take(refs, parts, parts, depth, depth, *([None] * 12))

    def place(up, down):
        shard = up_all.shape[0] // (parts * depth)
        for deep in range(depth):
            member = meta_ref[parts + 1] ^ deep
            for slot in range(parts):
                start = pl.multiple_of((meta_ref[slot] * depth + member) * shard, 16)
                up_all[pl.ds(start, shard), :] = up[deep][slot * shard : (slot + 1) * shard, :]
        place_shards(meta_ref, parts, down, down_all)

    if halves:
        pl.when(meta_ref[parts] == 0)(lambda: place(own, other))
        pl.when(meta_ref[parts] != 0)(lambda: place(other, own))
    else:
        place(own, other)
    stack_rows(norm, norm_all)
    stack_rows(branch, branch_all)
    inner[...] = matmul_nn(norm_all[...], up_all[...])
    grad[...] = matmul_nt(branch_all[...], down_all[...])
    up_bias[...] = jnp.zeros_like(up_bias)

    def chunk(step, carry):
        here = pl.ds(pl.multiple_of(step * CHUNK, CHUNK), CHUNK)
        value = inner[here, :] + vectors[7:8, :]
        square = value * value
        bent = jnp.tanh(GELU_SCALE * (value + GELU_CUBE * square * value))
        hidden[here, :] = (0.5 * value * (1.0 + bent)).astype(LOW)
        slope = 0.5 * (1.0 + bent) + 0.5 * value * (1.0 - bent * bent) * GELU_SCALE * (
            1.0 + 3.0 * GELU_CUBE * square
        )
        low = (grad[here, :] * slope).astype(LOW)
        inner_grad[here, :] = low
        up_bias[...] += jnp.sum(low.astype(WIDE), axis=0, keepdims=True)
        return carry

    lax.fori_loop(0, inner.shape[0] // CHUNK, chunk, 0)
    emit_rows(matmul_nt(inner_grad[...], up_all[...]), keep, send)


def feed_grad_kernel(parts, depth, halves, meta_ref, *refs):
    hidden, inner_grad, norm_all, branch_all, down_all, kept, *sent, fed_keep, fed_send, whole = refs
    hidden_shard = hidden.shape[1] // depth
    shard = norm_all.shape[1] // (parts * depth)

    def emit(half, outs):
        for deep in range(depth):
            out = outs[deep * len(outs) // depth].at[deep % (depth // len(outs))]
            member = meta_ref[parts + 1] ^ deep
            if half:
                start = pl.multiple_of(member * hidden_shard, 16)
                out[...] = whole[pl.ds(start, hidden_shard), :].astype(out.dtype)
            else:
                for slot in range(parts):
                    start = pl.multiple_of((meta_ref[slot] * depth + member) * shard, 16)
                    out[slot * shard : (slot + 1) * shard, :] = whole[
                        pl.ds(start, shard), :
                    ].astype(out.dtype)

    for half in range(2):
        if half:
            whole[...] = matmul_tn(hidden[...], branch_all[...])
        else:
            whole[...] = matmul_tn(norm_all[...], inner_grad[...])
        if halves:
            pl.when(meta_ref[parts] == half)(functools.partial(emit, half, [kept]))
            pl.when(meta_ref[parts] != half)(functools.partial(emit, half, sent))
        else:
            emit(half, sent if half else [kept])
    emit_rows(matmul_nn(hidden[...], down_all[...]), fed_keep, fed_send)


def fold_kernel(count, meta_ref, kept_ref, *refs):
    arrived, keep_ref, send_refs = refs[:count], refs[count], refs[count + 1 :]
    depth = kept_ref.shape[0]
    for deep in range(depth):
        piece = arrived[deep * count // depth][deep % (depth // count)].astype(WIDE)
        if deep:
            send_refs[deep - 1][...] = (kept_ref[deep] + piece).astype(LOW)
        else:
            keep_ref[...] = kept_ref[deep] + piece


def second_norm_grad_kernel(parts, meta_ref, *refs):
    keep, near, far, tokens, attended, branch, vectors, attn_grad, mixed_part, sums = refs
    grad = row_sum(keep, near, far)
    hat, inverse = normalize(tokens[...].astype(WIDE) + attended[...])
    part, gain_grad, bias_grad = normalize_back(grad, vectors[2:3, :], hat, inverse)
    mixed_part[...] = part
    branch_rows = branch[...].astype(WIDE)
    low = (branch_rows + part).astype(LOW)
    attn_grad[...] = low
    sums[...] = jnp.zeros_like(sums)
    sums[2:3, :] = gain_grad
    sums[3:4, :] = bias_grad
    sums[4:5, :] = jnp.sum(low.astype(WIDE), axis=0, keepdims=True)
    sums[5:6, :] = jnp.sum(branch_rows, axis=0, keepdims=True)


def context_grad_kernel(parts, heads, meta_ref, *refs):
    (
        attn, matrix, kvq, kv, context, stat, ctx_grad, attn_all, query_grad, kv_grad, score, dots,
        prob, grad,
    ) = take(refs, parts, *([None] * 13))
    stack_rows(attn, attn_all)
    ctx_grad[...] = matmul_nt(attn_all[...], matrix[...]).astype(LOW)
    earlier_backward(
        heads, parts, meta_ref, kvq, kv, ctx_grad, context, stat, query_grad, kv_grad, score, dots,
        prob, grad,
    )


def own_grad_kernel(parts, depth, heads, rows, meta_ref, *refs):
    (
        kvq, ctx_grad, context, stat, query_grad, low, attn_all, kvq_grad, out_grad, score, dots,
        prob, grad,
    ) = refs
    own_backward(
        heads, rows, meta_ref, kvq, ctx_grad, context, stat, query_grad, kvq_grad, score, dots,
        prob, grad,
    )
    out_grad[...] = matmul_tn(low[...], attn_all[...])


def projection_back_kernel(parts, meta_ref, *refs):
    own, arrived, matrix, kvq_grad, keep, send, bias = refs
    kv_width = arrived.shape[2]
    total = own[:, :kv_width]
    for piece in range(arrived.shape[0]):
        total = total + arrived[piece].astype(WIDE)
    kvq_grad[:, :kv_width] = total.astype(LOW)
    kvq_grad[:, kv_width:] = own[:, kv_width:].astype(LOW)
    emit_rows(matmul_nt(kvq_grad[...], matrix[...]), keep, send)
    bias[...] = jnp.sum(kvq_grad[...].astype(WIDE), axis=0, keepdims=True)


def projection_grad_kernel(parts, depth, halves, meta_ref, *refs):
    norm, kvq_grad, out_grad, kept, sent, whole, folded = refs
    columns = kvq_grad.shape[1]
    model = norm.shape[1]
    shard = model // (parts * depth)
    rest = model - columns
    slots = parts // 2
    extra = kept.shape[1] - slots * shard
    whole[...] = matmul_tn(norm[...], kvq_grad[...])

    def emit(half, out):
        for deep in range(depth):
            member = meta_ref[parts + 1] ^ deep
            for slot in range(slots):
                row = (meta_ref[half * slots + slot] * depth + member) * shard
                out[deep, slot * shard : (slot + 1) * shard] = whole[
                    pl.ds(pl.multiple_of(row, 16), shard), :
                ].astype(out.dtype)
            start = pl.multiple_of(member * shard, 16)
            folded[:shard, :] = out_grad[pl.ds(start, shard), :columns]
            for at in range(columns // rest):
                piece = out_grad[pl.ds(start + at * 16, 16), columns:]
                folded[shard:, at * rest : (at + 1) * rest] = piece
            out[deep, slots * shard :] = folded[half * extra : (half + 1) * extra, :].astype(
                out.dtype
            )

    for half in range(2):
        if halves:
            pl.when(meta_ref[parts] == half)(functools.partial(emit, half, kept))
            pl.when(meta_ref[parts] != half)(functools.partial(emit, half, sent))
        else:
            emit(half, sent if half else kept)


def unfold_kernel(parts, meta_ref, first_ref, second_ref, *refs):
    pieces, out_ref, folded = refs[:parts], refs[parts], refs[parts + 1]
    shard, columns = pieces[0].shape
    rest = out_ref.shape[1] - columns
    slots = parts // 2
    extra = folded.shape[0] // 2
    for half, ref in enumerate((first_ref, second_ref)):
        for slot in range(slots):
            pieces[half * slots + slot][...] = ref[slot * shard : (slot + 1) * shard, :].astype(LOW)
        folded[half * extra : (half + 1) * extra, :] = ref[slots * shard :, :].astype(WIDE)
    out_ref[:, :columns] = folded[:shard, :]
    for at in range(columns // rest):
        out_ref[at * 16 : (at + 1) * 16, columns:] = folded[shard:, at * rest : (at + 1) * rest]


def first_norm_grad_kernel(parts, meta_ref, *refs):
    keep, near, far, tokens, vectors, mixed_part, sums_in, kvq_bias, up_bias, out, sums = refs
    grad = row_sum(keep, near, far)
    hat, inverse = normalize(tokens[...].astype(WIDE))
    part, gain_grad, bias_grad = normalize_back(grad, vectors[0:1, :], hat, inverse)
    out[...] = (mixed_part[...] + part).astype(LOW)
    sums[...] = sums_in[...]
    sums[0:1, :] = gain_grad
    sums[1:2, :] = bias_grad
    sums[6:7, : kvq_bias.shape[1]] = kvq_bias[...]
    sums[7:8, :] = up_bias[...]


def local_call(kernel, operands, results, scratch=(), flops=0):
    smem = pl.BlockSpec(memory_space=pltpu.SMEM)
    vmem = pl.BlockSpec(memory_space=pltpu.VMEM)
    moved = sum(each.size * each.dtype.itemsize for each in tuple(operands) + tuple(results))
    return pl.pallas_call(
        kernel,
        name=getattr(kernel, "func", kernel).__name__,
        out_shape=tuple(results),
        in_specs=[smem] + [vmem] * (len(operands) - 1),
        out_specs=tuple([vmem] * len(results)),
        scratch_shapes=list(scratch),
        compiler_params=pltpu.CompilerParams(vmem_limit_bytes=VMEM_BYTES),
        cost_estimate=pl.CostEstimate(
            flops=flops // HURRY, bytes_accessed=moved // HURRY, transcendentals=0
        ),
    )(*operands)


def low_like(*shape):
    return jax.ShapeDtypeStruct(shape, LOW)


def wide_like(*shape):
    return jax.ShapeDtypeStruct(shape, WIDE)


def local(
    tokens, cotangent, ln1_gain, ln1_bias, qkv_weight, q_bias, v_bias, out_weight, out_bias,
    ln2_gain, ln2_bias, fc1_weight, fc1_bias, fc2_weight, fc2_bias,
):
    parts = lax.axis_size("dp")
    depth = lax.axis_size("fsdp")
    contexts = lax.axis_size("ctx")
    assert parts == depth
    mine = lax.axis_index("dp")
    deep = lax.axis_index("fsdp")
    rows, model = tokens.shape[1:]
    shard = ln1_gain.shape[0]
    heads = model // HEAD_DIM // parts
    width = heads * HEAD_DIM
    hidden_shard = fc1_bias.shape[0]
    hidden_part = hidden_shard * depth
    group = parts * rows
    meta = jnp.stack(
        [mine ^ slot for slot in range(parts)] + [lax.axis_index("ctx"), deep]
    ).astype(jnp.int32)

    halves = contexts == 2
    padded = -(-3 * width // 128) * 128
    split = local_call(
        functools.partial(split_kernel, parts, width),
        (
            meta, qkv_weight, fc1_weight,
            jnp.concatenate(
                [
                    ln1_gain, ln1_bias, ln2_gain, ln2_bias, out_bias, fc2_bias, q_bias, v_bias,
                    fc1_bias,
                ]
            ),
        ),
        [low_like(shard, padded + hidden_part)] * parts,
        [pltpu.VMEM((shard, padded - 3 * width), WIDE)],
    )
    split_arrived = send_pieces(split[1:], "dp")
    kvq_rows, *feeds = local_call(
        functools.partial(stack_kernel, parts, depth, halves),
        (meta, split[0], *split_arrived, fc2_weight, out_weight),
        [low_like(parts * shard + 16 + shard * model // (3 * width), 3 * width)]
        + [low_like(hidden_shard, model)] * (1 if halves else 2),
        [pltpu.VMEM((16, model), WIDE)],
    )
    kvq_pieces = gather_direct(kvq_rows, "fsdp")

    token_rows = transpose_homes(after(tokens[0].astype(LOW), split_arrived[1]))
    pieces = gather_pieces(after(token_rows, *split_arrived))

    kvq, kv, kvq_matrix, norm1_all, vectors = local_call(
        functools.partial(project_kernel, parts, depth),
        (meta, *pieces, *kvq_pieces),
        [
            low_like(group, 3 * width),
            low_like(group, 2 * width),
            low_like(model, 3 * width),
            low_like(group, model),
            wide_like(8, model),
        ],
        flops=2 * group * model * 3 * width,
    )
    kv_earlier = jnp.stack([shift(kv, "ctx", by) for by in range(1, contexts)])

    if halves:
        own_half = gather_direct(after(feeds[0], *kvq_pieces[1:]), "fsdp")
        other_half = [shift(after(feeds[0], kv_earlier), "ctx", 1)]
        for piece in own_half[1:]:
            other_half.append(shift(piece, "ctx", 1))
    else:
        own_half = gather_direct(feeds[0], "fsdp")
        other_half = gather_direct(feeds[1], "fsdp")
    grad_rows = transpose_homes(after(cotangent[0].astype(LOW), own_half[1]))
    branch_pieces = gather_pieces(grad_rows)

    score_flops = 2 * group * group * width
    wide_square = pltpu.VMEM((group, group), WIDE)
    low_square = pltpu.VMEM((group, group), LOW)
    acc, stat = local_call(
        functools.partial(own_forward, heads, rows),
        (meta, kvq),
        [wide_like(group, width), wide_like(group, 128)],
        [wide_square, low_square],
        flops=2 * score_flops,
    )
    context, context_low, stat = local_call(
        functools.partial(earlier_forward, heads, parts),
        (meta, kvq, kv_earlier, after(acc, own_half[1]), stat),
        [wide_like(group, width), low_like(group, width), wide_like(group, 128)],
        [wide_square, low_square, pltpu.VMEM((group, HEAD_DIM), WIDE)],
        flops=2 * score_flops,
    )
    out_matrix, attended_keep, attended_send = local_call(
        functools.partial(mix_kernel, parts, depth),
        (meta, after(context_low, *own_half[2:]), *kvq_pieces),
        [low_like(width, model), wide_like(2 * rows, model), low_like(2 * rows, model)],
        flops=2 * group * width * model,
    )
    attended_sum = sum_rows(attended_keep, attended_send)
    norm2, attended = local_call(
        functools.partial(second_norm_kernel, parts),
        (meta, *attended_sum, token_rows, vectors),
        [low_like(rows, model), wide_like(rows, model)],
    )

    norm2_pieces = gather_pieces(norm2)
    norm2_keep, norm2_send, *rest = local_call(
        functools.partial(feed_kernel, parts, depth, halves),
        (meta, *norm2_pieces, *branch_pieces, *own_half, *other_half, vectors),
        [wide_like(2 * rows, model), low_like(2 * rows, model)]
        + [low_like(group, hidden_part)] * 2
        + [low_like(group, model)] * 2
        + [low_like(hidden_part, model), wide_like(1, hidden_part)],
        [
            pltpu.VMEM((model, hidden_part), LOW),
            pltpu.VMEM((group, hidden_part), WIDE),
            pltpu.VMEM((group, hidden_part), WIDE),
        ],
        flops=6 * group * model * hidden_part,
    )
    hidden, inner_grad, norm2_all, branch_all, down_matrix, up_bias = rest
    norm2_sum = sum_rows(norm2_keep, norm2_send)
    kept_half, *sent_half, fed_keep, fed_send = local_call(
        functools.partial(feed_grad_kernel, parts, depth, halves),
        (meta, hidden, inner_grad, norm2_all, branch_all, down_matrix),
        [
            wide_like(depth, hidden_shard, model),
            low_like(depth // 2, hidden_shard, model),
            low_like(depth // 2, hidden_shard, model),
            wide_like(2 * rows, model),
            low_like(2 * rows, model),
        ],
        [pltpu.VMEM((max(model, hidden_part), max(model, hidden_part)), WIDE)],
        flops=6 * group * model * hidden_part,
    )
    attn_grad, mixed_part, sums = local_call(
        functools.partial(second_norm_grad_kernel, parts),
        (
            meta, after(norm2_sum[0], fed_keep), *norm2_sum[1:], token_rows, attended, grad_rows,
            vectors,
        ),
        [low_like(rows, model), wide_like(rows, model), wide_like(8, model)],
    )
    attn_pieces = gather_pieces(attn_grad)

    def fold(kept, sent, *later):
        arrived = [shift(sent[0], "ctx", 1)]
        for piece in sent[1:]:
            arrived.append(shift(after(piece, arrived[-1]), "ctx", 1))
        shape = kept.shape[1:]
        keep, *sends = local_call(
            functools.partial(fold_kernel, len(sent)),
            (meta, after(kept, *later), *arrived),
            [wide_like(*shape)] + [low_like(*shape)] * (depth - 1),
        )
        return keep, sends

    def direct_totals(*grads):
        return [
            owner_sum(grad[0].astype(WIDE), send_pieces(list(grad[1:].astype(LOW)), "fsdp"))
            for grad in grads
        ]

    def both_halves(mine_half, *later):
        arrived_half = shift(after(mine_half, *later) if later else mine_half, "ctx", 1)
        first = lax.axis_index("ctx") == 0
        return (
            jnp.where(first, mine_half, arrived_half), jnp.where(first, arrived_half, mine_half)
        )

    def owner_sum(keep, pieces):
        return sum_replicas(sum_all(keep, pieces).astype(LOW))

    fed_sum = sum_rows(fed_keep, after(fed_send, attn_pieces[-1]))

    ctx_grad, attn_all, query_grad, kv_grad = local_call(
        functools.partial(context_grad_kernel, parts, heads),
        (meta, *attn_pieces, out_matrix, kvq, kv_earlier, context, stat),
        [
            low_like(group, width),
            low_like(group, model),
            wide_like(group, width),
            low_like(*kv_earlier.shape),
        ],
        [wide_square, wide_square, low_square, low_square],
        flops=5 * score_flops,
    )
    if halves:
        half_keep, half_sends = fold(kept_half, sent_half, query_grad)
        farthest = swap(half_sends[-1], "fsdp", depth - 1)
        nearer = [after(send, farthest) for send in half_sends[:-1]]
        half_pieces = send_pieces(nearer, "fsdp") + [farthest]
    else:
        half_pieces = []
    if halves:
        query_grad = after(query_grad, half_keep)
    kv_arrived = jnp.stack(
        [shift(kv_grad[by - 1], "ctx", -by) for by in range(1, contexts)]
    )
    kvq_own, out_grad = local_call(
        functools.partial(own_grad_kernel, parts, depth, heads, rows),
        (meta, kvq, ctx_grad, context, stat, query_grad, context_low, attn_all),
        [wide_like(group, 3 * width), wide_like(width, model)],
        [wide_square, wide_square, low_square, low_square],
        flops=5 * score_flops,
    )
    kvq_grad, norm1_keep, norm1_send, kvq_bias = local_call(
        functools.partial(projection_back_kernel, parts),
        (meta, after(kvq_own, fed_sum[2], *half_pieces[-1:]), kv_arrived, kvq_matrix),
        [
            low_like(group, 3 * width),
            wide_like(2 * rows, model),
            low_like(2 * rows, model),
            wide_like(1, 3 * width),
        ],
        flops=2 * group * model * 3 * width,
    )
    norm1_sum = sum_rows(norm1_keep, norm1_send)
    share_rows = (parts * shard + shard * model // (3 * width)) // 2
    kept_share, sent_share = local_call(
        functools.partial(projection_grad_kernel, parts, depth, halves),
        (meta, norm1_all, kvq_grad, out_grad),
        [wide_like(depth, share_rows, 3 * width), low_like(depth, share_rows, 3 * width)],
        [
            pltpu.VMEM((model, 3 * width), WIDE),
            pltpu.VMEM((shard * model // (3 * width), 3 * width), WIDE),
        ],
        flops=2 * group * model * 3 * width,
    )
    input_part, sums = local_call(
        functools.partial(first_norm_grad_kernel, parts),
        (
            meta, after(norm1_sum[0], kept_share), *norm1_sum[1:], token_rows, vectors, mixed_part,
            sums, kvq_bias, up_bias,
        ),
        [low_like(rows, model), wide_like(8, model)],
    )

    if halves:
        share_keep, share_sends = fold(kept_share, [sent_share], input_part)
        share_pieces = send_pieces(share_sends, "fsdp")
        up_total, down_total = both_halves(
            sum_all(after(half_keep, input_part), half_pieces).astype(LOW)
        )
        first_share, second_share = both_halves(sum_all(share_keep, share_pieces).astype(LOW))
        sums = after(sums, share_pieces[0])
    else:
        share_pieces = []
        up_total, down_total = direct_totals(kept_half, jnp.concatenate(sent_half))
        first_share, second_share = direct_totals(kept_share, sent_share)
    up_total = after(up_total.astype(LOW), *share_pieces).reshape(parts, shard, hidden_part)
    down_total = down_total.astype(WIDE)
    (up_total,) = local_call(
        functools.partial(join_up_kernel, parts),
        (meta, up_total[0], *send_pieces([up_total[s] for s in range(1, parts)], "dp")),
        [wide_like(shard, parts * hidden_part)],
    )
    *kvq_total, out_total = local_call(
        functools.partial(unfold_kernel, parts),
        (meta, first_share, second_share),
        [low_like(shard, 3 * width)] * parts + [wide_like(shard, model)],
        [pltpu.VMEM((shard * model // (3 * width), 3 * width), WIDE)],
    )
    (qkv_total,) = local_call(
        functools.partial(join_qkv_kernel, parts, width),
        (meta, kvq_total[0], *send_pieces(kvq_total[1:], "dp")),
        [wide_like(shard, 3 * model)],
    )
    delta = row_sum(*fed_sum) + vectors[5:6] + attended
    delta = after(delta.astype(LOW), *share_pieces[:1])
    output = tokens[0] + transpose_homes(delta).astype(WIDE)
    input_rows = after(transpose_homes(input_part), *share_pieces)
    input_grad = cotangent[0] + input_rows.astype(WIDE)

    sums = sum_replicas(after(sum_doubling(sums, "fsdp"), *share_pieces))
    everywhere = sum_doubling(sums, "dp")
    owned = lax.dynamic_slice(everywhere, (0, (mine * depth + deep) * shard), (6, shard))
    value_bias = lax.dynamic_slice(sums, (6, width + deep * shard), (1, shard))[0]
    query_bias = lax.dynamic_slice(sums, (6, 2 * width + deep * shard), (1, shard))[0]
    inner_bias = lax.dynamic_slice(sums, (7, deep * hidden_shard), (1, hidden_shard))[0]

    return (
        output[None],
        input_grad[None],
        owned[0],
        owned[1],
        qkv_total,
        query_bias,
        value_bias,
        out_total,
        owned[4],
        owned[2],
        owned[3],
        up_total,
        inner_bias,
        down_total,
        owned[5],
    )


def solution(mesh):
    rows = P("dp", ("ctx", "fsdp"), None)
    vector = P(("dp", "fsdp"))
    matrix = P(("dp", "fsdp"), None)
    parameters = (
        vector, vector, matrix, vector, vector, matrix, vector, vector, vector, matrix, vector,
        matrix, vector,
    )
    return jax.shard_map(
        local,
        mesh=mesh,
        in_specs=(rows, rows) + parameters,
        out_specs=(rows, rows) + parameters,
        check_vma=False,
    )
```

```python
import functools

import jax
import jax.numpy as jnp
from jax import lax
from jax.experimental import pallas as pl
from jax.experimental.pallas import tpu as pltpu
from jax.sharding import PartitionSpec as P

HEAD_DIM = 64
EPSILON = 1e-05
SCALE = HEAD_DIM ** (-0.5)
MASKED = -1e30
CHUNK = 64
HURRY = 20
VMEM_BYTES = 16 * 1024 * 1024
GELU_SCALE = 0.7978845608
GELU_CUBE = 0.044715
LOW = jnp.bfloat16
WIDE = jnp.float32


def swap(value, axis, bit):
    count = lax.axis_size(axis)
    return lax.ppermute(value, axis, [(at, at ^ bit) for at in range(count)])


def shift(value, axis, by):
    count = lax.axis_size(axis)
    return lax.ppermute(value, axis, [(at, (at + by) % count) for at in range(count)])


def transpose_homes(value):
    side = lax.axis_size("dp")
    pairs = [(a * side + b, b * side + a) for a in range(side) for b in range(side)]
    return lax.ppermute(value, ("dp", "fsdp"), pairs)


def after(value, *others):
    return lax.optimization_barrier((value,) + others)[0]


def gather_pieces(block, *before_last):
    pieces = [block]
    count = lax.axis_size("dp")
    for slot in range(1, count):
        low_bit = slot & -slot
        source = pieces[slot ^ low_bit]
        if before_last and slot == count - 1:
            source = after(source, *before_last)
        pieces.append(swap(source, "dp", low_bit))
    return pieces


def send_pieces(sends, axis):
    return [swap(send, axis, slot) for slot, send in enumerate(sends, 1)]


def sum_rows(keep, send):
    assert lax.axis_size("dp") == 4
    near = swap(send, "dp", 1)
    rows = keep.shape[0] // 2
    far = swap((keep[rows:] + near[rows:].astype(WIDE)).astype(LOW), "dp", 2)
    return keep, near, far


def gather_direct(block, axis):
    return [block] + [swap(block, axis, slot) for slot in range(1, lax.axis_size(axis))]


def sum_doubling(value, axis):
    bit = 1
    while bit < lax.axis_size(axis):
        value = value + swap(value, axis, bit)
        bit *= 2
    return value


def sum_all(kept, arrived):
    total = kept
    for piece in arrived:
        total = total + piece.astype(WIDE)
    return total


def sum_replicas(value):
    if lax.axis_size("ctx") == 2:
        return value.astype(WIDE) + shift(value, "ctx", 1).astype(WIDE)
    return jnp.sum(lax.all_gather(value, "ctx").astype(WIDE), axis=0)


def matmul_nt(left, right):
    return lax.dot_general(left, right, (((1,), (1,)), ((), ())), preferred_element_type=WIDE)


def matmul_nn(left, right):
    return lax.dot_general(left, right, (((1,), (0,)), ((), ())), preferred_element_type=WIDE)


def matmul_tn(left, right):
    return lax.dot_general(left, right, (((0,), (0,)), ((), ())), preferred_element_type=WIDE)


def visible_block(place_ref, start, block_rows, columns):
    slot = start // block_rows
    query_pos = place_ref[slot] * block_rows + start % block_rows
    query_pos = query_pos + lax.broadcasted_iota(jnp.int32, (CHUNK, columns), 0)
    lane = lax.broadcasted_iota(jnp.int32, (CHUNK, columns), 1)
    key_pos = lane
    for at in range(columns // block_rows):
        inside = (lane >= at * block_rows) & (lane < (at + 1) * block_rows)
        key_pos = jnp.where(inside, place_ref[at] * block_rows + lane - at * block_rows, key_pos)
    return key_pos <= query_pos


def columns_of(head):
    return slice(head * HEAD_DIM, (head + 1) * HEAD_DIM)


def own_forward(heads, block_rows, place_ref, kvq_ref, acc_ref, stat_ref, score, prob):
    width = heads * HEAD_DIM
    rows = kvq_ref.shape[0]
    for head in range(heads):
        query = kvq_ref[:, 2 * width + head * HEAD_DIM : 2 * width + (head + 1) * HEAD_DIM]
        score[...] = matmul_nt(query, kvq_ref[:, columns_of(head)])

        def chunk(step, carry):
            start = pl.multiple_of(step * CHUNK, CHUNK)
            seen = visible_block(place_ref, start, block_rows, rows)
            scores = jnp.where(seen, score[pl.ds(start, CHUNK), :] * SCALE, MASKED)
            highest = jnp.max(scores, axis=1, keepdims=True)
            weight = jnp.exp(scores - highest)
            stat_ref[pl.ds(start, CHUNK), head : head + 1] = highest
            stat_ref[pl.ds(start, CHUNK), heads + head : heads + head + 1] = jnp.sum(
                weight, axis=1, keepdims=True
            )
            prob[pl.ds(start, CHUNK), :] = weight.astype(LOW)
            return carry

        lax.fori_loop(0, rows // CHUNK, chunk, 0)
        value = kvq_ref[:, width + head * HEAD_DIM : width + (head + 1) * HEAD_DIM]
        acc_ref[:, columns_of(head)] = matmul_nn(prob[...], value)


def earlier_forward(
    heads, slots, place_ref, kvq_ref, kv_ref, acc_in, stat_in, acc_ref, low_ref, stat_ref, score,
    prob, fade
):
    width = heads * HEAD_DIM
    rows = kvq_ref.shape[0]
    acc_ref[...] = acc_in[...]
    stat_ref[...] = stat_in[...]
    for piece in range(kv_ref.shape[0]):

        @pl.when(place_ref[slots] > piece)
        def _visit(piece=piece):
            for head in range(heads):
                query = kvq_ref[:, 2 * width + head * HEAD_DIM : 2 * width + (head + 1) * HEAD_DIM]
                score[...] = matmul_nt(query, kv_ref[piece, :, columns_of(head)])

                def chunk(step, carry):
                    here = pl.ds(pl.multiple_of(step * CHUNK, CHUNK), CHUNK)
                    scores = score[here, :] * SCALE
                    old = stat_ref[here, head : head + 1]
                    highest = jnp.maximum(old, jnp.max(scores, axis=1, keepdims=True))
                    weight = jnp.exp(scores - highest)
                    fading = jnp.exp(old - highest)
                    stat_ref[here, head : head + 1] = highest
                    total = stat_ref[here, heads + head : heads + head + 1]
                    stat_ref[here, heads + head : heads + head + 1] = total * fading + jnp.sum(
                        weight, axis=1, keepdims=True
                    )
                    fade[here, :] = jnp.broadcast_to(fading, (CHUNK, HEAD_DIM))
                    prob[here, :] = weight.astype(LOW)
                    return carry

                lax.fori_loop(0, rows // CHUNK, chunk, 0)
                value = kv_ref[piece, :, width + head * HEAD_DIM : width + (head + 1) * HEAD_DIM]
                acc_ref[:, columns_of(head)] = acc_ref[:, columns_of(head)] * fade[
                    ...
                ] + matmul_nn(prob[...], value)

    for head in range(heads):
        total = stat_ref[:, heads + head : heads + head + 1]
        context = acc_ref[:, columns_of(head)] / total
        acc_ref[:, columns_of(head)] = context
        low_ref[:, columns_of(head)] = context.astype(LOW)
        stat_ref[:, head : head + 1] = stat_ref[:, head : head + 1] + jnp.log(total)


def score_grads(here, seen, head, total, delta, score, dots, prob, grad):
    scores = score[here, :] * SCALE
    weight = jnp.exp(scores - total)
    if seen is not None:
        weight = jnp.where(seen, weight, 0.0)
    prob[here, :] = weight.astype(LOW)
    grad[here, :] = (weight * (dots[here, :] - delta) * SCALE).astype(LOW)


def delta_of(here, head, context_ref, ctx_grad_ref):
    product = context_ref[here, columns_of(head)] * ctx_grad_ref[here, columns_of(head)].astype(WIDE)
    return jnp.sum(product, axis=1, keepdims=True)


def earlier_backward(
    heads, slots, place_ref, kvq_ref, kv_ref, ctx_grad_ref, context_ref, stat_ref, query_grad_ref,
    kv_grad_ref, score, dots, prob, grad
):
    width = heads * HEAD_DIM
    rows = kvq_ref.shape[0]
    query_grad_ref[...] = jnp.zeros_like(query_grad_ref)
    for piece in range(kv_ref.shape[0]):

        @pl.when(place_ref[slots] <= piece)
        def _skip(piece=piece):
            kv_grad_ref[piece] = jnp.zeros(kv_grad_ref.shape[1:], kv_grad_ref.dtype)

        @pl.when(place_ref[slots] > piece)
        def _visit(piece=piece):
            for head in range(heads):
                query = kvq_ref[:, 2 * width + head * HEAD_DIM : 2 * width + (head + 1) * HEAD_DIM]
                value_at = slice(width + head * HEAD_DIM, width + (head + 1) * HEAD_DIM)
                key = kv_ref[piece, :, columns_of(head)]
                out_grad = ctx_grad_ref[:, columns_of(head)]
                score[...] = matmul_nt(query, key)
                dots[...] = matmul_nt(out_grad, kv_ref[piece, :, value_at])

                def chunk(step, carry):
                    here = pl.ds(pl.multiple_of(step * CHUNK, CHUNK), CHUNK)
                    total = stat_ref[here, head : head + 1]
                    delta = delta_of(here, head, context_ref, ctx_grad_ref)
                    score_grads(here, None, head, total, delta, score, dots, prob, grad)
                    return carry

                lax.fori_loop(0, rows // CHUNK, chunk, 0)
                kv_grad_ref[piece, :, columns_of(head)] = matmul_tn(grad[...], query).astype(LOW)
                kv_grad_ref[piece, :, value_at] = matmul_tn(prob[...], out_grad).astype(LOW)
                query_grad_ref[:, columns_of(head)] += matmul_nn(grad[...], key)


def own_backward(
    heads, block_rows, place_ref, kvq_ref, ctx_grad_ref, context_ref, stat_ref, query_grad_in,
    grad_ref, score, dots, prob, grad
):
    width = heads * HEAD_DIM
    rows = kvq_ref.shape[0]
    for head in range(heads):
        query_at = slice(2 * width + head * HEAD_DIM, 2 * width + (head + 1) * HEAD_DIM)
        value_at = slice(width + head * HEAD_DIM, width + (head + 1) * HEAD_DIM)
        query = kvq_ref[:, query_at]
        key = kvq_ref[:, columns_of(head)]
        out_grad = ctx_grad_ref[:, columns_of(head)]
        score[...] = matmul_nt(query, key)
        dots[...] = matmul_nt(out_grad, kvq_ref[:, value_at])

        def chunk(step, carry):
            start = pl.multiple_of(step * CHUNK, CHUNK)
            here = pl.ds(start, CHUNK)
            seen = visible_block(place_ref, start, block_rows, rows)
            total = stat_ref[here, head : head + 1]
            delta = delta_of(here, head, context_ref, ctx_grad_ref)
            score_grads(here, seen, head, total, delta, score, dots, prob, grad)
            return carry

        lax.fori_loop(0, rows // CHUNK, chunk, 0)
        grad_ref[:, columns_of(head)] = matmul_tn(grad[...], query)
        grad_ref[:, value_at] = matmul_tn(prob[...], out_grad)
        grad_ref[:, query_at] = query_grad_in[:, columns_of(head)] + matmul_nn(grad[...], key)


def normalize(values):
    centered = values - jnp.mean(values, axis=-1, keepdims=True)
    spread = jnp.mean(centered * centered, axis=-1, keepdims=True)
    inverse = lax.rsqrt(spread + EPSILON)
    return centered * inverse, inverse


def normalize_back(grad, gain, hat, inverse):
    scaled = grad * gain
    mean_scaled = jnp.mean(scaled, axis=-1, keepdims=True)
    mean_product = jnp.mean(scaled * hat, axis=-1, keepdims=True)
    part = inverse * (scaled - mean_scaled - hat * mean_product)
    gain_grad = jnp.sum(grad * hat, axis=0, keepdims=True)
    return part, gain_grad, jnp.sum(grad, axis=0, keepdims=True)


def take(refs, *counts):
    groups, at = [], 0
    for count in counts:
        if count is None:
            groups.append(refs[at])
            at += 1
        else:
            groups.append(refs[at : at + count])
            at += count
    return groups


def place_shards(meta_ref, parts, pieces, out_ref):
    rows = pieces[0].shape[0]
    for deep, piece in enumerate(pieces):
        start = pl.multiple_of((meta_ref[parts + 1] ^ deep) * rows, 16)
        out_ref[pl.ds(start, rows), :] = piece[...]


def stack_rows(pieces, out_ref):
    rows = pieces[0].shape[0]
    for slot, piece in enumerate(pieces):
        out_ref[slot * rows : (slot + 1) * rows, :] = piece[...]


def emit_rows(partial, keep_ref, send_ref):
    rows = keep_ref.shape[0] // 2
    for pair in range(2):
        here = slice(pair * rows, (pair + 1) * rows)
        keep_ref[here, :] = partial[2 * pair * rows : (2 * pair + 1) * rows]
        send_ref[here, :] = partial[(2 * pair + 1) * rows : (2 * pair + 2) * rows].astype(LOW)


def row_sum(keep, near, far):
    rows = far.shape[0]
    return keep[:rows, :] + near[:rows, :].astype(WIDE) + far[...].astype(WIDE)


def emit_blocks(meta_ref, parts, depth, whole_ref, keep_ref, send_refs):
    rows = keep_ref.shape[1]
    for deep in range(depth):
        member = meta_ref[parts + 1] ^ deep
        for slot in range(parts):
            start = pl.multiple_of((meta_ref[slot] * depth + member) * rows, 16)
            block = whole_ref[pl.ds(start, rows), :]
            if deep:
                send_refs[deep - 1][slot] = block.astype(LOW)
            else:
                keep_ref[slot] = block


def emit_shards(meta_ref, parts, whole_ref, keep_ref, send_refs):
    rows = keep_ref.shape[0]
    for deep in range(len(send_refs) + 1):
        start = pl.multiple_of((meta_ref[parts + 1] ^ deep) * rows, 16)
        block = whole_ref[pl.ds(start, rows), :]
        if deep:
            send_refs[deep - 1][...] = block.astype(LOW)
        else:
            keep_ref[...] = block


def stack_kernel(parts, depth, halves, meta_ref, *refs):
    split, down_weight, out_weight, kvq_rows, feeds, vectors = take(
        refs, parts, None, None, None, 1 if halves else 2, None
    )
    columns = kvq_rows.shape[1]
    shard = split[0].shape[0]
    model = vectors.shape[1]
    width = columns // 3
    hidden_shard = down_weight.shape[0]
    member = meta_ref[parts + 1]

    def placed(slot, start):
        rows = split[slot][:, columns : -feeds[0].shape[1]]
        row = lax.broadcasted_iota(jnp.int32, (rows.shape[1], model), 0)
        column = lax.broadcasted_iota(jnp.int32, (rows.shape[1], model), 1)
        chosen = jnp.where((column == start + row) & (row < shard), 1.0, 0.0)
        return matmul_nn(rows, chosen.astype(LOW))

    whole = sum(placed(slot, (meta_ref[slot] * depth + member) * shard) for slot in range(parts))
    vectors[...] = jnp.zeros_like(vectors)
    vectors[0:6, :] = whole[0:6]
    vectors[6:7, :] = (
        placed(0, width + member * shard)[7:8] + placed(0, 2 * width + member * shard)[6:7]
    )
    vectors[7:8, :] = sum(
        placed(0, member * hidden_shard + at * shard)[8 + at : 9 + at]
        for at in range(hidden_shard // shard)
    )
    for slot in range(parts):
        kvq_rows[slot * shard : (slot + 1) * shard, :] = split[slot][:, :columns]
    vectors[8:16, : model - columns] = vectors[0:8, columns:]
    first = parts * shard + 16
    kvq_rows[parts * shard : first, :] = vectors[:, :columns].astype(LOW)
    kvq_rows[first : first + shard, :] = out_weight[:, :columns].astype(LOW)
    rest = model - columns
    for at in range(columns // rest):
        kvq_rows[first + shard :, at * rest : (at + 1) * rest] = out_weight[
            at * 16 : (at + 1) * 16, columns:
        ].astype(LOW)

    def up(out):
        for slot in range(parts):
            out[slot * shard : (slot + 1) * shard, :] = split[slot][:, -out.shape[1] :]

    def down(out):
        out[...] = down_weight[...].astype(LOW)

    if halves:
        pl.when(meta_ref[parts] == 0)(lambda: up(feeds[0]))
        pl.when(meta_ref[parts] != 0)(lambda: down(feeds[0]))
    else:
        up(feeds[0])
        down(feeds[1])


def split_kernel(parts, width, meta_ref, qkv_ref, up_ref, *refs):
    vectors, outs, packed = take(refs, None, parts, None)
    model = parts * width
    shard = qkv_ref.shape[0]
    packed[...] = jnp.zeros_like(packed)
    values = vectors[...].reshape(1, vectors.shape[0])
    for row in range(vectors.shape[0] // shard):
        packed[row : row + 1, :shard] = values[:, row * shard : (row + 1) * shard]
    part = up_ref.shape[1] // parts
    for case in range(parts):

        @pl.when(meta_ref[0] == case)
        def _case(case=case):
            for slot in range(parts):
                owner = case ^ slot
                for at, first in enumerate((model, 2 * model, 0)):
                    start = first + owner * width
                    outs[slot][:, at * width : (at + 1) * width] = qkv_ref[
                        :, start : start + width
                    ].astype(LOW)
                outs[slot][:, 3 * width : -part] = packed[...].astype(LOW)
                outs[slot][:, -part:] = up_ref[:, owner * part : (owner + 1) * part].astype(LOW)


def join_kernel(parts, width, meta_ref, *refs):
    pieces, out_ref, up_ref, vectors = take(refs, parts, None, None, None)
    model = parts * width
    shard = out_ref.shape[0]
    hidden = up_ref.shape[1] // parts
    for case in range(parts):

        @pl.when(meta_ref[0] == case)
        def _case(case=case):
            for slot in range(parts):
                owner = case ^ slot
                for at, first in enumerate((model, 2 * model, 0)):
                    start = first + owner * width
                    out_ref[:, start : start + width] = pieces[slot][
                        :shard, at * width : (at + 1) * width
                    ].astype(WIDE)
                up_ref[:, owner * hidden : (owner + 1) * hidden] = pieces[slot][
                    :shard, -hidden:
                ].astype(WIDE)

    vectors[...] = sum(piece[shard:, : vectors.shape[1]].astype(WIDE) for piece in pieces)


def project_kernel(parts, depth, meta_ref, *refs):
    tokens, weight, kvq_ref, kv_ref, matrix_ref, norm_ref, vectors_ref = take(
        refs, parts, depth, None, None, None, None, None
    )
    columns = kvq_ref.shape[1]
    rows = tokens[0].shape[0]
    shard = matrix_ref.shape[0] // (parts * depth)
    for deep in range(depth):
        member = meta_ref[parts + 1] ^ deep
        for slot in range(parts):
            start = pl.multiple_of((meta_ref[slot] * depth + member) * shard, 16)
            matrix_ref[pl.ds(start, shard), :] = weight[deep][slot * shard : (slot + 1) * shard, :]
    folded = sum(piece[parts * shard : parts * shard + 16, :].astype(WIDE) for piece in weight)
    vectors_ref[:, :columns] = folded[:8]
    vectors_ref[:, columns:] = folded[8:, : vectors_ref.shape[1] - columns]
    for slot, piece in enumerate(tokens):

        def chunk(step, carry, slot=slot, piece=piece):
            here = pl.multiple_of(step * CHUNK, CHUNK)
            hat, _ = normalize(piece[pl.ds(here, CHUNK), :].astype(WIDE))
            norm_ref[pl.ds(slot * rows + here, CHUNK), :] = (
                hat * vectors_ref[0:1, :] + vectors_ref[1:2, :]
            ).astype(LOW)
            return carry

        lax.fori_loop(0, rows // CHUNK, chunk, 0)
    low = (matmul_nn(norm_ref[...], matrix_ref[...]) + vectors_ref[6:7, :columns]).astype(LOW)
    kvq_ref[...] = low
    kv_ref[...] = low[:, : kv_ref.shape[1]]


def mix_kernel(parts, depth, meta_ref, *refs):
    low, weight, matrix, keep, send = take(refs, None, depth, None, None, None)
    shard = matrix.shape[0] // depth
    columns = weight[0].shape[1]
    rest = matrix.shape[1] - columns
    first = parts * shard + 16
    for deep in range(depth):
        start = pl.multiple_of((meta_ref[parts + 1] ^ deep) * shard, 16)
        matrix[pl.ds(start, shard), :columns] = weight[deep][first : first + shard, :]
        for at in range(columns // rest):
            matrix[pl.ds(start + at * 16, 16), columns:] = weight[deep][
                first + shard :, at * rest : (at + 1) * rest
            ]
    emit_rows(matmul_nn(low[...], matrix[...]), keep, send)


def second_norm_kernel(parts, meta_ref, *refs):
    keep, near, far, tokens, vectors, out, attended_ref = refs
    attended = row_sum(keep, near, far) + vectors[4:5, :]
    attended_ref[...] = attended
    hat, _ = normalize(tokens[...].astype(WIDE) + attended)
    out[...] = (hat * vectors[2:3, :] + vectors[3:4, :]).astype(LOW)


def feed_kernel(parts, depth, halves, meta_ref, *refs):
    (
        norm, branch, own, other, vectors, keep, send, hidden, inner_grad, norm_all, branch_all,
        down_all, up_bias, up_all, inner, grad,
    ) = take(refs, parts, parts, depth, depth, *([None] * 12))

    def place(up, down):
        shard = up_all.shape[0] // (parts * depth)
        for deep in range(depth):
            member = meta_ref[parts + 1] ^ deep
            for slot in range(parts):
                start = pl.multiple_of((meta_ref[slot] * depth + member) * shard, 16)
                up_all[pl.ds(start, shard), :] = up[deep][slot * shard : (slot + 1) * shard, :]
        place_shards(meta_ref, parts, down, down_all)

    if halves:
        pl.when(meta_ref[parts] == 0)(lambda: place(own, other))
        pl.when(meta_ref[parts] != 0)(lambda: place(other, own))
    else:
        place(own, other)
    stack_rows(norm, norm_all)
    stack_rows(branch, branch_all)
    inner[...] = matmul_nn(norm_all[...], up_all[...])
    grad[...] = matmul_nt(branch_all[...], down_all[...])
    up_bias[...] = jnp.zeros_like(up_bias)

    def chunk(step, carry):
        here = pl.ds(pl.multiple_of(step * CHUNK, CHUNK), CHUNK)
        value = inner[here, :] + vectors[7:8, :]
        square = value * value
        bent = jnp.tanh(GELU_SCALE * (value + GELU_CUBE * square * value))
        hidden[here, :] = (0.5 * value * (1.0 + bent)).astype(LOW)
        slope = 0.5 * (1.0 + bent) + 0.5 * value * (1.0 - bent * bent) * GELU_SCALE * (
            1.0 + 3.0 * GELU_CUBE * square
        )
        low = (grad[here, :] * slope).astype(LOW)
        inner_grad[here, :] = low
        up_bias[...] += jnp.sum(low.astype(WIDE), axis=0, keepdims=True)
        return carry

    lax.fori_loop(0, inner.shape[0] // CHUNK, chunk, 0)
    emit_rows(matmul_nt(inner_grad[...], up_all[...]), keep, send)


def feed_grad_kernel(parts, depth, halves, meta_ref, *refs):
    hidden, inner_grad, norm_all, branch_all, down_all, kept, *sent, fed_keep, fed_send, whole = refs
    hidden_shard = hidden.shape[1] // depth
    shard = norm_all.shape[1] // (parts * depth)

    def emit(half, outs):
        for deep in range(depth):
            out = outs[deep * len(outs) // depth].at[deep % (depth // len(outs))]
            member = meta_ref[parts + 1] ^ deep
            if half:
                start = pl.multiple_of(member * hidden_shard, 16)
                out[...] = whole[pl.ds(start, hidden_shard), :].astype(out.dtype)
            else:
                for slot in range(parts):
                    start = pl.multiple_of((meta_ref[slot] * depth + member) * shard, 16)
                    out[slot * shard : (slot + 1) * shard, :] = whole[
                        pl.ds(start, shard), :
                    ].astype(out.dtype)

    for half in range(2):
        if half:
            whole[...] = matmul_tn(hidden[...], branch_all[...])
        else:
            whole[...] = matmul_tn(norm_all[...], inner_grad[...])
        if halves:
            pl.when(meta_ref[parts] == half)(functools.partial(emit, half, [kept]))
            pl.when(meta_ref[parts] != half)(functools.partial(emit, half, sent))
        else:
            emit(half, sent if half else [kept])
    emit_rows(matmul_nn(hidden[...], down_all[...]), fed_keep, fed_send)


def fold_kernel(count, meta_ref, kept_ref, *refs):
    arrived, keep_ref, send_refs = refs[:count], refs[count], refs[count + 1 :]
    depth = kept_ref.shape[0]
    for deep in range(depth):
        piece = arrived[deep * count // depth][deep % (depth // count)].astype(WIDE)
        if deep:
            send_refs[deep - 1][...] = (kept_ref[deep] + piece).astype(LOW)
        else:
            keep_ref[...] = kept_ref[deep] + piece


def second_norm_grad_kernel(parts, meta_ref, *refs):
    keep, near, far, tokens, attended, branch, vectors, attn_grad, mixed_part, sums = refs
    grad = row_sum(keep, near, far)
    hat, inverse = normalize(tokens[...].astype(WIDE) + attended[...])
    part, gain_grad, bias_grad = normalize_back(grad, vectors[2:3, :], hat, inverse)
    mixed_part[...] = part
    branch_rows = branch[...].astype(WIDE)
    low = (branch_rows + part).astype(LOW)
    attn_grad[...] = low
    sums[...] = jnp.zeros_like(sums)
    sums[2:3, :] = gain_grad
    sums[3:4, :] = bias_grad
    sums[4:5, :] = jnp.sum(low.astype(WIDE), axis=0, keepdims=True)
    sums[5:6, :] = jnp.sum(branch_rows, axis=0, keepdims=True)


def context_grad_kernel(parts, heads, meta_ref, *refs):
    (
        attn, matrix, kvq, kv, context, stat, ctx_grad, attn_all, query_grad, kv_grad, score, dots,
        prob, grad,
    ) = take(refs, parts, *([None] * 13))
    stack_rows(attn, attn_all)
    ctx_grad[...] = matmul_nt(attn_all[...], matrix[...]).astype(LOW)
    earlier_backward(
        heads, parts, meta_ref, kvq, kv, ctx_grad, context, stat, query_grad, kv_grad, score, dots,
        prob, grad,
    )


def own_grad_kernel(parts, depth, heads, rows, meta_ref, *refs):
    (
        kvq, ctx_grad, context, stat, query_grad, low, attn_all, kvq_grad, out_grad, score, dots,
        prob, grad,
    ) = refs
    own_backward(
        heads, rows, meta_ref, kvq, ctx_grad, context, stat, query_grad, kvq_grad, score, dots,
        prob, grad,
    )
    out_grad[...] = matmul_tn(low[...], attn_all[...])


def projection_back_kernel(parts, meta_ref, *refs):
    own, arrived, matrix, kvq_grad, keep, send, bias = refs
    kv_width = arrived.shape[2]
    total = own[:, :kv_width]
    for piece in range(arrived.shape[0]):
        total = total + arrived[piece].astype(WIDE)
    kvq_grad[:, :kv_width] = total.astype(LOW)
    kvq_grad[:, kv_width:] = own[:, kv_width:].astype(LOW)
    emit_rows(matmul_nt(kvq_grad[...], matrix[...]), keep, send)
    bias[...] = jnp.sum(kvq_grad[...].astype(WIDE), axis=0, keepdims=True)


def projection_grad_kernel(parts, depth, halves, meta_ref, *refs):
    norm, kvq_grad, out_grad, kept, sent, whole, folded = refs
    columns = kvq_grad.shape[1]
    model = norm.shape[1]
    shard = model // (parts * depth)
    rest = model - columns
    slots = parts // 2
    extra = kept.shape[1] - slots * shard
    whole[...] = matmul_tn(norm[...], kvq_grad[...])

    def emit(half, out):
        for deep in range(depth):
            member = meta_ref[parts + 1] ^ deep
            for slot in range(slots):
                row = (meta_ref[half * slots + slot] * depth + member) * shard
                out[deep, slot * shard : (slot + 1) * shard] = whole[
                    pl.ds(pl.multiple_of(row, 16), shard), :
                ].astype(out.dtype)
            start = pl.multiple_of(member * shard, 16)
            folded[:shard, :] = out_grad[pl.ds(start, shard), :columns]
            for at in range(columns // rest):
                piece = out_grad[pl.ds(start + at * 16, 16), columns:]
                folded[shard:, at * rest : (at + 1) * rest] = piece
            out[deep, slots * shard :] = folded[half * extra : (half + 1) * extra, :].astype(
                out.dtype
            )

    for half in range(2):
        if halves:
            pl.when(meta_ref[parts] == half)(functools.partial(emit, half, kept))
            pl.when(meta_ref[parts] != half)(functools.partial(emit, half, sent))
        else:
            emit(half, sent if half else kept)


def fold_vectors(sums, folded):
    rest = sums.shape[1] - folded.shape[1]
    folded[...] = jnp.zeros_like(folded)
    folded[0:8, :] = sums[:, : folded.shape[1]]
    folded[8:16, :rest] = sums[:, folded.shape[1] :]


def fold_share_kernel(meta_ref, kept, arrived, sums, keep, *refs):
    sends, folded = refs[:-1], refs[-1]
    rows = kept.shape[1]
    fold_vectors(sums, folded)
    keep[:rows, :] = kept[0] + arrived[0].astype(WIDE)
    keep[rows:, :] = folded[...]
    for deep, send in enumerate(sends, 1):
        send[:rows, :] = (kept[deep] + arrived[deep].astype(WIDE)).astype(LOW)
        send[rows:, :] = folded[...].astype(LOW)


def unfold_kernel(parts, halves, meta_ref, mine, arrived, *refs):
    sums, mine_feed, other_feed, pieces, out_ref, down_ref, vectors, folded = take(
        refs, 0 if halves else 1, None, None, parts, None, None, None, None
    )
    shard, columns = pieces[0].shape[0] - 16, vectors.shape[1]
    hidden = mine_feed.shape[1]
    rest = out_ref.shape[1] - columns
    slots = parts // 2
    extra = folded.shape[0] // 2

    def unfold(half, ref):
        for slot in range(slots):
            pieces[half * slots + slot][:shard, :columns] = ref[
                slot * shard : (slot + 1) * shard, :
            ].astype(LOW)
        start = slots * shard
        folded[half * extra : (half + 1) * extra, :] = ref[start : start + extra, :].astype(WIDE)

    def feeds(up, down):
        for slot in range(parts):
            pieces[slot][:shard, -hidden:] = up[slot * shard : (slot + 1) * shard, :].astype(LOW)
        down_ref[...] = down[...].astype(WIDE)

    if halves:
        first = meta_ref[parts] == 0
        pl.when(first)(lambda: feeds(mine_feed, other_feed))
        pl.when(jnp.logical_not(first))(lambda: feeds(other_feed, mine_feed))
        for half in range(2):
            pl.when(first)(functools.partial(unfold, half, arrived if half else mine))
            pl.when(jnp.logical_not(first))(
                functools.partial(unfold, half, mine if half else arrived)
            )
        start = slots * shard + extra
        vectors[...] = mine[start:, :].astype(WIDE) + arrived[start:, :].astype(WIDE)
    else:
        feeds(mine_feed, other_feed)
        unfold(0, mine)
        unfold(1, arrived)
        fold_vectors(sums[0], vectors)
    for piece in pieces:
        piece[shard:, :columns] = vectors[...].astype(LOW)
        piece[shard:, columns:] = jnp.zeros_like(piece[shard:, columns:])
        piece[:shard, columns:-hidden] = jnp.zeros_like(piece[:shard, columns:-hidden])
    out_ref[:, :columns] = folded[:shard, :]
    for at in range(columns // rest):
        out_ref[at * 16 : (at + 1) * 16, columns:] = folded[shard:, at * rest : (at + 1) * rest]


def first_norm_grad_kernel(parts, meta_ref, *refs):
    keep, near, far, tokens, vectors, mixed_part, sums_in, kvq_bias, up_bias, out, sums = refs
    grad = row_sum(keep, near, far)
    hat, inverse = normalize(tokens[...].astype(WIDE))
    part, gain_grad, bias_grad = normalize_back(grad, vectors[0:1, :], hat, inverse)
    out[...] = (mixed_part[...] + part).astype(LOW)
    sums[...] = sums_in[...]
    sums[0:1, :] = gain_grad
    sums[1:2, :] = bias_grad
    sums[6:7, : kvq_bias.shape[1]] = kvq_bias[...]
    sums[7:8, :] = up_bias[...]


def local_call(kernel, operands, results, scratch=(), flops=0):
    smem = pl.BlockSpec(memory_space=pltpu.SMEM)
    vmem = pl.BlockSpec(memory_space=pltpu.VMEM)
    moved = sum(each.size * each.dtype.itemsize for each in tuple(operands) + tuple(results))
    return pl.pallas_call(
        kernel,
        name=getattr(kernel, "func", kernel).__name__,
        out_shape=tuple(results),
        in_specs=[smem] + [vmem] * (len(operands) - 1),
        out_specs=tuple([vmem] * len(results)),
        scratch_shapes=list(scratch),
        compiler_params=pltpu.CompilerParams(vmem_limit_bytes=VMEM_BYTES),
        cost_estimate=pl.CostEstimate(
            flops=flops // HURRY, bytes_accessed=moved // HURRY, transcendentals=0
        ),
    )(*operands)


def low_like(*shape):
    return jax.ShapeDtypeStruct(shape, LOW)


def wide_like(*shape):
    return jax.ShapeDtypeStruct(shape, WIDE)


def local(
    tokens, cotangent, ln1_gain, ln1_bias, qkv_weight, q_bias, v_bias, out_weight, out_bias,
    ln2_gain, ln2_bias, fc1_weight, fc1_bias, fc2_weight, fc2_bias,
):
    parts = lax.axis_size("dp")
    depth = lax.axis_size("fsdp")
    contexts = lax.axis_size("ctx")
    assert parts == depth
    mine = lax.axis_index("dp")
    deep = lax.axis_index("fsdp")
    rows, model = tokens.shape[1:]
    shard = ln1_gain.shape[0]
    heads = model // HEAD_DIM // parts
    width = heads * HEAD_DIM
    hidden_shard = fc1_bias.shape[0]
    hidden_part = hidden_shard * depth
    group = parts * rows
    meta = jnp.stack(
        [mine ^ slot for slot in range(parts)] + [lax.axis_index("ctx"), deep]
    ).astype(jnp.int32)

    halves = contexts == 2
    padded = -(-3 * width // 128) * 128
    split = local_call(
        functools.partial(split_kernel, parts, width),
        (
            meta, qkv_weight, fc1_weight,
            jnp.concatenate(
                [
                    ln1_gain, ln1_bias, ln2_gain, ln2_bias, out_bias, fc2_bias, q_bias, v_bias,
                    fc1_bias,
                ]
            ),
        ),
        [low_like(shard, padded + hidden_part)] * parts,
        [pltpu.VMEM((shard, padded - 3 * width), WIDE)],
    )
    split_arrived = send_pieces(split[1:], "dp")
    kvq_rows, *feeds = local_call(
        functools.partial(stack_kernel, parts, depth, halves),
        (meta, split[0], *split_arrived, fc2_weight, out_weight),
        [low_like(parts * shard + 16 + shard * model // (3 * width), 3 * width)]
        + [low_like(hidden_shard, model)] * (1 if halves else 2),
        [pltpu.VMEM((16, model), WIDE)],
    )
    kvq_pieces = gather_direct(kvq_rows, "fsdp")

    token_rows = transpose_homes(after(tokens[0].astype(LOW), *split_arrived))
    pieces = gather_pieces(after(token_rows, kvq_pieces[1]), *kvq_pieces[2:])

    kvq, kv, kvq_matrix, norm1_all, vectors = local_call(
        functools.partial(project_kernel, parts, depth),
        (meta, *pieces, *kvq_pieces),
        [
            low_like(group, 3 * width),
            low_like(group, 2 * width),
            low_like(model, 3 * width),
            low_like(group, model),
            wide_like(8, model),
        ],
        flops=2 * group * model * 3 * width,
    )
    kv_earlier = jnp.stack([shift(kv, "ctx", by) for by in range(1, contexts)])

    if halves:
        own_half = gather_direct(after(feeds[0], *kvq_pieces[1:]), "fsdp")
    else:
        own_half = gather_direct(feeds[0], "fsdp")
        other_half = gather_direct(feeds[1], "fsdp")
    grad_rows = transpose_homes(after(cotangent[0].astype(LOW), own_half[1]))
    branch_pieces = gather_pieces(grad_rows)

    score_flops = 2 * group * group * width
    wide_square = pltpu.VMEM((group, group), WIDE)
    low_square = pltpu.VMEM((group, group), LOW)
    acc, stat = local_call(
        functools.partial(own_forward, heads, rows),
        (meta, kvq),
        [wide_like(group, width), wide_like(group, 128)],
        [wide_square, low_square],
        flops=2 * score_flops,
    )
    if halves:
        other_half = [shift(after(feeds[0], kv_earlier, acc), "ctx", 1)]
        other_half.append(shift(after(own_half[1], acc), "ctx", 1))
        other_half += [shift(piece, "ctx", 1) for piece in own_half[2:]]
    context, context_low, stat = local_call(
        functools.partial(earlier_forward, heads, parts),
        (meta, kvq, kv_earlier, after(acc, own_half[1]), stat),
        [wide_like(group, width), low_like(group, width), wide_like(group, 128)],
        [wide_square, low_square, pltpu.VMEM((group, HEAD_DIM), WIDE)],
        flops=2 * score_flops,
    )
    out_matrix, attended_keep, attended_send = local_call(
        functools.partial(mix_kernel, parts, depth),
        (meta, after(context_low, *own_half[2:], *other_half[:2]), *kvq_pieces),
        [low_like(width, model), wide_like(2 * rows, model), low_like(2 * rows, model)],
        flops=2 * group * width * model,
    )
    attended_sum = sum_rows(attended_keep, attended_send)
    norm2, attended = local_call(
        functools.partial(second_norm_kernel, parts),
        (meta, *attended_sum, token_rows, vectors),
        [low_like(rows, model), wide_like(rows, model)],
    )

    norm2_pieces = gather_pieces(norm2)
    norm2_keep, norm2_send, *rest = local_call(
        functools.partial(feed_kernel, parts, depth, halves),
        (meta, *norm2_pieces, *branch_pieces, *own_half, *other_half, vectors),
        [wide_like(2 * rows, model), low_like(2 * rows, model)]
        + [low_like(group, hidden_part)] * 2
        + [low_like(group, model)] * 2
        + [low_like(hidden_part, model), wide_like(1, hidden_part)],
        [
            pltpu.VMEM((model, hidden_part), LOW),
            pltpu.VMEM((group, hidden_part), WIDE),
            pltpu.VMEM((group, hidden_part), WIDE),
        ],
        flops=6 * group * model * hidden_part,
    )
    hidden, inner_grad, norm2_all, branch_all, down_matrix, up_bias = rest
    norm2_sum = sum_rows(norm2_keep, norm2_send)
    kept_half, *sent_half, fed_keep, fed_send = local_call(
        functools.partial(feed_grad_kernel, parts, depth, halves),
        (meta, hidden, inner_grad, norm2_all, branch_all, down_matrix),
        [
            wide_like(depth, hidden_shard, model),
            low_like(depth, hidden_shard, model),
            wide_like(2 * rows, model),
            low_like(2 * rows, model),
        ],
        [pltpu.VMEM((max(model, hidden_part), max(model, hidden_part)), WIDE)],
        flops=6 * group * model * hidden_part,
    )
    attn_grad, mixed_part, sums = local_call(
        functools.partial(second_norm_grad_kernel, parts),
        (
            meta, after(norm2_sum[0], fed_keep), *norm2_sum[1:], token_rows, attended, grad_rows,
            vectors,
        ),
        [low_like(rows, model), wide_like(rows, model), wide_like(8, model)],
    )
    attn_pieces = gather_pieces(attn_grad)

    def fold(kept, sent, *later):
        arrived = [shift(sent[0], "ctx", 1)]
        for piece in sent[1:]:
            arrived.append(shift(after(piece, arrived[-1]), "ctx", 1))
        shape = kept.shape[1:]
        keep, *sends = local_call(
            functools.partial(fold_kernel, len(sent)),
            (meta, after(kept, *later), *arrived),
            [wide_like(*shape)] + [low_like(*shape)] * (depth - 1),
        )
        return keep, sends

    def direct_totals(*grads):
        return [
            owner_sum(grad[0].astype(WIDE), send_pieces(list(grad[1:].astype(LOW)), "fsdp"))
            for grad in grads
        ]

    def owner_sum(keep, pieces):
        return sum_replicas(sum_all(keep, pieces).astype(LOW))

    fed_sum = sum_rows(fed_keep, after(fed_send, attn_pieces[-1]))

    ctx_grad, attn_all, query_grad, kv_grad = local_call(
        functools.partial(context_grad_kernel, parts, heads),
        (meta, *attn_pieces, out_matrix, kvq, kv_earlier, context, stat),
        [
            low_like(group, width),
            low_like(group, model),
            wide_like(group, width),
            low_like(*kv_earlier.shape),
        ],
        [wide_square, wide_square, low_square, low_square],
        flops=5 * score_flops,
    )
    if halves:
        half_keep, half_sends = fold(kept_half, sent_half, query_grad)
        farthest = swap(half_sends[-1], "fsdp", depth - 1)
        nearer = [after(send, farthest) for send in half_sends[:-1]]
        half_pieces = send_pieces(nearer, "fsdp") + [farthest]
    else:
        half_pieces = []
    if halves:
        query_grad = after(query_grad, half_keep)
    kv_arrived = jnp.stack(
        [shift(kv_grad[by - 1], "ctx", -by) for by in range(1, contexts)]
    )
    kvq_own, out_grad = local_call(
        functools.partial(own_grad_kernel, parts, depth, heads, rows),
        (meta, kvq, ctx_grad, context, stat, query_grad, context_low, attn_all),
        [wide_like(group, 3 * width), wide_like(width, model)],
        [wide_square, wide_square, low_square, low_square],
        flops=5 * score_flops,
    )
    kvq_grad, norm1_keep, norm1_send, kvq_bias = local_call(
        functools.partial(projection_back_kernel, parts),
        (meta, after(kvq_own, fed_sum[2], *half_pieces[-1:]), kv_arrived, kvq_matrix),
        [
            low_like(group, 3 * width),
            wide_like(2 * rows, model),
            low_like(2 * rows, model),
            wide_like(1, 3 * width),
        ],
        flops=2 * group * model * 3 * width,
    )
    norm1_sum = sum_rows(norm1_keep, norm1_send)
    share_rows = (parts * shard + shard * model // (3 * width)) // 2
    kept_share, sent_share = local_call(
        functools.partial(projection_grad_kernel, parts, depth, halves),
        (meta, norm1_all, after(kvq_grad, norm1_sum[1]), out_grad),
        [wide_like(depth, share_rows, 3 * width), low_like(depth, share_rows, 3 * width)],
        [
            pltpu.VMEM((model, 3 * width), WIDE),
            pltpu.VMEM((shard * model // (3 * width), 3 * width), WIDE),
        ],
        flops=2 * group * model * 3 * width,
    )
    input_part, sums = local_call(
        functools.partial(first_norm_grad_kernel, parts),
        (
            meta, after(norm1_sum[0], kept_share), *norm1_sum[1:], token_rows, vectors, mixed_part,
            sums, kvq_bias, up_bias,
        ),
        [low_like(rows, model), wide_like(8, model)],
    )

    input_rows = transpose_homes(input_part)
    if halves:
        shape = (share_rows + 16, 3 * width)
        share_keep, *share_sends = local_call(
            fold_share_kernel,
            (meta, after(kept_share, *half_pieces[:-1]), shift(sent_share, "ctx", 1), sums),
            [wide_like(*shape)] + [low_like(*shape)] * (depth - 1),
            [pltpu.VMEM((16, 3 * width), WIDE)],
        )
        share_pieces = send_pieces(share_sends, "fsdp")
        mine_half = sum_all(after(half_keep, share_pieces[0]), half_pieces).astype(LOW)
        feed_totals = (mine_half, shift(mine_half, "ctx", 1))
        mine_share = sum_all(share_keep, share_pieces).astype(LOW)
        shares = (mine_share, shift(after(mine_share, input_rows), "ctx", 1))
    else:
        share_pieces = []
        feed_totals = direct_totals(kept_half, sent_half[0])
        shares = (
            *direct_totals(kept_share, sent_share), sum_replicas(sum_doubling(sums, "fsdp"))
        )
    *totals, out_total, down_total, vector_part = local_call(
        functools.partial(unfold_kernel, parts, halves),
        (meta, *shares, *feed_totals),
        [low_like(shard + 16, padded + hidden_part)] * parts
        + [wide_like(shard, model), wide_like(hidden_shard, model), wide_like(16, 3 * width)],
        [pltpu.VMEM((shard * model // (3 * width), 3 * width), WIDE)],
    )
    qkv_total, up_total, vector_total = local_call(
        functools.partial(join_kernel, parts, width),
        (meta, totals[0], *send_pieces(totals[1:], "dp")),
        [
            wide_like(shard, 3 * model),
            wide_like(shard, parts * hidden_part),
            wide_like(16, 3 * width),
        ],
    )
    delta = row_sum(*fed_sum) + vectors[5:6] + attended
    delta = after(delta.astype(LOW), shares[1])
    output = tokens[0] + transpose_homes(delta).astype(WIDE)
    input_grad = cotangent[0] + input_rows.astype(WIDE)

    def vector_at(source, row, start, size):
        late = start >= 3 * width
        count = 8 if row == 0 else 1
        at = (row + jnp.where(late, 8, 0), start - jnp.where(late, 3 * width, 0))
        return lax.dynamic_slice(source, at, (count, size))

    owned = vector_at(vector_total, 0, (mine * depth + deep) * shard, shard)
    value_bias = vector_at(vector_part, 6, width + deep * shard, shard)[0]
    query_bias = vector_at(vector_part, 6, 2 * width + deep * shard, shard)[0]
    inner_bias = vector_at(vector_part, 7, deep * hidden_shard, hidden_shard)[0]

    return (
        output[None],
        input_grad[None],
        owned[0],
        owned[1],
        qkv_total,
        query_bias,
        value_bias,
        out_total,
        owned[4],
        owned[2],
        owned[3],
        up_total,
        inner_bias,
        down_total,
        owned[5],
    )


def solution(mesh):
    rows = P("dp", ("ctx", "fsdp"), None)
    vector = P(("dp", "fsdp"))
    matrix = P(("dp", "fsdp"), None)
    parameters = (
        vector, vector, matrix, vector, vector, matrix, vector, vector, vector, matrix, vector,
        matrix, vector,
    )
    return jax.shard_map(
        local,
        mesh=mesh,
        in_specs=(rows, rows) + parameters,
        out_specs=(rows, rows) + parameters,
        check_vma=False,
    )
```

```python
import functools

import jax
import jax.numpy as jnp
from jax import lax
from jax.experimental import pallas as pl
from jax.experimental.pallas import tpu as pltpu
from jax.sharding import PartitionSpec as P

HEAD_DIM = 64
EPSILON = 1e-05
SCALE = HEAD_DIM ** (-0.5)
MASKED = -1e30
CHUNK = 64
HURRY = 20
VMEM_BYTES = 16 * 1024 * 1024
GELU_SCALE = 0.7978845608
GELU_CUBE = 0.044715
LOW = jnp.bfloat16
WIDE = jnp.float32


def swap(value, axis, bit):
    count = lax.axis_size(axis)
    return lax.ppermute(value, axis, [(at, at ^ bit) for at in range(count)])


def shift(value, axis, by):
    count = lax.axis_size(axis)
    return lax.ppermute(value, axis, [(at, (at + by) % count) for at in range(count)])


def transpose_homes(value):
    side = lax.axis_size("dp")
    pairs = [(a * side + b, b * side + a) for a in range(side) for b in range(side)]
    return lax.ppermute(value, ("dp", "fsdp"), pairs)


def after(value, *others):
    return lax.optimization_barrier((value,) + others)[0]


def gather_pieces(block, *before_last):
    pieces = [block]
    count = lax.axis_size("dp")
    for slot in range(1, count):
        low_bit = slot & -slot
        source = pieces[slot ^ low_bit]
        if before_last and slot == count - 1:
            source = after(source, *before_last)
        pieces.append(swap(source, "dp", low_bit))
    return pieces


def send_pieces(sends, axis):
    return [swap(send, axis, slot) for slot, send in enumerate(sends, 1)]


def sum_rows(keep, send):
    assert lax.axis_size("dp") == 4
    near = swap(send, "dp", 1)
    rows = keep.shape[0] // 2
    far = swap((keep[rows:] + near[rows:].astype(WIDE)).astype(LOW), "dp", 2)
    return keep, near, far


def gather_direct(block, axis):
    return [block] + [swap(block, axis, slot) for slot in range(1, lax.axis_size(axis))]


def sum_doubling(value, axis):
    bit = 1
    while bit < lax.axis_size(axis):
        value = value + swap(value, axis, bit)
        bit *= 2
    return value


def sum_all(kept, arrived):
    total = kept
    for piece in arrived:
        total = total + piece.astype(WIDE)
    return total


def sum_replicas(value):
    if lax.axis_size("ctx") == 2:
        return value.astype(WIDE) + shift(value, "ctx", 1).astype(WIDE)
    return jnp.sum(lax.all_gather(value, "ctx").astype(WIDE), axis=0)


def matmul_nt(left, right):
    return lax.dot_general(left, right, (((1,), (1,)), ((), ())), preferred_element_type=WIDE)


def matmul_nn(left, right):
    return lax.dot_general(left, right, (((1,), (0,)), ((), ())), preferred_element_type=WIDE)


def matmul_tn(left, right):
    return lax.dot_general(left, right, (((0,), (0,)), ((), ())), preferred_element_type=WIDE)


def visible_block(place_ref, start, block_rows, columns):
    slot = start // block_rows
    query_pos = place_ref[slot] * block_rows + start % block_rows
    query_pos = query_pos + lax.broadcasted_iota(jnp.int32, (CHUNK, columns), 0)
    lane = lax.broadcasted_iota(jnp.int32, (CHUNK, columns), 1)
    key_pos = lane
    for at in range(columns // block_rows):
        inside = (lane >= at * block_rows) & (lane < (at + 1) * block_rows)
        key_pos = jnp.where(inside, place_ref[at] * block_rows + lane - at * block_rows, key_pos)
    return key_pos <= query_pos


def columns_of(head):
    return slice(head * HEAD_DIM, (head + 1) * HEAD_DIM)


def own_forward(heads, block_rows, place_ref, kvq_ref, acc_ref, stat_ref, score, prob):
    width = heads * HEAD_DIM
    rows = kvq_ref.shape[0]
    for head in range(heads):
        query = kvq_ref[:, 2 * width + head * HEAD_DIM : 2 * width + (head + 1) * HEAD_DIM]
        score[...] = matmul_nt(query, kvq_ref[:, columns_of(head)])

        def chunk(step, carry):
            start = pl.multiple_of(step * CHUNK, CHUNK)
            seen = visible_block(place_ref, start, block_rows, rows)
            scores = jnp.where(seen, score[pl.ds(start, CHUNK), :] * SCALE, MASKED)
            highest = jnp.max(scores, axis=1, keepdims=True)
            weight = jnp.exp(scores - highest)
            stat_ref[pl.ds(start, CHUNK), head : head + 1] = highest
            stat_ref[pl.ds(start, CHUNK), heads + head : heads + head + 1] = jnp.sum(
                weight, axis=1, keepdims=True
            )
            prob[pl.ds(start, CHUNK), :] = weight.astype(LOW)
            return carry

        lax.fori_loop(0, rows // CHUNK, chunk, 0)
        value = kvq_ref[:, width + head * HEAD_DIM : width + (head + 1) * HEAD_DIM]
        acc_ref[:, columns_of(head)] = matmul_nn(prob[...], value)


def earlier_forward(
    heads, slots, place_ref, kvq_ref, kv_ref, acc_in, stat_in, acc_ref, low_ref, stat_ref, score,
    prob, fade
):
    width = heads * HEAD_DIM
    rows = kvq_ref.shape[0]
    acc_ref[...] = acc_in[...]
    stat_ref[...] = stat_in[...]
    for piece in range(kv_ref.shape[0]):

        @pl.when(place_ref[slots] > piece)
        def _visit(piece=piece):
            for head in range(heads):
                query = kvq_ref[:, 2 * width + head * HEAD_DIM : 2 * width + (head + 1) * HEAD_DIM]
                score[...] = matmul_nt(query, kv_ref[piece, :, columns_of(head)])

                def chunk(step, carry):
                    here = pl.ds(pl.multiple_of(step * CHUNK, CHUNK), CHUNK)
                    scores = score[here, :] * SCALE
                    old = stat_ref[here, head : head + 1]
                    highest = jnp.maximum(old, jnp.max(scores, axis=1, keepdims=True))
                    weight = jnp.exp(scores - highest)
                    fading = jnp.exp(old - highest)
                    stat_ref[here, head : head + 1] = highest
                    total = stat_ref[here, heads + head : heads + head + 1]
                    stat_ref[here, heads + head : heads + head + 1] = total * fading + jnp.sum(
                        weight, axis=1, keepdims=True
                    )
                    fade[here, :] = jnp.broadcast_to(fading, (CHUNK, HEAD_DIM))
                    prob[here, :] = weight.astype(LOW)
                    return carry

                lax.fori_loop(0, rows // CHUNK, chunk, 0)
                value = kv_ref[piece, :, width + head * HEAD_DIM : width + (head + 1) * HEAD_DIM]
                acc_ref[:, columns_of(head)] = acc_ref[:, columns_of(head)] * fade[
                    ...
                ] + matmul_nn(prob[...], value)

    for head in range(heads):
        total = stat_ref[:, heads + head : heads + head + 1]
        context = acc_ref[:, columns_of(head)] / total
        acc_ref[:, columns_of(head)] = context
        low_ref[:, columns_of(head)] = context.astype(LOW)
        stat_ref[:, head : head + 1] = stat_ref[:, head : head + 1] + jnp.log(total)


def score_grads(here, seen, head, total, delta, score, dots, prob, grad):
    scores = score[here, :] * SCALE
    weight = jnp.exp(scores - total)
    if seen is not None:
        weight = jnp.where(seen, weight, 0.0)
    prob[here, :] = weight.astype(LOW)
    grad[here, :] = (weight * (dots[here, :] - delta) * SCALE).astype(LOW)


def delta_of(here, head, context_ref, ctx_grad_ref):
    product = context_ref[here, columns_of(head)] * ctx_grad_ref[here, columns_of(head)].astype(WIDE)
    return jnp.sum(product, axis=1, keepdims=True)


def earlier_backward(
    heads, slots, place_ref, kvq_ref, kv_ref, ctx_grad_ref, context_ref, stat_ref, query_grad_ref,
    kv_grad_ref, score, dots, prob, grad
):
    width = heads * HEAD_DIM
    rows = kvq_ref.shape[0]
    query_grad_ref[...] = jnp.zeros_like(query_grad_ref)
    for piece in range(kv_ref.shape[0]):

        @pl.when(place_ref[slots] <= piece)
        def _skip(piece=piece):
            kv_grad_ref[piece] = jnp.zeros(kv_grad_ref.shape[1:], kv_grad_ref.dtype)

        @pl.when(place_ref[slots] > piece)
        def _visit(piece=piece):
            for head in range(heads):
                query = kvq_ref[:, 2 * width + head * HEAD_DIM : 2 * width + (head + 1) * HEAD_DIM]
                value_at = slice(width + head * HEAD_DIM, width + (head + 1) * HEAD_DIM)
                key = kv_ref[piece, :, columns_of(head)]
                out_grad = ctx_grad_ref[:, columns_of(head)]
                score[...] = matmul_nt(query, key)
                dots[...] = matmul_nt(out_grad, kv_ref[piece, :, value_at])

                def chunk(step, carry):
                    here = pl.ds(pl.multiple_of(step * CHUNK, CHUNK), CHUNK)
                    total = stat_ref[here, head : head + 1]
                    delta = delta_of(here, head, context_ref, ctx_grad_ref)
                    score_grads(here, None, head, total, delta, score, dots, prob, grad)
                    return carry

                lax.fori_loop(0, rows // CHUNK, chunk, 0)
                kv_grad_ref[piece, :, columns_of(head)] = matmul_tn(grad[...], query).astype(LOW)
                kv_grad_ref[piece, :, value_at] = matmul_tn(prob[...], out_grad).astype(LOW)
                query_grad_ref[:, columns_of(head)] += matmul_nn(grad[...], key)


def own_backward(
    heads, block_rows, place_ref, kvq_ref, ctx_grad_ref, context_ref, stat_ref, query_grad_in,
    grad_ref, score, dots, prob, grad
):
    width = heads * HEAD_DIM
    rows = kvq_ref.shape[0]
    for head in range(heads):
        query_at = slice(2 * width + head * HEAD_DIM, 2 * width + (head + 1) * HEAD_DIM)
        value_at = slice(width + head * HEAD_DIM, width + (head + 1) * HEAD_DIM)
        query = kvq_ref[:, query_at]
        key = kvq_ref[:, columns_of(head)]
        out_grad = ctx_grad_ref[:, columns_of(head)]
        score[...] = matmul_nt(query, key)
        dots[...] = matmul_nt(out_grad, kvq_ref[:, value_at])

        def chunk(step, carry):
            start = pl.multiple_of(step * CHUNK, CHUNK)
            here = pl.ds(start, CHUNK)
            seen = visible_block(place_ref, start, block_rows, rows)
            total = stat_ref[here, head : head + 1]
            delta = delta_of(here, head, context_ref, ctx_grad_ref)
            score_grads(here, seen, head, total, delta, score, dots, prob, grad)
            return carry

        lax.fori_loop(0, rows // CHUNK, chunk, 0)
        grad_ref[:, columns_of(head)] = matmul_tn(grad[...], query)
        grad_ref[:, value_at] = matmul_tn(prob[...], out_grad)
        grad_ref[:, query_at] = query_grad_in[:, columns_of(head)] + matmul_nn(grad[...], key)


def normalize(values):
    centered = values - jnp.mean(values, axis=-1, keepdims=True)
    spread = jnp.mean(centered * centered, axis=-1, keepdims=True)
    inverse = lax.rsqrt(spread + EPSILON)
    return centered * inverse, inverse


def normalize_back(grad, gain, hat, inverse):
    scaled = grad * gain
    mean_scaled = jnp.mean(scaled, axis=-1, keepdims=True)
    mean_product = jnp.mean(scaled * hat, axis=-1, keepdims=True)
    part = inverse * (scaled - mean_scaled - hat * mean_product)
    gain_grad = jnp.sum(grad * hat, axis=0, keepdims=True)
    return part, gain_grad, jnp.sum(grad, axis=0, keepdims=True)


def take(refs, *counts):
    groups, at = [], 0
    for count in counts:
        if count is None:
            groups.append(refs[at])
            at += 1
        else:
            groups.append(refs[at : at + count])
            at += count
    return groups


def place_shards(meta_ref, parts, pieces, out_ref):
    rows = pieces[0].shape[0]
    for deep, piece in enumerate(pieces):
        start = pl.multiple_of((meta_ref[parts + 1] ^ deep) * rows, 16)
        out_ref[pl.ds(start, rows), :] = piece[...]


def stack_rows(pieces, out_ref):
    rows = pieces[0].shape[0]
    for slot, piece in enumerate(pieces):
        out_ref[slot * rows : (slot + 1) * rows, :] = piece[...]


def emit_rows(partial, keep_ref, send_ref):
    rows = keep_ref.shape[0] // 2
    for pair in range(2):
        here = slice(pair * rows, (pair + 1) * rows)
        keep_ref[here, :] = partial[2 * pair * rows : (2 * pair + 1) * rows]
        send_ref[here, :] = partial[(2 * pair + 1) * rows : (2 * pair + 2) * rows].astype(LOW)


def row_sum(keep, near, far):
    rows = far.shape[0]
    return keep[:rows, :] + near[:rows, :].astype(WIDE) + far[...].astype(WIDE)


def emit_blocks(meta_ref, parts, depth, whole_ref, keep_ref, send_refs):
    rows = keep_ref.shape[1]
    for deep in range(depth):
        member = meta_ref[parts + 1] ^ deep
        for slot in range(parts):
            start = pl.multiple_of((meta_ref[slot] * depth + member) * rows, 16)
            block = whole_ref[pl.ds(start, rows), :]
            if deep:
                send_refs[deep - 1][slot] = block.astype(LOW)
            else:
                keep_ref[slot] = block


def emit_shards(meta_ref, parts, whole_ref, keep_ref, send_refs):
    rows = keep_ref.shape[0]
    for deep in range(len(send_refs) + 1):
        start = pl.multiple_of((meta_ref[parts + 1] ^ deep) * rows, 16)
        block = whole_ref[pl.ds(start, rows), :]
        if deep:
            send_refs[deep - 1][...] = block.astype(LOW)
        else:
            keep_ref[...] = block


def stack_kernel(parts, depth, halves, meta_ref, *refs):
    split, down_weight, out_weight, kvq_own, kvq_other, feed_own, feed_other, vectors, folded = (
        take(refs, parts, *([None] * 8))
    )
    columns = kvq_own.shape[1]
    shard = split[0].shape[0]
    model = vectors.shape[1]
    width = columns // 3
    hidden_shard = down_weight.shape[0]
    member = meta_ref[parts + 1]

    def placed(slot, start):
        rows = split[slot][:, columns : -feed_own.shape[1]]
        row = lax.broadcasted_iota(jnp.int32, (rows.shape[1], model), 0)
        column = lax.broadcasted_iota(jnp.int32, (rows.shape[1], model), 1)
        chosen = jnp.where((column == start + row) & (row < shard), 1.0, 0.0)
        return matmul_nn(rows, chosen.astype(LOW))

    whole = sum(placed(slot, (meta_ref[slot] * depth + member) * shard) for slot in range(parts))
    vectors[...] = jnp.zeros_like(vectors)
    vectors[0:6, :] = whole[0:6]
    vectors[6:7, :] = (
        placed(0, width + member * shard)[7:8] + placed(0, 2 * width + member * shard)[6:7]
    )
    vectors[7:8, :] = sum(
        placed(0, member * hidden_shard + at * shard)[8 + at : 9 + at]
        for at in range(hidden_shard // shard)
    )
    vectors[8:16, : model - columns] = vectors[0:8, columns:]
    rest = model - columns
    folded[:shard, :] = out_weight[:, :columns]
    for at in range(columns // rest):
        folded[shard:, at * rest : (at + 1) * rest] = out_weight[at * 16 : (at + 1) * 16, columns:]
    slots = parts // 2
    extra = folded.shape[0] // 2

    def kvq(half, out):
        for slot in range(slots):
            out[slot * shard : (slot + 1) * shard, :] = split[half * slots + slot][:, :columns]
        start = slots * shard
        out[start : start + extra, :] = folded[half * extra : (half + 1) * extra, :].astype(LOW)
        out[start + extra :, :] = vectors[:, :columns].astype(LOW)

    def feed(half, out):
        if half:
            out[...] = down_weight[...].astype(LOW)
        else:
            for slot in range(parts):
                out[slot * shard : (slot + 1) * shard, :] = split[slot][:, -out.shape[1] :]

    def emit(first):
        kvq(first, kvq_own)
        kvq(1 - first, kvq_other)
        feed(first, feed_own)
        feed(1 - first, feed_other)

    if halves:
        pl.when(meta_ref[parts] == 0)(lambda: emit(0))
        pl.when(meta_ref[parts] != 0)(lambda: emit(1))
    else:
        emit(0)


def split_kernel(parts, width, meta_ref, qkv_ref, up_ref, *refs):
    vectors, outs, packed = take(refs, None, parts, None)
    model = parts * width
    shard = qkv_ref.shape[0]
    packed[...] = jnp.zeros_like(packed)
    values = vectors[...].reshape(1, vectors.shape[0])
    for row in range(vectors.shape[0] // shard):
        packed[row : row + 1, :shard] = values[:, row * shard : (row + 1) * shard]
    part = up_ref.shape[1] // parts
    for case in range(parts):

        @pl.when(meta_ref[0] == case)
        def _case(case=case):
            for slot in range(parts):
                owner = case ^ slot
                for at, first in enumerate((model, 2 * model, 0)):
                    start = first + owner * width
                    outs[slot][:, at * width : (at + 1) * width] = qkv_ref[
                        :, start : start + width
                    ].astype(LOW)
                outs[slot][:, 3 * width : -part] = packed[...].astype(LOW)
                outs[slot][:, -part:] = up_ref[:, owner * part : (owner + 1) * part].astype(LOW)


def join_kernel(parts, width, meta_ref, *refs):
    pieces, out_ref, up_ref, vectors = take(refs, parts, None, None, None)
    model = parts * width
    shard = out_ref.shape[0]
    hidden = up_ref.shape[1] // parts
    for case in range(parts):

        @pl.when(meta_ref[0] == case)
        def _case(case=case):
            for slot in range(parts):
                owner = case ^ slot
                for at, first in enumerate((model, 2 * model, 0)):
                    start = first + owner * width
                    out_ref[:, start : start + width] = pieces[slot][
                        :shard, at * width : (at + 1) * width
                    ].astype(WIDE)
                up_ref[:, owner * hidden : (owner + 1) * hidden] = pieces[slot][
                    :shard, -hidden:
                ].astype(WIDE)

    vectors[...] = sum(piece[shard:, : vectors.shape[1]].astype(WIDE) for piece in pieces)


def in_order(halves, parts, meta_ref, place, own, other):
    if halves:
        pl.when(meta_ref[parts] == 0)(lambda: place(own, other))
        pl.when(meta_ref[parts] != 0)(lambda: place(other, own))
    else:
        place(own, other)


def project_kernel(parts, depth, halves, meta_ref, *refs):
    tokens, own, other, kvq_ref, kv_ref, matrix_ref, norm_ref, vectors_ref = take(
        refs, parts, depth, depth, None, None, None, None, None
    )
    columns = kvq_ref.shape[1]
    rows = tokens[0].shape[0]
    shard = matrix_ref.shape[0] // (parts * depth)
    slots = parts // 2

    def place(*pair):
        for half, pieces in enumerate(pair):
            for deep in range(depth):
                member = meta_ref[parts + 1] ^ deep
                for slot in range(slots):
                    row = (meta_ref[half * slots + slot] * depth + member) * shard
                    matrix_ref[pl.ds(pl.multiple_of(row, 16), shard), :] = pieces[deep][
                        slot * shard : (slot + 1) * shard, :
                    ]

    in_order(halves, parts, meta_ref, place, own, other)
    folded = sum(piece[-16:, :].astype(WIDE) for piece in own)
    vectors_ref[:, :columns] = folded[:8]
    vectors_ref[:, columns:] = folded[8:, : vectors_ref.shape[1] - columns]
    for slot, piece in enumerate(tokens):

        def chunk(step, carry, slot=slot, piece=piece):
            here = pl.multiple_of(step * CHUNK, CHUNK)
            hat, _ = normalize(piece[pl.ds(here, CHUNK), :].astype(WIDE))
            norm_ref[pl.ds(slot * rows + here, CHUNK), :] = (
                hat * vectors_ref[0:1, :] + vectors_ref[1:2, :]
            ).astype(LOW)
            return carry

        lax.fori_loop(0, rows // CHUNK, chunk, 0)
    low = (matmul_nn(norm_ref[...], matrix_ref[...]) + vectors_ref[6:7, :columns]).astype(LOW)
    kvq_ref[...] = low
    kv_ref[...] = low[:, : kv_ref.shape[1]]


def mix_kernel(parts, depth, halves, meta_ref, *refs):
    low, own, other, matrix, keep, send = take(refs, None, depth, depth, None, None, None)
    shard = matrix.shape[0] // depth
    columns = own[0].shape[1]
    rest = matrix.shape[1] - columns
    at_first = parts // 2 * shard
    extra = own[0].shape[0] - at_first - 16

    def place(first, second):
        for deep in range(depth):
            start = pl.multiple_of((meta_ref[parts + 1] ^ deep) * shard, 16)
            split = at_first + shard - extra
            matrix[pl.ds(start, extra), :columns] = first[deep][at_first : at_first + extra, :]
            matrix[pl.ds(start + extra, shard - extra), :columns] = second[deep][
                at_first:split, :
            ]
            for at in range(columns // rest):
                matrix[pl.ds(start + at * 16, 16), columns:] = second[deep][
                    split : split + 16, at * rest : (at + 1) * rest
                ]

    in_order(halves, parts, meta_ref, place, own, other)
    emit_rows(matmul_nn(low[...], matrix[...]), keep, send)


def second_norm_kernel(parts, meta_ref, *refs):
    keep, near, far, tokens, vectors, out, attended_ref = refs
    attended = row_sum(keep, near, far) + vectors[4:5, :]
    attended_ref[...] = attended
    hat, _ = normalize(tokens[...].astype(WIDE) + attended)
    out[...] = (hat * vectors[2:3, :] + vectors[3:4, :]).astype(LOW)


def feed_kernel(parts, depth, halves, meta_ref, *refs):
    (
        norm, branch, own, other, vectors, keep, send, hidden, inner_grad, norm_all, branch_all,
        down_all, up_bias, up_all, inner, grad,
    ) = take(refs, parts, parts, depth, depth, *([None] * 12))

    def place(up, down):
        shard = up_all.shape[0] // (parts * depth)
        for deep in range(depth):
            member = meta_ref[parts + 1] ^ deep
            for slot in range(parts):
                start = pl.multiple_of((meta_ref[slot] * depth + member) * shard, 16)
                up_all[pl.ds(start, shard), :] = up[deep][slot * shard : (slot + 1) * shard, :]
        place_shards(meta_ref, parts, down, down_all)

    if halves:
        pl.when(meta_ref[parts] == 0)(lambda: place(own, other))
        pl.when(meta_ref[parts] != 0)(lambda: place(other, own))
    else:
        place(own, other)
    stack_rows(norm, norm_all)
    stack_rows(branch, branch_all)
    inner[...] = matmul_nn(norm_all[...], up_all[...])
    grad[...] = matmul_nt(branch_all[...], down_all[...])
    up_bias[...] = jnp.zeros_like(up_bias)

    def chunk(step, carry):
        here = pl.ds(pl.multiple_of(step * CHUNK, CHUNK), CHUNK)
        value = inner[here, :] + vectors[7:8, :]
        square = value * value
        bent = jnp.tanh(GELU_SCALE * (value + GELU_CUBE * square * value))
        hidden[here, :] = (0.5 * value * (1.0 + bent)).astype(LOW)
        slope = 0.5 * (1.0 + bent) + 0.5 * value * (1.0 - bent * bent) * GELU_SCALE * (
            1.0 + 3.0 * GELU_CUBE * square
        )
        low = (grad[here, :] * slope).astype(LOW)
        inner_grad[here, :] = low
        up_bias[...] += jnp.sum(low.astype(WIDE), axis=0, keepdims=True)
        return carry

    lax.fori_loop(0, inner.shape[0] // CHUNK, chunk, 0)
    emit_rows(matmul_nt(inner_grad[...], up_all[...]), keep, send)


def feed_grad_kernel(parts, depth, halves, meta_ref, *refs):
    hidden, inner_grad, norm_all, branch_all, down_all, kept, *sent, fed_keep, fed_send, whole = refs
    hidden_shard = hidden.shape[1] // depth
    shard = norm_all.shape[1] // (parts * depth)

    def emit(half, outs):
        for deep in range(depth):
            out = outs[deep * len(outs) // depth].at[deep % (depth // len(outs))]
            member = meta_ref[parts + 1] ^ deep
            if half:
                start = pl.multiple_of(member * hidden_shard, 16)
                out[...] = whole[pl.ds(start, hidden_shard), :].astype(out.dtype)
            else:
                for slot in range(parts):
                    start = pl.multiple_of((meta_ref[slot] * depth + member) * shard, 16)
                    out[slot * shard : (slot + 1) * shard, :] = whole[
                        pl.ds(start, shard), :
                    ].astype(out.dtype)

    for half in range(2):
        if half:
            whole[...] = matmul_tn(hidden[...], branch_all[...])
        else:
            whole[...] = matmul_tn(norm_all[...], inner_grad[...])
        if halves:
            pl.when(meta_ref[parts] == half)(functools.partial(emit, half, [kept]))
            pl.when(meta_ref[parts] != half)(functools.partial(emit, half, sent))
        else:
            emit(half, sent if half else [kept])
    emit_rows(matmul_nn(hidden[...], down_all[...]), fed_keep, fed_send)


def fold_kernel(count, meta_ref, kept_ref, *refs):
    arrived, keep_ref, send_refs = refs[:count], refs[count], refs[count + 1 :]
    depth = kept_ref.shape[0]
    for deep in range(depth):
        piece = arrived[deep * count // depth][deep % (depth // count)].astype(WIDE)
        if deep:
            send_refs[deep - 1][...] = (kept_ref[deep] + piece).astype(LOW)
        else:
            keep_ref[...] = kept_ref[deep] + piece


def second_norm_grad_kernel(parts, meta_ref, *refs):
    keep, near, far, tokens, attended, branch, vectors, attn_grad, mixed_part, sums = refs
    grad = row_sum(keep, near, far)
    hat, inverse = normalize(tokens[...].astype(WIDE) + attended[...])
    part, gain_grad, bias_grad = normalize_back(grad, vectors[2:3, :], hat, inverse)
    mixed_part[...] = part
    branch_rows = branch[...].astype(WIDE)
    low = (branch_rows + part).astype(LOW)
    attn_grad[...] = low
    sums[...] = jnp.zeros_like(sums)
    sums[2:3, :] = gain_grad
    sums[3:4, :] = bias_grad
    sums[4:5, :] = jnp.sum(low.astype(WIDE), axis=0, keepdims=True)
    sums[5:6, :] = jnp.sum(branch_rows, axis=0, keepdims=True)


def context_grad_kernel(parts, heads, meta_ref, *refs):
    (
        attn, matrix, kvq, kv, context, stat, ctx_grad, attn_all, query_grad, kv_grad, score, dots,
        prob, grad,
    ) = take(refs, parts, *([None] * 13))
    stack_rows(attn, attn_all)
    ctx_grad[...] = matmul_nt(attn_all[...], matrix[...]).astype(LOW)
    earlier_backward(
        heads, parts, meta_ref, kvq, kv, ctx_grad, context, stat, query_grad, kv_grad, score, dots,
        prob, grad,
    )


def own_grad_kernel(parts, depth, heads, rows, meta_ref, *refs):
    (
        kvq, ctx_grad, context, stat, query_grad, low, attn_all, kvq_grad, out_grad, score, dots,
        prob, grad,
    ) = refs
    own_backward(
        heads, rows, meta_ref, kvq, ctx_grad, context, stat, query_grad, kvq_grad, score, dots,
        prob, grad,
    )
    out_grad[...] = matmul_tn(low[...], attn_all[...])


def projection_back_kernel(parts, meta_ref, *refs):
    own, arrived, matrix, kvq_grad, keep, send, bias = refs
    kv_width = arrived.shape[2]
    total = own[:, :kv_width]
    for piece in range(arrived.shape[0]):
        total = total + arrived[piece].astype(WIDE)
    kvq_grad[:, :kv_width] = total.astype(LOW)
    kvq_grad[:, kv_width:] = own[:, kv_width:].astype(LOW)
    emit_rows(matmul_nt(kvq_grad[...], matrix[...]), keep, send)
    bias[...] = jnp.sum(kvq_grad[...].astype(WIDE), axis=0, keepdims=True)


def projection_grad_kernel(parts, depth, halves, meta_ref, *refs):
    norm, kvq_grad, out_grad, kept, sent, whole, folded = refs
    columns = kvq_grad.shape[1]
    model = norm.shape[1]
    shard = model // (parts * depth)
    rest = model - columns
    slots = parts // 2
    extra = kept.shape[1] - slots * shard
    whole[...] = matmul_tn(norm[...], kvq_grad[...])
    sent[:, kept.shape[1] :] = jnp.zeros_like(sent[:, kept.shape[1] :])

    def emit(half, out):
        for deep in range(depth):
            member = meta_ref[parts + 1] ^ deep
            for slot in range(slots):
                row = (meta_ref[half * slots + slot] * depth + member) * shard
                out[deep, slot * shard : (slot + 1) * shard] = whole[
                    pl.ds(pl.multiple_of(row, 16), shard), :
                ].astype(out.dtype)
            start = pl.multiple_of(member * shard, 16)
            folded[:shard, :] = out_grad[pl.ds(start, shard), :columns]
            for at in range(columns // rest):
                piece = out_grad[pl.ds(start + at * 16, 16), columns:]
                folded[shard:, at * rest : (at + 1) * rest] = piece
            first = slots * shard
            out[deep, first : first + extra] = folded[half * extra : (half + 1) * extra, :].astype(
                out.dtype
            )

    for half in range(2):
        if halves:
            pl.when(meta_ref[parts] == half)(functools.partial(emit, half, kept))
            pl.when(meta_ref[parts] != half)(functools.partial(emit, half, sent))
        else:
            emit(half, sent if half else kept)


def fold_vectors(sums, folded):
    rest = sums.shape[1] - folded.shape[1]
    folded[...] = jnp.zeros_like(folded)
    folded[0:8, :] = sums[:, : folded.shape[1]]
    folded[8:16, :rest] = sums[:, folded.shape[1] :]


def fold_share_kernel(meta_ref, kept, arrived, sums, keep, *refs):
    sends, folded = refs[:-1], refs[-1]
    rows = kept.shape[1]
    fold_vectors(sums, folded)
    keep[:rows, :] = kept[0] + arrived[0, :rows].astype(WIDE)
    keep[rows:, :] = folded[...]
    for deep, send in enumerate(sends, 1):
        send[:rows, :] = (kept[deep] + arrived[deep, :rows].astype(WIDE)).astype(LOW)
        send[rows:, :] = folded[...].astype(LOW)


def unfold_kernel(parts, halves, meta_ref, mine, arrived, *refs):
    sums, mine_feed, other_feed, pieces, out_ref, down_ref, vectors, folded = take(
        refs, 0 if halves else 1, None, None, parts, None, None, None, None
    )
    shard, columns = pieces[0].shape[0] - 16, vectors.shape[1]
    hidden = mine_feed.shape[1]
    rest = out_ref.shape[1] - columns
    slots = parts // 2
    extra = folded.shape[0] // 2

    def unfold(half, ref):
        for slot in range(slots):
            pieces[half * slots + slot][:shard, :columns] = ref[
                slot * shard : (slot + 1) * shard, :
            ].astype(LOW)
        start = slots * shard
        folded[half * extra : (half + 1) * extra, :] = ref[start : start + extra, :].astype(WIDE)

    def feeds(up, down):
        for slot in range(parts):
            pieces[slot][:shard, -hidden:] = up[slot * shard : (slot + 1) * shard, :].astype(LOW)
        down_ref[...] = down[...].astype(WIDE)

    if halves:
        first = meta_ref[parts] == 0
        pl.when(first)(lambda: feeds(mine_feed, other_feed))
        pl.when(jnp.logical_not(first))(lambda: feeds(other_feed, mine_feed))
        for half in range(2):
            pl.when(first)(functools.partial(unfold, half, arrived if half else mine))
            pl.when(jnp.logical_not(first))(
                functools.partial(unfold, half, mine if half else arrived)
            )
        start = slots * shard + extra
        vectors[...] = mine[start:, :].astype(WIDE) + arrived[start:, :].astype(WIDE)
    else:
        feeds(mine_feed, other_feed)
        unfold(0, mine)
        unfold(1, arrived)
        fold_vectors(sums[0], vectors)
    for piece in pieces:
        piece[shard:, :columns] = vectors[...].astype(LOW)
        piece[shard:, columns:] = jnp.zeros_like(piece[shard:, columns:])
        piece[:shard, columns:-hidden] = jnp.zeros_like(piece[:shard, columns:-hidden])
    out_ref[:, :columns] = folded[:shard, :]
    for at in range(columns // rest):
        out_ref[at * 16 : (at + 1) * 16, columns:] = folded[shard:, at * rest : (at + 1) * rest]


def first_norm_grad_kernel(parts, meta_ref, *refs):
    keep, near, far, tokens, vectors, mixed_part, sums_in, kvq_bias, up_bias, out, sums = refs
    grad = row_sum(keep, near, far)
    hat, inverse = normalize(tokens[...].astype(WIDE))
    part, gain_grad, bias_grad = normalize_back(grad, vectors[0:1, :], hat, inverse)
    out[...] = (mixed_part[...] + part).astype(LOW)
    sums[...] = sums_in[...]
    sums[0:1, :] = gain_grad
    sums[1:2, :] = bias_grad
    sums[6:7, : kvq_bias.shape[1]] = kvq_bias[...]
    sums[7:8, :] = up_bias[...]


def local_call(kernel, operands, results, scratch=(), flops=0):
    smem = pl.BlockSpec(memory_space=pltpu.SMEM)
    vmem = pl.BlockSpec(memory_space=pltpu.VMEM)
    moved = sum(each.size * each.dtype.itemsize for each in tuple(operands) + tuple(results))
    return pl.pallas_call(
        kernel,
        name=getattr(kernel, "func", kernel).__name__,
        out_shape=tuple(results),
        in_specs=[smem] + [vmem] * (len(operands) - 1),
        out_specs=tuple([vmem] * len(results)),
        scratch_shapes=list(scratch),
        compiler_params=pltpu.CompilerParams(vmem_limit_bytes=VMEM_BYTES),
        cost_estimate=pl.CostEstimate(
            flops=flops // HURRY, bytes_accessed=moved // HURRY, transcendentals=0
        ),
    )(*operands)


def low_like(*shape):
    return jax.ShapeDtypeStruct(shape, LOW)


def wide_like(*shape):
    return jax.ShapeDtypeStruct(shape, WIDE)


def local(
    tokens, cotangent, ln1_gain, ln1_bias, qkv_weight, q_bias, v_bias, out_weight, out_bias,
    ln2_gain, ln2_bias, fc1_weight, fc1_bias, fc2_weight, fc2_bias,
):
    parts = lax.axis_size("dp")
    depth = lax.axis_size("fsdp")
    contexts = lax.axis_size("ctx")
    assert parts == depth
    mine = lax.axis_index("dp")
    deep = lax.axis_index("fsdp")
    rows, model = tokens.shape[1:]
    shard = ln1_gain.shape[0]
    heads = model // HEAD_DIM // parts
    width = heads * HEAD_DIM
    hidden_shard = fc1_bias.shape[0]
    hidden_part = hidden_shard * depth
    group = parts * rows
    meta = jnp.stack(
        [mine ^ slot for slot in range(parts)] + [lax.axis_index("ctx"), deep]
    ).astype(jnp.int32)

    halves = contexts == 2
    padded = -(-3 * width // 128) * 128
    split = local_call(
        functools.partial(split_kernel, parts, width),
        (
            meta, qkv_weight, fc1_weight,
            jnp.concatenate(
                [
                    ln1_gain, ln1_bias, ln2_gain, ln2_bias, out_bias, fc2_bias, q_bias, v_bias,
                    fc1_bias,
                ]
            ),
        ),
        [low_like(shard, padded + hidden_part)] * parts,
        [pltpu.VMEM((shard, padded - 3 * width), WIDE)],
    )
    split_arrived = send_pieces(split[1:], "dp")
    folded_rows = shard * model // (3 * width)
    half_rows = parts // 2 * shard + folded_rows // 2 + 16
    kvq_mine, kvq_theirs, feed_mine, feed_theirs = local_call(
        functools.partial(stack_kernel, parts, depth, halves),
        (meta, split[0], *split_arrived, fc2_weight, out_weight),
        [low_like(half_rows, 3 * width)] * 2 + [low_like(hidden_shard, model)] * 2,
        [pltpu.VMEM((16, model), WIDE), pltpu.VMEM((folded_rows, 3 * width), WIDE)],
    )
    kvq_own = gather_direct(kvq_mine, "fsdp")
    if halves:
        kvq_other = [kvq_theirs] + [shift(piece, "ctx", 1) for piece in kvq_own[1:]]
    else:
        kvq_other = gather_direct(kvq_theirs, "fsdp")

    token_rows = transpose_homes(after(tokens[0].astype(LOW), *split_arrived))
    pieces = gather_pieces(after(token_rows, kvq_own[-1]), *kvq_own[1:])

    kvq, kv, kvq_matrix, norm1_all, vectors = local_call(
        functools.partial(project_kernel, parts, depth, halves),
        (meta, *pieces, *kvq_own, *kvq_other),
        [
            low_like(group, 3 * width),
            low_like(group, 2 * width),
            low_like(model, 3 * width),
            low_like(group, model),
            wide_like(8, model),
        ],
        flops=2 * group * model * 3 * width,
    )
    kv_earlier = jnp.stack([shift(kv, "ctx", by) for by in range(1, contexts)])

    if halves:
        own_half = gather_direct(after(feed_mine, *kvq_own[1:]), "fsdp")
    else:
        own_half = gather_direct(feed_mine, "fsdp")
        other_half = gather_direct(feed_theirs, "fsdp")
    grad_rows = transpose_homes(after(cotangent[0].astype(LOW), own_half[1]))
    branch_pieces = gather_pieces(grad_rows)

    score_flops = 2 * group * group * width
    wide_square = pltpu.VMEM((group, group), WIDE)
    low_square = pltpu.VMEM((group, group), LOW)
    acc, stat = local_call(
        functools.partial(own_forward, heads, rows),
        (meta, after(kvq, own_half[1])),
        [wide_like(group, width), wide_like(group, 128)],
        [wide_square, low_square],
        flops=2 * score_flops,
    )
    if halves:
        other_half = [feed_theirs, shift(after(own_half[1], acc), "ctx", 1)]
        other_half += [shift(piece, "ctx", 1) for piece in own_half[2:]]
    context, context_low, stat = local_call(
        functools.partial(earlier_forward, heads, parts),
        (meta, kvq, kv_earlier, after(acc, own_half[1]), stat),
        [wide_like(group, width), low_like(group, width), wide_like(group, 128)],
        [wide_square, low_square, pltpu.VMEM((group, HEAD_DIM), WIDE)],
        flops=2 * score_flops,
    )
    out_matrix, attended_keep, attended_send = local_call(
        functools.partial(mix_kernel, parts, depth, halves),
        (meta, after(context_low, *own_half[2:], other_half[1]), *kvq_own, *kvq_other),
        [low_like(width, model), wide_like(2 * rows, model), low_like(2 * rows, model)],
        flops=2 * group * width * model,
    )
    attended_sum = sum_rows(attended_keep, attended_send)
    norm2, attended = local_call(
        functools.partial(second_norm_kernel, parts),
        (meta, *attended_sum, token_rows, vectors),
        [low_like(rows, model), wide_like(rows, model)],
    )

    norm2_pieces = gather_pieces(norm2)
    norm2_keep, norm2_send, *rest = local_call(
        functools.partial(feed_kernel, parts, depth, halves),
        (meta, *norm2_pieces, *branch_pieces, *own_half, *other_half, vectors),
        [wide_like(2 * rows, model), low_like(2 * rows, model)]
        + [low_like(group, hidden_part)] * 2
        + [low_like(group, model)] * 2
        + [low_like(hidden_part, model), wide_like(1, hidden_part)],
        [
            pltpu.VMEM((model, hidden_part), LOW),
            pltpu.VMEM((group, hidden_part), WIDE),
            pltpu.VMEM((group, hidden_part), WIDE),
        ],
        flops=6 * group * model * hidden_part,
    )
    hidden, inner_grad, norm2_all, branch_all, down_matrix, up_bias = rest
    norm2_sum = sum_rows(norm2_keep, norm2_send)
    kept_half, *sent_half, fed_keep, fed_send = local_call(
        functools.partial(feed_grad_kernel, parts, depth, halves),
        (meta, hidden, inner_grad, norm2_all, branch_all, down_matrix),
        [
            wide_like(depth, hidden_shard, model),
            low_like(depth, hidden_shard, model),
            wide_like(2 * rows, model),
            low_like(2 * rows, model),
        ],
        [pltpu.VMEM((max(model, hidden_part), max(model, hidden_part)), WIDE)],
        flops=6 * group * model * hidden_part,
    )
    attn_grad, mixed_part, sums = local_call(
        functools.partial(second_norm_grad_kernel, parts),
        (
            meta, after(norm2_sum[0], fed_keep), *norm2_sum[1:], token_rows, attended, grad_rows,
            vectors,
        ),
        [low_like(rows, model), wide_like(rows, model), wide_like(8, model)],
    )
    attn_pieces = gather_pieces(attn_grad)

    def fold(kept, sent, *later):
        arrived = [shift(sent[0], "ctx", 1)]
        for piece in sent[1:]:
            arrived.append(shift(after(piece, arrived[-1]), "ctx", 1))
        shape = kept.shape[1:]
        keep, *sends = local_call(
            functools.partial(fold_kernel, len(sent)),
            (meta, after(kept, *later), *arrived),
            [wide_like(*shape)] + [low_like(*shape)] * (depth - 1),
        )
        return keep, sends

    def direct_totals(*grads):
        return [
            owner_sum(grad[0].astype(WIDE), send_pieces(list(grad[1:].astype(LOW)), "fsdp"))
            for grad in grads
        ]

    def owner_sum(keep, pieces):
        return sum_replicas(sum_all(keep, pieces).astype(LOW))

    fed_sum = sum_rows(fed_keep, after(fed_send, attn_pieces[-1]))

    ctx_grad, attn_all, query_grad, kv_grad = local_call(
        functools.partial(context_grad_kernel, parts, heads),
        (meta, *attn_pieces, out_matrix, kvq, kv_earlier, context, stat),
        [
            low_like(group, width),
            low_like(group, model),
            wide_like(group, width),
            low_like(*kv_earlier.shape),
        ],
        [wide_square, wide_square, low_square, low_square],
        flops=5 * score_flops,
    )
    if halves:
        half_keep, half_sends = fold(kept_half, sent_half, query_grad)
        farthest = swap(half_sends[-1], "fsdp", depth - 1)
        nearer = [after(send, farthest) for send in half_sends[:-1]]
        half_pieces = send_pieces(nearer, "fsdp") + [farthest]
    else:
        half_pieces = []
    if halves:
        query_grad = after(query_grad, half_keep)
    kv_arrived = jnp.stack(
        [shift(kv_grad[by - 1], "ctx", -by) for by in range(1, contexts)]
    )
    kvq_own, out_grad = local_call(
        functools.partial(own_grad_kernel, parts, depth, heads, rows),
        (meta, kvq, ctx_grad, context, stat, query_grad, context_low, attn_all),
        [wide_like(group, 3 * width), wide_like(width, model)],
        [wide_square, wide_square, low_square, low_square],
        flops=5 * score_flops,
    )
    kvq_grad, norm1_keep, norm1_send, kvq_bias = local_call(
        functools.partial(projection_back_kernel, parts),
        (meta, after(kvq_own, fed_sum[2], *half_pieces[-1:]), kv_arrived, kvq_matrix),
        [
            low_like(group, 3 * width),
            wide_like(2 * rows, model),
            low_like(2 * rows, model),
            wide_like(1, 3 * width),
        ],
        flops=2 * group * model * 3 * width,
    )
    norm1_sum = sum_rows(norm1_keep, norm1_send)
    share_rows = (parts * shard + shard * model // (3 * width)) // 2
    kept_share, sent_share = local_call(
        functools.partial(projection_grad_kernel, parts, depth, halves),
        (meta, norm1_all, after(kvq_grad, norm1_sum[1]), out_grad),
        [wide_like(depth, share_rows, 3 * width), low_like(depth, share_rows + 16, 3 * width)],
        [
            pltpu.VMEM((model, 3 * width), WIDE),
            pltpu.VMEM((shard * model // (3 * width), 3 * width), WIDE),
        ],
        flops=2 * group * model * 3 * width,
    )
    input_part, sums = local_call(
        functools.partial(first_norm_grad_kernel, parts),
        (
            meta, after(norm1_sum[0], kept_share), *norm1_sum[1:], token_rows, vectors, mixed_part,
            sums, kvq_bias, up_bias,
        ),
        [low_like(rows, model), wide_like(8, model)],
    )

    input_rows = transpose_homes(input_part)
    if halves:
        shape = (share_rows + 16, 3 * width)
        share_keep, *share_sends = local_call(
            fold_share_kernel,
            (meta, after(kept_share, *half_pieces[:-1]), shift(sent_share, "ctx", 1), sums),
            [wide_like(*shape)] + [low_like(*shape)] * (depth - 1),
            [pltpu.VMEM((16, 3 * width), WIDE)],
        )
        share_pieces = send_pieces(share_sends, "fsdp")
        mine_half = sum_all(after(half_keep, input_part), half_pieces).astype(LOW)
        feed_totals = (mine_half, shift(mine_half, "ctx", 1))
        mine_share = sum_all(share_keep, share_pieces).astype(LOW)
        shares = (mine_share, shift(after(mine_share, input_rows), "ctx", 1))
    else:
        share_pieces = []
        feed_totals = direct_totals(kept_half, sent_half[0])
        shares = (
            *direct_totals(kept_share, sent_share[:, :share_rows]), sum_replicas(sum_doubling(sums, "fsdp"))
        )
    delta = row_sum(*fed_sum) + vectors[5:6] + attended
    delta_rows = transpose_homes(after(delta.astype(LOW), shares[1]))
    output = tokens[0] + delta_rows.astype(WIDE)
    *totals, out_total, down_total, vector_part = local_call(
        functools.partial(unfold_kernel, parts, halves),
        (meta, *shares, *feed_totals),
        [low_like(shard + 16, padded + hidden_part)] * parts
        + [wide_like(shard, model), wide_like(hidden_shard, model), wide_like(16, 3 * width)],
        [pltpu.VMEM((shard * model // (3 * width), 3 * width), WIDE)],
    )
    qkv_total, up_total, vector_total = local_call(
        functools.partial(join_kernel, parts, width),
        (meta, totals[0], *send_pieces(totals[1:], "dp")),
        [
            wide_like(shard, 3 * model),
            wide_like(shard, parts * hidden_part),
            wide_like(16, 3 * width),
        ],
    )
    input_grad = cotangent[0] + input_rows.astype(WIDE)

    def vector_at(source, row, start, size):
        late = start >= 3 * width
        count = 8 if row == 0 else 1
        at = (row + jnp.where(late, 8, 0), start - jnp.where(late, 3 * width, 0))
        return lax.dynamic_slice(source, at, (count, size))

    owned = vector_at(vector_total, 0, (mine * depth + deep) * shard, shard)
    value_bias = vector_at(vector_part, 6, width + deep * shard, shard)[0]
    query_bias = vector_at(vector_part, 6, 2 * width + deep * shard, shard)[0]
    inner_bias = vector_at(vector_part, 7, deep * hidden_shard, hidden_shard)[0]

    return (
        output[None],
        input_grad[None],
        owned[0],
        owned[1],
        qkv_total,
        query_bias,
        value_bias,
        out_total,
        owned[4],
        owned[2],
        owned[3],
        up_total,
        inner_bias,
        down_total,
        owned[5],
    )


def solution(mesh):
    rows = P("dp", ("ctx", "fsdp"), None)
    vector = P(("dp", "fsdp"))
    matrix = P(("dp", "fsdp"), None)
    parameters = (
        vector, vector, matrix, vector, vector, matrix, vector, vector, vector, matrix, vector,
        matrix, vector,
    )
    return jax.shard_map(
        local,
        mesh=mesh,
        in_specs=(rows, rows) + parameters,
        out_specs=(rows, rows) + parameters,
        check_vma=False,
    )
```

```python
import functools

import jax
import jax.numpy as jnp
from jax import lax
from jax.experimental import pallas as pl
from jax.experimental.pallas import tpu as pltpu
from jax.sharding import PartitionSpec as P

HEAD_DIM = 64
EPSILON = 1e-05
SCALE = HEAD_DIM ** (-0.5)
MASKED = -1e30
CHUNK = 64
HURRY = 20
VMEM_BYTES = 16 * 1024 * 1024
GELU_SCALE = 0.7978845608
GELU_CUBE = 0.044715
LOW = jnp.bfloat16
WIDE = jnp.float32


def swap(value, axis, bit):
    count = lax.axis_size(axis)
    return lax.ppermute(value, axis, [(at, at ^ bit) for at in range(count)])


def shift(value, axis, by):
    count = lax.axis_size(axis)
    return lax.ppermute(value, axis, [(at, (at + by) % count) for at in range(count)])


def transpose_homes(value):
    side = lax.axis_size("dp")
    pairs = [(a * side + b, b * side + a) for a in range(side) for b in range(side)]
    return lax.ppermute(value, ("dp", "fsdp"), pairs)


def after(value, *others):
    return lax.optimization_barrier((value,) + others)[0]


def gather_pieces(block, *before_last):
    pieces = [block]
    count = lax.axis_size("dp")
    for slot in range(1, count):
        low_bit = slot & -slot
        source = pieces[slot ^ low_bit]
        if before_last and slot == count - 1:
            source = after(source, *before_last)
        pieces.append(swap(source, "dp", low_bit))
    return pieces


def send_pieces(sends, axis):
    return [swap(send, axis, slot) for slot, send in enumerate(sends, 1)]


def sum_rows(keep, send):
    assert lax.axis_size("dp") == 4
    near = swap(send, "dp", 1)
    rows = keep.shape[0] // 2
    far = swap((keep[rows:] + near[rows:].astype(WIDE)).astype(LOW), "dp", 2)
    return keep, near, far


def gather_direct(block, axis):
    return [block] + [swap(block, axis, slot) for slot in range(1, lax.axis_size(axis))]


def sum_doubling(value, axis):
    bit = 1
    while bit < lax.axis_size(axis):
        value = value + swap(value, axis, bit)
        bit *= 2
    return value


def sum_all(kept, arrived):
    total = kept
    for piece in arrived:
        total = total + piece.astype(WIDE)
    return total


def sum_replicas(value):
    if lax.axis_size("ctx") == 2:
        return value.astype(WIDE) + shift(value, "ctx", 1).astype(WIDE)
    return jnp.sum(lax.all_gather(value, "ctx").astype(WIDE), axis=0)


def matmul_nt(left, right):
    return lax.dot_general(left, right, (((1,), (1,)), ((), ())), preferred_element_type=WIDE)


def matmul_nn(left, right):
    return lax.dot_general(left, right, (((1,), (0,)), ((), ())), preferred_element_type=WIDE)


def matmul_tn(left, right):
    return lax.dot_general(left, right, (((0,), (0,)), ((), ())), preferred_element_type=WIDE)


def visible_block(place_ref, start, block_rows, columns):
    slot = start // block_rows
    query_pos = place_ref[slot] * block_rows + start % block_rows
    query_pos = query_pos + lax.broadcasted_iota(jnp.int32, (CHUNK, columns), 0)
    lane = lax.broadcasted_iota(jnp.int32, (CHUNK, columns), 1)
    key_pos = lane
    for at in range(columns // block_rows):
        inside = (lane >= at * block_rows) & (lane < (at + 1) * block_rows)
        key_pos = jnp.where(inside, place_ref[at] * block_rows + lane - at * block_rows, key_pos)
    return key_pos <= query_pos


def columns_of(head):
    return slice(head * HEAD_DIM, (head + 1) * HEAD_DIM)


def own_forward(heads, block_rows, place_ref, kvq_ref, acc_ref, stat_ref, score, prob):
    width = heads * HEAD_DIM
    rows = kvq_ref.shape[0]
    for head in range(heads):
        query = kvq_ref[:, 2 * width + head * HEAD_DIM : 2 * width + (head + 1) * HEAD_DIM]
        score[...] = matmul_nt(query, kvq_ref[:, columns_of(head)])

        def chunk(step, carry):
            start = pl.multiple_of(step * CHUNK, CHUNK)
            seen = visible_block(place_ref, start, block_rows, rows)
            scores = jnp.where(seen, score[pl.ds(start, CHUNK), :] * SCALE, MASKED)
            highest = jnp.max(scores, axis=1, keepdims=True)
            weight = jnp.exp(scores - highest)
            stat_ref[pl.ds(start, CHUNK), head : head + 1] = highest
            stat_ref[pl.ds(start, CHUNK), heads + head : heads + head + 1] = jnp.sum(
                weight, axis=1, keepdims=True
            )
            prob[pl.ds(start, CHUNK), :] = weight.astype(LOW)
            return carry

        lax.fori_loop(0, rows // CHUNK, chunk, 0)
        value = kvq_ref[:, width + head * HEAD_DIM : width + (head + 1) * HEAD_DIM]
        acc_ref[:, columns_of(head)] = matmul_nn(prob[...], value)


def earlier_forward(
    heads, slots, place_ref, kvq_ref, kv_ref, acc_in, stat_in, acc_ref, low_ref, stat_ref, score,
    prob, fade
):
    width = heads * HEAD_DIM
    rows = kvq_ref.shape[0]
    acc_ref[...] = acc_in[...]
    stat_ref[...] = stat_in[...]
    for piece in range(kv_ref.shape[0]):

        @pl.when(place_ref[slots] > piece)
        def _visit(piece=piece):
            for head in range(heads):
                query = kvq_ref[:, 2 * width + head * HEAD_DIM : 2 * width + (head + 1) * HEAD_DIM]
                score[...] = matmul_nt(query, kv_ref[piece, :, columns_of(head)])

                def chunk(step, carry):
                    here = pl.ds(pl.multiple_of(step * CHUNK, CHUNK), CHUNK)
                    scores = score[here, :] * SCALE
                    old = stat_ref[here, head : head + 1]
                    highest = jnp.maximum(old, jnp.max(scores, axis=1, keepdims=True))
                    weight = jnp.exp(scores - highest)
                    fading = jnp.exp(old - highest)
                    stat_ref[here, head : head + 1] = highest
                    total = stat_ref[here, heads + head : heads + head + 1]
                    stat_ref[here, heads + head : heads + head + 1] = total * fading + jnp.sum(
                        weight, axis=1, keepdims=True
                    )
                    fade[here, :] = jnp.broadcast_to(fading, (CHUNK, HEAD_DIM))
                    prob[here, :] = weight.astype(LOW)
                    return carry

                lax.fori_loop(0, rows // CHUNK, chunk, 0)
                value = kv_ref[piece, :, width + head * HEAD_DIM : width + (head + 1) * HEAD_DIM]
                acc_ref[:, columns_of(head)] = acc_ref[:, columns_of(head)] * fade[
                    ...
                ] + matmul_nn(prob[...], value)

    for head in range(heads):
        total = stat_ref[:, heads + head : heads + head + 1]
        context = acc_ref[:, columns_of(head)] / total
        acc_ref[:, columns_of(head)] = context
        low_ref[:, columns_of(head)] = context.astype(LOW)
        stat_ref[:, head : head + 1] = stat_ref[:, head : head + 1] + jnp.log(total)


def score_grads(here, seen, head, total, delta, score, dots, prob, grad):
    scores = score[here, :] * SCALE
    weight = jnp.exp(scores - total)
    if seen is not None:
        weight = jnp.where(seen, weight, 0.0)
    prob[here, :] = weight.astype(LOW)
    grad[here, :] = (weight * (dots[here, :] - delta) * SCALE).astype(LOW)


def delta_of(here, head, context_ref, ctx_grad_ref):
    product = context_ref[here, columns_of(head)] * ctx_grad_ref[here, columns_of(head)].astype(WIDE)
    return jnp.sum(product, axis=1, keepdims=True)


def earlier_backward(
    heads, slots, place_ref, kvq_ref, kv_ref, ctx_grad_ref, context_ref, stat_ref, query_grad_ref,
    kv_grad_ref, score, dots, prob, grad
):
    width = heads * HEAD_DIM
    rows = kvq_ref.shape[0]
    query_grad_ref[...] = jnp.zeros_like(query_grad_ref)
    for piece in range(kv_ref.shape[0]):

        @pl.when(place_ref[slots] <= piece)
        def _skip(piece=piece):
            kv_grad_ref[piece] = jnp.zeros(kv_grad_ref.shape[1:], kv_grad_ref.dtype)

        @pl.when(place_ref[slots] > piece)
        def _visit(piece=piece):
            for head in range(heads):
                query = kvq_ref[:, 2 * width + head * HEAD_DIM : 2 * width + (head + 1) * HEAD_DIM]
                value_at = slice(width + head * HEAD_DIM, width + (head + 1) * HEAD_DIM)
                key = kv_ref[piece, :, columns_of(head)]
                out_grad = ctx_grad_ref[:, columns_of(head)]
                score[...] = matmul_nt(query, key)
                dots[...] = matmul_nt(out_grad, kv_ref[piece, :, value_at])

                def chunk(step, carry):
                    here = pl.ds(pl.multiple_of(step * CHUNK, CHUNK), CHUNK)
                    total = stat_ref[here, head : head + 1]
                    delta = delta_of(here, head, context_ref, ctx_grad_ref)
                    score_grads(here, None, head, total, delta, score, dots, prob, grad)
                    return carry

                lax.fori_loop(0, rows // CHUNK, chunk, 0)
                kv_grad_ref[piece, :, columns_of(head)] = matmul_tn(grad[...], query).astype(LOW)
                kv_grad_ref[piece, :, value_at] = matmul_tn(prob[...], out_grad).astype(LOW)
                query_grad_ref[:, columns_of(head)] += matmul_nn(grad[...], key)


def own_backward(
    heads, block_rows, place_ref, kvq_ref, ctx_grad_ref, context_ref, stat_ref, query_grad_in,
    grad_ref, score, dots, prob, grad
):
    width = heads * HEAD_DIM
    rows = kvq_ref.shape[0]
    for head in range(heads):
        query_at = slice(2 * width + head * HEAD_DIM, 2 * width + (head + 1) * HEAD_DIM)
        value_at = slice(width + head * HEAD_DIM, width + (head + 1) * HEAD_DIM)
        query = kvq_ref[:, query_at]
        key = kvq_ref[:, columns_of(head)]
        out_grad = ctx_grad_ref[:, columns_of(head)]
        score[...] = matmul_nt(query, key)
        dots[...] = matmul_nt(out_grad, kvq_ref[:, value_at])

        def chunk(step, carry):
            start = pl.multiple_of(step * CHUNK, CHUNK)
            here = pl.ds(start, CHUNK)
            seen = visible_block(place_ref, start, block_rows, rows)
            total = stat_ref[here, head : head + 1]
            delta = delta_of(here, head, context_ref, ctx_grad_ref)
            score_grads(here, seen, head, total, delta, score, dots, prob, grad)
            return carry

        lax.fori_loop(0, rows // CHUNK, chunk, 0)
        grad_ref[:, columns_of(head)] = matmul_tn(grad[...], query)
        grad_ref[:, value_at] = matmul_tn(prob[...], out_grad)
        grad_ref[:, query_at] = query_grad_in[:, columns_of(head)] + matmul_nn(grad[...], key)


def normalize(values):
    centered = values - jnp.mean(values, axis=-1, keepdims=True)
    spread = jnp.mean(centered * centered, axis=-1, keepdims=True)
    inverse = lax.rsqrt(spread + EPSILON)
    return centered * inverse, inverse


def normalize_back(grad, gain, hat, inverse):
    scaled = grad * gain
    mean_scaled = jnp.mean(scaled, axis=-1, keepdims=True)
    mean_product = jnp.mean(scaled * hat, axis=-1, keepdims=True)
    part = inverse * (scaled - mean_scaled - hat * mean_product)
    gain_grad = jnp.sum(grad * hat, axis=0, keepdims=True)
    return part, gain_grad, jnp.sum(grad, axis=0, keepdims=True)


def take(refs, *counts):
    groups, at = [], 0
    for count in counts:
        if count is None:
            groups.append(refs[at])
            at += 1
        else:
            groups.append(refs[at : at + count])
            at += count
    return groups


def place_shards(meta_ref, parts, pieces, out_ref):
    rows = pieces[0].shape[0]
    for deep, piece in enumerate(pieces):
        start = pl.multiple_of((meta_ref[parts + 1] ^ deep) * rows, 16)
        out_ref[pl.ds(start, rows), :] = piece[...]


def stack_rows(pieces, out_ref):
    rows = pieces[0].shape[0]
    for slot, piece in enumerate(pieces):
        out_ref[slot * rows : (slot + 1) * rows, :] = piece[...]


def emit_rows(partial, keep_ref, send_ref):
    rows = keep_ref.shape[0] // 2
    for pair in range(2):
        here = slice(pair * rows, (pair + 1) * rows)
        keep_ref[here, :] = partial[2 * pair * rows : (2 * pair + 1) * rows]
        send_ref[here, :] = partial[(2 * pair + 1) * rows : (2 * pair + 2) * rows].astype(LOW)


def row_sum(keep, near, far):
    rows = far.shape[0]
    return keep[:rows, :] + near[:rows, :].astype(WIDE) + far[...].astype(WIDE)


def emit_blocks(meta_ref, parts, depth, whole_ref, keep_ref, send_refs):
    rows = keep_ref.shape[1]
    for deep in range(depth):
        member = meta_ref[parts + 1] ^ deep
        for slot in range(parts):
            start = pl.multiple_of((meta_ref[slot] * depth + member) * rows, 16)
            block = whole_ref[pl.ds(start, rows), :]
            if deep:
                send_refs[deep - 1][slot] = block.astype(LOW)
            else:
                keep_ref[slot] = block


def emit_shards(meta_ref, parts, whole_ref, keep_ref, send_refs):
    rows = keep_ref.shape[0]
    for deep in range(len(send_refs) + 1):
        start = pl.multiple_of((meta_ref[parts + 1] ^ deep) * rows, 16)
        block = whole_ref[pl.ds(start, rows), :]
        if deep:
            send_refs[deep - 1][...] = block.astype(LOW)
        else:
            keep_ref[...] = block


def stack_kernel(parts, depth, halves, meta_ref, *refs):
    split, down_weight, out_weight, kvq_own, kvq_other, feed_own, feed_other, vectors, folded = (
        take(refs, parts, *([None] * 8))
    )
    columns = kvq_own.shape[1]
    shard = split[0].shape[0]
    model = vectors.shape[1]
    width = columns // 3
    hidden_shard = down_weight.shape[0]
    member = meta_ref[parts + 1]

    def placed(slot, start):
        rows = split[slot][:, columns : -feed_own.shape[1]]
        row = lax.broadcasted_iota(jnp.int32, (rows.shape[1], model), 0)
        column = lax.broadcasted_iota(jnp.int32, (rows.shape[1], model), 1)
        chosen = jnp.where((column == start + row) & (row < shard), 1.0, 0.0)
        return matmul_nn(rows, chosen.astype(LOW))

    whole = sum(placed(slot, (meta_ref[slot] * depth + member) * shard) for slot in range(parts))
    vectors[...] = jnp.zeros_like(vectors)
    vectors[0:6, :] = whole[0:6]
    vectors[6:7, :] = (
        placed(0, width + member * shard)[7:8] + placed(0, 2 * width + member * shard)[6:7]
    )
    vectors[7:8, :] = sum(
        placed(0, member * hidden_shard + at * shard)[8 + at : 9 + at]
        for at in range(hidden_shard // shard)
    )
    vectors[8:16, : model - columns] = vectors[0:8, columns:]
    rest = model - columns
    folded[:shard, :] = out_weight[:, :columns]
    for at in range(columns // rest):
        folded[shard:, at * rest : (at + 1) * rest] = out_weight[at * 16 : (at + 1) * 16, columns:]
    slots = parts // 2
    extra = folded.shape[0] // 2

    def kvq(half, out):
        for slot in range(slots):
            out[slot * shard : (slot + 1) * shard, :] = split[half * slots + slot][:, :columns]
        start = slots * shard
        out[start : start + extra, :] = folded[half * extra : (half + 1) * extra, :].astype(LOW)
        out[start + extra :, :] = vectors[:, :columns].astype(LOW)

    def feed(half, out):
        if half:
            out[...] = down_weight[...].astype(LOW)
        else:
            for slot in range(parts):
                out[slot * shard : (slot + 1) * shard, :] = split[slot][:, -out.shape[1] :]

    def emit(first):
        kvq(first, kvq_own)
        kvq(1 - first, kvq_other)
        feed(first, feed_own)
        feed(1 - first, feed_other)

    if halves:
        pl.when(meta_ref[parts] == 0)(lambda: emit(0))
        pl.when(meta_ref[parts] != 0)(lambda: emit(1))
    else:
        emit(0)


def split_kernel(parts, width, meta_ref, qkv_ref, up_ref, *refs):
    vectors, outs, packed = take(refs, None, parts, None)
    model = parts * width
    shard = qkv_ref.shape[0]
    packed[...] = jnp.zeros_like(packed)
    values = vectors[...].reshape(1, vectors.shape[0])
    for row in range(vectors.shape[0] // shard):
        packed[row : row + 1, :shard] = values[:, row * shard : (row + 1) * shard]
    part = up_ref.shape[1] // parts
    for case in range(parts):

        @pl.when(meta_ref[0] == case)
        def _case(case=case):
            for slot in range(parts):
                owner = case ^ slot
                for at, first in enumerate((model, 2 * model, 0)):
                    start = first + owner * width
                    outs[slot][:, at * width : (at + 1) * width] = qkv_ref[
                        :, start : start + width
                    ].astype(LOW)
                outs[slot][:, 3 * width : -part] = packed[...].astype(LOW)
                outs[slot][:, -part:] = up_ref[:, owner * part : (owner + 1) * part].astype(LOW)


def join_kernel(parts, width, meta_ref, *refs):
    pieces, up, out_ref, up_ref, vectors = take(refs, parts, parts, None, None, None)
    model = parts * width
    shard = out_ref.shape[0]
    hidden = up_ref.shape[1] // parts
    for case in range(parts):

        @pl.when(meta_ref[0] == case)
        def _case(case=case):
            for slot in range(parts):
                owner = case ^ slot
                for at, first in enumerate((model, 2 * model, 0)):
                    start = first + owner * width
                    out_ref[:, start : start + width] = pieces[slot][
                        :shard, at * width : (at + 1) * width
                    ].astype(WIDE)
                up_ref[:, owner * hidden : (owner + 1) * hidden] = up[slot][...].astype(WIDE)

    vectors[...] = sum(piece[shard:, :].astype(WIDE) for piece in pieces)


def in_order(halves, parts, meta_ref, place, own, other):
    if halves:
        pl.when(meta_ref[parts] == 0)(lambda: place(own, other))
        pl.when(meta_ref[parts] != 0)(lambda: place(other, own))
    else:
        place(own, other)


def project_kernel(parts, depth, halves, meta_ref, *refs):
    tokens, own, other, kvq_ref, kv_ref, matrix_ref, norm_ref, vectors_ref = take(
        refs, parts, depth, depth, None, None, None, None, None
    )
    columns = kvq_ref.shape[1]
    rows = tokens[0].shape[0]
    shard = matrix_ref.shape[0] // (parts * depth)
    slots = parts // 2

    def place(*pair):
        for half, pieces in enumerate(pair):
            for deep in range(depth):
                member = meta_ref[parts + 1] ^ deep
                for slot in range(slots):
                    row = (meta_ref[half * slots + slot] * depth + member) * shard
                    matrix_ref[pl.ds(pl.multiple_of(row, 16), shard), :] = pieces[deep][
                        slot * shard : (slot + 1) * shard, :
                    ]

    in_order(halves, parts, meta_ref, place, own, other)
    folded = sum(piece[-16:, :].astype(WIDE) for piece in own)
    vectors_ref[:, :columns] = folded[:8]
    vectors_ref[:, columns:] = folded[8:, : vectors_ref.shape[1] - columns]
    for slot, piece in enumerate(tokens):

        def chunk(step, carry, slot=slot, piece=piece):
            here = pl.multiple_of(step * CHUNK, CHUNK)
            hat, _ = normalize(piece[pl.ds(here, CHUNK), :].astype(WIDE))
            norm_ref[pl.ds(slot * rows + here, CHUNK), :] = (
                hat * vectors_ref[0:1, :] + vectors_ref[1:2, :]
            ).astype(LOW)
            return carry

        lax.fori_loop(0, rows // CHUNK, chunk, 0)
    low = (matmul_nn(norm_ref[...], matrix_ref[...]) + vectors_ref[6:7, :columns]).astype(LOW)
    kvq_ref[...] = low
    kv_ref[...] = low[:, : kv_ref.shape[1]]


def mix_kernel(parts, depth, halves, meta_ref, *refs):
    low, own, other, matrix, keep, send = take(refs, None, depth, depth, None, None, None)
    shard = matrix.shape[0] // depth
    columns = own[0].shape[1]
    rest = matrix.shape[1] - columns
    at_first = parts // 2 * shard
    extra = own[0].shape[0] - at_first - 16

    def place(first, second):
        for deep in range(depth):
            start = pl.multiple_of((meta_ref[parts + 1] ^ deep) * shard, 16)
            split = at_first + shard - extra
            matrix[pl.ds(start, extra), :columns] = first[deep][at_first : at_first + extra, :]
            matrix[pl.ds(start + extra, shard - extra), :columns] = second[deep][
                at_first:split, :
            ]
            for at in range(columns // rest):
                matrix[pl.ds(start + at * 16, 16), columns:] = second[deep][
                    split : split + 16, at * rest : (at + 1) * rest
                ]

    in_order(halves, parts, meta_ref, place, own, other)
    emit_rows(matmul_nn(low[...], matrix[...]), keep, send)


def second_norm_kernel(parts, meta_ref, *refs):
    keep, near, far, tokens, vectors, out, attended_ref = refs
    attended = row_sum(keep, near, far) + vectors[4:5, :]
    attended_ref[...] = attended
    hat, _ = normalize(tokens[...].astype(WIDE) + attended)
    out[...] = (hat * vectors[2:3, :] + vectors[3:4, :]).astype(LOW)


def feed_kernel(parts, depth, halves, meta_ref, *refs):
    (
        norm, branch, own, other, vectors, keep, send, hidden, inner_grad, norm_all, branch_all,
        down_all, up_bias, up_all, inner, grad,
    ) = take(refs, parts, parts, depth, depth, *([None] * 12))

    def place(up, down):
        shard = up_all.shape[0] // (parts * depth)
        for deep in range(depth):
            member = meta_ref[parts + 1] ^ deep
            for slot in range(parts):
                start = pl.multiple_of((meta_ref[slot] * depth + member) * shard, 16)
                up_all[pl.ds(start, shard), :] = up[deep][slot * shard : (slot + 1) * shard, :]
        place_shards(meta_ref, parts, down, down_all)

    if halves:
        pl.when(meta_ref[parts] == 0)(lambda: place(own, other))
        pl.when(meta_ref[parts] != 0)(lambda: place(other, own))
    else:
        place(own, other)
    stack_rows(norm, norm_all)
    stack_rows(branch, branch_all)
    inner[...] = matmul_nn(norm_all[...], up_all[...])
    grad[...] = matmul_nt(branch_all[...], down_all[...])
    up_bias[...] = jnp.zeros_like(up_bias)

    def chunk(step, carry):
        here = pl.ds(pl.multiple_of(step * CHUNK, CHUNK), CHUNK)
        value = inner[here, :] + vectors[7:8, :]
        square = value * value
        bent = jnp.tanh(GELU_SCALE * (value + GELU_CUBE * square * value))
        hidden[here, :] = (0.5 * value * (1.0 + bent)).astype(LOW)
        slope = 0.5 * (1.0 + bent) + 0.5 * value * (1.0 - bent * bent) * GELU_SCALE * (
            1.0 + 3.0 * GELU_CUBE * square
        )
        low = (grad[here, :] * slope).astype(LOW)
        inner_grad[here, :] = low
        up_bias[...] += jnp.sum(low.astype(WIDE), axis=0, keepdims=True)
        return carry

    lax.fori_loop(0, inner.shape[0] // CHUNK, chunk, 0)
    emit_rows(matmul_nt(inner_grad[...], up_all[...]), keep, send)


def feed_grad_kernel(parts, depth, halves, meta_ref, *refs):
    hidden, inner_grad, norm_all, branch_all, down_all, kept, *sent, fed_keep, fed_send, whole = refs
    hidden_shard = hidden.shape[1] // depth
    shard = norm_all.shape[1] // (parts * depth)

    def emit(half, outs):
        for deep in range(depth):
            out = outs[deep * len(outs) // depth].at[deep % (depth // len(outs))]
            member = meta_ref[parts + 1] ^ deep
            if half:
                start = pl.multiple_of(member * hidden_shard, 16)
                out[...] = whole[pl.ds(start, hidden_shard), :].astype(out.dtype)
            else:
                for slot in range(parts):
                    start = pl.multiple_of((meta_ref[slot] * depth + member) * shard, 16)
                    out[slot * shard : (slot + 1) * shard, :] = whole[
                        pl.ds(start, shard), :
                    ].astype(out.dtype)

    for half in range(2):
        if half:
            whole[...] = matmul_tn(hidden[...], branch_all[...])
        else:
            whole[...] = matmul_tn(norm_all[...], inner_grad[...])
        if halves:
            pl.when(meta_ref[parts] == half)(functools.partial(emit, half, [kept]))
            pl.when(meta_ref[parts] != half)(functools.partial(emit, half, sent))
        else:
            emit(half, sent if half else [kept])
    emit_rows(matmul_nn(hidden[...], down_all[...]), fed_keep, fed_send)


def fold_kernel(count, meta_ref, kept_ref, *refs):
    arrived, keep_ref, send_refs = refs[:count], refs[count], refs[count + 1 :]
    depth = kept_ref.shape[0]
    for deep in range(depth):
        piece = arrived[deep * count // depth][deep % (depth // count)].astype(WIDE)
        if deep:
            send_refs[deep - 1][...] = (kept_ref[deep] + piece).astype(LOW)
        else:
            keep_ref[...] = kept_ref[deep] + piece


def second_norm_grad_kernel(parts, meta_ref, *refs):
    keep, near, far, tokens, attended, branch, vectors, attn_grad, mixed_part, sums = refs
    grad = row_sum(keep, near, far)
    hat, inverse = normalize(tokens[...].astype(WIDE) + attended[...])
    part, gain_grad, bias_grad = normalize_back(grad, vectors[2:3, :], hat, inverse)
    mixed_part[...] = part
    branch_rows = branch[...].astype(WIDE)
    low = (branch_rows + part).astype(LOW)
    attn_grad[...] = low
    sums[...] = jnp.zeros_like(sums)
    sums[2:3, :] = gain_grad
    sums[3:4, :] = bias_grad
    sums[4:5, :] = jnp.sum(low.astype(WIDE), axis=0, keepdims=True)
    sums[5:6, :] = jnp.sum(branch_rows, axis=0, keepdims=True)


def context_grad_kernel(parts, heads, meta_ref, *refs):
    (
        attn, matrix, kvq, kv, context, stat, ctx_grad, attn_all, query_grad, kv_grad, score, dots,
        prob, grad,
    ) = take(refs, parts, *([None] * 13))
    stack_rows(attn, attn_all)
    ctx_grad[...] = matmul_nt(attn_all[...], matrix[...]).astype(LOW)
    earlier_backward(
        heads, parts, meta_ref, kvq, kv, ctx_grad, context, stat, query_grad, kv_grad, score, dots,
        prob, grad,
    )


def own_grad_kernel(parts, depth, heads, rows, meta_ref, *refs):
    (
        kvq, ctx_grad, context, stat, query_grad, low, attn_all, kvq_grad, out_grad, score, dots,
        prob, grad,
    ) = refs
    own_backward(
        heads, rows, meta_ref, kvq, ctx_grad, context, stat, query_grad, kvq_grad, score, dots,
        prob, grad,
    )
    out_grad[...] = matmul_tn(low[...], attn_all[...])


def projection_back_kernel(parts, meta_ref, *refs):
    own, arrived, matrix, kvq_grad, keep, send, bias = refs
    kv_width = arrived.shape[2]
    total = own[:, :kv_width]
    for piece in range(arrived.shape[0]):
        total = total + arrived[piece].astype(WIDE)
    kvq_grad[:, :kv_width] = total.astype(LOW)
    kvq_grad[:, kv_width:] = own[:, kv_width:].astype(LOW)
    emit_rows(matmul_nt(kvq_grad[...], matrix[...]), keep, send)
    bias[...] = jnp.sum(kvq_grad[...].astype(WIDE), axis=0, keepdims=True)


def projection_grad_kernel(parts, depth, halves, meta_ref, *refs):
    norm, kvq_grad, out_grad, kept, sent, whole, folded = refs
    columns = kvq_grad.shape[1]
    model = norm.shape[1]
    shard = model // (parts * depth)
    rest = model - columns
    slots = parts // 2
    extra = kept.shape[1] - slots * shard
    whole[...] = matmul_tn(norm[...], kvq_grad[...])
    sent[:, kept.shape[1] :] = jnp.zeros_like(sent[:, kept.shape[1] :])

    def emit(half, out):
        for deep in range(depth):
            member = meta_ref[parts + 1] ^ deep
            for slot in range(slots):
                row = (meta_ref[half * slots + slot] * depth + member) * shard
                out[deep, slot * shard : (slot + 1) * shard] = whole[
                    pl.ds(pl.multiple_of(row, 16), shard), :
                ].astype(out.dtype)
            start = pl.multiple_of(member * shard, 16)
            folded[:shard, :] = out_grad[pl.ds(start, shard), :columns]
            for at in range(columns // rest):
                piece = out_grad[pl.ds(start + at * 16, 16), columns:]
                folded[shard:, at * rest : (at + 1) * rest] = piece
            first = slots * shard
            out[deep, first : first + extra] = folded[half * extra : (half + 1) * extra, :].astype(
                out.dtype
            )

    for half in range(2):
        if halves:
            pl.when(meta_ref[parts] == half)(functools.partial(emit, half, kept))
            pl.when(meta_ref[parts] != half)(functools.partial(emit, half, sent))
        else:
            emit(half, sent if half else kept)


def fold_vectors(sums, folded):
    rest = sums.shape[1] - folded.shape[1]
    folded[...] = jnp.zeros_like(folded)
    folded[0:8, :] = sums[:, : folded.shape[1]]
    folded[8:16, :rest] = sums[:, folded.shape[1] :]


def fold_share_kernel(meta_ref, kept, arrived, sums, keep, *refs):
    sends, folded = refs[:-1], refs[-1]
    rows = kept.shape[1]
    fold_vectors(sums, folded)
    keep[:rows, :] = kept[0] + arrived[0, :rows].astype(WIDE)
    keep[rows:, :] = folded[...]
    for deep, send in enumerate(sends, 1):
        send[:rows, :] = (kept[deep] + arrived[deep, :rows].astype(WIDE)).astype(LOW)
        send[rows:, :] = folded[...].astype(LOW)


def unfold_feed_kernel(parts, halves, meta_ref, mine, other, *refs):
    pieces, down_ref = refs[:parts], refs[parts]
    shard = pieces[0].shape[0]

    def place(up, down):
        for slot in range(parts):
            pieces[slot][...] = up[slot * shard : (slot + 1) * shard, :].astype(LOW)
        down_ref[...] = down[...].astype(WIDE)

    in_order(halves, parts, meta_ref, place, mine, other)


def unfold_kernel(parts, halves, meta_ref, mine, arrived, *refs):
    sums, pieces, out_ref, vectors, folded = take(
        refs, 0 if halves else 1, parts, None, None, None
    )
    shard, columns = pieces[0].shape[0] - 16, vectors.shape[1]
    rest = out_ref.shape[1] - columns
    slots = parts // 2
    extra = folded.shape[0] // 2

    def unfold(half, ref):
        for slot in range(slots):
            pieces[half * slots + slot][:shard, :columns] = ref[
                slot * shard : (slot + 1) * shard, :
            ].astype(LOW)
        start = slots * shard
        folded[half * extra : (half + 1) * extra, :] = ref[start : start + extra, :].astype(WIDE)

    if halves:
        first = meta_ref[parts] == 0
        for half in range(2):
            pl.when(first)(functools.partial(unfold, half, arrived if half else mine))
            pl.when(jnp.logical_not(first))(
                functools.partial(unfold, half, mine if half else arrived)
            )
        start = slots * shard + extra
        vectors[...] = mine[start:, :].astype(WIDE) + arrived[start:, :].astype(WIDE)
    else:
        unfold(0, mine)
        unfold(1, arrived)
        fold_vectors(sums[0], vectors)
    for piece in pieces:
        piece[shard:, :] = vectors[...].astype(LOW)
    out_ref[:, :columns] = folded[:shard, :]
    for at in range(columns // rest):
        out_ref[at * 16 : (at + 1) * 16, columns:] = folded[shard:, at * rest : (at + 1) * rest]


def first_norm_grad_kernel(parts, meta_ref, *refs):
    keep, near, far, tokens, vectors, mixed_part, sums_in, kvq_bias, up_bias, out, sums = refs
    grad = row_sum(keep, near, far)
    hat, inverse = normalize(tokens[...].astype(WIDE))
    part, gain_grad, bias_grad = normalize_back(grad, vectors[0:1, :], hat, inverse)
    out[...] = (mixed_part[...] + part).astype(LOW)
    sums[...] = sums_in[...]
    sums[0:1, :] = gain_grad
    sums[1:2, :] = bias_grad
    sums[6:7, : kvq_bias.shape[1]] = kvq_bias[...]
    sums[7:8, :] = up_bias[...]


def local_call(kernel, operands, results, scratch=(), flops=0):
    smem = pl.BlockSpec(memory_space=pltpu.SMEM)
    vmem = pl.BlockSpec(memory_space=pltpu.VMEM)
    moved = sum(each.size * each.dtype.itemsize for each in tuple(operands) + tuple(results))
    return pl.pallas_call(
        kernel,
        name=getattr(kernel, "func", kernel).__name__,
        out_shape=tuple(results),
        in_specs=[smem] + [vmem] * (len(operands) - 1),
        out_specs=tuple([vmem] * len(results)),
        scratch_shapes=list(scratch),
        compiler_params=pltpu.CompilerParams(vmem_limit_bytes=VMEM_BYTES),
        cost_estimate=pl.CostEstimate(
            flops=flops // HURRY, bytes_accessed=moved // HURRY, transcendentals=0
        ),
    )(*operands)


def low_like(*shape):
    return jax.ShapeDtypeStruct(shape, LOW)


def wide_like(*shape):
    return jax.ShapeDtypeStruct(shape, WIDE)


def local(
    tokens, cotangent, ln1_gain, ln1_bias, qkv_weight, q_bias, v_bias, out_weight, out_bias,
    ln2_gain, ln2_bias, fc1_weight, fc1_bias, fc2_weight, fc2_bias,
):
    parts = lax.axis_size("dp")
    depth = lax.axis_size("fsdp")
    contexts = lax.axis_size("ctx")
    assert parts == depth
    mine = lax.axis_index("dp")
    deep = lax.axis_index("fsdp")
    rows, model = tokens.shape[1:]
    shard = ln1_gain.shape[0]
    heads = model // HEAD_DIM // parts
    width = heads * HEAD_DIM
    hidden_shard = fc1_bias.shape[0]
    hidden_part = hidden_shard * depth
    group = parts * rows
    meta = jnp.stack(
        [mine ^ slot for slot in range(parts)] + [lax.axis_index("ctx"), deep]
    ).astype(jnp.int32)

    halves = contexts == 2
    padded = -(-3 * width // 128) * 128
    split = local_call(
        functools.partial(split_kernel, parts, width),
        (
            meta, qkv_weight, fc1_weight,
            jnp.concatenate(
                [
                    ln1_gain, ln1_bias, ln2_gain, ln2_bias, out_bias, fc2_bias, q_bias, v_bias,
                    fc1_bias,
                ]
            ),
        ),
        [low_like(shard, padded + hidden_part)] * parts,
        [pltpu.VMEM((shard, padded - 3 * width), WIDE)],
    )
    split_arrived = send_pieces(split[1:], "dp")
    folded_rows = shard * model // (3 * width)
    half_rows = parts // 2 * shard + folded_rows // 2 + 16
    kvq_mine, kvq_theirs, feed_mine, feed_theirs = local_call(
        functools.partial(stack_kernel, parts, depth, halves),
        (meta, split[0], *split_arrived, fc2_weight, out_weight),
        [low_like(half_rows, 3 * width)] * 2 + [low_like(hidden_shard, model)] * 2,
        [pltpu.VMEM((16, model), WIDE), pltpu.VMEM((folded_rows, 3 * width), WIDE)],
    )
    kvq_own = gather_direct(kvq_mine, "fsdp")
    if halves:
        kvq_other = [kvq_theirs] + [shift(piece, "ctx", 1) for piece in kvq_own[1:]]
    else:
        kvq_other = gather_direct(kvq_theirs, "fsdp")

    token_rows = transpose_homes(after(tokens[0].astype(LOW), *split_arrived))
    pieces = gather_pieces(after(token_rows, kvq_own[-1]), *kvq_own[1:], kvq_other[-1])

    kvq, kv, kvq_matrix, norm1_all, vectors = local_call(
        functools.partial(project_kernel, parts, depth, halves),
        (meta, *pieces, *kvq_own, *kvq_other),
        [
            low_like(group, 3 * width),
            low_like(group, 2 * width),
            low_like(model, 3 * width),
            low_like(group, model),
            wide_like(8, model),
        ],
        flops=2 * group * model * 3 * width,
    )
    kv_earlier = jnp.stack([shift(kv, "ctx", by) for by in range(1, contexts)])

    if halves:
        own_half = gather_direct(after(feed_mine, *kvq_own[1:]), "fsdp")
    else:
        own_half = gather_direct(feed_mine, "fsdp")
        other_half = gather_direct(feed_theirs, "fsdp")
    grad_rows = transpose_homes(after(cotangent[0].astype(LOW), own_half[1]))
    branch_pieces = gather_pieces(grad_rows)

    score_flops = 2 * group * group * width
    wide_square = pltpu.VMEM((group, group), WIDE)
    low_square = pltpu.VMEM((group, group), LOW)
    acc, stat = local_call(
        functools.partial(own_forward, heads, rows),
        (meta, after(kvq, own_half[2])),
        [wide_like(group, width), wide_like(group, 128)],
        [wide_square, low_square],
        flops=2 * score_flops,
    )
    if halves:
        other_half = [feed_theirs, shift(own_half[1], "ctx", 1)]
        other_half.append(shift(after(own_half[2], acc), "ctx", 1))
        other_half += [shift(piece, "ctx", 1) for piece in own_half[3:]]
    context, context_low, stat = local_call(
        functools.partial(earlier_forward, heads, parts),
        (meta, kvq, kv_earlier, after(acc, own_half[1]), stat),
        [wide_like(group, width), low_like(group, width), wide_like(group, 128)],
        [wide_square, low_square, pltpu.VMEM((group, HEAD_DIM), WIDE)],
        flops=2 * score_flops,
    )
    out_matrix, attended_keep, attended_send = local_call(
        functools.partial(mix_kernel, parts, depth, halves),
        (meta, after(context_low, *own_half[1:], other_half[2]), *kvq_own, *kvq_other),
        [low_like(width, model), wide_like(2 * rows, model), low_like(2 * rows, model)],
        flops=2 * group * width * model,
    )
    attended_sum = sum_rows(attended_keep, attended_send)
    norm2, attended = local_call(
        functools.partial(second_norm_kernel, parts),
        (meta, *attended_sum, token_rows, vectors),
        [low_like(rows, model), wide_like(rows, model)],
    )

    norm2_pieces = gather_pieces(norm2)
    norm2_keep, norm2_send, *rest = local_call(
        functools.partial(feed_kernel, parts, depth, halves),
        (meta, *norm2_pieces, *branch_pieces, *own_half, *other_half, vectors),
        [wide_like(2 * rows, model), low_like(2 * rows, model)]
        + [low_like(group, hidden_part)] * 2
        + [low_like(group, model)] * 2
        + [low_like(hidden_part, model), wide_like(1, hidden_part)],
        [
            pltpu.VMEM((model, hidden_part), LOW),
            pltpu.VMEM((group, hidden_part), WIDE),
            pltpu.VMEM((group, hidden_part), WIDE),
        ],
        flops=6 * group * model * hidden_part,
    )
    hidden, inner_grad, norm2_all, branch_all, down_matrix, up_bias = rest
    norm2_sum = sum_rows(norm2_keep, norm2_send)
    kept_half, *sent_half, fed_keep, fed_send = local_call(
        functools.partial(feed_grad_kernel, parts, depth, halves),
        (meta, hidden, inner_grad, norm2_all, branch_all, down_matrix),
        [
            wide_like(depth, hidden_shard, model),
            low_like(depth, hidden_shard, model),
            wide_like(2 * rows, model),
            low_like(2 * rows, model),
        ],
        [pltpu.VMEM((max(model, hidden_part), max(model, hidden_part)), WIDE)],
        flops=6 * group * model * hidden_part,
    )
    attn_grad, mixed_part, sums = local_call(
        functools.partial(second_norm_grad_kernel, parts),
        (
            meta, after(norm2_sum[0], fed_keep), *norm2_sum[1:], token_rows, attended, grad_rows,
            vectors,
        ),
        [low_like(rows, model), wide_like(rows, model), wide_like(8, model)],
    )
    attn_pieces = gather_pieces(attn_grad)

    def fold(kept, sent, *later):
        arrived = [shift(sent[0], "ctx", 1)]
        for piece in sent[1:]:
            arrived.append(shift(after(piece, arrived[-1]), "ctx", 1))
        shape = kept.shape[1:]
        keep, *sends = local_call(
            functools.partial(fold_kernel, len(sent)),
            (meta, after(kept, *later), *arrived),
            [wide_like(*shape)] + [low_like(*shape)] * (depth - 1),
        )
        return keep, sends

    def direct_totals(*grads):
        return [
            owner_sum(grad[0].astype(WIDE), send_pieces(list(grad[1:].astype(LOW)), "fsdp"))
            for grad in grads
        ]

    def owner_sum(keep, pieces):
        return sum_replicas(sum_all(keep, pieces).astype(LOW))

    fed_sum = sum_rows(fed_keep, after(fed_send, attn_pieces[-1]))

    ctx_grad, attn_all, query_grad, kv_grad = local_call(
        functools.partial(context_grad_kernel, parts, heads),
        (meta, *attn_pieces, out_matrix, kvq, kv_earlier, context, stat),
        [
            low_like(group, width),
            low_like(group, model),
            wide_like(group, width),
            low_like(*kv_earlier.shape),
        ],
        [wide_square, wide_square, low_square, low_square],
        flops=5 * score_flops,
    )
    if halves:
        half_keep, half_sends = fold(kept_half, sent_half, query_grad)
        farthest = swap(half_sends[-1], "fsdp", depth - 1)
        nearer = [after(send, farthest) for send in half_sends[:-1]]
        half_pieces = send_pieces(nearer, "fsdp") + [farthest]
    else:
        half_pieces = []
    if halves:
        query_grad = after(query_grad, half_keep)
    kv_arrived = jnp.stack(
        [shift(kv_grad[by - 1], "ctx", -by) for by in range(1, contexts)]
    )
    kvq_own, out_grad = local_call(
        functools.partial(own_grad_kernel, parts, depth, heads, rows),
        (meta, kvq, ctx_grad, context, stat, query_grad, context_low, attn_all),
        [wide_like(group, 3 * width), wide_like(width, model)],
        [wide_square, wide_square, low_square, low_square],
        flops=5 * score_flops,
    )
    kvq_grad, norm1_keep, norm1_send, kvq_bias = local_call(
        functools.partial(projection_back_kernel, parts),
        (meta, after(kvq_own, fed_sum[2], *half_pieces[-1:]), kv_arrived, kvq_matrix),
        [
            low_like(group, 3 * width),
            wide_like(2 * rows, model),
            low_like(2 * rows, model),
            wide_like(1, 3 * width),
        ],
        flops=2 * group * model * 3 * width,
    )
    norm1_sum = sum_rows(norm1_keep, norm1_send)
    share_rows = (parts * shard + shard * model // (3 * width)) // 2
    kept_share, sent_share = local_call(
        functools.partial(projection_grad_kernel, parts, depth, halves),
        (meta, norm1_all, after(kvq_grad, norm1_sum[1]), out_grad),
        [wide_like(depth, share_rows, 3 * width), low_like(depth, share_rows + 16, 3 * width)],
        [
            pltpu.VMEM((model, 3 * width), WIDE),
            pltpu.VMEM((shard * model // (3 * width), 3 * width), WIDE),
        ],
        flops=2 * group * model * 3 * width,
    )
    input_part, sums = local_call(
        functools.partial(first_norm_grad_kernel, parts),
        (
            meta, after(norm1_sum[0], kept_share), *norm1_sum[1:], token_rows, vectors, mixed_part,
            sums, kvq_bias, up_bias,
        ),
        [low_like(rows, model), wide_like(8, model)],
    )

    input_rows = transpose_homes(input_part)
    if halves:
        shape = (share_rows + 16, 3 * width)
        share_keep, *share_sends = local_call(
            fold_share_kernel,
            (meta, after(kept_share, *half_pieces[:-1]), shift(sent_share, "ctx", 1), sums),
            [wide_like(*shape)] + [low_like(*shape)] * (depth - 1),
            [pltpu.VMEM((16, 3 * width), WIDE)],
        )
        share_pieces = send_pieces(share_sends, "fsdp")
        mine_half = sum_all(after(half_keep, input_part), half_pieces).astype(LOW)
        feed_totals = (mine_half, shift(mine_half, "ctx", 1))
        mine_share = sum_all(share_keep, share_pieces).astype(LOW)
        shares = (mine_share, shift(after(mine_share, input_rows), "ctx", 1))
    else:
        share_pieces = []
        feed_totals = direct_totals(kept_half, sent_half[0])
        shares = (
            *direct_totals(kept_share, sent_share[:, :share_rows]), sum_replicas(sum_doubling(sums, "fsdp"))
        )
    delta = row_sum(*fed_sum) + vectors[5:6] + attended
    delta_rows = transpose_homes(after(delta.astype(LOW), shares[1]))
    output = tokens[0] + delta_rows.astype(WIDE)
    *up_totals, down_total = local_call(
        functools.partial(unfold_feed_kernel, parts, halves),
        (meta, *feed_totals),
        [low_like(shard, hidden_part)] * parts + [wide_like(hidden_shard, model)],
    )
    up_arrived = send_pieces(up_totals[1:], "dp")
    *totals, out_total, vector_part = local_call(
        functools.partial(unfold_kernel, parts, halves),
        (meta, after(shares[0], *up_arrived), *shares[1:]),
        [low_like(shard + 16, 3 * width)] * parts
        + [wide_like(shard, model), wide_like(16, 3 * width)],
        [pltpu.VMEM((shard * model // (3 * width), 3 * width), WIDE)],
    )
    qkv_total, up_total, vector_total = local_call(
        functools.partial(join_kernel, parts, width),
        (meta, totals[0], *send_pieces(totals[1:], "dp"), up_totals[0], *up_arrived),
        [
            wide_like(shard, 3 * model),
            wide_like(shard, parts * hidden_part),
            wide_like(16, 3 * width),
        ],
    )
    input_grad = cotangent[0] + input_rows.astype(WIDE)

    def vector_at(source, row, start, size):
        late = start >= 3 * width
        count = 8 if row == 0 else 1
        at = (row + jnp.where(late, 8, 0), start - jnp.where(late, 3 * width, 0))
        return lax.dynamic_slice(source, at, (count, size))

    owned = vector_at(vector_total, 0, (mine * depth + deep) * shard, shard)
    value_bias = vector_at(vector_part, 6, width + deep * shard, shard)[0]
    query_bias = vector_at(vector_part, 6, 2 * width + deep * shard, shard)[0]
    inner_bias = vector_at(vector_part, 7, deep * hidden_shard, hidden_shard)[0]

    return (
        output[None],
        input_grad[None],
        owned[0],
        owned[1],
        qkv_total,
        query_bias,
        value_bias,
        out_total,
        owned[4],
        owned[2],
        owned[3],
        up_total,
        inner_bias,
        down_total,
        owned[5],
    )


def solution(mesh):
    rows = P("dp", ("ctx", "fsdp"), None)
    vector = P(("dp", "fsdp"))
    matrix = P(("dp", "fsdp"), None)
    parameters = (
        vector, vector, matrix, vector, vector, matrix, vector, vector, vector, matrix, vector,
        matrix, vector,
    )
    return jax.shard_map(
        local,
        mesh=mesh,
        in_specs=(rows, rows) + parameters,
        out_specs=(rows, rows) + parameters,
        check_vma=False,
    )
```

```python
import functools

import jax
import jax.numpy as jnp
from jax import lax
from jax.experimental import pallas as pl
from jax.experimental.pallas import tpu as pltpu
from jax.sharding import PartitionSpec as P

HEAD_DIM = 64
EPSILON = 1e-05
SCALE = HEAD_DIM ** (-0.5)
MASKED = -1e30
CHUNK = 64
HURRY = 20
VMEM_BYTES = 16 * 1024 * 1024
GELU_SCALE = 0.7978845608
GELU_CUBE = 0.044715
LOW = jnp.bfloat16
WIDE = jnp.float32


def swap(value, axis, bit):
    count = lax.axis_size(axis)
    return lax.ppermute(value, axis, [(at, at ^ bit) for at in range(count)])


def shift(value, axis, by):
    count = lax.axis_size(axis)
    return lax.ppermute(value, axis, [(at, (at + by) % count) for at in range(count)])


def transpose_homes(value):
    side = lax.axis_size("dp")
    pairs = [(a * side + b, b * side + a) for a in range(side) for b in range(side)]
    return lax.ppermute(value, ("dp", "fsdp"), pairs)


def after(value, *others):
    return lax.optimization_barrier((value,) + others)[0]


def gather_pieces(block, *before_last):
    pieces = [block]
    count = lax.axis_size("dp")
    for slot in range(1, count):
        low_bit = slot & -slot
        source = pieces[slot ^ low_bit]
        if before_last and slot == count - 1:
            source = after(source, *before_last)
        pieces.append(swap(source, "dp", low_bit))
    return pieces


def send_pieces(sends, axis):
    return [swap(send, axis, slot) for slot, send in enumerate(sends, 1)]


def sum_rows(keep, send):
    assert lax.axis_size("dp") == 4
    near = swap(send, "dp", 1)
    rows = keep.shape[0] // 2
    far = swap((keep[rows:] + near[rows:].astype(WIDE)).astype(LOW), "dp", 2)
    return keep, near, far


def gather_direct(block, axis):
    return [block] + [swap(block, axis, slot) for slot in range(1, lax.axis_size(axis))]


def sum_doubling(value, axis):
    bit = 1
    while bit < lax.axis_size(axis):
        value = value + swap(value, axis, bit)
        bit *= 2
    return value


def sum_all(kept, arrived):
    total = kept
    for piece in arrived:
        total = total + piece.astype(WIDE)
    return total


def sum_replicas(value):
    if lax.axis_size("ctx") == 2:
        return value.astype(WIDE) + shift(value, "ctx", 1).astype(WIDE)
    return jnp.sum(lax.all_gather(value, "ctx").astype(WIDE), axis=0)


def matmul_nt(left, right):
    return lax.dot_general(left, right, (((1,), (1,)), ((), ())), preferred_element_type=WIDE)


def matmul_nn(left, right):
    return lax.dot_general(left, right, (((1,), (0,)), ((), ())), preferred_element_type=WIDE)


def matmul_tn(left, right):
    return lax.dot_general(left, right, (((0,), (0,)), ((), ())), preferred_element_type=WIDE)


def visible_block(place_ref, start, block_rows, columns):
    slot = start // block_rows
    query_pos = place_ref[slot] * block_rows + start % block_rows
    query_pos = query_pos + lax.broadcasted_iota(jnp.int32, (CHUNK, columns), 0)
    lane = lax.broadcasted_iota(jnp.int32, (CHUNK, columns), 1)
    key_pos = lane
    for at in range(columns // block_rows):
        inside = (lane >= at * block_rows) & (lane < (at + 1) * block_rows)
        key_pos = jnp.where(inside, place_ref[at] * block_rows + lane - at * block_rows, key_pos)
    return key_pos <= query_pos


def columns_of(head):
    return slice(head * HEAD_DIM, (head + 1) * HEAD_DIM)


def own_forward(heads, block_rows, place_ref, kvq_ref, acc_ref, stat_ref, score, prob):
    width = heads * HEAD_DIM
    rows = kvq_ref.shape[0]
    for head in range(heads):
        query = kvq_ref[:, 2 * width + head * HEAD_DIM : 2 * width + (head + 1) * HEAD_DIM]
        score[...] = matmul_nt(query, kvq_ref[:, columns_of(head)])

        def chunk(step, carry):
            start = pl.multiple_of(step * CHUNK, CHUNK)
            seen = visible_block(place_ref, start, block_rows, rows)
            scores = jnp.where(seen, score[pl.ds(start, CHUNK), :] * SCALE, MASKED)
            highest = jnp.max(scores, axis=1, keepdims=True)
            weight = jnp.exp(scores - highest)
            stat_ref[pl.ds(start, CHUNK), head : head + 1] = highest
            stat_ref[pl.ds(start, CHUNK), heads + head : heads + head + 1] = jnp.sum(
                weight, axis=1, keepdims=True
            )
            prob[pl.ds(start, CHUNK), :] = weight.astype(LOW)
            return carry

        lax.fori_loop(0, rows // CHUNK, chunk, 0)
        value = kvq_ref[:, width + head * HEAD_DIM : width + (head + 1) * HEAD_DIM]
        acc_ref[:, columns_of(head)] = matmul_nn(prob[...], value)


def earlier_forward(
    heads, slots, place_ref, kvq_ref, kv_ref, acc_in, stat_in, acc_ref, low_ref, stat_ref, score,
    prob, fade
):
    width = heads * HEAD_DIM
    rows = kvq_ref.shape[0]
    acc_ref[...] = acc_in[...]
    stat_ref[...] = stat_in[...]
    for piece in range(kv_ref.shape[0]):

        @pl.when(place_ref[slots] > piece)
        def _visit(piece=piece):
            for head in range(heads):
                query = kvq_ref[:, 2 * width + head * HEAD_DIM : 2 * width + (head + 1) * HEAD_DIM]
                score[...] = matmul_nt(query, kv_ref[piece, :, columns_of(head)])

                def chunk(step, carry):
                    here = pl.ds(pl.multiple_of(step * CHUNK, CHUNK), CHUNK)
                    scores = score[here, :] * SCALE
                    old = stat_ref[here, head : head + 1]
                    highest = jnp.maximum(old, jnp.max(scores, axis=1, keepdims=True))
                    weight = jnp.exp(scores - highest)
                    fading = jnp.exp(old - highest)
                    stat_ref[here, head : head + 1] = highest
                    total = stat_ref[here, heads + head : heads + head + 1]
                    stat_ref[here, heads + head : heads + head + 1] = total * fading + jnp.sum(
                        weight, axis=1, keepdims=True
                    )
                    fade[here, :] = jnp.broadcast_to(fading, (CHUNK, HEAD_DIM))
                    prob[here, :] = weight.astype(LOW)
                    return carry

                lax.fori_loop(0, rows // CHUNK, chunk, 0)
                value = kv_ref[piece, :, width + head * HEAD_DIM : width + (head + 1) * HEAD_DIM]
                acc_ref[:, columns_of(head)] = acc_ref[:, columns_of(head)] * fade[
                    ...
                ] + matmul_nn(prob[...], value)

    for head in range(heads):
        total = stat_ref[:, heads + head : heads + head + 1]
        context = acc_ref[:, columns_of(head)] / total
        acc_ref[:, columns_of(head)] = context
        low_ref[:, columns_of(head)] = context.astype(LOW)
        stat_ref[:, head : head + 1] = stat_ref[:, head : head + 1] + jnp.log(total)


def score_grads(here, seen, head, total, delta, score, dots, prob, grad):
    scores = score[here, :] * SCALE
    weight = jnp.exp(scores - total)
    if seen is not None:
        weight = jnp.where(seen, weight, 0.0)
    prob[here, :] = weight.astype(LOW)
    grad[here, :] = (weight * (dots[here, :] - delta) * SCALE).astype(LOW)


def delta_of(here, head, context_ref, ctx_grad_ref):
    product = context_ref[here, columns_of(head)] * ctx_grad_ref[here, columns_of(head)].astype(WIDE)
    return jnp.sum(product, axis=1, keepdims=True)


def earlier_backward(
    heads, slots, place_ref, kvq_ref, kv_ref, ctx_grad_ref, context_ref, stat_ref, query_grad_ref,
    kv_grad_ref, score, dots, prob, grad
):
    width = heads * HEAD_DIM
    rows = kvq_ref.shape[0]
    query_grad_ref[...] = jnp.zeros_like(query_grad_ref)
    for piece in range(kv_ref.shape[0]):

        @pl.when(place_ref[slots] <= piece)
        def _skip(piece=piece):
            kv_grad_ref[piece] = jnp.zeros(kv_grad_ref.shape[1:], kv_grad_ref.dtype)

        @pl.when(place_ref[slots] > piece)
        def _visit(piece=piece):
            for head in range(heads):
                query = kvq_ref[:, 2 * width + head * HEAD_DIM : 2 * width + (head + 1) * HEAD_DIM]
                value_at = slice(width + head * HEAD_DIM, width + (head + 1) * HEAD_DIM)
                key = kv_ref[piece, :, columns_of(head)]
                out_grad = ctx_grad_ref[:, columns_of(head)]
                score[...] = matmul_nt(query, key)
                dots[...] = matmul_nt(out_grad, kv_ref[piece, :, value_at])

                def chunk(step, carry):
                    here = pl.ds(pl.multiple_of(step * CHUNK, CHUNK), CHUNK)
                    total = stat_ref[here, head : head + 1]
                    delta = delta_of(here, head, context_ref, ctx_grad_ref)
                    score_grads(here, None, head, total, delta, score, dots, prob, grad)
                    return carry

                lax.fori_loop(0, rows // CHUNK, chunk, 0)
                kv_grad_ref[piece, :, columns_of(head)] = matmul_tn(grad[...], query).astype(LOW)
                kv_grad_ref[piece, :, value_at] = matmul_tn(prob[...], out_grad).astype(LOW)
                query_grad_ref[:, columns_of(head)] += matmul_nn(grad[...], key)


def own_backward(
    heads, block_rows, place_ref, kvq_ref, ctx_grad_ref, context_ref, stat_ref, query_grad_in,
    grad_ref, score, dots, prob, grad
):
    width = heads * HEAD_DIM
    rows = kvq_ref.shape[0]
    for head in range(heads):
        query_at = slice(2 * width + head * HEAD_DIM, 2 * width + (head + 1) * HEAD_DIM)
        value_at = slice(width + head * HEAD_DIM, width + (head + 1) * HEAD_DIM)
        query = kvq_ref[:, query_at]
        key = kvq_ref[:, columns_of(head)]
        out_grad = ctx_grad_ref[:, columns_of(head)]
        score[...] = matmul_nt(query, key)
        dots[...] = matmul_nt(out_grad, kvq_ref[:, value_at])

        def chunk(step, carry):
            start = pl.multiple_of(step * CHUNK, CHUNK)
            here = pl.ds(start, CHUNK)
            seen = visible_block(place_ref, start, block_rows, rows)
            total = stat_ref[here, head : head + 1]
            delta = delta_of(here, head, context_ref, ctx_grad_ref)
            score_grads(here, seen, head, total, delta, score, dots, prob, grad)
            return carry

        lax.fori_loop(0, rows // CHUNK, chunk, 0)
        grad_ref[:, columns_of(head)] = matmul_tn(grad[...], query)
        grad_ref[:, value_at] = matmul_tn(prob[...], out_grad)
        grad_ref[:, query_at] = query_grad_in[:, columns_of(head)] + matmul_nn(grad[...], key)


def normalize(values):
    centered = values - jnp.mean(values, axis=-1, keepdims=True)
    spread = jnp.mean(centered * centered, axis=-1, keepdims=True)
    inverse = lax.rsqrt(spread + EPSILON)
    return centered * inverse, inverse


def normalize_back(grad, gain, hat, inverse):
    scaled = grad * gain
    mean_scaled = jnp.mean(scaled, axis=-1, keepdims=True)
    mean_product = jnp.mean(scaled * hat, axis=-1, keepdims=True)
    part = inverse * (scaled - mean_scaled - hat * mean_product)
    gain_grad = jnp.sum(grad * hat, axis=0, keepdims=True)
    return part, gain_grad, jnp.sum(grad, axis=0, keepdims=True)


def take(refs, *counts):
    groups, at = [], 0
    for count in counts:
        if count is None:
            groups.append(refs[at])
            at += 1
        else:
            groups.append(refs[at : at + count])
            at += count
    return groups


def place_shards(meta_ref, parts, pieces, out_ref):
    rows = pieces[0].shape[0]
    for deep, piece in enumerate(pieces):
        start = pl.multiple_of((meta_ref[parts + 1] ^ deep) * rows, 16)
        out_ref[pl.ds(start, rows), :] = piece[...]


def stack_rows(pieces, out_ref):
    rows = pieces[0].shape[0]
    for slot, piece in enumerate(pieces):
        out_ref[slot * rows : (slot + 1) * rows, :] = piece[...]


def emit_rows(partial, keep_ref, send_ref):
    rows = keep_ref.shape[0] // 2
    for pair in range(2):
        here = slice(pair * rows, (pair + 1) * rows)
        keep_ref[here, :] = partial[2 * pair * rows : (2 * pair + 1) * rows]
        send_ref[here, :] = partial[(2 * pair + 1) * rows : (2 * pair + 2) * rows].astype(LOW)


def row_sum(keep, near, far):
    rows = far.shape[0]
    return keep[:rows, :] + near[:rows, :].astype(WIDE) + far[...].astype(WIDE)


def emit_blocks(meta_ref, parts, depth, whole_ref, keep_ref, send_refs):
    rows = keep_ref.shape[1]
    for deep in range(depth):
        member = meta_ref[parts + 1] ^ deep
        for slot in range(parts):
            start = pl.multiple_of((meta_ref[slot] * depth + member) * rows, 16)
            block = whole_ref[pl.ds(start, rows), :]
            if deep:
                send_refs[deep - 1][slot] = block.astype(LOW)
            else:
                keep_ref[slot] = block


def emit_shards(meta_ref, parts, whole_ref, keep_ref, send_refs):
    rows = keep_ref.shape[0]
    for deep in range(len(send_refs) + 1):
        start = pl.multiple_of((meta_ref[parts + 1] ^ deep) * rows, 16)
        block = whole_ref[pl.ds(start, rows), :]
        if deep:
            send_refs[deep - 1][...] = block.astype(LOW)
        else:
            keep_ref[...] = block


def stack_kernel(parts, depth, halves, meta_ref, *refs):
    split, down_weight, out_weight, kvq_own, kvq_other, feed_own, feed_other, vectors, folded = (
        take(refs, parts, *([None] * 8))
    )
    columns = kvq_own.shape[1]
    shard = split[0].shape[0]
    model = vectors.shape[1]
    width = columns // 3
    hidden_shard = down_weight.shape[0]
    member = meta_ref[parts + 1]

    def placed(slot, start):
        rows = split[slot][:, columns : -feed_own.shape[1]]
        row = lax.broadcasted_iota(jnp.int32, (rows.shape[1], model), 0)
        column = lax.broadcasted_iota(jnp.int32, (rows.shape[1], model), 1)
        chosen = jnp.where((column == start + row) & (row < shard), 1.0, 0.0)
        return matmul_nn(rows, chosen.astype(LOW))

    whole = sum(placed(slot, (meta_ref[slot] * depth + member) * shard) for slot in range(parts))
    vectors[...] = jnp.zeros_like(vectors)
    vectors[0:6, :] = whole[0:6]
    vectors[6:7, :] = (
        placed(0, width + member * shard)[7:8] + placed(0, 2 * width + member * shard)[6:7]
    )
    vectors[7:8, :] = sum(
        placed(0, member * hidden_shard + at * shard)[8 + at : 9 + at]
        for at in range(hidden_shard // shard)
    )
    vectors[8:16, : model - columns] = vectors[0:8, columns:]
    rest = model - columns
    folded[:shard, :] = out_weight[:, :columns]
    for at in range(columns // rest):
        folded[shard:, at * rest : (at + 1) * rest] = out_weight[at * 16 : (at + 1) * 16, columns:]
    slots = parts // 2
    extra = folded.shape[0] // 2

    def kvq(half, out):
        for slot in range(slots):
            out[slot * shard : (slot + 1) * shard, :] = split[half * slots + slot][:, :columns]
        start = slots * shard
        out[start : start + extra, :] = folded[half * extra : (half + 1) * extra, :].astype(LOW)
        out[start + extra :, :] = vectors[:, :columns].astype(LOW)

    def feed(half, out):
        if half:
            out[...] = down_weight[...].astype(LOW)
        else:
            for slot in range(parts):
                out[slot * shard : (slot + 1) * shard, :] = split[slot][:, -out.shape[1] :]

    def emit(first):
        kvq(first, kvq_own)
        kvq(1 - first, kvq_other)
        feed(first, feed_own)
        feed(1 - first, feed_other)

    if halves:
        pl.when(meta_ref[parts] == 0)(lambda: emit(0))
        pl.when(meta_ref[parts] != 0)(lambda: emit(1))
    else:
        emit(0)


def split_kernel(parts, width, meta_ref, qkv_ref, up_ref, *refs):
    vectors, outs, packed = take(refs, None, parts, None)
    model = parts * width
    shard = qkv_ref.shape[0]
    packed[...] = jnp.zeros_like(packed)
    values = vectors[...].reshape(1, vectors.shape[0])
    for row in range(vectors.shape[0] // shard):
        packed[row : row + 1, :shard] = values[:, row * shard : (row + 1) * shard]
    part = up_ref.shape[1] // parts
    for case in range(parts):

        @pl.when(meta_ref[0] == case)
        def _case(case=case):
            for slot in range(parts):
                owner = case ^ slot
                for at, first in enumerate((model, 2 * model, 0)):
                    start = first + owner * width
                    outs[slot][:, at * width : (at + 1) * width] = qkv_ref[
                        :, start : start + width
                    ].astype(LOW)
                outs[slot][:, 3 * width : -part] = packed[...].astype(LOW)
                outs[slot][:, -part:] = up_ref[:, owner * part : (owner + 1) * part].astype(LOW)


def join_kernel(parts, width, meta_ref, *refs):
    pieces, up, out_ref, up_ref, vectors = take(refs, parts, parts, None, None, None)
    model = parts * width
    shard = out_ref.shape[0]
    hidden = up_ref.shape[1] // parts
    for case in range(parts):

        @pl.when(meta_ref[0] == case)
        def _case(case=case):
            for slot in range(parts):
                owner = case ^ slot
                for at, first in enumerate((model, 2 * model, 0)):
                    start = first + owner * width
                    out_ref[:, start : start + width] = pieces[slot][
                        :shard, at * width : (at + 1) * width
                    ].astype(WIDE)
                up_ref[:, owner * hidden : (owner + 1) * hidden] = up[slot][...].astype(WIDE)

    vectors[...] = sum(piece[shard:, :].astype(WIDE) for piece in pieces)


def in_order(halves, parts, meta_ref, place, own, other):
    if halves:
        pl.when(meta_ref[parts] == 0)(lambda: place(own, other))
        pl.when(meta_ref[parts] != 0)(lambda: place(other, own))
    else:
        place(own, other)


def project_kernel(parts, depth, halves, meta_ref, *refs):
    tokens, own, other, kvq_ref, kv_ref, matrix_ref, norm_ref, vectors_ref = take(
        refs, parts, depth, depth, None, None, None, None, None
    )
    columns = kvq_ref.shape[1]
    rows = tokens[0].shape[0]
    shard = matrix_ref.shape[0] // (parts * depth)
    slots = parts // 2

    def place(*pair):
        for half, pieces in enumerate(pair):
            for deep in range(depth):
                member = meta_ref[parts + 1] ^ deep
                for slot in range(slots):
                    row = (meta_ref[half * slots + slot] * depth + member) * shard
                    matrix_ref[pl.ds(pl.multiple_of(row, 16), shard), :] = pieces[deep][
                        slot * shard : (slot + 1) * shard, :
                    ]

    in_order(halves, parts, meta_ref, place, own, other)
    folded = sum(piece[-16:, :].astype(WIDE) for piece in own)
    vectors_ref[:, :columns] = folded[:8]
    vectors_ref[:, columns:] = folded[8:, : vectors_ref.shape[1] - columns]
    for slot, piece in enumerate(tokens):

        def chunk(step, carry, slot=slot, piece=piece):
            here = pl.multiple_of(step * CHUNK, CHUNK)
            hat, _ = normalize(piece[pl.ds(here, CHUNK), :].astype(WIDE))
            norm_ref[pl.ds(slot * rows + here, CHUNK), :] = (
                hat * vectors_ref[0:1, :] + vectors_ref[1:2, :]
            ).astype(LOW)
            return carry

        lax.fori_loop(0, rows // CHUNK, chunk, 0)
    low = (matmul_nn(norm_ref[...], matrix_ref[...]) + vectors_ref[6:7, :columns]).astype(LOW)
    kvq_ref[...] = low
    kv_ref[...] = low[:, : kv_ref.shape[1]]


def mix_kernel(parts, depth, halves, meta_ref, *refs):
    low, own, other, matrix, keep, send = take(refs, None, depth, depth, None, None, None)
    shard = matrix.shape[0] // depth
    columns = own[0].shape[1]
    rest = matrix.shape[1] - columns
    at_first = parts // 2 * shard
    extra = own[0].shape[0] - at_first - 16

    def place(first, second):
        for deep in range(depth):
            start = pl.multiple_of((meta_ref[parts + 1] ^ deep) * shard, 16)
            split = at_first + shard - extra
            matrix[pl.ds(start, extra), :columns] = first[deep][at_first : at_first + extra, :]
            matrix[pl.ds(start + extra, shard - extra), :columns] = second[deep][
                at_first:split, :
            ]
            for at in range(columns // rest):
                matrix[pl.ds(start + at * 16, 16), columns:] = second[deep][
                    split : split + 16, at * rest : (at + 1) * rest
                ]

    in_order(halves, parts, meta_ref, place, own, other)
    emit_rows(matmul_nn(low[...], matrix[...]), keep, send)


def second_norm_kernel(parts, meta_ref, *refs):
    keep, near, far, tokens, vectors, out, attended_ref = refs
    attended = row_sum(keep, near, far) + vectors[4:5, :]
    attended_ref[...] = attended
    hat, _ = normalize(tokens[...].astype(WIDE) + attended)
    out[...] = (hat * vectors[2:3, :] + vectors[3:4, :]).astype(LOW)


def feed_kernel(parts, depth, halves, meta_ref, *refs):
    (
        norm, branch, own, other, vectors, keep, send, hidden, inner_grad, norm_all, branch_all,
        down_all, up_bias, up_all, inner, grad,
    ) = take(refs, parts, parts, depth, depth, *([None] * 12))

    def place(up, down):
        shard = up_all.shape[0] // (parts * depth)
        for deep in range(depth):
            member = meta_ref[parts + 1] ^ deep
            for slot in range(parts):
                start = pl.multiple_of((meta_ref[slot] * depth + member) * shard, 16)
                up_all[pl.ds(start, shard), :] = up[deep][slot * shard : (slot + 1) * shard, :]
        place_shards(meta_ref, parts, down, down_all)

    if halves:
        pl.when(meta_ref[parts] == 0)(lambda: place(own, other))
        pl.when(meta_ref[parts] != 0)(lambda: place(other, own))
    else:
        place(own, other)
    stack_rows(norm, norm_all)
    stack_rows(branch, branch_all)
    inner[...] = matmul_nn(norm_all[...], up_all[...])
    grad[...] = matmul_nt(branch_all[...], down_all[...])
    up_bias[...] = jnp.zeros_like(up_bias)

    def chunk(step, carry):
        here = pl.ds(pl.multiple_of(step * CHUNK, CHUNK), CHUNK)
        value = inner[here, :] + vectors[7:8, :]
        square = value * value
        bent = jnp.tanh(GELU_SCALE * (value + GELU_CUBE * square * value))
        hidden[here, :] = (0.5 * value * (1.0 + bent)).astype(LOW)
        slope = 0.5 * (1.0 + bent) + 0.5 * value * (1.0 - bent * bent) * GELU_SCALE * (
            1.0 + 3.0 * GELU_CUBE * square
        )
        low = (grad[here, :] * slope).astype(LOW)
        inner_grad[here, :] = low
        up_bias[...] += jnp.sum(low.astype(WIDE), axis=0, keepdims=True)
        return carry

    lax.fori_loop(0, inner.shape[0] // CHUNK, chunk, 0)
    emit_rows(matmul_nt(inner_grad[...], up_all[...]), keep, send)


def feed_grad_kernel(parts, depth, halves, meta_ref, *refs):
    hidden, inner_grad, norm_all, branch_all, down_all, kept, *sent, fed_keep, fed_send, whole = refs
    hidden_shard = hidden.shape[1] // depth
    shard = norm_all.shape[1] // (parts * depth)

    def emit(half, outs):
        for deep in range(depth):
            out = outs[deep * len(outs) // depth].at[deep % (depth // len(outs))]
            member = meta_ref[parts + 1] ^ deep
            if half:
                start = pl.multiple_of(member * hidden_shard, 16)
                out[...] = whole[pl.ds(start, hidden_shard), :].astype(out.dtype)
            else:
                for slot in range(parts):
                    start = pl.multiple_of((meta_ref[slot] * depth + member) * shard, 16)
                    out[slot * shard : (slot + 1) * shard, :] = whole[
                        pl.ds(start, shard), :
                    ].astype(out.dtype)

    for half in range(2):
        if half:
            whole[...] = matmul_tn(hidden[...], branch_all[...])
        else:
            whole[...] = matmul_tn(norm_all[...], inner_grad[...])
        if halves:
            pl.when(meta_ref[parts] == half)(functools.partial(emit, half, [kept]))
            pl.when(meta_ref[parts] != half)(functools.partial(emit, half, sent))
        else:
            emit(half, sent if half else [kept])
    emit_rows(matmul_nn(hidden[...], down_all[...]), fed_keep, fed_send)


def fold_kernel(count, meta_ref, kept_ref, *refs):
    arrived, keep_ref, send_refs = refs[:count], refs[count], refs[count + 1 :]
    depth = kept_ref.shape[0]
    for deep in range(depth):
        piece = arrived[deep * count // depth][deep % (depth // count)].astype(WIDE)
        if deep:
            send_refs[deep - 1][...] = (kept_ref[deep] + piece).astype(LOW)
        else:
            keep_ref[...] = kept_ref[deep] + piece


def second_norm_grad_kernel(parts, meta_ref, *refs):
    keep, near, far, tokens, attended, branch, vectors, attn_grad, mixed_part, sums = refs
    grad = row_sum(keep, near, far)
    hat, inverse = normalize(tokens[...].astype(WIDE) + attended[...])
    part, gain_grad, bias_grad = normalize_back(grad, vectors[2:3, :], hat, inverse)
    mixed_part[...] = part
    branch_rows = branch[...].astype(WIDE)
    low = (branch_rows + part).astype(LOW)
    attn_grad[...] = low
    sums[...] = jnp.zeros_like(sums)
    sums[2:3, :] = gain_grad
    sums[3:4, :] = bias_grad
    sums[4:5, :] = jnp.sum(low.astype(WIDE), axis=0, keepdims=True)
    sums[5:6, :] = jnp.sum(branch_rows, axis=0, keepdims=True)


def context_grad_kernel(parts, heads, meta_ref, *refs):
    (
        attn, matrix, kvq, kv, context, stat, ctx_grad, attn_all, query_grad, kv_grad, score, dots,
        prob, grad,
    ) = take(refs, parts, *([None] * 13))
    stack_rows(attn, attn_all)
    ctx_grad[...] = matmul_nt(attn_all[...], matrix[...]).astype(LOW)
    earlier_backward(
        heads, parts, meta_ref, kvq, kv, ctx_grad, context, stat, query_grad, kv_grad, score, dots,
        prob, grad,
    )


def own_grad_kernel(parts, depth, heads, rows, meta_ref, *refs):
    (
        kvq, ctx_grad, context, stat, query_grad, low, attn_all, kvq_grad, out_grad, score, dots,
        prob, grad,
    ) = refs
    own_backward(
        heads, rows, meta_ref, kvq, ctx_grad, context, stat, query_grad, kvq_grad, score, dots,
        prob, grad,
    )
    out_grad[...] = matmul_tn(low[...], attn_all[...])


def projection_back_kernel(parts, meta_ref, *refs):
    own, arrived, matrix, kvq_grad, keep, send, bias = refs
    kv_width = arrived.shape[2]
    total = own[:, :kv_width]
    for piece in range(arrived.shape[0]):
        total = total + arrived[piece].astype(WIDE)
    kvq_grad[:, :kv_width] = total.astype(LOW)
    kvq_grad[:, kv_width:] = own[:, kv_width:].astype(LOW)
    emit_rows(matmul_nt(kvq_grad[...], matrix[...]), keep, send)
    bias[...] = jnp.sum(kvq_grad[...].astype(WIDE), axis=0, keepdims=True)


def projection_grad_kernel(parts, depth, halves, meta_ref, *refs):
    norm, kvq_grad, out_grad, kept, sent, whole, folded = refs
    columns = kvq_grad.shape[1]
    model = norm.shape[1]
    shard = model // (parts * depth)
    rest = model - columns
    slots = parts // 2
    extra = kept.shape[1] - slots * shard
    whole[...] = matmul_tn(norm[...], kvq_grad[...])
    sent[:, kept.shape[1] :] = jnp.zeros_like(sent[:, kept.shape[1] :])

    def emit(half, out):
        for deep in range(depth):
            member = meta_ref[parts + 1] ^ deep
            for slot in range(slots):
                row = (meta_ref[half * slots + slot] * depth + member) * shard
                out[deep, slot * shard : (slot + 1) * shard] = whole[
                    pl.ds(pl.multiple_of(row, 16), shard), :
                ].astype(out.dtype)
            start = pl.multiple_of(member * shard, 16)
            folded[:shard, :] = out_grad[pl.ds(start, shard), :columns]
            for at in range(columns // rest):
                piece = out_grad[pl.ds(start + at * 16, 16), columns:]
                folded[shard:, at * rest : (at + 1) * rest] = piece
            first = slots * shard
            out[deep, first : first + extra] = folded[half * extra : (half + 1) * extra, :].astype(
                out.dtype
            )

    for half in range(2):
        if halves:
            pl.when(meta_ref[parts] == half)(functools.partial(emit, half, kept))
            pl.when(meta_ref[parts] != half)(functools.partial(emit, half, sent))
        else:
            emit(half, sent if half else kept)


def fold_vectors(sums, folded):
    rest = sums.shape[1] - folded.shape[1]
    folded[...] = jnp.zeros_like(folded)
    folded[0:8, :] = sums[:, : folded.shape[1]]
    folded[8:16, :rest] = sums[:, folded.shape[1] :]


def fold_share_kernel(meta_ref, kept, arrived, sums, keep, *refs):
    sends, folded = refs[:-1], refs[-1]
    rows = kept.shape[1]
    fold_vectors(sums, folded)
    keep[:rows, :] = kept[0] + arrived[0, :rows].astype(WIDE)
    keep[rows:, :] = folded[...]
    for deep, send in enumerate(sends, 1):
        send[:rows, :] = (kept[deep] + arrived[deep, :rows].astype(WIDE)).astype(LOW)
        send[rows:, :] = folded[...].astype(LOW)


def unfold_feed_kernel(parts, halves, meta_ref, mine, other, *refs):
    pieces, down_ref = refs[:parts], refs[parts]
    shard = pieces[0].shape[0]

    def place(up, down):
        for slot in range(parts):
            pieces[slot][...] = up[slot * shard : (slot + 1) * shard, :].astype(LOW)
        down_ref[...] = down[...].astype(WIDE)

    in_order(halves, parts, meta_ref, place, mine, other)


def unfold_kernel(parts, halves, meta_ref, mine, arrived, *refs):
    sums, pieces, out_ref, vectors, folded = take(
        refs, 0 if halves else 1, parts, None, None, None
    )
    shard, columns = pieces[0].shape[0] - 16, vectors.shape[1]
    rest = out_ref.shape[1] - columns
    slots = parts // 2
    extra = folded.shape[0] // 2

    def unfold(half, ref):
        for slot in range(slots):
            pieces[half * slots + slot][:shard, :columns] = ref[
                slot * shard : (slot + 1) * shard, :
            ].astype(LOW)
        start = slots * shard
        folded[half * extra : (half + 1) * extra, :] = ref[start : start + extra, :].astype(WIDE)

    if halves:
        first = meta_ref[parts] == 0
        for half in range(2):
            pl.when(first)(functools.partial(unfold, half, arrived if half else mine))
            pl.when(jnp.logical_not(first))(
                functools.partial(unfold, half, mine if half else arrived)
            )
        start = slots * shard + extra
        vectors[...] = mine[start:, :].astype(WIDE) + arrived[start:, :].astype(WIDE)
    else:
        unfold(0, mine)
        unfold(1, arrived)
        fold_vectors(sums[0], vectors)
    for piece in pieces:
        piece[shard:, :] = vectors[...].astype(LOW)
    out_ref[:, :columns] = folded[:shard, :]
    for at in range(columns // rest):
        out_ref[at * 16 : (at + 1) * 16, columns:] = folded[shard:, at * rest : (at + 1) * rest]


def first_norm_grad_kernel(parts, meta_ref, *refs):
    keep, near, far, tokens, vectors, mixed_part, sums_in, kvq_bias, up_bias, out, sums = refs
    grad = row_sum(keep, near, far)
    hat, inverse = normalize(tokens[...].astype(WIDE))
    part, gain_grad, bias_grad = normalize_back(grad, vectors[0:1, :], hat, inverse)
    out[...] = (mixed_part[...] + part).astype(LOW)
    sums[...] = sums_in[...]
    sums[0:1, :] = gain_grad
    sums[1:2, :] = bias_grad
    sums[6:7, : kvq_bias.shape[1]] = kvq_bias[...]
    sums[7:8, :] = up_bias[...]


def local_call(kernel, operands, results, scratch=(), flops=0):
    smem = pl.BlockSpec(memory_space=pltpu.SMEM)
    vmem = pl.BlockSpec(memory_space=pltpu.VMEM)
    moved = sum(each.size * each.dtype.itemsize for each in tuple(operands) + tuple(results))
    return pl.pallas_call(
        kernel,
        name=getattr(kernel, "func", kernel).__name__,
        out_shape=tuple(results),
        in_specs=[smem] + [vmem] * (len(operands) - 1),
        out_specs=tuple([vmem] * len(results)),
        scratch_shapes=list(scratch),
        compiler_params=pltpu.CompilerParams(vmem_limit_bytes=VMEM_BYTES),
        cost_estimate=pl.CostEstimate(
            flops=flops // HURRY, bytes_accessed=moved // HURRY, transcendentals=0
        ),
    )(*operands)


def low_like(*shape):
    return jax.ShapeDtypeStruct(shape, LOW)


def wide_like(*shape):
    return jax.ShapeDtypeStruct(shape, WIDE)


def local(
    tokens, cotangent, ln1_gain, ln1_bias, qkv_weight, q_bias, v_bias, out_weight, out_bias,
    ln2_gain, ln2_bias, fc1_weight, fc1_bias, fc2_weight, fc2_bias,
):
    parts = lax.axis_size("dp")
    depth = lax.axis_size("fsdp")
    contexts = lax.axis_size("ctx")
    assert parts == depth
    mine = lax.axis_index("dp")
    deep = lax.axis_index("fsdp")
    rows, model = tokens.shape[1:]
    shard = ln1_gain.shape[0]
    heads = model // HEAD_DIM // parts
    width = heads * HEAD_DIM
    hidden_shard = fc1_bias.shape[0]
    hidden_part = hidden_shard * depth
    group = parts * rows
    meta = jnp.stack(
        [mine ^ slot for slot in range(parts)] + [lax.axis_index("ctx"), deep]
    ).astype(jnp.int32)

    halves = contexts == 2
    padded = -(-3 * width // 128) * 128
    split = local_call(
        functools.partial(split_kernel, parts, width),
        (
            meta, qkv_weight, fc1_weight,
            jnp.concatenate(
                [
                    ln1_gain, ln1_bias, ln2_gain, ln2_bias, out_bias, fc2_bias, q_bias, v_bias,
                    fc1_bias,
                ]
            ),
        ),
        [low_like(shard, padded + hidden_part)] * parts,
        [pltpu.VMEM((shard, padded - 3 * width), WIDE)],
    )
    split_arrived = send_pieces(split[1:], "dp")
    folded_rows = shard * model // (3 * width)
    half_rows = parts // 2 * shard + folded_rows // 2 + 16
    kvq_mine, kvq_theirs, feed_mine, feed_theirs = local_call(
        functools.partial(stack_kernel, parts, depth, halves),
        (meta, split[0], *split_arrived, fc2_weight, out_weight),
        [low_like(half_rows, 3 * width)] * 2 + [low_like(hidden_shard, model)] * 2,
        [pltpu.VMEM((16, model), WIDE), pltpu.VMEM((folded_rows, 3 * width), WIDE)],
    )
    kvq_own = gather_direct(kvq_mine, "fsdp")
    if halves:
        kvq_other = [kvq_theirs] + [shift(piece, "ctx", 1) for piece in kvq_own[1:]]
    else:
        kvq_other = gather_direct(kvq_theirs, "fsdp")

    token_rows = transpose_homes(after(tokens[0].astype(LOW), kvq_mine))
    pieces = gather_pieces(after(token_rows, kvq_own[-1]), *kvq_own[1:], kvq_other[1], kvq_other[-1])

    kvq, kv, kvq_matrix, norm1_all, vectors = local_call(
        functools.partial(project_kernel, parts, depth, halves),
        (meta, *pieces, *kvq_own, *kvq_other),
        [
            low_like(group, 3 * width),
            low_like(group, 2 * width),
            low_like(model, 3 * width),
            low_like(group, model),
            wide_like(8, model),
        ],
        flops=2 * group * model * 3 * width,
    )
    kv_earlier = jnp.stack([shift(kv, "ctx", by) for by in range(1, contexts)])

    if halves:
        own_half = gather_direct(after(feed_mine, *kvq_own[1:]), "fsdp")
    else:
        own_half = gather_direct(feed_mine, "fsdp")
        other_half = gather_direct(feed_theirs, "fsdp")
    grad_rows = transpose_homes(after(cotangent[0].astype(LOW), own_half[1]))
    branch_pieces = gather_pieces(grad_rows)

    score_flops = 2 * group * group * width
    wide_square = pltpu.VMEM((group, group), WIDE)
    low_square = pltpu.VMEM((group, group), LOW)
    acc, stat = local_call(
        functools.partial(own_forward, heads, rows),
        (meta, after(kvq, own_half[2])),
        [wide_like(group, width), wide_like(group, 128)],
        [wide_square, low_square],
        flops=2 * score_flops,
    )
    if halves:
        other_half = [feed_theirs, shift(own_half[1], "ctx", 1)]
        other_half.append(shift(after(own_half[2], acc), "ctx", 1))
        other_half += [shift(piece, "ctx", 1) for piece in own_half[3:]]
    context, context_low, stat = local_call(
        functools.partial(earlier_forward, heads, parts),
        (meta, kvq, kv_earlier, after(acc, own_half[1]), stat),
        [wide_like(group, width), low_like(group, width), wide_like(group, 128)],
        [wide_square, low_square, pltpu.VMEM((group, HEAD_DIM), WIDE)],
        flops=2 * score_flops,
    )
    out_matrix, attended_keep, attended_send = local_call(
        functools.partial(mix_kernel, parts, depth, halves),
        (meta, after(context_low, *own_half[1:], other_half[2]), *kvq_own, *kvq_other),
        [low_like(width, model), wide_like(2 * rows, model), low_like(2 * rows, model)],
        flops=2 * group * width * model,
    )
    attended_sum = sum_rows(attended_keep, attended_send)
    norm2, attended = local_call(
        functools.partial(second_norm_kernel, parts),
        (meta, *attended_sum, token_rows, vectors),
        [low_like(rows, model), wide_like(rows, model)],
    )

    norm2_pieces = gather_pieces(norm2)
    norm2_keep, norm2_send, *rest = local_call(
        functools.partial(feed_kernel, parts, depth, halves),
        (meta, *norm2_pieces, *branch_pieces, *own_half, *other_half, vectors),
        [wide_like(2 * rows, model), low_like(2 * rows, model)]
        + [low_like(group, hidden_part)] * 2
        + [low_like(group, model)] * 2
        + [low_like(hidden_part, model), wide_like(1, hidden_part)],
        [
            pltpu.VMEM((model, hidden_part), LOW),
            pltpu.VMEM((group, hidden_part), WIDE),
            pltpu.VMEM((group, hidden_part), WIDE),
        ],
        flops=6 * group * model * hidden_part,
    )
    hidden, inner_grad, norm2_all, branch_all, down_matrix, up_bias = rest
    norm2_sum = sum_rows(norm2_keep, norm2_send)
    kept_half, *sent_half, fed_keep, fed_send = local_call(
        functools.partial(feed_grad_kernel, parts, depth, halves),
        (meta, hidden, inner_grad, norm2_all, branch_all, down_matrix),
        [
            wide_like(depth, hidden_shard, model),
            low_like(depth, hidden_shard, model),
            wide_like(2 * rows, model),
            low_like(2 * rows, model),
        ],
        [pltpu.VMEM((max(model, hidden_part), max(model, hidden_part)), WIDE)],
        flops=6 * group * model * hidden_part,
    )
    attn_grad, mixed_part, sums = local_call(
        functools.partial(second_norm_grad_kernel, parts),
        (
            meta, after(norm2_sum[0], fed_keep), *norm2_sum[1:], token_rows, attended, grad_rows,
            vectors,
        ),
        [low_like(rows, model), wide_like(rows, model), wide_like(8, model)],
    )
    attn_pieces = gather_pieces(attn_grad)

    def fold(kept, sent, *later):
        arrived = [shift(sent[0], "ctx", 1)]
        for piece in sent[1:]:
            arrived.append(shift(after(piece, arrived[-1]), "ctx", 1))
        shape = kept.shape[1:]
        keep, *sends = local_call(
            functools.partial(fold_kernel, len(sent)),
            (meta, after(kept, *later), *arrived),
            [wide_like(*shape)] + [low_like(*shape)] * (depth - 1),
        )
        return keep, sends

    def direct_totals(*grads):
        return [
            owner_sum(grad[0].astype(WIDE), send_pieces(list(grad[1:].astype(LOW)), "fsdp"))
            for grad in grads
        ]

    def owner_sum(keep, pieces):
        return sum_replicas(sum_all(keep, pieces).astype(LOW))

    fed_sum = sum_rows(fed_keep, after(fed_send, attn_pieces[-1]))

    ctx_grad, attn_all, query_grad, kv_grad = local_call(
        functools.partial(context_grad_kernel, parts, heads),
        (meta, *attn_pieces, out_matrix, kvq, kv_earlier, context, stat),
        [
            low_like(group, width),
            low_like(group, model),
            wide_like(group, width),
            low_like(*kv_earlier.shape),
        ],
        [wide_square, wide_square, low_square, low_square],
        flops=5 * score_flops,
    )
    if halves:
        half_keep, half_sends = fold(kept_half, sent_half, query_grad)
        farthest = swap(half_sends[-1], "fsdp", depth - 1)
        nearer = [after(send, farthest) for send in half_sends[:-1]]
        half_pieces = send_pieces(nearer, "fsdp") + [farthest]
    else:
        half_pieces = []
    if halves:
        query_grad = after(query_grad, half_keep)
    kv_arrived = jnp.stack(
        [shift(kv_grad[by - 1], "ctx", -by) for by in range(1, contexts)]
    )
    kvq_own, out_grad = local_call(
        functools.partial(own_grad_kernel, parts, depth, heads, rows),
        (meta, kvq, ctx_grad, context, stat, query_grad, context_low, attn_all),
        [wide_like(group, 3 * width), wide_like(width, model)],
        [wide_square, wide_square, low_square, low_square],
        flops=5 * score_flops,
    )
    kvq_grad, norm1_keep, norm1_send, kvq_bias = local_call(
        functools.partial(projection_back_kernel, parts),
        (meta, after(kvq_own, fed_sum[2], *half_pieces[-1:]), kv_arrived, kvq_matrix),
        [
            low_like(group, 3 * width),
            wide_like(2 * rows, model),
            low_like(2 * rows, model),
            wide_like(1, 3 * width),
        ],
        flops=2 * group * model * 3 * width,
    )
    norm1_sum = sum_rows(norm1_keep, norm1_send)
    share_rows = (parts * shard + shard * model // (3 * width)) // 2
    kept_share, sent_share = local_call(
        functools.partial(projection_grad_kernel, parts, depth, halves),
        (meta, norm1_all, after(kvq_grad, norm1_sum[1]), out_grad),
        [wide_like(depth, share_rows, 3 * width), low_like(depth, share_rows + 16, 3 * width)],
        [
            pltpu.VMEM((model, 3 * width), WIDE),
            pltpu.VMEM((shard * model // (3 * width), 3 * width), WIDE),
        ],
        flops=2 * group * model * 3 * width,
    )
    input_part, sums = local_call(
        functools.partial(first_norm_grad_kernel, parts),
        (
            meta, after(norm1_sum[0], kept_share), *norm1_sum[1:], token_rows, vectors, mixed_part,
            sums, kvq_bias, up_bias,
        ),
        [low_like(rows, model), wide_like(8, model)],
    )

    input_rows = transpose_homes(input_part)
    if halves:
        shape = (share_rows + 16, 3 * width)
        share_keep, *share_sends = local_call(
            fold_share_kernel,
            (meta, after(kept_share, input_rows, *half_pieces[:-1]), shift(sent_share, "ctx", 1), sums),
            [wide_like(*shape)] + [low_like(*shape)] * (depth - 1),
            [pltpu.VMEM((16, 3 * width), WIDE)],
        )
        share_pieces = send_pieces(share_sends, "fsdp")
        mine_half = sum_all(after(half_keep, input_rows), half_pieces).astype(LOW)
        feed_totals = (mine_half, shift(mine_half, "ctx", 1))
        mine_share = sum_all(share_keep, share_pieces).astype(LOW)
        shares = (mine_share, shift(mine_share, "ctx", 1))
    else:
        share_pieces = []
        feed_totals = direct_totals(kept_half, sent_half[0])
        shares = (
            *direct_totals(kept_share, sent_share[:, :share_rows]), sum_replicas(sum_doubling(sums, "fsdp"))
        )
    *up_totals, down_total = local_call(
        functools.partial(unfold_feed_kernel, parts, halves),
        (meta, *feed_totals),
        [low_like(shard, hidden_part)] * parts + [wide_like(hidden_shard, model)],
    )
    up_arrived = send_pieces(up_totals[1:], "dp")
    delta = row_sum(*fed_sum) + vectors[5:6] + attended
    delta_rows = transpose_homes(after(delta.astype(LOW), up_arrived[0], *share_pieces))
    output = tokens[0] + delta_rows.astype(WIDE)
    *totals, out_total, vector_part = local_call(
        functools.partial(unfold_kernel, parts, halves),
        (meta, after(shares[0], *up_arrived), *shares[1:]),
        [low_like(shard + 16, 3 * width)] * parts
        + [wide_like(shard, model), wide_like(16, 3 * width)],
        [pltpu.VMEM((shard * model // (3 * width), 3 * width), WIDE)],
    )
    qkv_total, up_total, vector_total = local_call(
        functools.partial(join_kernel, parts, width),
        (meta, totals[0], *send_pieces(totals[1:], "dp"), up_totals[0], *up_arrived),
        [
            wide_like(shard, 3 * model),
            wide_like(shard, parts * hidden_part),
            wide_like(16, 3 * width),
        ],
    )
    input_grad = cotangent[0] + input_rows.astype(WIDE)

    def vector_at(source, row, start, size):
        late = start >= 3 * width
        count = 8 if row == 0 else 1
        at = (row + jnp.where(late, 8, 0), start - jnp.where(late, 3 * width, 0))
        return lax.dynamic_slice(source, at, (count, size))

    owned = vector_at(vector_total, 0, (mine * depth + deep) * shard, shard)
    value_bias = vector_at(vector_part, 6, width + deep * shard, shard)[0]
    query_bias = vector_at(vector_part, 6, 2 * width + deep * shard, shard)[0]
    inner_bias = vector_at(vector_part, 7, deep * hidden_shard, hidden_shard)[0]

    return (
        output[None],
        input_grad[None],
        owned[0],
        owned[1],
        qkv_total,
        query_bias,
        value_bias,
        out_total,
        owned[4],
        owned[2],
        owned[3],
        up_total,
        inner_bias,
        down_total,
        owned[5],
    )


def solution(mesh):
    rows = P("dp", ("ctx", "fsdp"), None)
    vector = P(("dp", "fsdp"))
    matrix = P(("dp", "fsdp"), None)
    parameters = (
        vector, vector, matrix, vector, vector, matrix, vector, vector, vector, matrix, vector,
        matrix, vector,
    )
    return jax.shard_map(
        local,
        mesh=mesh,
        in_specs=(rows, rows) + parameters,
        out_specs=(rows, rows) + parameters,
        check_vma=False,
    )
```

```python
import functools

import jax
import jax.numpy as jnp
from jax import lax
from jax.experimental import pallas as pl
from jax.experimental.pallas import tpu as pltpu
from jax.sharding import PartitionSpec as P

HEAD_DIM = 64
EPSILON = 1e-05
SCALE = HEAD_DIM ** (-0.5)
MASKED = -1e30
CHUNK = 64
HURRY = 20
VMEM_BYTES = 16 * 1024 * 1024
GELU_SCALE = 0.7978845608
GELU_CUBE = 0.044715
LOW = jnp.bfloat16
WIDE = jnp.float32


def swap(value, axis, bit):
    count = lax.axis_size(axis)
    return lax.ppermute(value, axis, [(at, at ^ bit) for at in range(count)])


def shift(value, axis, by):
    count = lax.axis_size(axis)
    return lax.ppermute(value, axis, [(at, (at + by) % count) for at in range(count)])


def transpose_homes(value):
    side = lax.axis_size("dp")
    pairs = [(a * side + b, b * side + a) for a in range(side) for b in range(side)]
    return lax.ppermute(value, ("dp", "fsdp"), pairs)


def after(value, *others):
    return lax.optimization_barrier((value,) + others)[0]


def gather_pieces(block, *before_last):
    pieces = [block]
    count = lax.axis_size("dp")
    for slot in range(1, count):
        low_bit = slot & -slot
        source = pieces[slot ^ low_bit]
        if before_last and slot == count - 1:
            source = after(source, *before_last)
        pieces.append(swap(source, "dp", low_bit))
    return pieces


def send_pieces(sends, axis):
    return [swap(send, axis, slot) for slot, send in enumerate(sends, 1)]


def sum_rows(keep, send):
    assert lax.axis_size("dp") == 4
    near = swap(send, "dp", 1)
    rows = keep.shape[0] // 2
    far = swap((keep[rows:] + near[rows:].astype(WIDE)).astype(LOW), "dp", 2)
    return keep, near, far


def gather_direct(block, axis):
    return [block] + [swap(block, axis, slot) for slot in range(1, lax.axis_size(axis))]


def sum_doubling(value, axis):
    bit = 1
    while bit < lax.axis_size(axis):
        value = value + swap(value, axis, bit)
        bit *= 2
    return value


def sum_all(kept, arrived):
    total = kept
    for piece in arrived:
        total = total + piece.astype(WIDE)
    return total


def sum_replicas(value):
    if lax.axis_size("ctx") == 2:
        return value.astype(WIDE) + shift(value, "ctx", 1).astype(WIDE)
    return jnp.sum(lax.all_gather(value, "ctx").astype(WIDE), axis=0)


def matmul_nt(left, right):
    return lax.dot_general(left, right, (((1,), (1,)), ((), ())), preferred_element_type=WIDE)


def matmul_nn(left, right):
    return lax.dot_general(left, right, (((1,), (0,)), ((), ())), preferred_element_type=WIDE)


def matmul_tn(left, right):
    return lax.dot_general(left, right, (((0,), (0,)), ((), ())), preferred_element_type=WIDE)


def visible_block(place_ref, start, block_rows, columns):
    slot = start // block_rows
    query_pos = place_ref[slot] * block_rows + start % block_rows
    query_pos = query_pos + lax.broadcasted_iota(jnp.int32, (CHUNK, columns), 0)
    lane = lax.broadcasted_iota(jnp.int32, (CHUNK, columns), 1)
    key_pos = lane
    for at in range(columns // block_rows):
        inside = (lane >= at * block_rows) & (lane < (at + 1) * block_rows)
        key_pos = jnp.where(inside, place_ref[at] * block_rows + lane - at * block_rows, key_pos)
    return key_pos <= query_pos


def columns_of(head):
    return slice(head * HEAD_DIM, (head + 1) * HEAD_DIM)


def own_forward(heads, block_rows, place_ref, kvq_ref, acc_ref, stat_ref, score, prob):
    width = heads * HEAD_DIM
    rows = kvq_ref.shape[0]
    for head in range(heads):
        query = kvq_ref[:, 2 * width + head * HEAD_DIM : 2 * width + (head + 1) * HEAD_DIM]
        score[...] = matmul_nt(query, kvq_ref[:, columns_of(head)])

        def chunk(step, carry):
            start = pl.multiple_of(step * CHUNK, CHUNK)
            seen = visible_block(place_ref, start, block_rows, rows)
            scores = jnp.where(seen, score[pl.ds(start, CHUNK), :] * SCALE, MASKED)
            highest = jnp.max(scores, axis=1, keepdims=True)
            weight = jnp.exp(scores - highest)
            stat_ref[pl.ds(start, CHUNK), head : head + 1] = highest
            stat_ref[pl.ds(start, CHUNK), heads + head : heads + head + 1] = jnp.sum(
                weight, axis=1, keepdims=True
            )
            prob[pl.ds(start, CHUNK), :] = weight.astype(LOW)
            return carry

        lax.fori_loop(0, rows // CHUNK, chunk, 0)
        value = kvq_ref[:, width + head * HEAD_DIM : width + (head + 1) * HEAD_DIM]
        acc_ref[:, columns_of(head)] = matmul_nn(prob[...], value)


def earlier_forward(
    heads, slots, place_ref, kvq_ref, kv_ref, acc_in, stat_in, acc_ref, low_ref, stat_ref, score,
    prob, fade
):
    width = heads * HEAD_DIM
    rows = kvq_ref.shape[0]
    acc_ref[...] = acc_in[...]
    stat_ref[...] = stat_in[...]
    for piece in range(kv_ref.shape[0]):

        @pl.when(place_ref[slots] > piece)
        def _visit(piece=piece):
            for head in range(heads):
                query = kvq_ref[:, 2 * width + head * HEAD_DIM : 2 * width + (head + 1) * HEAD_DIM]
                score[...] = matmul_nt(query, kv_ref[piece, :, columns_of(head)])

                def chunk(step, carry):
                    here = pl.ds(pl.multiple_of(step * CHUNK, CHUNK), CHUNK)
                    scores = score[here, :] * SCALE
                    old = stat_ref[here, head : head + 1]
                    highest = jnp.maximum(old, jnp.max(scores, axis=1, keepdims=True))
                    weight = jnp.exp(scores - highest)
                    fading = jnp.exp(old - highest)
                    stat_ref[here, head : head + 1] = highest
                    total = stat_ref[here, heads + head : heads + head + 1]
                    stat_ref[here, heads + head : heads + head + 1] = total * fading + jnp.sum(
                        weight, axis=1, keepdims=True
                    )
                    fade[here, :] = jnp.broadcast_to(fading, (CHUNK, HEAD_DIM))
                    prob[here, :] = weight.astype(LOW)
                    return carry

                lax.fori_loop(0, rows // CHUNK, chunk, 0)
                value = kv_ref[piece, :, width + head * HEAD_DIM : width + (head + 1) * HEAD_DIM]
                acc_ref[:, columns_of(head)] = acc_ref[:, columns_of(head)] * fade[
                    ...
                ] + matmul_nn(prob[...], value)

    for head in range(heads):
        total = stat_ref[:, heads + head : heads + head + 1]
        context = acc_ref[:, columns_of(head)] / total
        acc_ref[:, columns_of(head)] = context
        low_ref[:, columns_of(head)] = context.astype(LOW)
        stat_ref[:, head : head + 1] = stat_ref[:, head : head + 1] + jnp.log(total)


def score_grads(here, seen, head, total, delta, score, dots, prob, grad):
    scores = score[here, :] * SCALE
    weight = jnp.exp(scores - total)
    if seen is not None:
        weight = jnp.where(seen, weight, 0.0)
    prob[here, :] = weight.astype(LOW)
    grad[here, :] = (weight * (dots[here, :] - delta) * SCALE).astype(LOW)


def delta_of(here, head, context_ref, ctx_grad_ref):
    product = context_ref[here, columns_of(head)] * ctx_grad_ref[here, columns_of(head)].astype(WIDE)
    return jnp.sum(product, axis=1, keepdims=True)


def earlier_backward(
    heads, slots, place_ref, kvq_ref, kv_ref, ctx_grad_ref, context_ref, stat_ref, query_grad_ref,
    kv_grad_ref, score, dots, prob, grad
):
    width = heads * HEAD_DIM
    rows = kvq_ref.shape[0]
    query_grad_ref[...] = jnp.zeros_like(query_grad_ref)
    for piece in range(kv_ref.shape[0]):

        @pl.when(place_ref[slots] <= piece)
        def _skip(piece=piece):
            kv_grad_ref[piece] = jnp.zeros(kv_grad_ref.shape[1:], kv_grad_ref.dtype)

        @pl.when(place_ref[slots] > piece)
        def _visit(piece=piece):
            for head in range(heads):
                query = kvq_ref[:, 2 * width + head * HEAD_DIM : 2 * width + (head + 1) * HEAD_DIM]
                value_at = slice(width + head * HEAD_DIM, width + (head + 1) * HEAD_DIM)
                key = kv_ref[piece, :, columns_of(head)]
                out_grad = ctx_grad_ref[:, columns_of(head)]
                score[...] = matmul_nt(query, key)
                dots[...] = matmul_nt(out_grad, kv_ref[piece, :, value_at])

                def chunk(step, carry):
                    here = pl.ds(pl.multiple_of(step * CHUNK, CHUNK), CHUNK)
                    total = stat_ref[here, head : head + 1]
                    delta = delta_of(here, head, context_ref, ctx_grad_ref)
                    score_grads(here, None, head, total, delta, score, dots, prob, grad)
                    return carry

                lax.fori_loop(0, rows // CHUNK, chunk, 0)
                kv_grad_ref[piece, :, columns_of(head)] = matmul_tn(grad[...], query).astype(LOW)
                kv_grad_ref[piece, :, value_at] = matmul_tn(prob[...], out_grad).astype(LOW)
                query_grad_ref[:, columns_of(head)] += matmul_nn(grad[...], key)


def own_backward(
    heads, block_rows, place_ref, kvq_ref, ctx_grad_ref, context_ref, stat_ref, query_grad_in,
    grad_ref, score, dots, prob, grad
):
    width = heads * HEAD_DIM
    rows = kvq_ref.shape[0]
    for head in range(heads):
        query_at = slice(2 * width + head * HEAD_DIM, 2 * width + (head + 1) * HEAD_DIM)
        value_at = slice(width + head * HEAD_DIM, width + (head + 1) * HEAD_DIM)
        query = kvq_ref[:, query_at]
        key = kvq_ref[:, columns_of(head)]
        out_grad = ctx_grad_ref[:, columns_of(head)]
        score[...] = matmul_nt(query, key)
        dots[...] = matmul_nt(out_grad, kvq_ref[:, value_at])

        def chunk(step, carry):
            start = pl.multiple_of(step * CHUNK, CHUNK)
            here = pl.ds(start, CHUNK)
            seen = visible_block(place_ref, start, block_rows, rows)
            total = stat_ref[here, head : head + 1]
            delta = delta_of(here, head, context_ref, ctx_grad_ref)
            score_grads(here, seen, head, total, delta, score, dots, prob, grad)
            return carry

        lax.fori_loop(0, rows // CHUNK, chunk, 0)
        grad_ref[:, columns_of(head)] = matmul_tn(grad[...], query)
        grad_ref[:, value_at] = matmul_tn(prob[...], out_grad)
        grad_ref[:, query_at] = query_grad_in[:, columns_of(head)] + matmul_nn(grad[...], key)


def normalize(values):
    centered = values - jnp.mean(values, axis=-1, keepdims=True)
    spread = jnp.mean(centered * centered, axis=-1, keepdims=True)
    inverse = lax.rsqrt(spread + EPSILON)
    return centered * inverse, inverse


def normalize_back(grad, gain, hat, inverse):
    scaled = grad * gain
    mean_scaled = jnp.mean(scaled, axis=-1, keepdims=True)
    mean_product = jnp.mean(scaled * hat, axis=-1, keepdims=True)
    part = inverse * (scaled - mean_scaled - hat * mean_product)
    gain_grad = jnp.sum(grad * hat, axis=0, keepdims=True)
    return part, gain_grad, jnp.sum(grad, axis=0, keepdims=True)


def take(refs, *counts):
    groups, at = [], 0
    for count in counts:
        if count is None:
            groups.append(refs[at])
            at += 1
        else:
            groups.append(refs[at : at + count])
            at += count
    return groups


def place_shards(meta_ref, parts, pieces, out_ref):
    rows = pieces[0].shape[0]
    for deep, piece in enumerate(pieces):
        start = pl.multiple_of((meta_ref[parts + 1] ^ deep) * rows, 16)
        out_ref[pl.ds(start, rows), :] = piece[...]


def stack_rows(pieces, out_ref):
    rows = pieces[0].shape[0]
    for slot, piece in enumerate(pieces):
        out_ref[slot * rows : (slot + 1) * rows, :] = piece[...]


def emit_rows(partial, keep_ref, send_ref):
    rows = keep_ref.shape[0] // 2
    for pair in range(2):
        here = slice(pair * rows, (pair + 1) * rows)
        keep_ref[here, :] = partial[2 * pair * rows : (2 * pair + 1) * rows]
        send_ref[here, :] = partial[(2 * pair + 1) * rows : (2 * pair + 2) * rows].astype(LOW)


def row_sum(keep, near, far):
    rows = far.shape[0]
    return keep[:rows, :] + near[:rows, :].astype(WIDE) + far[...].astype(WIDE)


def emit_blocks(meta_ref, parts, depth, whole_ref, keep_ref, send_refs):
    rows = keep_ref.shape[1]
    for deep in range(depth):
        member = meta_ref[parts + 1] ^ deep
        for slot in range(parts):
            start = pl.multiple_of((meta_ref[slot] * depth + member) * rows, 16)
            block = whole_ref[pl.ds(start, rows), :]
            if deep:
                send_refs[deep - 1][slot] = block.astype(LOW)
            else:
                keep_ref[slot] = block


def emit_shards(meta_ref, parts, whole_ref, keep_ref, send_refs):
    rows = keep_ref.shape[0]
    for deep in range(len(send_refs) + 1):
        start = pl.multiple_of((meta_ref[parts + 1] ^ deep) * rows, 16)
        block = whole_ref[pl.ds(start, rows), :]
        if deep:
            send_refs[deep - 1][...] = block.astype(LOW)
        else:
            keep_ref[...] = block


def stack_kernel(parts, depth, halves, meta_ref, *refs):
    split, down_weight, out_weight, kvq_own, kvq_other, feed_own, feed_other, vectors, folded = (
        take(refs, parts, *([None] * 8))
    )
    columns = kvq_own.shape[1]
    shard = split[0].shape[0]
    model = vectors.shape[1]
    width = columns // 3
    hidden_shard = down_weight.shape[0]
    member = meta_ref[parts + 1]

    def placed(slot, start):
        rows = split[slot][:, columns : -feed_own.shape[1]]
        row = lax.broadcasted_iota(jnp.int32, (rows.shape[1], model), 0)
        column = lax.broadcasted_iota(jnp.int32, (rows.shape[1], model), 1)
        chosen = jnp.where((column == start + row) & (row < shard), 1.0, 0.0)
        return matmul_nn(rows, chosen.astype(LOW))

    whole = sum(placed(slot, (meta_ref[slot] * depth + member) * shard) for slot in range(parts))
    vectors[...] = jnp.zeros_like(vectors)
    vectors[0:6, :] = whole[0:6]
    vectors[6:7, :] = (
        placed(0, width + member * shard)[7:8] + placed(0, 2 * width + member * shard)[6:7]
    )
    vectors[7:8, :] = sum(
        placed(0, member * hidden_shard + at * shard)[8 + at : 9 + at]
        for at in range(hidden_shard // shard)
    )
    vectors[8:16, : model - columns] = vectors[0:8, columns:]
    rest = model - columns
    folded[:shard, :] = out_weight[:, :columns]
    for at in range(columns // rest):
        folded[shard:, at * rest : (at + 1) * rest] = out_weight[at * 16 : (at + 1) * 16, columns:]
    slots = parts // 2
    extra = folded.shape[0] // 2

    def kvq(half, out):
        for slot in range(slots):
            out[slot * shard : (slot + 1) * shard, :] = split[half * slots + slot][:, :columns]
        start = slots * shard
        out[start : start + extra, :] = folded[half * extra : (half + 1) * extra, :].astype(LOW)
        out[start + extra :, :] = vectors[:, :columns].astype(LOW)

    def feed(half, out):
        if half:
            out[...] = down_weight[...].astype(LOW)
        else:
            for slot in range(parts):
                out[slot * shard : (slot + 1) * shard, :] = split[slot][:, -out.shape[1] :]

    def emit(first):
        kvq(first, kvq_own)
        kvq(1 - first, kvq_other)
        feed(first, feed_own)
        feed(1 - first, feed_other)

    if halves:
        pl.when(meta_ref[parts] == 0)(lambda: emit(0))
        pl.when(meta_ref[parts] != 0)(lambda: emit(1))
    else:
        emit(0)


def split_kernel(parts, width, meta_ref, qkv_ref, up_ref, *refs):
    vectors, outs, packed = take(refs, None, parts, None)
    model = parts * width
    shard = qkv_ref.shape[0]
    packed[...] = jnp.zeros_like(packed)
    values = vectors[...].reshape(1, vectors.shape[0])
    for row in range(vectors.shape[0] // shard):
        packed[row : row + 1, :shard] = values[:, row * shard : (row + 1) * shard]
    part = up_ref.shape[1] // parts
    for case in range(parts):

        @pl.when(meta_ref[0] == case)
        def _case(case=case):
            for slot in range(parts):
                owner = case ^ slot
                for at, first in enumerate((model, 2 * model, 0)):
                    start = first + owner * width
                    outs[slot][:, at * width : (at + 1) * width] = qkv_ref[
                        :, start : start + width
                    ].astype(LOW)
                outs[slot][:, 3 * width : -part] = packed[...].astype(LOW)
                outs[slot][:, -part:] = up_ref[:, owner * part : (owner + 1) * part].astype(LOW)


def join_kernel(parts, width, meta_ref, *refs):
    pieces, up, out_ref, up_ref, vectors = take(refs, parts, parts, None, None, None)
    model = parts * width
    shard = out_ref.shape[0]
    hidden = up_ref.shape[1] // parts
    for case in range(parts):

        @pl.when(meta_ref[0] == case)
        def _case(case=case):
            for slot in range(parts):
                owner = case ^ slot
                for at, first in enumerate((model, 2 * model, 0)):
                    start = first + owner * width
                    out_ref[:, start : start + width] = pieces[slot][
                        :shard, at * width : (at + 1) * width
                    ].astype(WIDE)
                up_ref[:, owner * hidden : (owner + 1) * hidden] = up[slot][...].astype(WIDE)

    vectors[...] = sum(piece[shard:, :].astype(WIDE) for piece in pieces)


def in_order(halves, parts, meta_ref, place, own, other):
    if halves:
        pl.when(meta_ref[parts] == 0)(lambda: place(own, other))
        pl.when(meta_ref[parts] != 0)(lambda: place(other, own))
    else:
        place(own, other)


def project_kernel(parts, depth, halves, meta_ref, *refs):
    tokens, own, other, kvq_ref, kv_ref, matrix_ref, norm_ref, vectors_ref = take(
        refs, parts, depth, depth, None, None, None, None, None
    )
    columns = kvq_ref.shape[1]
    rows = tokens[0].shape[0]
    shard = matrix_ref.shape[0] // (parts * depth)
    slots = parts // 2

    def place(*pair):
        for half, pieces in enumerate(pair):
            for deep in range(depth):
                member = meta_ref[parts + 1] ^ deep
                for slot in range(slots):
                    row = (meta_ref[half * slots + slot] * depth + member) * shard
                    matrix_ref[pl.ds(pl.multiple_of(row, 16), shard), :] = pieces[deep][
                        slot * shard : (slot + 1) * shard, :
                    ]

    in_order(halves, parts, meta_ref, place, own, other)
    folded = sum(piece[-16:, :].astype(WIDE) for piece in own)
    vectors_ref[:, :columns] = folded[:8]
    vectors_ref[:, columns:] = folded[8:, : vectors_ref.shape[1] - columns]
    for slot, piece in enumerate(tokens):

        def chunk(step, carry, slot=slot, piece=piece):
            here = pl.multiple_of(step * CHUNK, CHUNK)
            hat, _ = normalize(piece[pl.ds(here, CHUNK), :].astype(WIDE))
            norm_ref[pl.ds(slot * rows + here, CHUNK), :] = (
                hat * vectors_ref[0:1, :] + vectors_ref[1:2, :]
            ).astype(LOW)
            return carry

        lax.fori_loop(0, rows // CHUNK, chunk, 0)
    low = (matmul_nn(norm_ref[...], matrix_ref[...]) + vectors_ref[6:7, :columns]).astype(LOW)
    kvq_ref[...] = low
    kv_ref[...] = low[:, : kv_ref.shape[1]]


def mix_kernel(parts, depth, halves, meta_ref, *refs):
    low, own, other, matrix, keep, send = take(refs, None, depth, depth, None, None, None)
    shard = matrix.shape[0] // depth
    columns = own[0].shape[1]
    rest = matrix.shape[1] - columns
    at_first = parts // 2 * shard
    extra = own[0].shape[0] - at_first - 16

    def place(first, second):
        for deep in range(depth):
            start = pl.multiple_of((meta_ref[parts + 1] ^ deep) * shard, 16)
            split = at_first + shard - extra
            matrix[pl.ds(start, extra), :columns] = first[deep][at_first : at_first + extra, :]
            matrix[pl.ds(start + extra, shard - extra), :columns] = second[deep][
                at_first:split, :
            ]
            for at in range(columns // rest):
                matrix[pl.ds(start + at * 16, 16), columns:] = second[deep][
                    split : split + 16, at * rest : (at + 1) * rest
                ]

    in_order(halves, parts, meta_ref, place, own, other)
    emit_rows(matmul_nn(low[...], matrix[...]), keep, send)


def second_norm_kernel(parts, meta_ref, *refs):
    keep, near, far, tokens, vectors, out, attended_ref = refs
    attended = row_sum(keep, near, far) + vectors[4:5, :]
    attended_ref[...] = attended
    hat, _ = normalize(tokens[...].astype(WIDE) + attended)
    out[...] = (hat * vectors[2:3, :] + vectors[3:4, :]).astype(LOW)


def feed_kernel(parts, depth, halves, meta_ref, *refs):
    (
        norm, branch, own, other, vectors, keep, send, hidden, inner_grad, norm_all, branch_all,
        down_all, up_bias, up_all, inner, grad,
    ) = take(refs, parts, parts, depth, depth, *([None] * 12))

    def place(up, down):
        shard = up_all.shape[0] // (parts * depth)
        for deep in range(depth):
            member = meta_ref[parts + 1] ^ deep
            for slot in range(parts):
                start = pl.multiple_of((meta_ref[slot] * depth + member) * shard, 16)
                up_all[pl.ds(start, shard), :] = up[deep][slot * shard : (slot + 1) * shard, :]
        place_shards(meta_ref, parts, down, down_all)

    if halves:
        pl.when(meta_ref[parts] == 0)(lambda: place(own, other))
        pl.when(meta_ref[parts] != 0)(lambda: place(other, own))
    else:
        place(own, other)
    stack_rows(norm, norm_all)
    stack_rows(branch, branch_all)
    inner[...] = matmul_nn(norm_all[...], up_all[...])
    grad[...] = matmul_nt(branch_all[...], down_all[...])
    up_bias[...] = jnp.zeros_like(up_bias)

    def chunk(step, carry):
        here = pl.ds(pl.multiple_of(step * CHUNK, CHUNK), CHUNK)
        value = inner[here, :] + vectors[7:8, :]
        square = value * value
        bent = jnp.tanh(GELU_SCALE * (value + GELU_CUBE * square * value))
        hidden[here, :] = (0.5 * value * (1.0 + bent)).astype(LOW)
        slope = 0.5 * (1.0 + bent) + 0.5 * value * (1.0 - bent * bent) * GELU_SCALE * (
            1.0 + 3.0 * GELU_CUBE * square
        )
        low = (grad[here, :] * slope).astype(LOW)
        inner_grad[here, :] = low
        up_bias[...] += jnp.sum(low.astype(WIDE), axis=0, keepdims=True)
        return carry

    lax.fori_loop(0, inner.shape[0] // CHUNK, chunk, 0)
    emit_rows(matmul_nt(inner_grad[...], up_all[...]), keep, send)


def feed_grad_kernel(parts, depth, halves, meta_ref, *refs):
    hidden, inner_grad, norm_all, branch_all, down_all, kept, *sent, fed_keep, fed_send, whole = refs
    hidden_shard = hidden.shape[1] // depth
    shard = norm_all.shape[1] // (parts * depth)

    def emit(half, outs):
        for deep in range(depth):
            out = outs[deep * len(outs) // depth].at[deep % (depth // len(outs))]
            member = meta_ref[parts + 1] ^ deep
            if half:
                start = pl.multiple_of(member * hidden_shard, 16)
                out[...] = whole[pl.ds(start, hidden_shard), :].astype(out.dtype)
            else:
                for slot in range(parts):
                    start = pl.multiple_of((meta_ref[slot] * depth + member) * shard, 16)
                    out[slot * shard : (slot + 1) * shard, :] = whole[
                        pl.ds(start, shard), :
                    ].astype(out.dtype)

    for half in range(2):
        if half:
            whole[...] = matmul_tn(hidden[...], branch_all[...])
        else:
            whole[...] = matmul_tn(norm_all[...], inner_grad[...])
        if halves:
            pl.when(meta_ref[parts] == half)(functools.partial(emit, half, [kept]))
            pl.when(meta_ref[parts] != half)(functools.partial(emit, half, sent))
        else:
            emit(half, sent if half else [kept])
    emit_rows(matmul_nn(hidden[...], down_all[...]), fed_keep, fed_send)


def fold_kernel(count, meta_ref, kept_ref, *refs):
    arrived, keep_ref, send_refs = refs[:count], refs[count], refs[count + 1 :]
    depth = kept_ref.shape[0]
    for deep in range(depth):
        piece = arrived[deep * count // depth][deep % (depth // count)].astype(WIDE)
        if deep:
            send_refs[deep - 1][...] = (kept_ref[deep] + piece).astype(LOW)
        else:
            keep_ref[...] = kept_ref[deep] + piece


def second_norm_grad_kernel(parts, meta_ref, *refs):
    keep, near, far, tokens, attended, branch, vectors, attn_grad, mixed_part, sums = refs
    grad = row_sum(keep, near, far)
    hat, inverse = normalize(tokens[...].astype(WIDE) + attended[...])
    part, gain_grad, bias_grad = normalize_back(grad, vectors[2:3, :], hat, inverse)
    mixed_part[...] = part
    branch_rows = branch[...].astype(WIDE)
    low = (branch_rows + part).astype(LOW)
    attn_grad[...] = low
    sums[...] = jnp.zeros_like(sums)
    sums[2:3, :] = gain_grad
    sums[3:4, :] = bias_grad
    sums[4:5, :] = jnp.sum(low.astype(WIDE), axis=0, keepdims=True)
    sums[5:6, :] = jnp.sum(branch_rows, axis=0, keepdims=True)


def context_grad_kernel(parts, heads, meta_ref, *refs):
    (
        attn, matrix, kvq, kv, context, stat, ctx_grad, attn_all, query_grad, kv_grad, score, dots,
        prob, grad,
    ) = take(refs, parts, *([None] * 13))
    stack_rows(attn, attn_all)
    ctx_grad[...] = matmul_nt(attn_all[...], matrix[...]).astype(LOW)
    earlier_backward(
        heads, parts, meta_ref, kvq, kv, ctx_grad, context, stat, query_grad, kv_grad, score, dots,
        prob, grad,
    )


def own_grad_kernel(parts, depth, heads, rows, meta_ref, *refs):
    (
        kvq, ctx_grad, context, stat, query_grad, low, attn_all, kvq_grad, out_grad, score, dots,
        prob, grad,
    ) = refs
    own_backward(
        heads, rows, meta_ref, kvq, ctx_grad, context, stat, query_grad, kvq_grad, score, dots,
        prob, grad,
    )
    out_grad[...] = matmul_tn(low[...], attn_all[...])


def projection_back_kernel(parts, meta_ref, *refs):
    own, arrived, matrix, kvq_grad, keep, send, bias = refs
    kv_width = arrived.shape[2]
    total = own[:, :kv_width]
    for piece in range(arrived.shape[0]):
        total = total + arrived[piece].astype(WIDE)
    kvq_grad[:, :kv_width] = total.astype(LOW)
    kvq_grad[:, kv_width:] = own[:, kv_width:].astype(LOW)
    emit_rows(matmul_nt(kvq_grad[...], matrix[...]), keep, send)
    bias[...] = jnp.sum(kvq_grad[...].astype(WIDE), axis=0, keepdims=True)


def projection_grad_kernel(parts, depth, halves, meta_ref, *refs):
    norm, kvq_grad, out_grad, kept, sent, whole, folded = refs
    columns = kvq_grad.shape[1]
    model = norm.shape[1]
    shard = model // (parts * depth)
    rest = model - columns
    slots = parts // 2
    extra = kept.shape[1] - slots * shard
    whole[...] = matmul_tn(norm[...], kvq_grad[...])
    sent[:, kept.shape[1] :] = jnp.zeros_like(sent[:, kept.shape[1] :])

    def emit(half, out):
        for deep in range(depth):
            member = meta_ref[parts + 1] ^ deep
            for slot in range(slots):
                row = (meta_ref[half * slots + slot] * depth + member) * shard
                out[deep, slot * shard : (slot + 1) * shard] = whole[
                    pl.ds(pl.multiple_of(row, 16), shard), :
                ].astype(out.dtype)
            start = pl.multiple_of(member * shard, 16)
            folded[:shard, :] = out_grad[pl.ds(start, shard), :columns]
            for at in range(columns // rest):
                piece = out_grad[pl.ds(start + at * 16, 16), columns:]
                folded[shard:, at * rest : (at + 1) * rest] = piece
            first = slots * shard
            out[deep, first : first + extra] = folded[half * extra : (half + 1) * extra, :].astype(
                out.dtype
            )

    for half in range(2):
        if halves:
            pl.when(meta_ref[parts] == half)(functools.partial(emit, half, kept))
            pl.when(meta_ref[parts] != half)(functools.partial(emit, half, sent))
        else:
            emit(half, sent if half else kept)


def fold_vectors(sums, folded):
    rest = sums.shape[1] - folded.shape[1]
    folded[...] = jnp.zeros_like(folded)
    folded[0:8, :] = sums[:, : folded.shape[1]]
    folded[8:16, :rest] = sums[:, folded.shape[1] :]


def fold_share_kernel(meta_ref, kept, arrived, sums, keep, *refs):
    sends, folded = refs[:-1], refs[-1]
    rows = kept.shape[1]
    fold_vectors(sums, folded)
    keep[:rows, :] = kept[0] + arrived[0, :rows].astype(WIDE)
    keep[rows:, :] = folded[...]
    for deep, send in enumerate(sends, 1):
        send[:rows, :] = (kept[deep] + arrived[deep, :rows].astype(WIDE)).astype(LOW)
        send[rows:, :] = folded[...].astype(LOW)


def unfold_feed_kernel(parts, halves, meta_ref, mine, other, *refs):
    pieces, down_ref = refs[:parts], refs[parts]
    shard = pieces[0].shape[0]

    def place(up, down):
        for slot in range(parts):
            pieces[slot][...] = up[slot * shard : (slot + 1) * shard, :].astype(LOW)
        down_ref[...] = down[...].astype(WIDE)

    in_order(halves, parts, meta_ref, place, mine, other)


def unfold_kernel(parts, halves, meta_ref, mine, arrived, *refs):
    sums, pieces, out_ref, vectors, folded = take(
        refs, 0 if halves else 1, parts, None, None, None
    )
    shard, columns = pieces[0].shape[0] - 16, vectors.shape[1]
    rest = out_ref.shape[1] - columns
    slots = parts // 2
    extra = folded.shape[0] // 2

    def unfold(half, ref):
        for slot in range(slots):
            pieces[half * slots + slot][:shard, :columns] = ref[
                slot * shard : (slot + 1) * shard, :
            ].astype(LOW)
        start = slots * shard
        folded[half * extra : (half + 1) * extra, :] = ref[start : start + extra, :].astype(WIDE)

    if halves:
        first = meta_ref[parts] == 0
        for half in range(2):
            pl.when(first)(functools.partial(unfold, half, arrived if half else mine))
            pl.when(jnp.logical_not(first))(
                functools.partial(unfold, half, mine if half else arrived)
            )
        start = slots * shard + extra
        vectors[...] = mine[start:, :].astype(WIDE) + arrived[start:, :].astype(WIDE)
    else:
        unfold(0, mine)
        unfold(1, arrived)
        fold_vectors(sums[0], vectors)
    for piece in pieces:
        piece[shard:, :] = vectors[...].astype(LOW)
    out_ref[:, :columns] = folded[:shard, :]
    for at in range(columns // rest):
        out_ref[at * 16 : (at + 1) * 16, columns:] = folded[shard:, at * rest : (at + 1) * rest]


def first_norm_grad_kernel(parts, meta_ref, *refs):
    keep, near, far, tokens, vectors, mixed_part, sums_in, kvq_bias, up_bias, out, sums = refs
    grad = row_sum(keep, near, far)
    hat, inverse = normalize(tokens[...].astype(WIDE))
    part, gain_grad, bias_grad = normalize_back(grad, vectors[0:1, :], hat, inverse)
    out[...] = (mixed_part[...] + part).astype(LOW)
    sums[...] = sums_in[...]
    sums[0:1, :] = gain_grad
    sums[1:2, :] = bias_grad
    sums[6:7, : kvq_bias.shape[1]] = kvq_bias[...]
    sums[7:8, :] = up_bias[...]


def local_call(kernel, operands, results, scratch=(), flops=0):
    smem = pl.BlockSpec(memory_space=pltpu.SMEM)
    vmem = pl.BlockSpec(memory_space=pltpu.VMEM)
    moved = sum(each.size * each.dtype.itemsize for each in tuple(operands) + tuple(results))
    return pl.pallas_call(
        kernel,
        name=getattr(kernel, "func", kernel).__name__,
        out_shape=tuple(results),
        in_specs=[smem] + [vmem] * (len(operands) - 1),
        out_specs=tuple([vmem] * len(results)),
        scratch_shapes=list(scratch),
        compiler_params=pltpu.CompilerParams(vmem_limit_bytes=VMEM_BYTES),
        cost_estimate=pl.CostEstimate(
            flops=flops // HURRY, bytes_accessed=moved // HURRY, transcendentals=0
        ),
    )(*operands)


def low_like(*shape):
    return jax.ShapeDtypeStruct(shape, LOW)


def wide_like(*shape):
    return jax.ShapeDtypeStruct(shape, WIDE)


def local(
    tokens, cotangent, ln1_gain, ln1_bias, qkv_weight, q_bias, v_bias, out_weight, out_bias,
    ln2_gain, ln2_bias, fc1_weight, fc1_bias, fc2_weight, fc2_bias,
):
    parts = lax.axis_size("dp")
    depth = lax.axis_size("fsdp")
    contexts = lax.axis_size("ctx")
    assert parts == depth
    mine = lax.axis_index("dp")
    deep = lax.axis_index("fsdp")
    rows, model = tokens.shape[1:]
    shard = ln1_gain.shape[0]
    heads = model // HEAD_DIM // parts
    width = heads * HEAD_DIM
    hidden_shard = fc1_bias.shape[0]
    hidden_part = hidden_shard * depth
    group = parts * rows
    meta = jnp.stack(
        [mine ^ slot for slot in range(parts)] + [lax.axis_index("ctx"), deep]
    ).astype(jnp.int32)

    halves = contexts == 2
    padded = -(-3 * width // 128) * 128
    split = local_call(
        functools.partial(split_kernel, parts, width),
        (
            meta, qkv_weight, fc1_weight,
            jnp.concatenate(
                [
                    ln1_gain, ln1_bias, ln2_gain, ln2_bias, out_bias, fc2_bias, q_bias, v_bias,
                    fc1_bias,
                ]
            ),
        ),
        [low_like(shard, padded + hidden_part)] * parts,
        [pltpu.VMEM((shard, padded - 3 * width), WIDE)],
    )
    split_arrived = send_pieces(split[1:], "dp")
    folded_rows = shard * model // (3 * width)
    half_rows = parts // 2 * shard + folded_rows // 2 + 16
    kvq_mine, kvq_theirs, feed_mine, feed_theirs = local_call(
        functools.partial(stack_kernel, parts, depth, halves),
        (meta, split[0], *split_arrived, fc2_weight, out_weight),
        [low_like(half_rows, 3 * width)] * 2 + [low_like(hidden_shard, model)] * 2,
        [pltpu.VMEM((16, model), WIDE), pltpu.VMEM((folded_rows, 3 * width), WIDE)],
    )
    kvq_own = gather_direct(kvq_mine, "fsdp")
    if halves:
        kvq_other = [kvq_theirs] + [shift(piece, "ctx", 1) for piece in kvq_own[1:]]
    else:
        kvq_other = gather_direct(kvq_theirs, "fsdp")

    token_rows = transpose_homes(after(tokens[0].astype(LOW), kvq_mine))
    pieces = gather_pieces(after(token_rows, kvq_own[-1]), *kvq_own[1:], kvq_other[1], kvq_other[-1])

    kvq, kv, kvq_matrix, norm1_all, vectors = local_call(
        functools.partial(project_kernel, parts, depth, halves),
        (meta, *pieces, *kvq_own, *kvq_other),
        [
            low_like(group, 3 * width),
            low_like(group, 2 * width),
            low_like(model, 3 * width),
            low_like(group, model),
            wide_like(8, model),
        ],
        flops=2 * group * model * 3 * width,
    )
    kv_earlier = jnp.stack([shift(kv, "ctx", by) for by in range(1, contexts)])

    if halves:
        own_half = gather_direct(after(feed_mine, *kvq_own[1:]), "fsdp")
    else:
        own_half = gather_direct(feed_mine, "fsdp")
        other_half = gather_direct(feed_theirs, "fsdp")
    grad_rows = transpose_homes(after(cotangent[0].astype(LOW), own_half[1]))
    branch_pieces = gather_pieces(grad_rows)

    score_flops = 2 * group * group * width
    wide_square = pltpu.VMEM((group, group), WIDE)
    low_square = pltpu.VMEM((group, group), LOW)
    acc, stat = local_call(
        functools.partial(own_forward, heads, rows),
        (meta, after(kvq, own_half[2])),
        [wide_like(group, width), wide_like(group, 128)],
        [wide_square, low_square],
        flops=2 * score_flops,
    )
    if halves:
        other_half = [feed_theirs, shift(own_half[1], "ctx", 1)]
        other_half.append(shift(after(own_half[2], acc), "ctx", 1))
        other_half += [shift(piece, "ctx", 1) for piece in own_half[3:]]
    context, context_low, stat = local_call(
        functools.partial(earlier_forward, heads, parts),
        (meta, kvq, kv_earlier, after(acc, own_half[1]), stat),
        [wide_like(group, width), low_like(group, width), wide_like(group, 128)],
        [wide_square, low_square, pltpu.VMEM((group, HEAD_DIM), WIDE)],
        flops=2 * score_flops,
    )
    out_matrix, attended_keep, attended_send = local_call(
        functools.partial(mix_kernel, parts, depth, halves),
        (meta, after(context_low, *own_half[1:], other_half[2]), *kvq_own, *kvq_other),
        [low_like(width, model), wide_like(2 * rows, model), low_like(2 * rows, model)],
        flops=2 * group * width * model,
    )
    attended_sum = sum_rows(attended_keep, attended_send)
    norm2, attended = local_call(
        functools.partial(second_norm_kernel, parts),
        (meta, *attended_sum, token_rows, vectors),
        [low_like(rows, model), wide_like(rows, model)],
    )

    norm2_pieces = gather_pieces(norm2)
    norm2_keep, norm2_send, *rest = local_call(
        functools.partial(feed_kernel, parts, depth, halves),
        (meta, *norm2_pieces, *branch_pieces, *own_half, *other_half, vectors),
        [wide_like(2 * rows, model), low_like(2 * rows, model)]
        + [low_like(group, hidden_part)] * 2
        + [low_like(group, model)] * 2
        + [low_like(hidden_part, model), wide_like(1, hidden_part)],
        [
            pltpu.VMEM((model, hidden_part), LOW),
            pltpu.VMEM((group, hidden_part), WIDE),
            pltpu.VMEM((group, hidden_part), WIDE),
        ],
        flops=6 * group * model * hidden_part,
    )
    hidden, inner_grad, norm2_all, branch_all, down_matrix, up_bias = rest
    norm2_sum = sum_rows(norm2_keep, norm2_send)
    kept_half, *sent_half, fed_keep, fed_send = local_call(
        functools.partial(feed_grad_kernel, parts, depth, halves),
        (meta, hidden, inner_grad, norm2_all, branch_all, down_matrix),
        [
            wide_like(depth, hidden_shard, model),
            low_like(depth, hidden_shard, model),
            wide_like(2 * rows, model),
            low_like(2 * rows, model),
        ],
        [pltpu.VMEM((max(model, hidden_part), max(model, hidden_part)), WIDE)],
        flops=6 * group * model * hidden_part,
    )
    attn_grad, mixed_part, sums = local_call(
        functools.partial(second_norm_grad_kernel, parts),
        (
            meta, after(norm2_sum[0], fed_keep), *norm2_sum[1:], token_rows, attended, grad_rows,
            vectors,
        ),
        [low_like(rows, model), wide_like(rows, model), wide_like(8, model)],
    )
    attn_pieces = gather_pieces(attn_grad)

    def fold(kept, sent, *later):
        arrived = [shift(sent[0], "ctx", 1)]
        for piece in sent[1:]:
            arrived.append(shift(after(piece, arrived[-1]), "ctx", 1))
        shape = kept.shape[1:]
        keep, *sends = local_call(
            functools.partial(fold_kernel, len(sent)),
            (meta, after(kept, *later), *arrived),
            [wide_like(*shape)] + [low_like(*shape)] * (depth - 1),
        )
        return keep, sends

    def direct_totals(*grads):
        return [
            owner_sum(grad[0].astype(WIDE), send_pieces(list(grad[1:].astype(LOW)), "fsdp"))
            for grad in grads
        ]

    def owner_sum(keep, pieces):
        return sum_replicas(sum_all(keep, pieces).astype(LOW))

    fed_sum = sum_rows(fed_keep, after(fed_send, attn_pieces[-1]))

    ctx_grad, attn_all, query_grad, kv_grad = local_call(
        functools.partial(context_grad_kernel, parts, heads),
        (meta, *attn_pieces, out_matrix, kvq, kv_earlier, context, stat),
        [
            low_like(group, width),
            low_like(group, model),
            wide_like(group, width),
            low_like(*kv_earlier.shape),
        ],
        [wide_square, wide_square, low_square, low_square],
        flops=5 * score_flops,
    )
    if halves:
        half_keep, half_sends = fold(kept_half, sent_half, query_grad)
        farthest = swap(half_sends[-1], "fsdp", depth - 1)
        nearer = [after(send, farthest) for send in half_sends[:-1]]
        half_pieces = send_pieces(nearer, "fsdp") + [farthest]
    else:
        half_pieces = []
    if halves:
        query_grad = after(query_grad, half_keep)
    kv_arrived = jnp.stack(
        [shift(kv_grad[by - 1], "ctx", -by) for by in range(1, contexts)]
    )
    kvq_own, out_grad = local_call(
        functools.partial(own_grad_kernel, parts, depth, heads, rows),
        (meta, kvq, ctx_grad, context, stat, query_grad, context_low, attn_all),
        [wide_like(group, 3 * width), wide_like(width, model)],
        [wide_square, wide_square, low_square, low_square],
        flops=5 * score_flops,
    )
    kvq_grad, norm1_keep, norm1_send, kvq_bias = local_call(
        functools.partial(projection_back_kernel, parts),
        (meta, after(kvq_own, fed_sum[2], *half_pieces[-1:]), kv_arrived, kvq_matrix),
        [
            low_like(group, 3 * width),
            wide_like(2 * rows, model),
            low_like(2 * rows, model),
            wide_like(1, 3 * width),
        ],
        flops=2 * group * model * 3 * width,
    )
    norm1_sum = sum_rows(norm1_keep, norm1_send)
    share_rows = (parts * shard + shard * model // (3 * width)) // 2
    kept_share, sent_share = local_call(
        functools.partial(projection_grad_kernel, parts, depth, halves),
        (meta, norm1_all, after(kvq_grad, norm1_sum[1]), out_grad),
        [wide_like(depth, share_rows, 3 * width), low_like(depth, share_rows + 16, 3 * width)],
        [
            pltpu.VMEM((model, 3 * width), WIDE),
            pltpu.VMEM((shard * model // (3 * width), 3 * width), WIDE),
        ],
        flops=2 * group * model * 3 * width,
    )
    input_part, sums = local_call(
        functools.partial(first_norm_grad_kernel, parts),
        (
            meta, after(norm1_sum[0], kept_share), *norm1_sum[1:], token_rows, vectors, mixed_part,
            sums, kvq_bias, up_bias,
        ),
        [low_like(rows, model), wide_like(8, model)],
    )

    input_rows = transpose_homes(input_part)
    delta = row_sum(*fed_sum) + vectors[5:6] + attended
    delta_rows = transpose_homes(after(delta.astype(LOW), input_part))
    output = tokens[0] + delta_rows.astype(WIDE)
    if halves:
        shape = (share_rows + 16, 3 * width)
        share_keep, *share_sends = local_call(
            fold_share_kernel,
            (meta, after(kept_share, input_rows, delta_rows, *half_pieces[:-1]), shift(sent_share, "ctx", 1), sums),
            [wide_like(*shape)] + [low_like(*shape)] * (depth - 1),
            [pltpu.VMEM((16, 3 * width), WIDE)],
        )
        share_pieces = send_pieces(share_sends, "fsdp")
        mine_half = sum_all(after(half_keep, input_rows), half_pieces).astype(LOW)
        feed_totals = (mine_half, shift(mine_half, "ctx", 1))
        mine_share = sum_all(share_keep, share_pieces).astype(LOW)
        shares = (mine_share, shift(mine_share, "ctx", 1))
    else:
        share_pieces = []
        feed_totals = direct_totals(kept_half, sent_half[0])
        shares = (
            *direct_totals(kept_share, sent_share[:, :share_rows]), sum_replicas(sum_doubling(sums, "fsdp"))
        )
    *up_totals, down_total = local_call(
        functools.partial(unfold_feed_kernel, parts, halves),
        (meta, *feed_totals),
        [low_like(shard, hidden_part)] * parts + [wide_like(hidden_shard, model)],
    )
    up_arrived = send_pieces(up_totals[1:], "dp")
    *totals, out_total, vector_part = local_call(
        functools.partial(unfold_kernel, parts, halves),
        (meta, after(shares[0], *up_arrived), *shares[1:]),
        [low_like(shard + 16, 3 * width)] * parts
        + [wide_like(shard, model), wide_like(16, 3 * width)],
        [pltpu.VMEM((shard * model // (3 * width), 3 * width), WIDE)],
    )
    qkv_total, up_total, vector_total = local_call(
        functools.partial(join_kernel, parts, width),
        (meta, totals[0], *send_pieces(totals[1:], "dp"), up_totals[0], *up_arrived),
        [
            wide_like(shard, 3 * model),
            wide_like(shard, parts * hidden_part),
            wide_like(16, 3 * width),
        ],
    )
    input_grad = cotangent[0] + input_rows.astype(WIDE)

    def vector_at(source, row, start, size):
        late = start >= 3 * width
        count = 8 if row == 0 else 1
        at = (row + jnp.where(late, 8, 0), start - jnp.where(late, 3 * width, 0))
        return lax.dynamic_slice(source, at, (count, size))

    owned = vector_at(vector_total, 0, (mine * depth + deep) * shard, shard)
    value_bias = vector_at(vector_part, 6, width + deep * shard, shard)[0]
    query_bias = vector_at(vector_part, 6, 2 * width + deep * shard, shard)[0]
    inner_bias = vector_at(vector_part, 7, deep * hidden_shard, hidden_shard)[0]

    return (
        output[None],
        input_grad[None],
        owned[0],
        owned[1],
        qkv_total,
        query_bias,
        value_bias,
        out_total,
        owned[4],
        owned[2],
        owned[3],
        up_total,
        inner_bias,
        down_total,
        owned[5],
    )


def solution(mesh):
    rows = P("dp", ("ctx", "fsdp"), None)
    vector = P(("dp", "fsdp"))
    matrix = P(("dp", "fsdp"), None)
    parameters = (
        vector, vector, matrix, vector, vector, matrix, vector, vector, vector, matrix, vector,
        matrix, vector,
    )
    return jax.shard_map(
        local,
        mesh=mesh,
        in_specs=(rows, rows) + parameters,
        out_specs=(rows, rows) + parameters,
        check_vma=False,
    )
```
